32 devices in a mesh: ctx: 8 (over y, x, core), fsdp: 4 (over z).
Axes of the slice: x: 2, y: 2, z: 4, core: 2. Of those that a mesh axis runs over, the one named last changes fastest.
Arguments:
- tokens: bfloat16 [4, 1024, 1024], P('fsdp', 'ctx'), may hold values from -6 to 6
- cotangent: bfloat16 [4, 1024, 1024], P('fsdp', 'ctx'), may hold values from -6 to 6
- stretch_order: int32 [16], replicated, may hold values from 0 to 15, as said below
- doc_lengths: int32 [4, 3], P('fsdp'), may hold values from 1 to 896, 1024 in all within a row
- master: float32 [15730944], P(('ctx', 'fsdp'))
- first_moment: float32 [15730944], P(('ctx', 'fsdp'))
- second_moment: float32 [15730944], P(('ctx', 'fsdp')), as said below
Outputs:
- layer_out: bfloat16 [4, 1024, 1024], P('fsdp', 'ctx')
- input_grad: bfloat16 [4, 1024, 1024], P('fsdp', 'ctx')
- new_master: float32 [15730944], P(('ctx', 'fsdp'))
- new_first: float32 [15730944], P(('ctx', 'fsdp'))
- new_second: float32 [15730944], P(('ctx', 'fsdp'))
The draws below stay inside these ranges and needn't reach their ends.
Inputs may be any that keep to these rules, and one draw needn't show every extreme that they name: `stretch_order`: slots 2 j and 2 j + 1 hold two stretches c and 15 - c; every stretch appears once. `doc_lengths`: each row sums to 1024; its largest entry is exactly 896. `second_moment`: every entry is positive.
All inputs are finite; a program needn't handle non-finite values.
Results may differ from the reference program's by a relative error of at most 0.017.
Values may be sent and summed in bfloat16 or wider, within the bound.
A program may use at most 256 MiB of HBM per device.

```python
import math
import jax
import jax.numpy as jnp
import numpy as np
from jax import lax

MODEL_WIDTH = 1024
QUERY_HEADS = 16
KEY_VALUE_HEADS = 8
HEAD_SIZE = 128
FEED_WIDTH = 3072
STRETCH = 64
DOCS = 3
STEP = 7
STRETCHES = 16
LENGTH = 1024
SEQS = 4
PARAMS = 15730944
PDEV = 491592
N_CTX = 8
N_FSDP = 4


def segment_values(settings):
    count_of_shards = PARAMS // PDEV
    document_spans = [MODEL_WIDTH // count_of_shards * (QUERY_HEADS + 2 * KEY_VALUE_HEADS) * HEAD_SIZE, QUERY_HEADS * HEAD_SIZE // count_of_shards * MODEL_WIDTH, MODEL_WIDTH // count_of_shards * 2 * FEED_WIDTH, FEED_WIDTH // count_of_shards * MODEL_WIDTH, (2 * MODEL_WIDTH + 2 * HEAD_SIZE) // count_of_shards]
    column = jnp.arange(PARAMS, dtype=jnp.int32) % PDEV
    result = jnp.zeros((PARAMS,), jnp.float32)
    offset = 0
    for shard_span, setting in zip(document_spans, settings):
        inside = (column >= offset) & (column < offset + shard_span)
        result = jnp.where(inside, jnp.float32(setting), result)
        offset += shard_span
    return result


def grad_sizes():
    root_tokens = (SEQS * LENGTH) ** 0.5
    return [0.5 * root_tokens, 3.4 * root_tokens * LENGTH ** (-0.5), 0.3 * root_tokens, 0.6 * root_tokens, 2.0 * root_tokens]


def draw_stretch_order(key, part):
    key = jax.random.fold_in(key, 4)
    key_perm, key_flip = jax.random.split(key)
    half_count = STRETCHES // 2
    picked = jax.random.permutation(key_perm, jnp.arange(half_count, dtype=jnp.int32)).astype(jnp.int32)
    flipped = jax.random.randint(key_flip, (half_count,), 0, 2, dtype=jnp.int32)
    mirror = STRETCHES - 1 - picked
    leading = jnp.where(flipped == 1, picked, mirror)
    trailing = jnp.where(flipped == 1, mirror, picked)
    return jnp.stack([leading, trailing], axis=1).reshape(STRETCHES).astype(jnp.int32)


def draw_master(key, part):
    key = jax.random.fold_in(key, 11)
    key_matrix, key_gain = jax.random.split(key)
    spread = segment_values([MODEL_WIDTH ** (-0.5), (LENGTH / (3.0 * QUERY_HEADS * HEAD_SIZE)) ** 0.5, MODEL_WIDTH ** (-0.5), FEED_WIDTH ** (-0.5), 0.0])
    centre = segment_values([0.0, 0.0, 0.0, 0.0, 1.0])
    gain_spread = segment_values([0.0, 0.0, 0.0, 0.0, 0.3])
    matrix = jax.random.uniform(key_matrix, (PARAMS,), jnp.float32, -1.732, 1.732)
    jitter = jax.random.uniform(key_gain, (PARAMS,), jnp.float32, -1.0, 1.0)
    return centre + spread * matrix + gain_spread * jitter


def draw_first_moment(key, part):
    key = jax.random.fold_in(key, 12)
    return segment_values(grad_sizes()) * jax.random.normal(key, (PARAMS,), jnp.float32)


def draw_second_moment(key, part):
    key = jax.random.fold_in(key, 13)
    sizes_now = segment_values(grad_sizes())
    factor = 2.0 ** jax.random.uniform(key, (PARAMS,), jnp.float32, -1.0, 3.0)
    return sizes_now * sizes_now * factor


def steps_of(key, shape, shards, smallest, largest):
    factor_of, own = 1.0, jax.random.fold_in(key, 6)
    for position, shards_of in shards:
        heights = jnp.exp(jax.random.uniform(jax.random.fold_in(own, position), (shards_of,), jnp.float32, smallest / len(shards), largest / len(shards)))
        factor_of = factor_of * jnp.repeat(heights, shape[position] // shards_of).reshape([-1 if axis == position else 1 for axis in range(len(shape))])
    return factor_of


def length_profile(number_of, total, reach, skew):
    loads = [(1 << 20) // math.isqrt(standing ** skew) + 1 for standing in range(2, number_of + 1)]
    rest, holding = total - reach - (number_of - 1), [1] * (number_of - 1)
    while rest > 0:
        candidates = [i for i in range(number_of - 1) if holding[i] < reach]
        mass, left = sum([loads[i] for i in candidates]), rest
        for i in candidates:
            extra = min(reach - holding[i], max(1, left * loads[i] // mass), rest)
            holding[i] = holding[i] + extra
            rest = rest - extra
    return np.array([reach] + holding)


def uneven(rng, count, total, bound, slope):
    if count == 2:
        one = jax.random.randint(rng, (), max(1, total - bound), min(bound, total - 1) + 1)
        return jnp.stack([one, total - one])
    sizes = jnp.asarray(length_profile(count, total, bound, slope), jnp.int32)
    twos = (count - 1) // 2
    giver, receiver = sizes[1:1 + 2 * twos:2], sizes[2:2 + 2 * twos:2]
    slack = jnp.minimum(giver - 1, bound - receiver)
    moved = jax.random.randint(jax.random.fold_in(rng, 1), (twos,), 0, 1 << 20) % (slack + 1)
    sizes = sizes.at[1:1 + 2 * twos:2].set(giver - moved).at[2:2 + 2 * twos:2].set(receiver + moved)
    return sizes[jax.random.permutation(jax.random.fold_in(rng, 2), count)]


def centred(rng, dims, scale, most, cuts=(), held_as=jnp.bfloat16):
    values = jax.random.normal(rng, dims, jnp.float32) * scale
    if len(cuts) > 0:
        values = steps_of(rng, dims, cuts, -0.22, 0.18) * values
    return jnp.clip(values, min=-most, max=most).astype(held_as)


def setup_inputs(seed: int = 0) -> dict:
    seeds = jax.random.split(jax.random.key(seed), 8)
    tokens = centred(seeds[0], (SEQS, LENGTH, MODEL_WIDTH), 1.0, 6.0, ((0, 4), (1, 8)))
    cotangent = centred(seeds[1], (SEQS, LENGTH, MODEL_WIDTH), 1.0, 6.0, ((0, 4), (1, 8)))
    stretch_order = draw_stretch_order(jax.random.fold_in(seeds[7], 71), 0)
    doc_lengths = jax.vmap(lambda own: uneven(own, DOCS, LENGTH, LENGTH - 2 * STRETCH, 0))(jax.random.split(seeds[3], SEQS)).reshape((SEQS, DOCS)).astype(jnp.int32)
    master = draw_master(jax.random.fold_in(seeds[7], 71), 0)
    first_moment = draw_first_moment(jax.random.fold_in(seeds[7], 71), 0)
    second_moment = draw_second_moment(jax.random.fold_in(seeds[7], 71), 0)
    return {"tokens": tokens, "cotangent": cotangent, "stretch_order": stretch_order, "doc_lengths": doc_lengths, "master": master, "first_moment": first_moment, "second_moment": second_moment}


NORM_EPS = 1e-06
ROPE_BASE = 1000000.0
BETA_ONE = 0.5
BETA_TWO = 0.5
DECAY_RATE = 0.1
ADAM_EPS = 1e-08
MASKED = -1e+30

@jax.custom_vjp
def low(v):
    return lax.optimization_barrier(v.astype(jnp.bfloat16)).astype(jnp.float32)

@jax.custom_vjp
def low_back(v):
    return v

def low_keep(v):
    return (low(v), None)

def low_pass(kept, grad):
    return (grad,)

def back_keep(v):
    return (v, None)

def back_low(kept, grad):
    return (low(grad),)
low.defvjp(low_keep, low_pass)
low_back.defvjp(back_keep, back_low)

def segment_shapes():
    return [(MODEL_WIDTH, (QUERY_HEADS + 2 * KEY_VALUE_HEADS) * HEAD_SIZE), (QUERY_HEADS * HEAD_SIZE, MODEL_WIDTH), (MODEL_WIDTH, 2 * FEED_WIDTH), (FEED_WIDTH, MODEL_WIDTH), (2 * MODEL_WIDTH + 2 * HEAD_SIZE, 1)]

def unpack(flat_params, count_of_shards):
    param_table = flat_params.reshape(count_of_shards, -1)
    pieces = []
    offset = 0
    for row_total, column_total in segment_shapes():
        shard_span = row_total // count_of_shards * column_total
        pieces.append(param_table[:, offset:offset + shard_span].reshape(row_total, column_total))
        offset += shard_span
    return pieces

def pack(matrices, count_of_shards):
    return jnp.concatenate([matrix.reshape(count_of_shards, -1) for matrix in matrices], axis=1).reshape(-1)

def rate_rows(count_of_shards, seq_length):
    settings = [(MODEL_WIDTH ** (-0.5), DECAY_RATE), ((seq_length / (3.0 * QUERY_HEADS * HEAD_SIZE)) ** 0.5, DECAY_RATE), (MODEL_WIDTH ** (-0.5), DECAY_RATE), (FEED_WIDTH ** (-0.5), DECAY_RATE), (0.2, 0.0)]
    step_parts = []
    decay_parts = []
    for (row_total, column_total), (step_rate, decay_value) in zip(segment_shapes(), settings):
        shard_span = row_total // count_of_shards * column_total
        step_parts.append(jnp.full((shard_span,), step_rate, jnp.float32))
        decay_parts.append(jnp.full((shard_span,), decay_value, jnp.float32))
    return (jnp.concatenate(step_parts), jnp.concatenate(decay_parts))

def slot_positions(stretch_order, first_row, count_of_rows):
    row_ids = first_row + jnp.arange(count_of_rows, dtype=jnp.int32)
    slot_ids = row_ids // STRETCH
    slot_table = jnp.arange(stretch_order.shape[0], dtype=jnp.int32)
    stretch_ids = lax.optimization_barrier(jnp.sum(jnp.where(slot_ids[:, None] == slot_table[None, :], stretch_order[None, :], 0), axis=1)).astype(jnp.int32)
    return (stretch_ids * STRETCH + row_ids % STRETCH).astype(jnp.int32)

def documents(positions, doc_lengths):
    doc_ends = jnp.cumsum(doc_lengths, axis=1).astype(jnp.int32)
    doc_starts = (doc_ends - doc_lengths).astype(jnp.int32)
    passed = positions[None, :, None] >= doc_ends[:, None, :-1]
    doc_ids = lax.optimization_barrier(jnp.sum(passed.astype(jnp.int32), axis=2)).astype(jnp.int32)
    doc_table = jnp.arange(doc_lengths.shape[1], dtype=jnp.int32)
    owner = doc_ids[:, :, None] == doc_table[None, None, :]
    start_of = lax.optimization_barrier(jnp.sum(jnp.where(owner, doc_starts[:, None, :], 0), axis=2)).astype(jnp.int32)
    return (doc_ids, (positions[None, :] - start_of).astype(jnp.int32))

def rope_tables(relative):
    half_dim = HEAD_SIZE // 2
    frequency = ROPE_BASE ** (-(jnp.arange(half_dim, dtype=jnp.float32) * 2.0 / HEAD_SIZE))
    angles = relative.astype(jnp.float32)[..., None] * frequency
    cosine_table = jnp.cos(angles)
    sine_values = jnp.sin(angles)
    return (jnp.concatenate([cosine_table, cosine_table], axis=-1), jnp.concatenate([sine_values, sine_values], axis=-1))

def rotate(values, cosine_table, sine_values):
    half_dim = values.shape[-1] // 2
    turned = jnp.concatenate([-values[..., half_dim:], values[..., :half_dim]], axis=-1)
    return values * cosine_table[..., None, :] + turned * sine_values[..., None, :]

def rms_norm(values, scaling):
    factor = lax.rsqrt(lax.optimization_barrier(jnp.mean(values * values, axis=-1, keepdims=True)) + NORM_EPS)
    return values * factor * scaling

def product(left, right):
    return jnp.dot(left, right, preferred_element_type=jnp.float32, precision=lax.Precision.HIGHEST)

def attend(queries, keys, values, positions, doc_ids):
    current_length = queries.shape[0]
    block_rows = min(512, current_length)
    query_groups = QUERY_HEADS // KEY_VALUE_HEADS
    keys_all = jnp.repeat(keys, query_groups, axis=1)
    values_all = jnp.repeat(values, query_groups, axis=1)
    score_scale = HEAD_SIZE ** (-0.5)

    def one_block(inputs):
        query_block, pos_block, doc_block = inputs
        scores = jnp.einsum('qhd,khd->hqk', query_block, keys_all, precision=lax.Precision.HIGHEST) * score_scale
        scores = low_back(scores)
        allowed = (doc_block[:, None] == doc_ids[None, :]) & (positions[None, :] <= pos_block[:, None])
        scores = jnp.where(allowed[None], scores, MASKED)
        weights = jnp.exp(scores - lax.optimization_barrier(jnp.max(scores, axis=-1, keepdims=True)))
        probabilities = low(weights / lax.optimization_barrier(jnp.sum(weights, axis=-1, keepdims=True)))
        return jnp.einsum('hqk,khd->qhd', probabilities, values_all, precision=lax.Precision.HIGHEST)
    block_count = current_length // block_rows
    outputs = lax.map(jax.checkpoint(one_block), (queries.reshape(block_count, block_rows, QUERY_HEADS, HEAD_SIZE), positions.reshape(block_count, block_rows), doc_ids.reshape(block_count, block_rows)))
    return outputs.reshape(current_length, QUERY_HEADS * HEAD_SIZE)

def layer(x_in, w_qkv, w_out, w_gate_up, w_down, gains, positions, doc_ids, relative):
    g_attn = gains[:MODEL_WIDTH]
    g_mlp = gains[MODEL_WIDTH:2 * MODEL_WIDTH]
    g_query = gains[2 * MODEL_WIDTH:2 * MODEL_WIDTH + HEAD_SIZE]
    g_key = gains[2 * MODEL_WIDTH + HEAD_SIZE:]
    current_length = x_in.shape[0]
    normed_one = low(rms_norm(x_in, g_attn))
    projected_output = low_back(product(normed_one, w_qkv))
    query_raw = projected_output[:, :QUERY_HEADS * HEAD_SIZE].reshape(current_length, QUERY_HEADS, HEAD_SIZE)
    unrotated_keys = projected_output[:, QUERY_HEADS * HEAD_SIZE:(QUERY_HEADS + KEY_VALUE_HEADS) * HEAD_SIZE].reshape(current_length, KEY_VALUE_HEADS, HEAD_SIZE)
    unprojected_values = projected_output[:, (QUERY_HEADS + KEY_VALUE_HEADS) * HEAD_SIZE:].reshape(current_length, KEY_VALUE_HEADS, HEAD_SIZE)
    cosine_table, sine_values = rope_tables(relative)
    queries = low(rotate(rms_norm(query_raw, g_query), cosine_table, sine_values))
    keys = low(rotate(rms_norm(unrotated_keys, g_key), cosine_table, sine_values))
    values = low(unprojected_values)
    attn = low_back(low(attend(queries, keys, values, positions, doc_ids)))
    resid = x_in + low_back(product(attn, w_out))
    normed_two = low(rms_norm(resid, g_mlp))
    gate_up = low_back(product(normed_two, w_gate_up))
    hidden = low(jax.nn.silu(gate_up[:, :FEED_WIDTH]) * gate_up[:, FEED_WIDTH:])
    return resid + low_back(product(hidden, w_down))

def reference(tokens, cotangent, stretch_order, doc_lengths, master, first_moment, second_moment):
    count_of_shards = N_CTX * N_FSDP
    pieces = unpack(low(master), count_of_shards)
    positions = slot_positions(stretch_order, 0, LENGTH)
    doc_ids, relative = documents(positions, doc_lengths)

    def one_sequence(totals, item):
        x_seq, grad_seq, doc_seq, rel_seq = item

        def run(x_in, w_qkv, w_out, w_gate_up, w_down, gains):
            return layer(x_in, w_qkv, w_out, w_gate_up, w_down, gains.reshape(-1), positions, doc_seq, rel_seq)
        result, pull = jax.vjp(run, x_seq.astype(jnp.float32), *pieces)
        grads = pull(grad_seq.astype(jnp.float32))
        totals = tuple((total + grad for total, grad in zip(totals, grads[1:])))
        return (totals, (result.astype(jnp.bfloat16), grads[0].astype(jnp.bfloat16)))
    zeros = tuple((jnp.zeros(piece.shape, jnp.float32) for piece in pieces))
    totals, (layer_out, input_grad) = lax.scan(one_sequence, zeros, (tokens, cotangent, doc_ids, relative))
    grad = pack(list(totals), count_of_shards)
    step_row, decay_row = rate_rows(count_of_shards, LENGTH)
    step_rate = jnp.tile(step_row, count_of_shards)
    decay_value = jnp.tile(decay_row, count_of_shards)
    new_first = BETA_ONE * first_moment + (1.0 - BETA_ONE) * grad
    new_second = BETA_TWO * second_moment + (1.0 - BETA_TWO) * grad * grad
    normalized = new_first / (1.0 - BETA_ONE ** STEP) / (jnp.sqrt(new_second / (1.0 - BETA_TWO ** STEP)) + ADAM_EPS)
    new_master = master - step_rate * (normalized + decay_value * master)
    return (layer_out, input_grad, new_master, new_first, new_second)
```

```python
import functools

import jax
import jax.numpy as jnp
from jax import lax
from jax.experimental import pallas as pl
from jax.experimental.pallas import tpu as pltpu
from jax.sharding import PartitionSpec as P

MODEL_WIDTH = 1024
QUERY_HEADS = 16
KEY_VALUE_HEADS = 8
HEAD_SIZE = 128
FEED_WIDTH = 3072
STRETCH = 64
STEP = 7


NORM_EPS = 1e-06
ROPE_BASE = 1000000.0
BETA_ONE = 0.5
BETA_TWO = 0.5
DECAY_RATE = 0.1
ADAM_EPS = 1e-08
MASKED = -1e30


def from_behind(x, axis, by):
    peers = lax.axis_size(axis)
    return lax.ppermute(x, axis, [(i, (i + by) % peers) for i in range(peers)])


def segment_shapes():
    return [
        (MODEL_WIDTH, (QUERY_HEADS + 2 * KEY_VALUE_HEADS) * HEAD_SIZE),
        (QUERY_HEADS * HEAD_SIZE, MODEL_WIDTH),
        (MODEL_WIDTH, 2 * FEED_WIDTH),
        (FEED_WIDTH, MODEL_WIDTH),
        (2 * MODEL_WIDTH + 2 * HEAD_SIZE, 1),
    ]


def unpack(flat_params, count_of_shards):
    param_table = flat_params.reshape(count_of_shards, -1)
    pieces = []
    offset = 0
    for row_total, column_total in segment_shapes():
        shard_span = row_total // count_of_shards * column_total
        pieces.append(param_table[:, offset : offset + shard_span].reshape(row_total, column_total))
        offset += shard_span
    return pieces


def pack(matrices, count_of_shards):
    return jnp.concatenate(
        [matrix.reshape(count_of_shards, -1) for matrix in matrices], axis=1
    ).reshape(-1)


def rate_rows(count_of_shards, seq_length):
    settings = [
        (MODEL_WIDTH ** (-0.5), DECAY_RATE),
        ((seq_length / (3.0 * QUERY_HEADS * HEAD_SIZE)) ** 0.5, DECAY_RATE),
        (MODEL_WIDTH ** (-0.5), DECAY_RATE),
        (FEED_WIDTH ** (-0.5), DECAY_RATE),
        (0.2, 0.0),
    ]
    step_parts = []
    decay_parts = []
    for (row_total, column_total), (step_rate, decay_value) in zip(segment_shapes(), settings):
        shard_span = row_total // count_of_shards * column_total
        step_parts.append(jnp.full((shard_span,), step_rate, jnp.float32))
        decay_parts.append(jnp.full((shard_span,), decay_value, jnp.float32))
    return (jnp.concatenate(step_parts), jnp.concatenate(decay_parts))


def slot_positions(stretch_order, first_row, count_of_rows):
    row_ids = first_row + jnp.arange(count_of_rows, dtype=jnp.int32)
    slot_ids = row_ids // STRETCH
    slot_table = jnp.arange(stretch_order.shape[0], dtype=jnp.int32)
    stretch_ids = jnp.sum(
        jnp.where(slot_ids[:, None] == slot_table[None, :], stretch_order[None, :], 0), axis=1
    )
    return stretch_ids * STRETCH + row_ids % STRETCH


def documents(positions, doc_lengths):
    doc_ends = jnp.cumsum(doc_lengths, axis=1)
    doc_starts = doc_ends - doc_lengths
    passed = positions[None, :, None] >= doc_ends[:, None, :-1]
    doc_ids = jnp.sum(passed.astype(jnp.int32), axis=2)
    doc_table = jnp.arange(doc_lengths.shape[1], dtype=jnp.int32)
    owner = doc_ids[:, :, None] == doc_table[None, None, :]
    start_of = jnp.sum(jnp.where(owner, doc_starts[:, None, :], 0), axis=2)
    return (doc_ids, positions[None, :] - start_of)


def key_mask(stretch_order, doc_lengths, query_pos, query_doc, first_row, count_of_rows):
    key_pos = slot_positions(stretch_order, first_row, count_of_rows)
    key_doc, _ = documents(key_pos, doc_lengths)
    same_doc = query_doc[:, :, None] == key_doc[:, None, :]
    return same_doc & (key_pos[None, None, :] <= query_pos[None, :, None])


def rope_tables(relative):
    half_dim = HEAD_SIZE // 2
    frequency = ROPE_BASE ** (-(jnp.arange(half_dim, dtype=jnp.float32) * 2.0 / HEAD_SIZE))
    angles = relative.astype(jnp.float32)[..., None] * frequency
    cosine_table = jnp.cos(angles)
    sine_values = jnp.sin(angles)
    return (
        jnp.concatenate([cosine_table, cosine_table], axis=-1),
        jnp.concatenate([sine_values, sine_values], axis=-1),
    )


def rotate(values, cosine_table, sine_values):
    half_dim = values.shape[-1] // 2
    turned = jnp.concatenate([-values[..., half_dim:], values[..., :half_dim]], axis=-1)
    return values * cosine_table[..., None, :] + turned * sine_values[..., None, :]


def rotate_back(grads, cosine_table, sine_values):
    half_dim = grads.shape[-1] // 2
    moved = grads * sine_values[..., None, :]
    unturned = jnp.concatenate([moved[..., half_dim:], -moved[..., :half_dim]], axis=-1)
    return grads * cosine_table[..., None, :] + unturned


def rms_norm(values, scaling):
    factor = lax.rsqrt(jnp.mean(values * values, axis=-1, keepdims=True) + NORM_EPS)
    return values * factor * scaling


def norm_back(values, grads, scaling):
    factor = lax.rsqrt(jnp.mean(values * values, axis=-1, keepdims=True) + NORM_EPS)
    unit_values = values * factor
    scaled_grads = grads * scaling
    inner = jnp.mean(scaled_grads * unit_values, axis=-1, keepdims=True)
    return (factor * (scaled_grads - unit_values * inner), grads * unit_values)


def attend_block(state, queries, key_value_block, allowed, score_scale):
    running, top_now, total_now = state
    sequence_count, count_of_keys = (key_value_block.shape[1], key_value_block.shape[2])
    block_keys = key_value_block[0].reshape(
        sequence_count, count_of_keys, KEY_VALUE_HEADS, HEAD_SIZE
    )
    block_values = key_value_block[1].reshape(
        sequence_count, count_of_keys, KEY_VALUE_HEADS, HEAD_SIZE
    )
    mask_wide = allowed[:, :, None, None, :]
    scores = (
        jnp.einsum("sqhgd,snhd->sqhgn", queries, block_keys, preferred_element_type=jnp.float32)
        * score_scale
    )
    new_top = jnp.maximum(top_now, jnp.max(jnp.where(mask_wide, scores, MASKED), axis=-1))
    weights = jnp.where(mask_wide, jnp.exp(scores - new_top[..., None]), 0.0)
    factor = jnp.exp(top_now - new_top)
    total_now = total_now * factor + jnp.sum(weights, axis=-1)
    running = running * factor[..., None] + jnp.einsum(
        "sqhgn,snhd->sqhgd",
        weights.astype(jnp.bfloat16),
        block_values,
        preferred_element_type=jnp.float32,
    )
    return (running, new_top, total_now)


def backward_block(
    queries, attention_gradient, log_total, delta, key_value_block, allowed, score_scale
):
    sequence_count, count_of_keys = (key_value_block.shape[1], key_value_block.shape[2])
    block_keys = key_value_block[0].reshape(
        sequence_count, count_of_keys, KEY_VALUE_HEADS, HEAD_SIZE
    )
    block_values = key_value_block[1].reshape(
        sequence_count, count_of_keys, KEY_VALUE_HEADS, HEAD_SIZE
    )
    mask_wide = allowed[:, :, None, None, :]
    scores = (
        jnp.einsum("sqhgd,snhd->sqhgn", queries, block_keys, preferred_element_type=jnp.float32)
        * score_scale
    )
    probabilities = jnp.where(mask_wide, jnp.exp(scores - log_total[..., None]), 0.0)
    value_gradient = jnp.einsum(
        "sqhgn,sqhgd->snhd",
        probabilities.astype(jnp.bfloat16),
        attention_gradient,
        preferred_element_type=jnp.float32,
    )
    grad_probs = jnp.einsum(
        "sqhgd,snhd->sqhgn", attention_gradient, block_values, preferred_element_type=jnp.float32
    )
    grad_scores = (probabilities * (grad_probs - delta[..., None])).astype(jnp.bfloat16)
    grad_queries = (
        jnp.einsum("sqhgn,snhd->sqhgd", grad_scores, block_keys, preferred_element_type=jnp.float32)
        * score_scale
    )
    key_gradient = (
        jnp.einsum("sqhgn,sqhgd->snhd", grad_scores, queries, preferred_element_type=jnp.float32)
        * score_scale
    )
    grad_pair = jnp.stack(
        [
            key_gradient.reshape(sequence_count, count_of_keys, KEY_VALUE_HEADS * HEAD_SIZE),
            value_gradient.reshape(sequence_count, count_of_keys, KEY_VALUE_HEADS * HEAD_SIZE),
        ]
    )
    return (grad_queries, grad_pair)


def summed(part, count_of_shards):
    return lax.psum_scatter(
        part.reshape(-1), ("ctx", "fsdp"), scatter_dimension=0, tiled=True
    )


def local(tokens, cotangent, stretch_order, doc_lengths, master, first_moment, second_moment):
    cycle_size = lax.axis_size("ctx")
    ctx_index = lax.axis_index("ctx")
    count_of_shards = cycle_size * lax.axis_size("fsdp")
    sequence_count, count_of_rows, _ = tokens.shape
    seq_length = count_of_rows * cycle_size
    query_groups = QUERY_HEADS // KEY_VALUE_HEADS
    score_scale = HEAD_SIZE ** (-0.5)
    gathered = lax.all_gather(master.astype(jnp.bfloat16), ("ctx", "fsdp"), axis=0, tiled=True)
    w_qkv, w_out, w_gate_up, w_down, gain_column = unpack(gathered, count_of_shards)
    gains = gain_column.reshape(-1).astype(jnp.float32)
    g_attn = gains[:MODEL_WIDTH]
    g_mlp = gains[MODEL_WIDTH : 2 * MODEL_WIDTH]
    g_query = gains[2 * MODEL_WIDTH : 2 * MODEL_WIDTH + HEAD_SIZE]
    g_key = gains[2 * MODEL_WIDTH + HEAD_SIZE :]
    query_pos = slot_positions(stretch_order, ctx_index * count_of_rows, count_of_rows)
    query_doc, relative = documents(query_pos, doc_lengths)
    cosine_table, sine_values = rope_tables(relative)
    x_in = tokens.astype(jnp.float32)
    normed_one = rms_norm(x_in, g_attn).astype(jnp.bfloat16)
    projected_output = jnp.einsum(
        "sqd,de->sqe", normed_one, w_qkv, preferred_element_type=jnp.float32
    )
    query_raw = projected_output[:, :, : QUERY_HEADS * HEAD_SIZE].reshape(
        sequence_count, count_of_rows, QUERY_HEADS, HEAD_SIZE
    )
    unrotated_keys = projected_output[
        :, :, QUERY_HEADS * HEAD_SIZE : (QUERY_HEADS + KEY_VALUE_HEADS) * HEAD_SIZE
    ].reshape(sequence_count, count_of_rows, KEY_VALUE_HEADS, HEAD_SIZE)
    unprojected_values = projected_output[:, :, (QUERY_HEADS + KEY_VALUE_HEADS) * HEAD_SIZE :]
    queries = (
        rotate(rms_norm(query_raw, g_query), cosine_table, sine_values)
        .astype(jnp.bfloat16)
        .reshape(sequence_count, count_of_rows, KEY_VALUE_HEADS, query_groups, HEAD_SIZE)
    )
    keys_rot = rotate(rms_norm(unrotated_keys, g_key), cosine_table, sine_values).reshape(
        sequence_count, count_of_rows, KEY_VALUE_HEADS * HEAD_SIZE
    )
    kv_local = jnp.stack([keys_rot, unprojected_values]).astype(jnp.bfloat16)
    statistic_shape = (sequence_count, count_of_rows, KEY_VALUE_HEADS, query_groups)
    initial = (
        jnp.zeros(statistic_shape + (HEAD_SIZE,), jnp.float32),
        jnp.full(statistic_shape, MASKED, jnp.float32),
        jnp.zeros(statistic_shape, jnp.float32),
    )
    state = initial
    piece = lax.all_gather(kv_local, "ctx", axis=2, tiled=True)
    key_total = piece.shape[2]

    def key_step(inner, block_index):
        first_row = block_index * count_of_rows
        key_value_block = lax.dynamic_slice_in_dim(piece, first_row, count_of_rows, 2)
        allowed = key_mask(
            stretch_order, doc_lengths, query_pos, query_doc, first_row, count_of_rows
        )
        return (attend_block(inner, queries, key_value_block, allowed, score_scale), None)

    state, _ = lax.scan(key_step, state, jnp.arange(key_total // count_of_rows, dtype=jnp.int32))
    running, top_now, total_now = state
    attn = running / total_now[..., None]
    log_total = top_now + jnp.log(total_now)
    attn_low = attn.reshape(sequence_count, count_of_rows, QUERY_HEADS * HEAD_SIZE).astype(
        jnp.bfloat16
    )
    resid = x_in + jnp.einsum("sqa,ad->sqd", attn_low, w_out, preferred_element_type=jnp.float32)
    normed_two = rms_norm(resid, g_mlp).astype(jnp.bfloat16)
    gate_up = jnp.einsum("sqd,de->sqe", normed_two, w_gate_up, preferred_element_type=jnp.float32)
    gate = gate_up[:, :, :FEED_WIDTH]
    up_part = gate_up[:, :, FEED_WIDTH:]
    sigmoid_gate = jax.nn.sigmoid(gate)
    hidden = (gate * sigmoid_gate * up_part).astype(jnp.bfloat16)
    mlp_out = jnp.einsum("sqf,fd->sqd", hidden, w_down, preferred_element_type=jnp.float32)
    layer_out = (resid + mlp_out).astype(jnp.bfloat16)
    grad_w_down = jnp.einsum("sqf,sqd->fd", hidden, cotangent, preferred_element_type=jnp.float32)
    grad_hidden = jnp.einsum("sqd,fd->sqf", cotangent, w_down, preferred_element_type=jnp.float32)
    grad_gate = grad_hidden * up_part * sigmoid_gate * (1.0 + gate * (1.0 - sigmoid_gate))
    grad_up = grad_hidden * gate * sigmoid_gate
    grad_gate_up = jnp.concatenate([grad_gate, grad_up], axis=-1).astype(jnp.bfloat16)
    grad_w_gate_up = jnp.einsum(
        "sqd,sqe->de", normed_two, grad_gate_up, preferred_element_type=jnp.float32
    )
    grad_normed_two = jnp.einsum(
        "sqe,de->sqd", grad_gate_up, w_gate_up, preferred_element_type=jnp.float32
    )
    back_two, mlp_gain_terms = norm_back(resid, grad_normed_two, g_mlp)
    grad_resid = cotangent.astype(jnp.float32) + back_two
    grad_branch = grad_resid.astype(jnp.bfloat16)
    grad_w_out = jnp.einsum(
        "sqa,sqd->ad", attn_low, grad_branch, preferred_element_type=jnp.float32
    )
    attention_gradient = jnp.einsum(
        "sqd,ad->sqa", grad_branch, w_out, preferred_element_type=jnp.float32
    ).astype(jnp.bfloat16)
    attention_head_gradient = attention_gradient.reshape(
        sequence_count, count_of_rows, KEY_VALUE_HEADS, query_groups, HEAD_SIZE
    )
    delta = jnp.sum(attention_head_gradient.astype(jnp.float32) * attn, axis=-1)

    def grads_from(turn_index, kv_now, key_value_gradients, grad_queries):
        source_dev = (ctx_index - turn_index) % cycle_size
        allowed = key_mask(
            stretch_order,
            doc_lengths,
            query_pos,
            query_doc,
            source_dev * count_of_rows,
            count_of_rows,
        )
        part_queries, part_pair = backward_block(
            queries, attention_head_gradient, log_total, delta, kv_now, allowed, score_scale
        )
        return (key_value_gradients + part_pair, grad_queries + part_queries)

    def pass_grads(key_value_gradients):
        return from_behind(key_value_gradients.astype(jnp.bfloat16), "ctx", 1).astype(
            key_value_gradients.dtype
        )

    def turn_step(turn_index, state):
        kv_now, key_value_gradients, grad_queries = state
        key_value_gradients, grad_queries = grads_from(
            turn_index, kv_now, key_value_gradients, grad_queries
        )
        kv_now = from_behind(kv_now, "ctx", 1)
        key_value_gradients = pass_grads(key_value_gradients)
        return (kv_now, key_value_gradients, grad_queries)

    start_state = (
        kv_local,
        jnp.zeros(kv_local.shape, jnp.float32),
        jnp.zeros(statistic_shape + (HEAD_SIZE,), jnp.float32),
    )
    kv_now, key_value_gradients, grad_queries = lax.fori_loop(
        0, cycle_size - 1, turn_step, start_state
    )
    key_value_gradients, grad_queries = grads_from(
        cycle_size - 1, kv_now, key_value_gradients, grad_queries
    )
    key_value_gradients = pass_grads(key_value_gradients)
    grad_query_rot = rotate_back(
        grad_queries.reshape(sequence_count, count_of_rows, QUERY_HEADS, HEAD_SIZE),
        cosine_table,
        sine_values,
    )
    grad_key_rot = rotate_back(
        key_value_gradients[0].reshape(sequence_count, count_of_rows, KEY_VALUE_HEADS, HEAD_SIZE),
        cosine_table,
        sine_values,
    )
    grad_query_raw, query_gain_terms = norm_back(query_raw, grad_query_rot, g_query)
    unrotated_key_gradient, key_gain_terms = norm_back(unrotated_keys, grad_key_rot, g_key)
    grad_projected = jnp.concatenate(
        [
            grad_query_raw.reshape(sequence_count, count_of_rows, QUERY_HEADS * HEAD_SIZE),
            unrotated_key_gradient.reshape(
                sequence_count, count_of_rows, KEY_VALUE_HEADS * HEAD_SIZE
            ),
            key_value_gradients[1],
        ],
        axis=-1,
    ).astype(jnp.bfloat16)
    grad_w_qkv = jnp.einsum(
        "sqd,sqe->de", normed_one, grad_projected, preferred_element_type=jnp.float32
    )
    grad_normed_one = jnp.einsum(
        "sqe,de->sqd", grad_projected, w_qkv, preferred_element_type=jnp.float32
    )
    back_one, attn_gain_terms = norm_back(x_in, grad_normed_one, g_attn)
    input_grad = (grad_resid + back_one).astype(jnp.bfloat16)
    grad_gains = jnp.concatenate(
        [
            jnp.sum(attn_gain_terms, axis=(0, 1)),
            jnp.sum(mlp_gain_terms, axis=(0, 1)),
            jnp.sum(query_gain_terms, axis=(0, 1, 2)),
            jnp.sum(key_gain_terms, axis=(0, 1, 2)),
        ]
    ).reshape(-1, 1)
    grad = jnp.concatenate(
        [
            summed(part, count_of_shards)
            for part in (grad_w_qkv, grad_w_out, grad_w_gate_up, grad_w_down, grad_gains)
        ]
    )
    new_master, new_first, new_second = adam(
        grad, master, first_moment, second_moment, count_of_shards, seq_length
    )
    return (layer_out, input_grad, new_master, new_first, new_second)


MESH = pl.DeviceIdType.MESH
F32 = jnp.float32
BF16 = jnp.bfloat16
CTX = 8
CHIPS = 4
GROUP = QUERY_HEADS // KEY_VALUE_HEADS
QCOLS = GROUP * HEAD_SIZE
PCOLS = QCOLS + 2 * HEAD_SIZE
HID = FEED_WIDTH // CTX
GAIN_WIDTH = 2 * MODEL_WIDTH + 2 * HEAD_SIZE
TILE = 256


def dot(a, b, dims=((1,), (0,))):
    return lax.dot_general(a, b, (dims, ((), ())), preferred_element_type=F32)


NT = ((1,), (1,))
TN = ((0,), (0,))


def layer_kernel(
    zsize,
    x_ref,
    cot_ref,
    wq_in,
    wo_in,
    wgu_in,
    wd_in,
    gains_in,
    cos_ref,
    sin_ref,
    kpos_ref,
    qpos_ref,
    qstart_ref,
    out_ref,
    xgrad_ref,
    gq_ref,
    go_ref,
    ggu_ref,
    gd_ref,
    gg_ref,
    n1,
    cot,
    n2,
    gb,
    wq,
    wo,
    wgu,
    wd,
    qraw,
    kraw,
    q_s,
    k_s,
    v_s,
    kt_s,
    vt_s,
    probs,
    attn,
    attn_low,
    hidden,
    ggu,
    gattn,
    dq_s,
    dk_s,
    dv_s,
    gp,
    psnd,
    prcv,
    csnd,
    crcv,
    own,
    acc,
    resid_s,
    gresid_s,
    gwq,
    gwo,
    gwgu,
    gwd,
    lwq,
    lwo,
    lwgu,
    lwd,
    asq,
    asg,
    arg_,
    gz,
    gpl,
    gains,
    hz,
    hpl,
    hrow,
    ag_s,
    ag_r,
    rs_ps,
    rs_pr,
    rs_cs,
    rs_cr,
    a2a_s,
    a2a_r,
    zg_s,
    zg_r,
    g_s,
    g_r,
    loc,
):
    c = lax.axis_index("ctx")
    z = lax.axis_index("fsdp")
    core = c % 2
    chip = c // 2
    cx = chip % 2
    cy = chip // 2
    slot = core * CHIPS + chip
    sib = c + 1 - 2 * core
    tiles = n1.shape[0] * n1.shape[1] // TILE
    rows = n1.shape[1]
    half = CHIPS * rows

    def chip_at(i):
        return ((cy + i // 2) % 2) * 2 + (cx + i % 2) % 2

    def rcopy(src, dst, ssem, rsem, to_c, to_z):
        return pltpu.make_async_remote_copy(
            src_ref=src,
            dst_ref=dst,
            send_sem=ssem,
            recv_sem=rsem,
            device_id=(to_c, to_z),
            device_id_type=MESH,
        )

    def loop(lo, hi, body):
        def step(i, carry):
            body(i)
            return carry

        lax.fori_loop(lo, hi, step, 0)

    barrier = pltpu.get_barrier_semaphore()

    def greet_plane(i):
        pl.semaphore_signal(
            barrier, inc=1, device_id=((c + i) % CTX, z), device_id_type=MESH
        )

    def greet_z(i):
        pl.semaphore_signal(
            barrier, inc=1, device_id=(c, (z + i) % zsize), device_id_type=MESH
        )

    loop(1, CTX, greet_plane)
    loop(1, zsize, greet_z)
    pl.semaphore_wait(barrier, CTX - 1 + zsize - 1)

    def ag_direct(n, buf, i):
        if i == 0:
            return rcopy(buf.at[slot], buf.at[slot], ag_s.at[n, 0], ag_r.at[n, 0], sib, z)
        return rcopy(
            buf.at[slot],
            buf.at[slot],
            ag_s.at[n, i],
            ag_r.at[n, i],
            chip_at(i) * 2 + core,
            z,
        )

    def ag_landed(n, buf, i):
        there = core * CHIPS + chip_at(i)
        return rcopy(buf.at[there], buf.at[there], ag_s.at[n, i], ag_r.at[n, i], sib, z)

    def ag_forward(n, buf, i):
        there = core * CHIPS + chip_at(i)
        return rcopy(buf.at[there], buf.at[there], ag_s.at[n, 3 + i], ag_r.at[n, 3 + i], sib, z)

    def ag_forwarded(n, buf, i):
        there = (1 - core) * CHIPS + chip_at(i)
        return rcopy(buf.at[there], buf.at[there], ag_s.at[n, 3 + i], ag_r.at[n, 3 + i], sib, z)

    def ag_start(n, buf):
        for i in (3, 1, 2, 0):
            ag_direct(n, buf, i).start()

    def ag_pass(n, buf):
        for i in (1, 2, 3):
            ag_landed(n, buf, i).wait_recv()
            ag_forward(n, buf, i).start()

    def ag_finish(n, buf):
        other = (1 - core) * CHIPS + chip
        rcopy(buf.at[other], buf.at[other], ag_s.at[n, 0], ag_r.at[n, 0], sib, z).wait_recv()
        for i in (1, 2, 3):
            ag_forwarded(n, buf, i).wait_recv()

    def ag_drain(n, buf):
        for i in range(4):
            ag_direct(n, buf, i).wait_send()
        for i in (1, 2, 3):
            ag_forward(n, buf, i).wait_send()

    def rs_pair(r):
        return rcopy(psnd, prcv.at[r], rs_ps.at[r], rs_pr.at[r], sib, z)

    def rs_chip(r, i):
        return rcopy(
            csnd.at[i - 1],
            crcv.at[r, i - 1],
            rs_cs.at[r, i - 1],
            rs_cr.at[r, i - 1],
            chip_at(i) * 2 + core,
            z,
        )

    def rs_start(r, part):
        if r > 0:
            rs_pair(r - 1).wait_send()

        def give(n):
            cols = pl.ds(pl.multiple_of(n * TILE, TILE), TILE)
            psnd[:, :, cols] = part(1 - core, n).astype(BF16).reshape(CHIPS, rows, TILE)

        def keep(n):
            cols = pl.ds(pl.multiple_of(n * TILE, TILE), TILE)
            own[:, :, cols] = part(core, n).reshape(CHIPS, rows, TILE)

        loop(0, MODEL_WIDTH // TILE, give)
        rs_pair(r).start()
        loop(0, MODEL_WIDTH // TILE, keep)
        if r > 0:
            for i in (1, 2, 3):
                rs_chip(r - 1, i).wait_send()
        rs_pair(r).wait_recv()
        for i in (3, 1, 2):
            there = chip_at(i)
            csnd[i - 1] = (own[there] + prcv[r, there].astype(F32)).astype(BF16)
            rs_chip(r, i).start()
        acc[r] = own[chip] + prcv[r, chip].astype(F32)

    def rs_finish(r):
        total = acc[r]
        for i in (1, 2, 3):
            rs_chip(r, i).wait_recv()
            total = total + crcv[r, i - 1].astype(F32)
        return total

    def a2a(n, src, dst_of, i):
        to = (c + i) % CTX
        return rcopy(src.at[to], dst_of(c), a2a_s.at[n, i], a2a_r.at[n, i], to, z)

    def a2a_landed(n, dst_of, i):
        frm = (c + CTX - i) % CTX
        return rcopy(dst_of(frm), dst_of(frm), a2a_s.at[n, i], a2a_r.at[n, i], sib, z)

    def a2a_start(n, src, dst_of):
        loop(1, CTX, lambda i: a2a(n, src, dst_of, i).start())

    def a2a_wait(n, dst_of):
        loop(1, CTX, lambda i: a2a_landed(n, dst_of, i).wait_recv())

    def a2a_drain(n, src, dst_of):
        loop(1, CTX, lambda i: a2a(n, src, dst_of, i).wait_send())

    def zg(n, src, dst_of, i):
        return rcopy(src, dst_of(z), zg_s.at[n, i], zg_r.at[n, i], c, (z + i) % zsize)

    def zg_landed(n, dst_of, i):
        there = dst_of((z + zsize - i) % zsize)
        return rcopy(there, there, zg_s.at[n, i], zg_r.at[n, i], sib, z)

    def zg_start(n, src, dst_of):
        for i in range(1, zsize):
            zg(n, src, dst_of, i).start()

    def zg_wait(n, dst_of):
        for i in range(1, zsize):
            zg_landed(n, dst_of, i).wait_recv()

    def zg_drain(n, src, dst_of):
        for i in range(1, zsize):
            zg(n, src, dst_of, i).wait_send()

    def zr(n, src_of, land, i):
        to = (z + i) % zsize
        return rcopy(src_of(to), land.at[i - 1], zg_s.at[n, i], zg_r.at[n, i], c, to)

    def zr_start(n, src_of, land):
        for i in range(1, zsize):
            zr(n, src_of, land, i).start()

    def zr_finish(n, src_of, land):
        total = src_of(z)[...].astype(F32)
        for i in range(1, zsize):
            zr(n, src_of, land, i).wait_recv()
            total = total + land[i - 1].astype(F32)
        return total

    def zr_drain(n, src_of, land):
        for i in range(1, zsize):
            zr(n, src_of, land, i).wait_send()

    def row_z(n, src, land, i):
        return rcopy(src, land.at[z], g_s.at[n, i], g_r.at[n, i], c, (z + i) % zsize)

    def row_plane(n, src, land, i):
        return rcopy(
            src, land.at[c], g_s.at[n, zsize + i], g_r.at[n, zsize + i], (c + i) % CTX, z
        )

    def row_z_wait(n, land):
        def one(i):
            there = land.at[(z + zsize - i) % zsize]
            rcopy(there, there, g_s.at[n, i], g_r.at[n, i], sib, z).wait_recv()

        loop(1, zsize, one)

    def row_plane_wait(n, land):
        def one(i):
            there = land.at[(c + CTX - i) % CTX]
            rcopy(there, there, g_s.at[n, zsize + i], g_r.at[n, zsize + i], sib, z).wait_recv()

        loop(1, CTX, one)

    wq_at = lambda j: wq.at[j, z]
    wgu_at = lambda j: wgu.at[j, z]
    wq_z = lambda j: wq.at[:, j]
    wgu_z = lambda j: wgu.at[:, j]
    wo_z = lambda j: wo.at[j]
    wd_z = lambda j: wd.at[j]

    gz[z] = gains_in[...]
    loop(1, zsize, lambda i: row_z(0, gains_in, gz, i).start())
    a2a_start(0, wq_in, wq_at)
    wq[c, z] = wq_in[c]
    wo[z] = wo_in[...]
    wd[z] = wd_in[...]
    wgu[c, z] = wgu_in[c]
    cot[slot] = cot_ref[...]

    row_z_wait(0, gz)
    gpl[c] = jnp.sum(gz[...], axis=0)
    loop(1, CTX, lambda i: row_plane(0, gpl.at[c], gpl, i).start())

    a2a_wait(0, wq_at)
    zg_start(0, wq_z(z), wq_z)
    zg_start(1, wo_in, wo_z)
    a2a_start(1, wgu_in, wgu_at)

    row_plane_wait(0, gpl)
    gains[...] = jnp.sum(gpl[...], axis=0)
    g_attn = gains[:, :MODEL_WIDTH]
    x_own = x_ref[...].astype(F32)
    s_one = lax.rsqrt(jnp.mean(x_own * x_own, axis=-1, keepdims=True) + NORM_EPS)
    n1[slot] = (x_own * s_one * g_attn).astype(BF16)
    ag_start(0, n1)
    a2a_wait(1, wgu_at)
    ag_pass(0, n1)
    ag_finish(0, n1)
    ag_start(1, cot)
    zg_wait(0, wq_z)
    zg_start(2, wgu_z(z), wgu_z)

    g_query = gains[:, 2 * MODEL_WIDTH : 2 * MODEL_WIDTH + HEAD_SIZE]
    g_key = gains[:, 2 * MODEL_WIDTH + HEAD_SIZE :]

    def tile_rows(t):
        return pl.ds(pl.multiple_of(t * TILE, TILE), TILE)

    def two(buf, t):
        return buf[pl.ds(t * (TILE // rows), TILE // rows)].reshape(TILE, buf.shape[-1])

    def turned(v):
        return pltpu.roll(v, HEAD_SIZE // 2, 1)

    def project(t):
        at = tile_rows(t)
        cosine, sine = cos_ref[at, :], sin_ref[at, :]

        def normed(raw, gain):
            scale = lax.rsqrt(jnp.mean(raw * raw, axis=-1, keepdims=True) + NORM_EPS)
            y = raw * scale * gain
            return y * cosine + turned(y) * sine

        out = dot(two(n1, t), wq[...].reshape(MODEL_WIDTH, PCOLS))
        for h in range(GROUP):
            raw = out[:, h * HEAD_SIZE : (h + 1) * HEAD_SIZE]
            qraw[at, h * HEAD_SIZE : (h + 1) * HEAD_SIZE] = raw
            q_s[h, at, :] = normed(raw, g_query).astype(BF16)
        raw = out[:, QCOLS : QCOLS + HEAD_SIZE]
        kraw[at, :] = raw
        keys = normed(raw, g_key)
        values = out[:, QCOLS + HEAD_SIZE :]
        k_s[at, :] = keys.astype(BF16)
        v_s[at, :] = values.astype(BF16)
        kt_s[:, at] = keys.T.astype(BF16)
        vt_s[:, at] = values.T.astype(BF16)

    loop(0, tiles, project)
    ag_pass(1, cot)

    scale = HEAD_SIZE ** (-0.5)

    def attend(t):
        at = tile_rows(t)
        kpos = kpos_ref[...]
        kept = (kpos <= qpos_ref[:, at]) & (kpos >= qstart_ref[:, at])
        for h in range(GROUP):
            scores = jnp.where(kept, dot(k_s[...], q_s[h, at, :], NT) * scale, MASKED)
            weights = jnp.exp(scores - jnp.max(scores, axis=0, keepdims=True))
            share = 1.0 / jnp.sum(weights, axis=0, keepdims=True)
            low = (weights * share).astype(BF16)
            probs[h, t] = low
            mixed = dot(vt_s[...], low).T
            attn[at, h * HEAD_SIZE : (h + 1) * HEAD_SIZE] = mixed
            attn_low[at, h * HEAD_SIZE : (h + 1) * HEAD_SIZE] = mixed.astype(BF16)

    loop(0, tiles, attend)

    zg_wait(1, wo_z)
    zg_start(3, wd_in, wd_z)

    def n_cols(n):
        return pl.ds(pl.multiple_of(n * TILE, TILE), TILE)

    def half_rows(which):
        return pl.ds(pl.multiple_of(which * half, half), half)

    def half_slots(buf, which):
        return buf[pl.ds(which * CHIPS, CHIPS)].reshape(half, buf.shape[-1])

    def out_part(which, n):
        return dot(
            attn_low[half_rows(which), :], wo[:, :, n_cols(n)].reshape(QCOLS, TILE)
        )

    rs_start(0, out_part)
    ag_finish(1, cot)
    resid = x_ref[...].astype(F32) + rs_finish(0)
    resid_s[...] = resid
    g_mlp = gains[:, MODEL_WIDTH : 2 * MODEL_WIDTH]
    s_two = lax.rsqrt(jnp.mean(resid * resid, axis=-1, keepdims=True) + NORM_EPS)
    n2[slot] = (resid * s_two * g_mlp).astype(BF16)
    ag_start(2, n2)
    ag_pass(2, n2)
    ag_finish(2, n2)

    zg_wait(2, wgu_z)
    zg_wait(3, wd_z)

    def feed(t):
        at = tile_rows(t)
        both = dot(two(n2, t), wgu[...].reshape(MODEL_WIDTH, 2 * HID))
        ghid = dot(two(cot, t), wd[...].reshape(HID, MODEL_WIDTH), NT)
        gate, up = both[:, :HID], both[:, HID:]
        sig = 1.0 / (1.0 + jnp.exp(-gate))
        silu = gate * sig
        hidden[at, :] = (silu * up).astype(BF16)
        ggu[at, :HID] = (ghid * up * sig * (1.0 + gate * (1.0 - sig))).astype(BF16)
        ggu[at, HID:] = (ghid * silu).astype(BF16)

    loop(0, tiles, feed)

    def back_two_part(which, n):
        per = MODEL_WIDTH // CTX
        there = wgu[pl.ds(n * (TILE // per), TILE // per)].reshape(TILE, 2 * HID)
        return dot(ggu[half_rows(which), :], there, NT)

    rs_start(1, back_two_part)

    def down_grad(n):
        there = cot[:, :, n_cols(n)].reshape(2 * half, TILE)
        gwd[:, :, n_cols(n)] = (
            dot(hidden[...], there, TN).astype(BF16).reshape(zsize, HID // zsize, TILE)
        )

    loop(0, MODEL_WIDTH // TILE, down_grad)
    gwd_z = lambda j: gwd.at[j]
    zr_start(4, gwd_z, lwd)

    def gate_up_grad(n):
        per = MODEL_WIDTH // CTX
        there = n2[:, :, n_cols(n)].reshape(2 * half, TILE)
        gwgu[pl.ds(n * (TILE // per), TILE // per)] = (
            dot(there, ggu[...], TN)
            .astype(BF16)
            .reshape(TILE // per, zsize, per // zsize, 2 * HID)
        )

    loop(0, MODEL_WIDTH // TILE, gate_up_grad)
    gwgu_z = lambda j: gwgu.at[:, j]
    zr_start(5, gwgu_z, lwgu)

    def norm_back(values, grads, gain):
        factor = lax.rsqrt(jnp.mean(values * values, axis=-1, keepdims=True) + NORM_EPS)
        unit = values * factor
        scaled = grads * gain
        inner = jnp.mean(scaled * unit, axis=-1, keepdims=True)
        return factor * (scaled - unit * inner), jnp.sum(grads * unit, axis=0, keepdims=True)

    back, terms = norm_back(resid_s[...], rs_finish(1), g_mlp)
    hrow[:, MODEL_WIDTH : 2 * MODEL_WIDTH] = terms
    gresid = cot_ref[...].astype(F32) + back
    gresid_s[...] = gresid
    gb[slot] = gresid.astype(BF16)
    ag_start(3, gb)

    def down_part(which, n):
        return dot(hidden[half_rows(which), :], wd[:, :, n_cols(n)].reshape(HID, TILE))

    ag_pass(3, gb)
    rs_start(2, down_part)
    ag_finish(3, gb)

    def attn_grad(t):
        gattn[tile_rows(t), :] = dot(
            two(gb, t), wo[...].reshape(QCOLS, MODEL_WIDTH), NT
        ).astype(BF16)

    loop(0, tiles, attn_grad)
    dk_s[...] = jnp.zeros_like(dk_s)
    dv_s[...] = jnp.zeros_like(dv_s)

    def attend_back(t):
        at = tile_rows(t)
        for h in range(GROUP):
            head = slice(h * HEAD_SIZE, (h + 1) * HEAD_SIZE)
            grads = gattn[at, head]
            delta = jnp.sum((grads.astype(F32) * attn[at, head]).T, axis=0, keepdims=True)
            low = probs[h, t]
            gprobs = dot(v_s[...], grads, NT)
            gscores = (low.astype(F32) * (gprobs - delta)).astype(BF16)
            dv_s[...] += dot(low, grads)
            dk_s[...] += dot(gscores, q_s[h, at, :])
            dq_s[at, head] = dot(kt_s[...], gscores).T

    loop(0, tiles, attend_back)

    def out_grad(n):
        there = gb[:, :, n_cols(n)].reshape(2 * half, TILE)
        gwo[:, :, n_cols(n)] = (
            dot(attn_low[...], there, TN).astype(BF16).reshape(zsize, QCOLS // zsize, TILE)
        )

    loop(0, MODEL_WIDTH // TILE, out_grad)
    gwo_z = lambda j: gwo.at[j]
    zr_start(6, gwo_z, lwo)

    hrow[:, 2 * MODEL_WIDTH :] = jnp.zeros((1, 2 * HEAD_SIZE), F32)

    def project_back(t):
        at = tile_rows(t)
        cosine, sine = cos_ref[at, :], sin_ref[at, :]

        def one(raw, grads, gain):
            grads = grads * scale
            grads = grads * cosine - turned(grads) * sine
            return norm_back(raw, grads, gain)

        lo = 2 * MODEL_WIDTH
        for h in range(GROUP):
            head = slice(h * HEAD_SIZE, (h + 1) * HEAD_SIZE)
            back, terms = one(qraw[at, head], dq_s[at, head], g_query)
            gp[at, head] = back.astype(BF16)
            hrow[:, lo : lo + HEAD_SIZE] += terms
        back, terms = one(kraw[at, :], dk_s[at, :], g_key)
        gp[at, QCOLS : QCOLS + HEAD_SIZE] = back.astype(BF16)
        hrow[:, lo + HEAD_SIZE :] += terms
        gp[at, QCOLS + HEAD_SIZE :] = dv_s[at, :].astype(BF16)

    loop(0, tiles, project_back)

    def qkv_grad(n):
        per = MODEL_WIDTH // CTX
        there = n1[:, :, n_cols(n)].reshape(2 * half, TILE)
        gwq[pl.ds(n * (TILE // per), TILE // per)] = (
            dot(there, gp[...], TN)
            .astype(BF16)
            .reshape(TILE // per, zsize, per // zsize, PCOLS)
        )

    loop(0, MODEL_WIDTH // TILE, qkv_grad)
    gwq_z = lambda j: gwq.at[:, j]
    zr_start(7, gwq_z, lwq)

    def back_one_part(which, n):
        per = MODEL_WIDTH // CTX
        there = wq[pl.ds(n * (TILE // per), TILE // per)].reshape(TILE, PCOLS)
        return dot(gp[half_rows(which), :], there, NT)

    out_ref[...] = (resid_s[...] + rs_finish(2)).astype(BF16)
    rs_start(3, back_one_part)

    gd_ref[...] = zr_finish(4, gwd_z, lwd)
    asg[...] = zr_finish(5, gwgu_z, lwgu).astype(BF16)
    arg_at = lambda j: arg_.at[j]
    a2a_start(2, asg, arg_at)
    arg_[c] = asg[c]

    back, terms = norm_back(x_ref[...].astype(F32), rs_finish(3), gains[:, :MODEL_WIDTH])
    xgrad_ref[...] = (gresid_s[...] + back).astype(BF16)
    hrow[:, :MODEL_WIDTH] = terms
    hz[z] = hrow[...]
    loop(1, zsize, lambda i: row_z(1, hrow, hz, i).start())
    go_ref[...] = zr_finish(6, gwo_z, lwo)
    row_z_wait(1, hz)
    hpl[c] = jnp.sum(hz[...], axis=0)
    loop(1, CTX, lambda i: row_plane(1, hpl.at[c], hpl, i).start())
    a2a_wait(2, arg_at)
    ggu_ref[...] = arg_[...].astype(F32)
    row_plane_wait(1, hpl)
    gg_ref[...] = jnp.sum(hpl[...], axis=0)

    asq[...] = zr_finish(7, gwq_z, lwq).astype(BF16)
    gq_at = lambda j: gq_ref.at[j]
    a2a_start(3, asq, gq_at)
    gq_ref[c] = asq[c]
    a2a_wait(3, gq_at)

    for n, buf in enumerate((n1, cot, n2, gb)):
        ag_drain(n, buf)
    rs_pair(3).wait_send()
    for i in (1, 2, 3):
        rs_chip(3, i).wait_send()
    a2a_drain(0, wq_in, wq_at)
    a2a_drain(1, wgu_in, wgu_at)
    a2a_drain(2, asg, arg_at)
    a2a_drain(3, asq, gq_at)
    zg_drain(0, wq_z(z), wq_z)
    zg_drain(1, wo_in, wo_z)
    zg_drain(2, wgu_z(z), wgu_z)
    zg_drain(3, wd_in, wd_z)
    zr_drain(4, gwd_z, lwd)
    zr_drain(5, gwgu_z, lwgu)
    zr_drain(6, gwo_z, lwo)
    zr_drain(7, gwq_z, lwq)
    loop(1, zsize, lambda i: row_z(0, gains_in, gz, i).wait_send())
    loop(1, CTX, lambda i: row_plane(0, gpl.at[c], gpl, i).wait_send())
    loop(1, zsize, lambda i: row_z(1, hrow, hz, i).wait_send())
    loop(1, CTX, lambda i: row_plane(1, hpl.at[c], hpl, i).wait_send())


def layer_call(zsize, rows, *operands):
    length = CTX * rows
    tiles = length // TILE
    width = MODEL_WIDTH
    per = width // CTX // zsize
    vm = pltpu.VMEM
    dma = pltpu.SemaphoreType.DMA
    shape = jax.ShapeDtypeStruct
    full = vm((CTX, rows, width), BF16)
    scratch = [
        full,
        full,
        full,
        full,
        vm((CTX, zsize, per, PCOLS), BF16),
        vm((zsize, QCOLS // zsize, width), BF16),
        vm((CTX, zsize, per, 2 * HID), BF16),
        vm((zsize, HID // zsize, width), BF16),
        vm((length, QCOLS), F32),
        vm((length, HEAD_SIZE), F32),
        vm((GROUP, length, HEAD_SIZE), BF16),
        vm((length, HEAD_SIZE), BF16),
        vm((length, HEAD_SIZE), BF16),
        vm((HEAD_SIZE, length), BF16),
        vm((HEAD_SIZE, length), BF16),
        vm((GROUP, tiles, length, TILE), BF16),
        vm((length, QCOLS), F32),
        vm((length, QCOLS), BF16),
        vm((length, HID), BF16),
        vm((length, 2 * HID), BF16),
        vm((length, QCOLS), BF16),
        vm((length, QCOLS), F32),
        vm((length, HEAD_SIZE), F32),
        vm((length, HEAD_SIZE), F32),
        vm((length, PCOLS), BF16),
        vm((CHIPS, rows, width), BF16),
        vm((4, CHIPS, rows, width), BF16),
        vm((CHIPS - 1, rows, width), BF16),
        vm((4, CHIPS - 1, rows, width), BF16),
        vm((CHIPS, rows, width), F32),
        vm((4, rows, width), F32),
        vm((rows, width), F32),
        vm((rows, width), F32),
        vm((CTX, zsize, per, PCOLS), BF16),
        vm((zsize, QCOLS // zsize, width), BF16),
        vm((CTX, zsize, per, 2 * HID), BF16),
        vm((zsize, HID // zsize, width), BF16),
        vm((zsize - 1, CTX, per, PCOLS), BF16),
        vm((zsize - 1, QCOLS // zsize, width), BF16),
        vm((zsize - 1, CTX, per, 2 * HID), BF16),
        vm((zsize - 1, HID // zsize, width), BF16),
        vm((CTX, per, PCOLS), BF16),
        vm((CTX, per, 2 * HID), BF16),
        vm((CTX, per, 2 * HID), BF16),
        vm((zsize, 1, GAIN_WIDTH), F32),
        vm((CTX, 1, GAIN_WIDTH), F32),
        vm((1, GAIN_WIDTH), F32),
        vm((zsize, 1, GAIN_WIDTH), F32),
        vm((CTX, 1, GAIN_WIDTH), F32),
        vm((1, GAIN_WIDTH), F32),
        dma((4, 7)),
        dma((4, 7)),
        dma((4,)),
        dma((4,)),
        dma((4, 3)),
        dma((4, 3)),
        dma((4, CTX)),
        dma((4, CTX)),
        dma((8, zsize)),
        dma((8, zsize)),
        dma((2, zsize + CTX)),
        dma((2, zsize + CTX)),
        dma((4,)),
    ]
    return pl.pallas_call(
        functools.partial(layer_kernel, zsize),
        out_shape=(
            shape((rows, width), BF16),
            shape((rows, width), BF16),
            shape((CTX, per, PCOLS), BF16),
            shape((QCOLS // zsize, width), F32),
            shape((CTX, per, 2 * HID), F32),
            shape((HID // zsize, width), F32),
            shape((1, GAIN_WIDTH), F32),
        ),
        in_specs=[pl.BlockSpec(memory_space=pltpu.VMEM)] * len(operands),
        out_specs=[pl.BlockSpec(memory_space=pltpu.VMEM)] * 7,
        scratch_shapes=scratch,
        compiler_params=pltpu.CompilerParams(
            collective_id=1, has_side_effects=True, vmem_limit_bytes=62 << 20
        ),
        name="layer",
    )(*operands)


def local_planes(tokens, cotangent, stretch_order, doc_lengths, master, first_moment, second_moment):
    cycle_size = lax.axis_size("ctx")
    zsize = lax.axis_size("fsdp")
    shards = cycle_size * zsize
    j = lax.axis_index("ctx") * zsize + lax.axis_index("fsdp")
    _, rows, width = tokens.shape
    length = rows * cycle_size
    spans = [r // shards * w for r, w in segment_shapes()]
    ends = [sum(spans[: i + 1]) for i in range(5)]
    low = master.astype(BF16)
    per = width // shards
    kv = KEY_VALUE_HEADS * HEAD_SIZE
    seg = low[: ends[0]].reshape(per, -1)
    wq_in = jnp.concatenate(
        [
            seg[:, : 2 * kv].reshape(per, CTX, QCOLS),
            seg[:, 2 * kv : 3 * kv].reshape(per, CTX, HEAD_SIZE),
            seg[:, 3 * kv :].reshape(per, CTX, HEAD_SIZE),
        ],
        axis=2,
    ).transpose(1, 0, 2)
    wo_in = low[ends[0] : ends[1]].reshape(-1, width)
    seg = low[ends[1] : ends[2]].reshape(per, 2, CTX, HID)
    wgu_in = seg.transpose(2, 0, 1, 3).reshape(CTX, per, 2 * HID)
    wd_in = low[ends[2] : ends[3]].reshape(-1, width)
    own_gains = low[ends[3] :].astype(F32)
    gains_in = lax.dynamic_update_slice(
        jnp.zeros((1, GAIN_WIDTH), F32), own_gains[None, :], (0, j * spans[4])
    )

    def slots(v):
        return v.reshape(CHIPS, 2, rows).transpose(1, 0, 2).reshape(length)

    pos = slot_positions(stretch_order, 0, length)
    _, relative = documents(pos, doc_lengths)
    pos, relative = slots(pos), slots(relative[0])
    cosine, sine = rope_tables(relative)
    sine = jnp.concatenate([-sine[:, : HEAD_SIZE // 2], sine[:, HEAD_SIZE // 2 :]], axis=1)
    out, xgrad, gq, go, ggu, gd, gg = layer_call(
        zsize,
        rows,
        tokens[0],
        cotangent[0],
        wq_in,
        wo_in,
        wgu_in,
        wd_in,
        gains_in,
        cosine,
        sine,
        pos[:, None],
        pos[None, :],
        (pos - relative)[None, :],
    )
    gq = gq.astype(F32)
    gq_rows = jnp.concatenate(
        [
            gq[:, :, :QCOLS].transpose(1, 0, 2).reshape(per, -1),
            gq[:, :, QCOLS : QCOLS + HEAD_SIZE].transpose(1, 0, 2).reshape(per, -1),
            gq[:, :, QCOLS + HEAD_SIZE :].transpose(1, 0, 2).reshape(per, -1),
        ],
        axis=1,
    )
    ggu_rows = ggu.reshape(CTX, per, 2, HID).transpose(1, 2, 0, 3)
    grad = jnp.concatenate(
        [
            gq_rows.reshape(-1),
            go.reshape(-1),
            ggu_rows.reshape(-1),
            gd.reshape(-1),
            lax.dynamic_slice(gg, (0, j * spans[4]), (1, spans[4])).reshape(-1),
        ]
    )
    new = adam(grad, master, first_moment, second_moment, shards, length)
    return (out[None], xgrad[None], *new)


def adam(grad, master, first_moment, second_moment, shards, length):
    step_rate, decay_value = rate_rows(shards, length)
    new_first = BETA_ONE * first_moment + (1.0 - BETA_ONE) * grad
    new_second = BETA_TWO * second_moment + (1.0 - BETA_TWO) * grad * grad
    normalized = (
        new_first
        / (1.0 - BETA_ONE**STEP)
        / (jnp.sqrt(new_second / (1.0 - BETA_TWO**STEP)) + ADAM_EPS)
    )
    new_master = master - step_rate * (normalized + decay_value * master)
    return new_master, new_first, new_second


def solution(mesh):
    placed = (
        P("fsdp", "ctx", None),
        P("fsdp", "ctx", None),
        P(),
        P("fsdp", None),
        P(("ctx", "fsdp")),
        P(("ctx", "fsdp")),
        P(("ctx", "fsdp")),
    )
    plane = mesh.shape["ctx"] == CTX and KEY_VALUE_HEADS == CTX
    return jax.shard_map(
        local_planes if plane else local,
        mesh=mesh,
        in_specs=placed,
        out_specs=(
            P("fsdp", "ctx", None),
            P("fsdp", "ctx", None),
            P(("ctx", "fsdp")),
            P(("ctx", "fsdp")),
            P(("ctx", "fsdp")),
        ),
        check_vma=False,
    )
```

```python
import math

import jax
import jax.numpy as jnp
from jax import lax
from jax.experimental import pallas as pl
from jax.experimental.pallas import tpu as pltpu
from jax.sharding import PartitionSpec as P

MODEL_WIDTH = 1024
QUERY_HEADS = 16
KEY_VALUE_HEADS = 8
HEAD_SIZE = 128
FEED_WIDTH = 3072
STRETCH = 64
STEP = 7


NORM_EPS = 1e-06
ROPE_BASE = 1000000.0
BETA_ONE = 0.5
BETA_TWO = 0.5
DECAY_RATE = 0.1
ADAM_EPS = 1e-08
MASKED = -1e30


def from_behind(x, axis, by):
    peers = lax.axis_size(axis)
    return lax.ppermute(x, axis, [(i, (i + by) % peers) for i in range(peers)])


def segment_shapes():
    return [
        (MODEL_WIDTH, (QUERY_HEADS + 2 * KEY_VALUE_HEADS) * HEAD_SIZE),
        (QUERY_HEADS * HEAD_SIZE, MODEL_WIDTH),
        (MODEL_WIDTH, 2 * FEED_WIDTH),
        (FEED_WIDTH, MODEL_WIDTH),
        (2 * MODEL_WIDTH + 2 * HEAD_SIZE, 1),
    ]


def unpack(flat_params, count_of_shards):
    param_table = flat_params.reshape(count_of_shards, -1)
    pieces = []
    offset = 0
    for row_total, column_total in segment_shapes():
        shard_span = row_total // count_of_shards * column_total
        pieces.append(param_table[:, offset : offset + shard_span].reshape(row_total, column_total))
        offset += shard_span
    return pieces


def pack(matrices, count_of_shards):
    return jnp.concatenate(
        [matrix.reshape(count_of_shards, -1) for matrix in matrices], axis=1
    ).reshape(-1)


def slot_positions(stretch_order, first_row, count_of_rows):
    row_ids = first_row + jnp.arange(count_of_rows, dtype=jnp.int32)
    slot_ids = row_ids // STRETCH
    slot_table = jnp.arange(stretch_order.shape[0], dtype=jnp.int32)
    stretch_ids = jnp.sum(
        jnp.where(slot_ids[:, None] == slot_table[None, :], stretch_order[None, :], 0), axis=1
    )
    return stretch_ids * STRETCH + row_ids % STRETCH


def documents(positions, doc_lengths):
    doc_ends = jnp.cumsum(doc_lengths, axis=1)
    doc_starts = doc_ends - doc_lengths
    passed = positions[None, :, None] >= doc_ends[:, None, :-1]
    doc_ids = jnp.sum(passed.astype(jnp.int32), axis=2)
    doc_table = jnp.arange(doc_lengths.shape[1], dtype=jnp.int32)
    owner = doc_ids[:, :, None] == doc_table[None, None, :]
    start_of = jnp.sum(jnp.where(owner, doc_starts[:, None, :], 0), axis=2)
    return (doc_ids, positions[None, :] - start_of)


def key_mask(stretch_order, doc_lengths, query_pos, query_doc, first_row, count_of_rows):
    key_pos = slot_positions(stretch_order, first_row, count_of_rows)
    key_doc, _ = documents(key_pos, doc_lengths)
    same_doc = query_doc[:, :, None] == key_doc[:, None, :]
    return same_doc & (key_pos[None, None, :] <= query_pos[None, :, None])


def rope_tables(relative):
    half_dim = HEAD_SIZE // 2
    frequency = ROPE_BASE ** (-(jnp.arange(half_dim, dtype=jnp.float32) * 2.0 / HEAD_SIZE))
    angles = relative.astype(jnp.float32)[..., None] * frequency
    cosine_table = jnp.cos(angles)
    sine_values = jnp.sin(angles)
    return (
        jnp.concatenate([cosine_table, cosine_table], axis=-1),
        jnp.concatenate([sine_values, sine_values], axis=-1),
    )


def rotate(values, cosine_table, sine_values):
    half_dim = values.shape[-1] // 2
    turned = jnp.concatenate([-values[..., half_dim:], values[..., :half_dim]], axis=-1)
    return values * cosine_table[..., None, :] + turned * sine_values[..., None, :]


def rotate_back(grads, cosine_table, sine_values):
    half_dim = grads.shape[-1] // 2
    moved = grads * sine_values[..., None, :]
    unturned = jnp.concatenate([moved[..., half_dim:], -moved[..., :half_dim]], axis=-1)
    return grads * cosine_table[..., None, :] + unturned


def rms_norm(values, scaling):
    factor = lax.rsqrt(jnp.mean(values * values, axis=-1, keepdims=True) + NORM_EPS)
    return values * factor * scaling


def norm_back(values, grads, scaling):
    factor = lax.rsqrt(jnp.mean(values * values, axis=-1, keepdims=True) + NORM_EPS)
    unit_values = values * factor
    scaled_grads = grads * scaling
    inner = jnp.mean(scaled_grads * unit_values, axis=-1, keepdims=True)
    return (factor * (scaled_grads - unit_values * inner), grads * unit_values)


def attend_block(state, queries, key_value_block, allowed, score_scale):
    running, top_now, total_now = state
    sequence_count, count_of_keys = (key_value_block.shape[1], key_value_block.shape[2])
    block_keys = key_value_block[0].reshape(
        sequence_count, count_of_keys, KEY_VALUE_HEADS, HEAD_SIZE
    )
    block_values = key_value_block[1].reshape(
        sequence_count, count_of_keys, KEY_VALUE_HEADS, HEAD_SIZE
    )
    mask_wide = allowed[:, :, None, None, :]
    scores = (
        jnp.einsum("sqhgd,snhd->sqhgn", queries, block_keys, preferred_element_type=jnp.float32)
        * score_scale
    )
    new_top = jnp.maximum(top_now, jnp.max(jnp.where(mask_wide, scores, MASKED), axis=-1))
    weights = jnp.where(mask_wide, jnp.exp(scores - new_top[..., None]), 0.0)
    factor = jnp.exp(top_now - new_top)
    total_now = total_now * factor + jnp.sum(weights, axis=-1)
    running = running * factor[..., None] + jnp.einsum(
        "sqhgn,snhd->sqhgd",
        weights.astype(jnp.bfloat16),
        block_values,
        preferred_element_type=jnp.float32,
    )
    return (running, new_top, total_now)


def backward_block(
    queries, attention_gradient, log_total, delta, key_value_block, allowed, score_scale
):
    sequence_count, count_of_keys = (key_value_block.shape[1], key_value_block.shape[2])
    block_keys = key_value_block[0].reshape(
        sequence_count, count_of_keys, KEY_VALUE_HEADS, HEAD_SIZE
    )
    block_values = key_value_block[1].reshape(
        sequence_count, count_of_keys, KEY_VALUE_HEADS, HEAD_SIZE
    )
    mask_wide = allowed[:, :, None, None, :]
    scores = (
        jnp.einsum("sqhgd,snhd->sqhgn", queries, block_keys, preferred_element_type=jnp.float32)
        * score_scale
    )
    probabilities = jnp.where(mask_wide, jnp.exp(scores - log_total[..., None]), 0.0)
    value_gradient = jnp.einsum(
        "sqhgn,sqhgd->snhd",
        probabilities.astype(jnp.bfloat16),
        attention_gradient,
        preferred_element_type=jnp.float32,
    )
    grad_probs = jnp.einsum(
        "sqhgd,snhd->sqhgn", attention_gradient, block_values, preferred_element_type=jnp.float32
    )
    grad_scores = (probabilities * (grad_probs - delta[..., None])).astype(jnp.bfloat16)
    grad_queries = (
        jnp.einsum("sqhgn,snhd->sqhgd", grad_scores, block_keys, preferred_element_type=jnp.float32)
        * score_scale
    )
    key_gradient = (
        jnp.einsum("sqhgn,sqhgd->snhd", grad_scores, queries, preferred_element_type=jnp.float32)
        * score_scale
    )
    grad_pair = jnp.stack(
        [
            key_gradient.reshape(sequence_count, count_of_keys, KEY_VALUE_HEADS * HEAD_SIZE),
            value_gradient.reshape(sequence_count, count_of_keys, KEY_VALUE_HEADS * HEAD_SIZE),
        ]
    )
    return (grad_queries, grad_pair)


def summed(part, count_of_shards):
    return lax.psum_scatter(
        part.reshape(-1), ("ctx", "fsdp"), scatter_dimension=0, tiled=True
    )


def local(tokens, cotangent, stretch_order, doc_lengths, master, first_moment, second_moment):
    cycle_size = lax.axis_size("ctx")
    ctx_index = lax.axis_index("ctx")
    count_of_shards = cycle_size * lax.axis_size("fsdp")
    sequence_count, count_of_rows, _ = tokens.shape
    seq_length = count_of_rows * cycle_size
    query_groups = QUERY_HEADS // KEY_VALUE_HEADS
    score_scale = HEAD_SIZE ** (-0.5)
    gathered = lax.all_gather(master.astype(jnp.bfloat16), ("ctx", "fsdp"), axis=0, tiled=True)
    w_qkv, w_out, w_gate_up, w_down, gain_column = unpack(gathered, count_of_shards)
    gains = gain_column.reshape(-1).astype(jnp.float32)
    g_attn = gains[:MODEL_WIDTH]
    g_mlp = gains[MODEL_WIDTH : 2 * MODEL_WIDTH]
    g_query = gains[2 * MODEL_WIDTH : 2 * MODEL_WIDTH + HEAD_SIZE]
    g_key = gains[2 * MODEL_WIDTH + HEAD_SIZE :]
    query_pos = slot_positions(stretch_order, ctx_index * count_of_rows, count_of_rows)
    query_doc, relative = documents(query_pos, doc_lengths)
    cosine_table, sine_values = rope_tables(relative)
    x_in = tokens.astype(jnp.float32)
    normed_one = rms_norm(x_in, g_attn).astype(jnp.bfloat16)
    projected_output = jnp.einsum(
        "sqd,de->sqe", normed_one, w_qkv, preferred_element_type=jnp.float32
    )
    query_raw = projected_output[:, :, : QUERY_HEADS * HEAD_SIZE].reshape(
        sequence_count, count_of_rows, QUERY_HEADS, HEAD_SIZE
    )
    unrotated_keys = projected_output[
        :, :, QUERY_HEADS * HEAD_SIZE : (QUERY_HEADS + KEY_VALUE_HEADS) * HEAD_SIZE
    ].reshape(sequence_count, count_of_rows, KEY_VALUE_HEADS, HEAD_SIZE)
    unprojected_values = projected_output[:, :, (QUERY_HEADS + KEY_VALUE_HEADS) * HEAD_SIZE :]
    queries = (
        rotate(rms_norm(query_raw, g_query), cosine_table, sine_values)
        .astype(jnp.bfloat16)
        .reshape(sequence_count, count_of_rows, KEY_VALUE_HEADS, query_groups, HEAD_SIZE)
    )
    keys_rot = rotate(rms_norm(unrotated_keys, g_key), cosine_table, sine_values).reshape(
        sequence_count, count_of_rows, KEY_VALUE_HEADS * HEAD_SIZE
    )
    kv_local = jnp.stack([keys_rot, unprojected_values]).astype(jnp.bfloat16)
    statistic_shape = (sequence_count, count_of_rows, KEY_VALUE_HEADS, query_groups)
    initial = (
        jnp.zeros(statistic_shape + (HEAD_SIZE,), jnp.float32),
        jnp.full(statistic_shape, MASKED, jnp.float32),
        jnp.zeros(statistic_shape, jnp.float32),
    )
    state = initial
    piece = lax.all_gather(kv_local, "ctx", axis=2, tiled=True)
    key_total = piece.shape[2]

    def key_step(inner, block_index):
        first_row = block_index * count_of_rows
        key_value_block = lax.dynamic_slice_in_dim(piece, first_row, count_of_rows, 2)
        allowed = key_mask(
            stretch_order, doc_lengths, query_pos, query_doc, first_row, count_of_rows
        )
        return (attend_block(inner, queries, key_value_block, allowed, score_scale), None)

    state, _ = lax.scan(key_step, state, jnp.arange(key_total // count_of_rows, dtype=jnp.int32))
    running, top_now, total_now = state
    attn = running / total_now[..., None]
    log_total = top_now + jnp.log(total_now)
    attn_low = attn.reshape(sequence_count, count_of_rows, QUERY_HEADS * HEAD_SIZE).astype(
        jnp.bfloat16
    )
    resid = x_in + jnp.einsum("sqa,ad->sqd", attn_low, w_out, preferred_element_type=jnp.float32)
    normed_two = rms_norm(resid, g_mlp).astype(jnp.bfloat16)
    gate_up = jnp.einsum("sqd,de->sqe", normed_two, w_gate_up, preferred_element_type=jnp.float32)
    gate = gate_up[:, :, :FEED_WIDTH]
    up_part = gate_up[:, :, FEED_WIDTH:]
    sigmoid_gate = jax.nn.sigmoid(gate)
    hidden = (gate * sigmoid_gate * up_part).astype(jnp.bfloat16)
    mlp_out = jnp.einsum("sqf,fd->sqd", hidden, w_down, preferred_element_type=jnp.float32)
    layer_out = (resid + mlp_out).astype(jnp.bfloat16)
    grad_w_down = jnp.einsum("sqf,sqd->fd", hidden, cotangent, preferred_element_type=jnp.float32)
    grad_hidden = jnp.einsum("sqd,fd->sqf", cotangent, w_down, preferred_element_type=jnp.float32)
    grad_gate = grad_hidden * up_part * sigmoid_gate * (1.0 + gate * (1.0 - sigmoid_gate))
    grad_up = grad_hidden * gate * sigmoid_gate
    grad_gate_up = jnp.concatenate([grad_gate, grad_up], axis=-1).astype(jnp.bfloat16)
    grad_w_gate_up = jnp.einsum(
        "sqd,sqe->de", normed_two, grad_gate_up, preferred_element_type=jnp.float32
    )
    grad_normed_two = jnp.einsum(
        "sqe,de->sqd", grad_gate_up, w_gate_up, preferred_element_type=jnp.float32
    )
    back_two, mlp_gain_terms = norm_back(resid, grad_normed_two, g_mlp)
    grad_resid = cotangent.astype(jnp.float32) + back_two
    grad_branch = grad_resid.astype(jnp.bfloat16)
    grad_w_out = jnp.einsum(
        "sqa,sqd->ad", attn_low, grad_branch, preferred_element_type=jnp.float32
    )
    attention_gradient = jnp.einsum(
        "sqd,ad->sqa", grad_branch, w_out, preferred_element_type=jnp.float32
    ).astype(jnp.bfloat16)
    attention_head_gradient = attention_gradient.reshape(
        sequence_count, count_of_rows, KEY_VALUE_HEADS, query_groups, HEAD_SIZE
    )
    delta = jnp.sum(attention_head_gradient.astype(jnp.float32) * attn, axis=-1)

    def grads_from(turn_index, kv_now, key_value_gradients, grad_queries):
        source_dev = (ctx_index - turn_index) % cycle_size
        allowed = key_mask(
            stretch_order,
            doc_lengths,
            query_pos,
            query_doc,
            source_dev * count_of_rows,
            count_of_rows,
        )
        part_queries, part_pair = backward_block(
            queries, attention_head_gradient, log_total, delta, kv_now, allowed, score_scale
        )
        return (key_value_gradients + part_pair, grad_queries + part_queries)

    def pass_grads(key_value_gradients):
        return from_behind(key_value_gradients.astype(jnp.bfloat16), "ctx", 1).astype(
            key_value_gradients.dtype
        )

    def turn_step(turn_index, state):
        kv_now, key_value_gradients, grad_queries = state
        key_value_gradients, grad_queries = grads_from(
            turn_index, kv_now, key_value_gradients, grad_queries
        )
        kv_now = from_behind(kv_now, "ctx", 1)
        key_value_gradients = pass_grads(key_value_gradients)
        return (kv_now, key_value_gradients, grad_queries)

    start_state = (
        kv_local,
        jnp.zeros(kv_local.shape, jnp.float32),
        jnp.zeros(statistic_shape + (HEAD_SIZE,), jnp.float32),
    )
    kv_now, key_value_gradients, grad_queries = lax.fori_loop(
        0, cycle_size - 1, turn_step, start_state
    )
    key_value_gradients, grad_queries = grads_from(
        cycle_size - 1, kv_now, key_value_gradients, grad_queries
    )
    key_value_gradients = pass_grads(key_value_gradients)
    grad_query_rot = rotate_back(
        grad_queries.reshape(sequence_count, count_of_rows, QUERY_HEADS, HEAD_SIZE),
        cosine_table,
        sine_values,
    )
    grad_key_rot = rotate_back(
        key_value_gradients[0].reshape(sequence_count, count_of_rows, KEY_VALUE_HEADS, HEAD_SIZE),
        cosine_table,
        sine_values,
    )
    grad_query_raw, query_gain_terms = norm_back(query_raw, grad_query_rot, g_query)
    unrotated_key_gradient, key_gain_terms = norm_back(unrotated_keys, grad_key_rot, g_key)
    grad_projected = jnp.concatenate(
        [
            grad_query_raw.reshape(sequence_count, count_of_rows, QUERY_HEADS * HEAD_SIZE),
            unrotated_key_gradient.reshape(
                sequence_count, count_of_rows, KEY_VALUE_HEADS * HEAD_SIZE
            ),
            key_value_gradients[1],
        ],
        axis=-1,
    ).astype(jnp.bfloat16)
    grad_w_qkv = jnp.einsum(
        "sqd,sqe->de", normed_one, grad_projected, preferred_element_type=jnp.float32
    )
    grad_normed_one = jnp.einsum(
        "sqe,de->sqd", grad_projected, w_qkv, preferred_element_type=jnp.float32
    )
    back_one, attn_gain_terms = norm_back(x_in, grad_normed_one, g_attn)
    input_grad = (grad_resid + back_one).astype(jnp.bfloat16)
    grad_gains = jnp.concatenate(
        [
            jnp.sum(attn_gain_terms, axis=(0, 1)),
            jnp.sum(mlp_gain_terms, axis=(0, 1)),
            jnp.sum(query_gain_terms, axis=(0, 1, 2)),
            jnp.sum(key_gain_terms, axis=(0, 1, 2)),
        ]
    ).reshape(-1, 1)
    grad = jnp.concatenate(
        [
            summed(part, count_of_shards)
            for part in (grad_w_qkv, grad_w_out, grad_w_gate_up, grad_w_down, grad_gains)
        ]
    )
    new_master, new_first, new_second = adam(
        grad, master, first_moment, second_moment, count_of_shards, seq_length
    )
    return (layer_out, input_grad, new_master, new_first, new_second)


MESH = pl.DeviceIdType.MESH
F32 = jnp.float32
BF16 = jnp.bfloat16
CTX = 8
CHIPS = 4
GROUP = QUERY_HEADS // KEY_VALUE_HEADS
QCOLS = GROUP * HEAD_SIZE
PCOLS = QCOLS + 2 * HEAD_SIZE
HID = FEED_WIDTH // CTX
GAIN_WIDTH = 2 * MODEL_WIDTH + 2 * HEAD_SIZE
TILE = 256


def dot(a, b, dims=((1,), (0,))):
    return lax.dot_general(a, b, (dims, ((), ())), preferred_element_type=F32)


NT = ((1,), (1,))
TN = ((0,), (0,))


def layer_kernel(
    order_ref,
    doc_ref,
    x_hbm,
    cot_hbm,
    master_hbm,
    out_ref,
    xgrad_ref,
    lin_ref,
    flat,
    flat_gains,
    lines,
    wq_in,
    wgu_in,
    gains_in,
    cos_ref,
    sin_ref,
    kpos_ref,
    qpos_ref,
    qstart_ref,
    xg,
    n1,
    cot,
    n2,
    gb,
    wq,
    wo,
    wgu,
    wd,
    qraw,
    kraw,
    q_s,
    k_s,
    v_s,
    kt_s,
    vt_s,
    probs,
    attn,
    attn_low,
    hidden,
    ggu,
    gattn,
    dk_s,
    dv_s,
    gp,
    psnd,
    prcv,
    csnd,
    crcv,
    own,
    acc,
    resid_s,
    gresid_s,
    gwq,
    gwo,
    gwgu,
    gwd,
    lwq,
    lwo,
    lwgu,
    lwd,
    asq,
    asg,
    arq,
    arg_,
    sum_sq,
    sum_o,
    sum_d,
    sum_gu,
    gz,
    gpl,
    gains,
    hz,
    hpl,
    hrow,
    ag_s,
    ag_r,
    rs_ps,
    rs_pr,
    rs_cs,
    rs_cr,
    a2a_s,
    a2a_r,
    zg_s,
    zg_r,
    zr_s,
    zr_r,
    g_s,
    g_r,
    loc,
):
    c = lax.axis_index("ctx")
    z = lax.axis_index("fsdp")
    core = c % 2
    chip = c // 2
    cx = chip % 2
    cy = chip // 2
    slot = core * CHIPS + chip
    sib = c + 1 - 2 * core
    tiles = n1.shape[0] * n1.shape[1] // TILE
    rows = n1.shape[1]
    half = CHIPS * rows

    def chip_at(i):
        return ((cy + i // 2) % 2) * 2 + (cx + i % 2) % 2

    def rcopy(src, dst, ssem, rsem, to_c, to_z):
        return pltpu.make_async_remote_copy(
            src_ref=src,
            dst_ref=dst,
            send_sem=ssem,
            recv_sem=rsem,
            device_id=(to_c, to_z),
            device_id_type=MESH,
        )

    def loop(lo, hi, body):
        def step(i, carry):
            body(i)
            return carry

        lax.fori_loop(lo, hi, step, 0)

    spans = [r // (4 * CTX) * w for r, w in segment_shapes()]
    ends = [sum(spans[: i + 1]) for i in range(5)]
    tail = ends[3]
    fetch = [
        pltpu.make_async_copy(
            master_hbm.at[pl.ds(0, ends[1])], flat.at[pl.ds(0, ends[1])], loc.at[0]
        ),
        pltpu.make_async_copy(master_hbm.at[pl.ds(tail, spans[4])], flat_gains, loc.at[3]),
        pltpu.make_async_copy(
            master_hbm.at[pl.ds(ends[1], tail - ends[1])],
            flat.at[pl.ds(ends[1], tail - ends[1])],
            loc.at[4],
        ),
        pltpu.make_async_copy(x_hbm.at[0], xg.at[slot], loc.at[1]),
        pltpu.make_async_copy(cot_hbm.at[0], cot.at[slot], loc.at[2]),
    ]
    for copy in fetch:
        copy.start()
    barrier = pltpu.get_barrier_semaphore()

    def greet_plane(i):
        pl.semaphore_signal(
            barrier, inc=1, device_id=((c + i) % CTX, z), device_id_type=MESH
        )

    def greet_z(i):
        pl.semaphore_signal(
            barrier, inc=1, device_id=(c, (z + i) % 4), device_id_type=MESH
        )

    loop(1, CTX, greet_plane)
    loop(1, 4, greet_z)

    def to_lines(i):
        lines[pl.ds(pl.multiple_of(i * 128, 128), 128), :] = flat[
            pl.ds(pl.multiple_of(i * 128 * 128, 128 * 128), 128 * 128)
        ].reshape(128, 128)

    def qkv_group(j, part):
        return (GROUP * j + part) if part < GROUP else KEY_VALUE_HEADS * part + j

    def feed_group(j, part):
        per = HID // 128
        return j * per + part if part < per else CTX * per + j * per + part - per

    def line_rows(first, group, groups, count):
        return pl.ds(first // 128 + group, count, stride=groups)

    per_run = wq_in.shape[1]
    fetch[0].wait()
    fetch[1].wait()
    loop(0, ends[1] // (128 * 128), to_lines)
    for g in range(MODEL_WIDTH // 128):
        wo[z, :, g * 128 : (g + 1) * 128] = lines[
            line_rows(ends[0], g, MODEL_WIDTH // 128, wo.shape[1]), :
        ].astype(BF16)
    qkv_groups = CTX * PCOLS // 128
    for j in range(CTX):
        for part in range(PCOLS // 128):
            wq_in[j, :, part * 128 : (part + 1) * 128] = lines[
                line_rows(0, qkv_group(j, part), qkv_groups, per_run), :
            ].astype(BF16)
    own_gains = flat_gains[...].reshape(1, spans[4]).astype(BF16).astype(F32)
    gains_in[...] = pltpu.roll(
        jnp.concatenate([own_gains, jnp.zeros((1, GAIN_WIDTH - spans[4]), F32)], axis=1),
        spans[4] * (4 * c + z),
        1,
    )

    fetch[2].wait()
    loop(ends[2] // (128 * 128), ends[3] // (128 * 128), to_lines)
    for g in range(MODEL_WIDTH // 128):
        wd[z, :, g * 128 : (g + 1) * 128] = lines[
            line_rows(ends[2], g, MODEL_WIDTH // 128, wd.shape[1]), :
        ].astype(BF16)
    pl.semaphore_wait(barrier, CTX - 1 + 4 - 1)

    mid = rows // 2
    XN, YN, ACROSS = 1, 2, 3
    whole, top, bottom = pl.ds(0, rows), pl.ds(0, mid), pl.ds(mid, mid)

    def ag_piece(n, buf, k):
        origin, part, to = (
            (0, whole, sib),
            (0, top, XN),
            (0, bottom, XN),
            (0, bottom, YN),
            (0, top, YN),
            (XN, top, YN),
            (YN, bottom, XN),
            (XN, whole, sib),
            (YN, whole, sib),
            (ACROSS, top, sib),
            (ACROSS, bottom, sib),
        )[k]
        there = buf.at[core * CHIPS + chip_at(origin), part]
        target = sib if to is sib else chip_at(to) * 2 + core
        return rcopy(there, there, ag_s.at[n, k], ag_r.at[n, k], target, z)

    def ag_landed(n, buf, k):
        origin, part, own_core = (
            (0, whole, False),
            (XN, top, True),
            (XN, bottom, True),
            (YN, bottom, True),
            (YN, top, True),
            (ACROSS, top, True),
            (ACROSS, bottom, True),
            (XN, whole, False),
            (YN, whole, False),
            (ACROSS, top, False),
            (ACROSS, bottom, False),
        )[k]
        which = core if own_core else 1 - core
        there = buf.at[which * CHIPS + chip_at(origin), part]
        return rcopy(there, there, ag_s.at[n, k], ag_r.at[n, k], sib, z)

    def ag_start(n, buf):
        for k in (1, 3, 2, 4, 0):
            ag_piece(n, buf, k).start()

    def ag_pass_near(n, buf):
        for landed, onward in ((1, 5), (3, 6), (2, 7), (4, 8)):
            ag_landed(n, buf, landed).wait_recv()
            ag_piece(n, buf, onward).start()

    def ag_pass_across(n, buf):
        for landed, onward in ((5, 9), (6, 10)):
            ag_landed(n, buf, landed).wait_recv()
            ag_piece(n, buf, onward).start()

    def ag_finish_near(n, buf):
        for k in (0, 7):
            ag_landed(n, buf, k).wait_recv()

    def ag_finish(n, buf):
        for k in (8, 9, 10):
            ag_landed(n, buf, k).wait_recv()

    def ag_drain(n, buf):
        for k in range(11):
            ag_piece(n, buf, k).wait_send()

    def gathered_tiles(n, buf, body, between=None):
        ag_pass_near(n, buf)
        ag_finish_near(n, buf)
        loop(0, 2, lambda k: body(2 * k + cy))
        if between is not None:
            between()
        ag_pass_across(n, buf)
        ag_finish(n, buf)
        loop(0, 2, lambda k: body(2 * k + 1 - cy))

    wide = MODEL_WIDTH // 2

    def rs_pair(r, h):
        return rcopy(psnd.at[r % 2, h], prcv.at[r % 2, h], rs_ps.at[r, h], rs_pr.at[r, h], sib, z)

    def rs_chip(r, k):
        to = chip_at((XN, XN, YN, YN, YN, XN)[k]) * 2 + core
        return rcopy(csnd.at[r % 2, k], crcv.at[r % 2, k], rs_cs.at[r, k], rs_cr.at[r, k], to, z)

    def rs_give(r, part, h):
        def one(n):
            out = part(1 - core, h * (wide // TILE) + n).astype(BF16)
            cols = pl.ds(pl.multiple_of(n * TILE, TILE), TILE)
            psnd[r % 2, h, :, :, cols] = out.reshape(CHIPS, rows, TILE)

        loop(0, wide // TILE, one)
        rs_pair(r, h).start()

    def rs_keep(r, part, h):
        def one(n):
            out = part(core, h * (wide // TILE) + n)
            cols = pl.ds(pl.multiple_of(n * TILE, TILE), TILE)
            own[h, :, :, cols] = out.reshape(CHIPS, rows, TILE)

        loop(0, wide // TILE, one)

    def pair_sum(r, h, i):
        return own[h, chip_at(i)] + prcv[r % 2, h, chip_at(i)].astype(F32)

    def rs_send(r, h):
        rs_pair(r, h).wait_recv()
        csnd[r % 2, 2 * h] = pair_sum(r, h, ACROSS).astype(BF16)
        rs_chip(r, 2 * h).start()
        csnd[r % 2, 2 * h + 1] = pair_sum(r, h, (XN, YN)[h]).astype(BF16)
        rs_chip(r, 2 * h + 1).start()
        acc[r % 2, :, h * wide : (h + 1) * wide] = pair_sum(r, h, 0)

    def rs_begin(r, part):
        if r > 1:
            rs_drain(r - 2)
        for h in range(2):
            rs_give(r, part, h)
            rs_keep(r, part, h)
            rs_send(r, h)

    def rs_compute(r, part):
        if r > 1:
            rs_drain(r - 2)
        for h in range(2):
            rs_give(r, part, h)
        for h in range(2):
            rs_keep(r, part, h)

    def rs_drain(r):
        for h in range(2):
            rs_pair(r, h).wait_send()
        for k in range(6):
            rs_chip(r, k).wait_send()

    def rs_relay(r):
        for h, second in ((0, YN), (1, XN)):
            rs_chip(r, 2 * h).wait_recv()
            csnd[r % 2, 4 + h] = (pair_sum(r, h, second) + crcv[r % 2, 2 * h].astype(F32)).astype(BF16)
            rs_chip(r, 4 + h).start()

    def rs_finish(r):
        halves = []
        for h in range(2):
            rs_chip(r, 2 * h + 1).wait_recv()
            rs_chip(r, 4 + h).wait_recv()
            halves.append(
                acc[r % 2, :, h * wide : (h + 1) * wide]
                + crcv[r % 2, 2 * h + 1].astype(F32)
                + crcv[r % 2, 4 + h].astype(F32)
            )
        return jnp.concatenate(halves, axis=1)

    def a2a(n, src, dst_of, i):
        to = (c + i) % CTX
        return rcopy(src.at[to], dst_of(c), a2a_s.at[n, i], a2a_r.at[n, i], to, z)

    def a2a_landed(n, dst_of, i):
        frm = (c + CTX - i) % CTX
        return rcopy(dst_of(frm), dst_of(frm), a2a_s.at[n, i], a2a_r.at[n, i], sib, z)

    def a2a_start(n, src, dst_of):
        loop(1, CTX, lambda i: a2a(n, src, dst_of, i).start())

    def a2a_half(n, src, dst_of, h):
        def one(i):
            pl.when((c + i) % CTX // (CTX // 2) == h)(a2a(n, src, dst_of, i).start)

        loop(1, CTX, one)

    def a2a_wait(n, dst_of):
        loop(1, CTX, lambda i: a2a_landed(n, dst_of, i).wait_recv())

    def a2a_drain(n, src, dst_of):
        loop(1, CTX, lambda i: a2a(n, src, dst_of, i).wait_send())

    inner = (z == 1) | (z == 2)
    outer = jnp.logical_not(inner)
    far = 3 * (2 - z)

    def zg(n, of, j, to, sem):
        return rcopy(of(j), of(j), zg_s.at[n, sem], zg_r.at[n, j], c, to)

    def zg_own(n, of):
        return (
            (z < 3, zg(n, of, z, z + 1, 4)),
            (z > 0, zg(n, of, z, z - 1, 5)),
        )

    def zg_onward(n, of):
        return (
            zg(n, of, z - 1, z + 1, 0),
            zg(n, of, z + 1, z - 1, 1),
            zg(n, of, far, 3 * (z - 1), 2),
        )

    def zg_start(n, of):
        for there, copy in zg_own(n, of):
            pl.when(there)(copy.start)

    def zg_near(n, of):
        def run():
            for k, j in ((0, z - 1), (1, z + 1)):
                zg(n, of, j, z, 0).wait_recv()
                zg_onward(n, of)[k].start()

        pl.when(inner)(run)

    def zg_far(n, of):
        def run():
            zg(n, of, far, z, 0).wait_recv()
            zg_onward(n, of)[2].start()

        pl.when(inner)(run)

    def zg_wait(n, of):
        def run():
            for i in (1, 2, 3):
                zg(n, of, (z + i) % 4, z, 0).wait_recv()

        pl.when(outer)(run)

    def zg_drain(n, of):
        for there, copy in zg_own(n, of):
            pl.when(there)(copy.wait_send)

        def run():
            for copy in zg_onward(n, of):
                copy.wait_send()

        pl.when(inner)(run)

    def zr(n, of, land, d, to, spot):
        return rcopy(of(d), land(spot), zr_s.at[n, d], zr_r.at[n, spot], c, to)

    def zr_add(n, of, land, d):
        rcopy(land(d), land(d), zr_s.at[n, d], zr_r.at[n, d], sib, z).wait_recv()
        mine = of(d)
        mine[...] = (mine[...].astype(F32) + land(d)[...].astype(F32)).astype(BF16)

    ENDS = ((0, 3, 1, 3), (3, 0, 2, 0), (0, 2, 1, 2), (3, 1, 2, 1), (0, 1, 1, 1), (3, 2, 2, 4))
    FIRST = ((1, 3, 2, 3), (2, 0, 1, 0))
    SECOND = ((1, 2, 2, 2), (2, 1, 1, 4), (1, 0, 0, 4), (2, 3, 3, 3))

    def zr_start(n, of, land):
        for device, d, to, spot in ENDS:
            pl.when(z == device)(zr(n, of, land, d, to, spot).start)

    def zr_pass(n, of, land, steps):
        for device, d, to, spot in steps:

            def run(d=d, to=to, spot=spot):
                zr_add(n, of, land, d)
                zr(n, of, land, d, to, spot).start()

            pl.when(z == device)(run)

    def zr_first(n, of, land):
        zr_pass(n, of, land, FIRST)

    def zr_second(n, of, land):
        zr_pass(n, of, land, SECOND)

    def zr_finish(n, of, land, total):
        total[...] = of(z)[...].astype(F32)

        def add(spot):
            rcopy(land(spot), land(spot), zr_s.at[n, 0], zr_r.at[n, spot], sib, z).wait_recv()
            total[...] += land(spot)[...].astype(F32)

        pl.when(z > 0)(lambda: add(z))
        pl.when(z < 3)(lambda: add(4))

    def zr_drain(n, of, land):
        for device, d, to, spot in ENDS + FIRST + SECOND:
            pl.when(z == device)(zr(n, of, land, d, to, spot).wait_send)

    def row_z(n, src, land, i):
        return rcopy(src, land.at[z], g_s.at[n, i], g_r.at[n, i], c, (z + i) % 4)

    def row_plane(n, src, land, i):
        return rcopy(
            src, land.at[c], g_s.at[n, 4 + i], g_r.at[n, 4 + i], (c + i) % CTX, z
        )

    def row_z_wait(n, land):
        def one(i):
            there = land.at[(z + 4 - i) % 4]
            rcopy(there, there, g_s.at[n, i], g_r.at[n, i], sib, z).wait_recv()

        loop(1, 4, one)

    def row_plane_wait(n, land):
        def one(i):
            there = land.at[(c + CTX - i) % CTX]
            rcopy(there, there, g_s.at[n, 4 + i], g_r.at[n, 4 + i], sib, z).wait_recv()

        loop(1, CTX, one)

    def halves(ref):
        half_of = lambda h: lambda j: ref.at[pl.ds(h * (CTX // 2), CTX // 2), j]
        return half_of(0), half_of(1)

    def land_halves(ref):
        half_of = lambda h: lambda j: ref.at[j, pl.ds(h * (CTX // 2), CTX // 2)]
        return half_of(0), half_of(1)

    wq_at = lambda j: wq.at[j, z]
    wgu_at = lambda j: wgu.at[j, z]
    g_q = (0, lambda j: wq.at[:, j])
    g_o = (1, lambda j: wo.at[j])
    g_gu1, g_gu2 = ((2 + h, of) for h, of in enumerate(halves(wgu)))
    g_d = (4, lambda j: wd.at[j])
    r_d = (0, lambda j: gwd.at[j], lambda j: lwd.at[j])
    r_gu1, r_gu2 = (
        (1 + h, *both) for h, both in enumerate(zip(halves(gwgu), land_halves(lwgu)))
    )
    r_o = (3, lambda j: gwo.at[j], lambda j: lwo.at[j])
    r_q1, r_q2 = (
        (4 + h, *both) for h, both in enumerate(zip(halves(gwq), land_halves(lwq)))
    )

    lines[pl.ds(tail // 128, 8), :] = jnp.zeros((8, 128), F32)
    gz[z] = gains_in[...]
    loop(1, 4, lambda i: row_z(0, gains_in, gz, i).start())
    a2a_start(0, wq_in, wq_at)
    zg_start(*g_o)
    fetch[3].wait()
    ag_start(0, xg)

    def share(frm):
        there = wq.at[frm, z]
        for k, to, here in ((4, z + 1, z < 3), (5, z - 1, z > 0)):
            pl.when(here)(rcopy(there, there, zg_s.at[0, k], zg_r.at[0, z], c, to).start)

    def share_landed(i):
        a2a_landed(0, wq_at, i).wait_recv()
        share((c + CTX - i) % CTX)

    wq[c, z] = wq_in[c]
    share(c)
    loop(ends[1] // (128 * 128), ends[2] // (128 * 128), to_lines)
    feed_groups = 2 * FEED_WIDTH // 128
    for j in range(CTX):
        for part in range(2 * HID // 128):
            wgu_in[j, :, part * 128 : (part + 1) * 128] = lines[
                line_rows(ends[1], feed_group(j, part), feed_groups, per_run), :
            ].astype(BF16)
    loop(1, CTX, share_landed)
    row_z_wait(0, gz)
    gpl[c] = jnp.sum(gz[...], axis=0)
    loop(1, CTX, lambda i: row_plane(0, gpl.at[c], gpl, i).start())
    wgu[c, z] = wgu_in[c]
    zg_near(*g_o)
    fetch[4].wait()
    doc_ends = [doc_ref[0, 0]]
    for j in range(1, doc_ref.shape[1] - 1):
        doc_ends.append(doc_ends[-1] + doc_ref[0, j])

    def doc_start(pos):
        start = jnp.zeros_like(pos)
        for end in doc_ends:
            start = jnp.where(pos >= end, end, start)
        return start

    def tables(s):
        first = 2 * (2 * (s % CHIPS) + s // CHIPS)
        lead = order_ref[first] * STRETCH
        trail = order_ref[first + 1] * STRETCH - STRETCH
        at = pl.ds(pl.multiple_of(s * rows, rows), rows)

        def positions(shape, axis):
            index = lax.broadcasted_iota(jnp.int32, shape, axis)
            return index + jnp.where(index < STRETCH, lead, trail)

        across = positions((1, rows), 1)
        qpos_ref[:, at] = across
        qstart_ref[:, at] = doc_start(across)
        down = positions((rows, HEAD_SIZE), 0)
        kpos_ref[at, :] = down
        lane = lax.broadcasted_iota(jnp.int32, (1, HEAD_SIZE), 1)
        upper = lane >= HEAD_SIZE // 2
        index = jnp.where(upper, lane - HEAD_SIZE // 2, lane).astype(F32)
        frequency = jnp.exp(index * (-2.0 / HEAD_SIZE * math.log(ROPE_BASE)))
        angles = (down - doc_start(down)).astype(F32) * frequency
        sine = jnp.sin(angles)
        cos_ref[at, :] = jnp.cos(angles)
        sin_ref[at, :] = jnp.where(upper, sine, -sine)

    loop(0, CTX, tables)
    ag_pass_near(0, xg)
    zg_near(*g_q)
    zg_far(*g_o)
    ag_finish_near(0, xg)
    ag_pass_across(0, xg)
    ag_finish(0, xg)
    a2a_start(1, wgu_in, wgu_at)
    ag_start(1, cot)
    zg_far(*g_q)
    row_plane_wait(0, gpl)
    gains[...] = jnp.sum(gpl[...], axis=0)
    g_attn = gains[:, :MODEL_WIDTH]
    zg_wait(*g_q)

    g_query = gains[:, 2 * MODEL_WIDTH : 2 * MODEL_WIDTH + HEAD_SIZE]
    g_key = gains[:, 2 * MODEL_WIDTH + HEAD_SIZE :]

    def tile_rows(t):
        return pl.ds(pl.multiple_of(t * TILE, TILE), TILE)

    def two(buf, t):
        return buf[pl.ds(t * (TILE // rows), TILE // rows)].reshape(TILE, buf.shape[-1])

    def turned(v):
        return pltpu.roll(v, HEAD_SIZE // 2, 1)

    def project(t):
        at = tile_rows(t)
        cosine, sine = cos_ref[at, :], sin_ref[at, :]

        def normed(raw, gain):
            scale = lax.rsqrt(jnp.mean(raw * raw, axis=-1, keepdims=True) + NORM_EPS)
            y = raw * scale * gain
            return y * cosine + turned(y) * sine

        x_tile = two(xg, t).astype(F32)
        x_scale = lax.rsqrt(jnp.mean(x_tile * x_tile, axis=-1, keepdims=True) + NORM_EPS)
        normed_one = (x_tile * x_scale * g_attn).astype(BF16)
        n1[pl.ds(t * (TILE // rows), TILE // rows)] = normed_one.reshape(
            TILE // rows, rows, MODEL_WIDTH
        )
        out = dot(normed_one, wq[...].reshape(MODEL_WIDTH, PCOLS))
        for h in range(GROUP):
            raw = out[:, h * HEAD_SIZE : (h + 1) * HEAD_SIZE]
            qraw[at, h * HEAD_SIZE : (h + 1) * HEAD_SIZE] = raw
            q_s[h, at, :] = normed(raw, g_query).astype(BF16)
        raw = out[:, QCOLS : QCOLS + HEAD_SIZE]
        kraw[at, :] = raw
        keys = normed(raw, g_key)
        values = out[:, QCOLS + HEAD_SIZE :]
        k_s[at, :] = keys.astype(BF16)
        v_s[at, :] = values.astype(BF16)
        kt_s[:, at] = keys.T.astype(BF16)
        vt_s[:, at] = values.T.astype(BF16)

    loop(0, tiles, project)
    a2a_wait(1, wgu_at)
    zg_start(*g_gu1)
    zg_start(*g_gu2)
    zg_start(*g_d)
    scale = HEAD_SIZE ** (-0.5)

    def attend(t):
        at = tile_rows(t)
        kpos = jnp.concatenate([kpos_ref[...]] * (TILE // HEAD_SIZE), axis=1)
        kept = (kpos <= qpos_ref[:, at]) & (kpos >= qstart_ref[:, at])
        for h in range(GROUP):
            scores = jnp.where(kept, dot(k_s[...], q_s[h, at, :], NT) * scale, MASKED)
            weights = jnp.exp(scores - jnp.max(scores, axis=0, keepdims=True))
            share = 1.0 / jnp.sum(weights, axis=0, keepdims=True)
            low = (weights * share).astype(BF16)
            probs[h, t] = low
            mixed = dot(vt_s[...], low).T
            attn[at, h * HEAD_SIZE : (h + 1) * HEAD_SIZE] = mixed
            attn_low[at, h * HEAD_SIZE : (h + 1) * HEAD_SIZE] = mixed.astype(BF16)

    loop(0, tiles // 2, attend)
    ag_pass_near(1, cot)
    loop(tiles // 2, tiles, attend)

    zg_wait(*g_o)
    ag_pass_across(1, cot)

    def n_cols(n):
        return pl.ds(pl.multiple_of(n * TILE, TILE), TILE)

    def half_rows(which):
        return pl.ds(pl.multiple_of(which * half, half), half)

    def half_slots(buf, which):
        return buf[pl.ds(which * CHIPS, CHIPS)].reshape(half, buf.shape[-1])

    def out_part(which, n):
        return dot(
            attn_low[half_rows(which), :], wo[:, :, n_cols(n)].reshape(QCOLS, TILE)
        )

    rs_begin(0, out_part)
    zg_near(*g_gu1)
    rs_relay(0)
    zg_near(*g_gu2)
    resid = xg[slot].astype(F32) + rs_finish(0)
    resid_s[...] = resid
    g_mlp = gains[:, MODEL_WIDTH : 2 * MODEL_WIDTH]
    s_two = lax.rsqrt(jnp.mean(resid * resid, axis=-1, keepdims=True) + NORM_EPS)
    n2[slot] = (resid * s_two * g_mlp).astype(BF16)
    ag_start(2, n2)
    ag_finish_near(1, cot)
    ag_finish(1, cot)
    zg_far(*g_gu1)
    zg_near(*g_d)
    ag_pass_near(2, n2)
    ag_finish_near(2, n2)
    zg_far(*g_gu2)
    ag_pass_across(2, n2)
    ag_finish(2, n2)
    zg_far(*g_d)
    zg_wait(*g_gu1)
    zg_wait(*g_gu2)

    def feed(t):
        at = tile_rows(t)
        both = dot(two(n2, t), wgu[...].reshape(MODEL_WIDTH, 2 * HID))
        gate, up = both[:, :HID], both[:, HID:]
        sig = 1.0 / (1.0 + jnp.exp(-gate))
        silu = gate * sig
        hidden[at, :] = (silu * up).astype(BF16)
        ggu[at, :HID] = (up * sig * (1.0 + gate * (1.0 - sig))).astype(BF16)
        ggu[at, HID:] = silu.astype(BF16)

    loop(0, tiles, feed)

    def down_grad(n):
        there = cot[:, :, n_cols(n)].reshape(2 * half, TILE)
        gwd[:, :, n_cols(n)] = (
            dot(hidden[...], there, TN).astype(BF16).reshape(4, HID // 4, TILE)
        )

    loop(0, MODEL_WIDTH // TILE, down_grad)
    zr_start(*r_d)
    zg_wait(*g_d)

    def feed_back(t):
        at = tile_rows(t)
        ghid = dot(two(cot, t), wd[...].reshape(HID, MODEL_WIDTH), NT)
        ggu[at, :HID] = (ghid * ggu[at, :HID].astype(F32)).astype(BF16)
        ggu[at, HID:] = (ghid * ggu[at, HID:].astype(F32)).astype(BF16)

    loop(0, tiles, feed_back)

    def back_two_part(which, n):
        per = MODEL_WIDTH // CTX
        there = wgu[pl.ds(n * (TILE // per), TILE // per)].reshape(TILE, 2 * HID)
        return dot(ggu[half_rows(which), :], there, NT)

    rs_begin(1, back_two_part)

    def gate_up_grad(n):
        per = MODEL_WIDTH // CTX
        there = n2[:, :, n_cols(n)].reshape(2 * half, TILE)
        gwgu[pl.ds(n * (TILE // per), TILE // per)] = (
            dot(there, ggu[...], TN)
            .astype(BF16)
            .reshape(TILE // per, 4, per // 4, 2 * HID)
        )

    loop(0, MODEL_WIDTH // TILE // 2, gate_up_grad)
    zr_start(*r_gu1)
    loop(MODEL_WIDTH // TILE // 2, MODEL_WIDTH // TILE, gate_up_grad)
    zr_start(*r_gu2)
    zr_first(*r_d)
    rs_relay(1)


    def norm_back(values, grads, gain):
        factor = lax.rsqrt(jnp.mean(values * values, axis=-1, keepdims=True) + NORM_EPS)
        unit = values * factor
        scaled = grads * gain
        inner = jnp.mean(scaled * unit, axis=-1, keepdims=True)
        return factor * (scaled - unit * inner), jnp.sum(grads * unit, axis=0, keepdims=True)

    back, terms = norm_back(resid_s[...], rs_finish(1), g_mlp)
    hrow[:, MODEL_WIDTH : 2 * MODEL_WIDTH] = terms
    gresid = cot[slot].astype(F32) + back
    gresid_s[...] = gresid
    gb[slot] = gresid.astype(BF16)
    def down_part(which, n):
        return dot(hidden[half_rows(which), :], wd[:, :, n_cols(n)].reshape(HID, TILE))

    ag_start(3, gb)
    rs_compute(2, down_part)
    zr_second(*r_d)

    def attn_grad(t):
        gattn[tile_rows(t), :] = dot(
            two(gb, t), wo[...].reshape(QCOLS, MODEL_WIDTH), NT
        ).astype(BF16)

    gathered_tiles(3, gb, attn_grad, lambda: zr_first(*r_gu1))
    rs_send(2, 0)
    rs_send(2, 1)

    dk_s[...] = jnp.zeros_like(dk_s)
    dv_s[...] = jnp.zeros_like(dv_s)

    def attend_back(t):
        at = tile_rows(t)
        for h in range(GROUP):
            head = slice(h * HEAD_SIZE, (h + 1) * HEAD_SIZE)
            grads = gattn[at, head]
            delta = jnp.sum((grads.astype(F32) * attn[at, head]).T, axis=0, keepdims=True)
            low = probs[h, t]
            gprobs = dot(v_s[...], grads, NT)
            gscores = (low.astype(F32) * (gprobs - delta)).astype(BF16)
            dv_s[...] += dot(low, grads)
            dk_s[...] += dot(gscores, q_s[h, at, :])
            attn[at, head] = dot(kt_s[...], gscores).T

    loop(0, tiles // 2, attend_back)
    zr_second(*r_gu1)
    loop(tiles // 2, tiles, attend_back)
    rs_relay(2)
    zr_first(*r_gu2)

    hrow[:, 2 * MODEL_WIDTH :] = jnp.zeros((1, 2 * HEAD_SIZE), F32)

    def project_back(t):
        at = tile_rows(t)
        cosine, sine = cos_ref[at, :], sin_ref[at, :]

        def one(raw, grads, gain):
            grads = grads * scale
            grads = grads * cosine - turned(grads) * sine
            return norm_back(raw, grads, gain)

        lo = 2 * MODEL_WIDTH
        for h in range(GROUP):
            head = slice(h * HEAD_SIZE, (h + 1) * HEAD_SIZE)
            back, terms = one(qraw[at, head], attn[at, head], g_query)
            gp[at, head] = back.astype(BF16)
            hrow[:, lo : lo + HEAD_SIZE] += terms
        back, terms = one(kraw[at, :], dk_s[at, :], g_key)
        gp[at, QCOLS : QCOLS + HEAD_SIZE] = back.astype(BF16)
        hrow[:, lo + HEAD_SIZE :] += terms
        gp[at, QCOLS + HEAD_SIZE :] = dv_s[at, :].astype(BF16)

    loop(0, tiles, project_back)

    def qkv_grad(n):
        per = MODEL_WIDTH // CTX
        there = n1[:, :, n_cols(n)].reshape(2 * half, TILE)
        gwq[pl.ds(n * (TILE // per), TILE // per)] = (
            dot(there, gp[...], TN)
            .astype(BF16)
            .reshape(TILE // per, 4, per // 4, PCOLS)
        )

    loop(0, MODEL_WIDTH // TILE // 2, qkv_grad)
    zr_start(*r_q1)
    loop(MODEL_WIDTH // TILE // 2, MODEL_WIDTH // TILE, qkv_grad)
    zr_start(*r_q2)
    zr_second(*r_gu2)

    def back_one_part(which, n):
        per = MODEL_WIDTH // CTX
        there = wq[pl.ds(n * (TILE // per), TILE // per)].reshape(TILE, PCOLS)
        return dot(gp[half_rows(which), :], there, NT)

    rs_begin(3, back_one_part)
    zr_first(*r_q1)

    def out_grad(n):
        there = gb[:, :, n_cols(n)].reshape(2 * half, TILE)
        gwo[:, :, n_cols(n)] = (
            dot(attn_low[...], there, TN).astype(BF16).reshape(4, QCOLS // 4, TILE)
        )

    loop(0, MODEL_WIDTH // TILE, out_grad)
    zr_start(*r_o)
    zr_first(*r_q2)
    rs_relay(3)
    zr_second(*r_q1)
    zr_finish(*r_d, sum_d)
    for g in range(MODEL_WIDTH // 128):
        lines[line_rows(ends[2], g, MODEL_WIDTH // 128, sum_d.shape[0]), :] = sum_d[
            :, g * 128 : (g + 1) * 128
        ]
    zr_finish(*r_gu1, sum_gu.at[pl.ds(0, CTX // 2)])
    zr_finish(*r_gu2, sum_gu.at[pl.ds(CTX // 2, CTX // 2)])
    asg[...] = sum_gu[...].astype(BF16)
    arg_at = lambda j: arg_.at[j]
    a2a_start(2, asg, arg_at)
    arg_[c] = asg[c]
    zr_second(*r_q2)
    back, terms = norm_back(xg[slot].astype(F32), rs_finish(3), gains[:, :MODEL_WIDTH])
    xgrad_ref[0] = (gresid_s[...] + back).astype(BF16)
    hrow[:, :MODEL_WIDTH] = terms
    hz[z] = hrow[...]
    loop(1, 4, lambda i: row_z(1, hrow, hz, i).start())
    zr_first(*r_o)
    out_ref[0] = (resid_s[...] + rs_finish(2)).astype(BF16)
    arq_at = lambda j: arq.at[j]
    first_half, second_half = pl.ds(0, CTX // 2), pl.ds(CTX // 2, CTX // 2)
    zr_finish(*r_q1, sum_sq.at[first_half])
    asq[first_half] = sum_sq[first_half].astype(BF16)
    a2a_half(3, asq, arq_at, 0)
    zr_finish(*r_q2, sum_sq.at[second_half])
    asq[second_half] = sum_sq[second_half].astype(BF16)
    a2a_half(3, asq, arq_at, 1)
    arq[c] = asq[c]
    zr_second(*r_o)
    row_z_wait(1, hz)
    hpl[c] = jnp.sum(hz[...], axis=0)
    loop(1, CTX, lambda i: row_plane(1, hpl.at[c], hpl, i).start())
    a2a_wait(2, arg_at)
    for j in range(CTX):
        for part in range(2 * HID // 128):
            lines[line_rows(ends[1], feed_group(j, part), feed_groups, per_run), :] = arg_[
                j, :, part * 128 : (part + 1) * 128
            ].astype(F32)
    a2a_wait(3, arq_at)
    for j in range(CTX):
        for part in range(PCOLS // 128):
            lines[line_rows(0, qkv_group(j, part), qkv_groups, per_run), :] = arq[
                j, :, part * 128 : (part + 1) * 128
            ].astype(F32)
    split = ends[0] // 128, ends[1] // 128
    stores = [
        pltpu.make_async_copy(
            lines.at[pl.ds(first, last - first)], lin_ref.at[pl.ds(first, last - first)], loc.at[k]
        )
        for k, (first, last) in enumerate(
            ((0, split[0]), (split[1], tail // 128), split, (tail // 128, tail // 128 + 8))
        )
    ]
    stores[0].start()
    stores[1].start()
    zr_finish(*r_o, sum_o)
    for g in range(MODEL_WIDTH // 128):
        lines[line_rows(ends[0], g, MODEL_WIDTH // 128, sum_o.shape[0]), :] = sum_o[
            :, g * 128 : (g + 1) * 128
        ]
    stores[2].start()
    row_plane_wait(1, hpl)
    total = jnp.sum(hpl[...], axis=0)
    lines[pl.ds(tail // 128, 1), :] = pltpu.roll(
        total, GAIN_WIDTH - spans[4] * (4 * c + z), 1
    )[:, :128]
    stores[3].start()

    for n, buf in enumerate((xg, cot, n2, gb)):
        ag_drain(n, buf)
    rs_drain(2)
    rs_drain(3)
    a2a_drain(0, wq_in, wq_at)
    a2a_drain(1, wgu_in, wgu_at)
    a2a_drain(2, asg, arg_at)
    a2a_drain(3, asq, arq_at)
    for item in (g_q, g_o, g_gu1, g_gu2, g_d):
        zg_drain(*item)
    for item in (r_d, r_gu1, r_gu2, r_o, r_q1, r_q2):
        zr_drain(*item)
    loop(1, 4, lambda i: row_z(0, gains_in, gz, i).wait_send())
    loop(1, CTX, lambda i: row_plane(0, gpl.at[c], gpl, i).wait_send())
    loop(1, 4, lambda i: row_z(1, hrow, hz, i).wait_send())
    loop(1, CTX, lambda i: row_plane(1, hpl.at[c], hpl, i).wait_send())
    for copy in stores:
        copy.wait()


def layer_call(tokens, cotangent, stretch_order, doc_lengths, master):
    _, rows, width = tokens.shape
    length = CTX * rows
    tiles = length // TILE
    per = width // CTX // 4
    entries = master.shape[0] // 1024 * 1024
    vm = pltpu.VMEM
    dma = pltpu.SemaphoreType.DMA
    shape = jax.ShapeDtypeStruct
    full = vm((CTX, rows, width), BF16)
    scratch = [
        vm((entries,), F32),
        vm((master.shape[0] - entries,), F32),
        vm((entries // 128 + 8, 128), F32),
        vm((CTX, per, PCOLS), BF16),
        vm((CTX, per, 2 * HID), BF16),
        vm((1, GAIN_WIDTH), F32),
        vm((length, HEAD_SIZE), F32),
        vm((length, HEAD_SIZE), F32),
        vm((length, HEAD_SIZE), jnp.int32),
        vm((1, length), jnp.int32),
        vm((1, length), jnp.int32),
        full,
        full,
        full,
        full,
        full,
        vm((CTX, 4, per, PCOLS), BF16),
        vm((4, QCOLS // 4, width), BF16),
        vm((CTX, 4, per, 2 * HID), BF16),
        vm((4, HID // 4, width), BF16),
        vm((length, QCOLS), F32),
        vm((length, HEAD_SIZE), F32),
        vm((GROUP, length, HEAD_SIZE), BF16),
        vm((length, HEAD_SIZE), BF16),
        vm((length, HEAD_SIZE), BF16),
        vm((HEAD_SIZE, length), BF16),
        vm((HEAD_SIZE, length), BF16),
        vm((GROUP, tiles, length, TILE), BF16),
        vm((length, QCOLS), F32),
        vm((length, QCOLS), BF16),
        vm((length, HID), BF16),
        vm((length, 2 * HID), BF16),
        vm((length, QCOLS), BF16),
        vm((length, HEAD_SIZE), F32),
        vm((length, HEAD_SIZE), F32),
        vm((length, PCOLS), BF16),
        vm((2, 2, CHIPS, rows, width // 2), BF16),
        vm((2, 2, CHIPS, rows, width // 2), BF16),
        vm((2, 6, rows, width // 2), BF16),
        vm((2, 6, rows, width // 2), BF16),
        vm((2, CHIPS, rows, width // 2), F32),
        vm((2, rows, width), F32),
        vm((rows, width), F32),
        vm((rows, width), F32),
        vm((CTX, 4, per, PCOLS), BF16),
        vm((4, QCOLS // 4, width), BF16),
        vm((CTX, 4, per, 2 * HID), BF16),
        vm((4, HID // 4, width), BF16),
        vm((5, CTX, per, PCOLS), BF16),
        vm((5, QCOLS // 4, width), BF16),
        vm((5, CTX, per, 2 * HID), BF16),
        vm((5, HID // 4, width), BF16),
        vm((CTX, per, PCOLS), BF16),
        vm((CTX, per, 2 * HID), BF16),
        vm((CTX, per, PCOLS), BF16),
        vm((CTX, per, 2 * HID), BF16),
        vm((CTX, per, PCOLS), F32),
        vm((QCOLS // 4, width), F32),
        vm((HID // 4, width), F32),
        vm((CTX, per, 2 * HID), F32),
        vm((4, 1, GAIN_WIDTH), F32),
        vm((CTX, 1, GAIN_WIDTH), F32),
        vm((1, GAIN_WIDTH), F32),
        vm((4, 1, GAIN_WIDTH), F32),
        vm((CTX, 1, GAIN_WIDTH), F32),
        vm((1, GAIN_WIDTH), F32),
        dma((4, 11)),
        dma((4, 11)),
        dma((4, 2)),
        dma((4, 2)),
        dma((4, 6)),
        dma((4, 6)),
        dma((4, CTX)),
        dma((4, CTX)),
        dma((5, 6)),
        dma((5, 4)),
        dma((6, 4)),
        dma((6, 5)),
        dma((2, 4 + CTX)),
        dma((2, 4 + CTX)),
        dma((5,)),
    ]
    smem = pl.BlockSpec(memory_space=pltpu.SMEM)
    vmem = pl.BlockSpec(memory_space=pltpu.VMEM)
    anywhere = pl.BlockSpec(memory_space=pl.ANY)
    return pl.pallas_call(
        layer_kernel,
        out_shape=(
            shape((1, rows, width), BF16),
            shape((1, rows, width), BF16),
            shape((entries // 128 + 8, 128), F32),
        ),
        in_specs=[smem, smem, anywhere, anywhere, anywhere],
        out_specs=[vmem, vmem, anywhere],
        scratch_shapes=scratch,
        compiler_params=pltpu.CompilerParams(
            collective_id=1, has_side_effects=True, vmem_limit_bytes=63 << 20
        ),
        name="layer",
    )(stretch_order, doc_lengths, tokens, cotangent, master)


def local_planes(tokens, cotangent, stretch_order, doc_lengths, master, first_moment, second_moment):
    shards = lax.axis_size("ctx") * lax.axis_size("fsdp")
    length = tokens.shape[1] * lax.axis_size("ctx")
    out, xgrad, lines = layer_call(
        tokens, cotangent, stretch_order, doc_lengths, master
    )
    grad = lines.reshape(-1)[: master.shape[0]]
    new = adam(grad, master, first_moment, second_moment, shards, length)
    return (out, xgrad, *new)


def step_settings(length):
    return [
        (MODEL_WIDTH ** (-0.5), DECAY_RATE),
        ((length / (3.0 * QUERY_HEADS * HEAD_SIZE)) ** 0.5, DECAY_RATE),
        (MODEL_WIDTH ** (-0.5), DECAY_RATE),
        (FEED_WIDTH ** (-0.5), DECAY_RATE),
        (0.2, 0.0),
    ]


def rates(shards, length):
    settings = step_settings(length)
    spans = [r // shards * w for r, w in segment_shapes()]
    index = lax.iota(jnp.int32, sum(spans))
    step_rate = jnp.full(index.shape, settings[0][0], F32)
    decay_value = jnp.full(index.shape, settings[0][1], F32)
    first = 0
    for span, (step, decay) in zip(spans, settings):
        step_rate = jnp.where(index >= first, step, step_rate)
        decay_value = jnp.where(index >= first, decay, decay_value)
        first += span
    return step_rate, decay_value


def adam(grad, master, first_moment, second_moment, shards, length):
    step_rate, decay_value = rates(shards, length)
    new_first = BETA_ONE * first_moment + (1.0 - BETA_ONE) * grad
    new_second = BETA_TWO * second_moment + (1.0 - BETA_TWO) * grad * grad
    normalized = (
        new_first
        / (1.0 - BETA_ONE**STEP)
        / (jnp.sqrt(new_second / (1.0 - BETA_TWO**STEP)) + ADAM_EPS)
    )
    new_master = master - step_rate * (normalized + decay_value * master)
    return new_master, new_first, new_second


def solution(mesh):
    placed = (
        P("fsdp", "ctx", None),
        P("fsdp", "ctx", None),
        P(),
        P("fsdp", None),
        P(("ctx", "fsdp")),
        P(("ctx", "fsdp")),
        P(("ctx", "fsdp")),
    )
    plane = mesh.shape["ctx"] == CTX == KEY_VALUE_HEADS and mesh.shape["fsdp"] == 4
    return jax.shard_map(
        local_planes if plane else local,
        mesh=mesh,
        in_specs=placed,
        out_specs=(
            P("fsdp", "ctx", None),
            P("fsdp", "ctx", None),
            P(("ctx", "fsdp")),
            P(("ctx", "fsdp")),
            P(("ctx", "fsdp")),
        ),
        check_vma=False,
    )
```

```python
import math

import jax
import jax.numpy as jnp
from jax import lax
from jax.experimental import pallas as pl
from jax.experimental.pallas import tpu as pltpu
from jax.sharding import PartitionSpec as P

MODEL_WIDTH = 1024
QUERY_HEADS = 16
KEY_VALUE_HEADS = 8
HEAD_SIZE = 128
FEED_WIDTH = 3072
STRETCH = 64
STEP = 7


NORM_EPS = 1e-06
ROPE_BASE = 1000000.0
BETA_ONE = 0.5
BETA_TWO = 0.5
DECAY_RATE = 0.1
ADAM_EPS = 1e-08
MASKED = -1e30


def from_behind(x, axis, by):
    peers = lax.axis_size(axis)
    return lax.ppermute(x, axis, [(i, (i + by) % peers) for i in range(peers)])


def segment_shapes():
    return [
        (MODEL_WIDTH, (QUERY_HEADS + 2 * KEY_VALUE_HEADS) * HEAD_SIZE),
        (QUERY_HEADS * HEAD_SIZE, MODEL_WIDTH),
        (MODEL_WIDTH, 2 * FEED_WIDTH),
        (FEED_WIDTH, MODEL_WIDTH),
        (2 * MODEL_WIDTH + 2 * HEAD_SIZE, 1),
    ]


def unpack(flat_params, count_of_shards):
    param_table = flat_params.reshape(count_of_shards, -1)
    pieces = []
    offset = 0
    for row_total, column_total in segment_shapes():
        shard_span = row_total // count_of_shards * column_total
        pieces.append(param_table[:, offset : offset + shard_span].reshape(row_total, column_total))
        offset += shard_span
    return pieces


def pack(matrices, count_of_shards):
    return jnp.concatenate(
        [matrix.reshape(count_of_shards, -1) for matrix in matrices], axis=1
    ).reshape(-1)


def slot_positions(stretch_order, first_row, count_of_rows):
    row_ids = first_row + jnp.arange(count_of_rows, dtype=jnp.int32)
    slot_ids = row_ids // STRETCH
    slot_table = jnp.arange(stretch_order.shape[0], dtype=jnp.int32)
    stretch_ids = jnp.sum(
        jnp.where(slot_ids[:, None] == slot_table[None, :], stretch_order[None, :], 0), axis=1
    )
    return stretch_ids * STRETCH + row_ids % STRETCH


def documents(positions, doc_lengths):
    doc_ends = jnp.cumsum(doc_lengths, axis=1)
    doc_starts = doc_ends - doc_lengths
    passed = positions[None, :, None] >= doc_ends[:, None, :-1]
    doc_ids = jnp.sum(passed.astype(jnp.int32), axis=2)
    doc_table = jnp.arange(doc_lengths.shape[1], dtype=jnp.int32)
    owner = doc_ids[:, :, None] == doc_table[None, None, :]
    start_of = jnp.sum(jnp.where(owner, doc_starts[:, None, :], 0), axis=2)
    return (doc_ids, positions[None, :] - start_of)


def key_mask(stretch_order, doc_lengths, query_pos, query_doc, first_row, count_of_rows):
    key_pos = slot_positions(stretch_order, first_row, count_of_rows)
    key_doc, _ = documents(key_pos, doc_lengths)
    same_doc = query_doc[:, :, None] == key_doc[:, None, :]
    return same_doc & (key_pos[None, None, :] <= query_pos[None, :, None])


def rope_tables(relative):
    half_dim = HEAD_SIZE // 2
    frequency = ROPE_BASE ** (-(jnp.arange(half_dim, dtype=jnp.float32) * 2.0 / HEAD_SIZE))
    angles = relative.astype(jnp.float32)[..., None] * frequency
    cosine_table = jnp.cos(angles)
    sine_values = jnp.sin(angles)
    return (
        jnp.concatenate([cosine_table, cosine_table], axis=-1),
        jnp.concatenate([sine_values, sine_values], axis=-1),
    )


def rotate(values, cosine_table, sine_values):
    half_dim = values.shape[-1] // 2
    turned = jnp.concatenate([-values[..., half_dim:], values[..., :half_dim]], axis=-1)
    return values * cosine_table[..., None, :] + turned * sine_values[..., None, :]


def rotate_back(grads, cosine_table, sine_values):
    half_dim = grads.shape[-1] // 2
    moved = grads * sine_values[..., None, :]
    unturned = jnp.concatenate([moved[..., half_dim:], -moved[..., :half_dim]], axis=-1)
    return grads * cosine_table[..., None, :] + unturned


def rms_norm(values, scaling):
    factor = lax.rsqrt(jnp.mean(values * values, axis=-1, keepdims=True) + NORM_EPS)
    return values * factor * scaling


def norm_back(values, grads, scaling):
    factor = lax.rsqrt(jnp.mean(values * values, axis=-1, keepdims=True) + NORM_EPS)
    unit_values = values * factor
    scaled_grads = grads * scaling
    inner = jnp.mean(scaled_grads * unit_values, axis=-1, keepdims=True)
    return (factor * (scaled_grads - unit_values * inner), grads * unit_values)


def attend_block(state, queries, key_value_block, allowed, score_scale):
    running, top_now, total_now = state
    sequence_count, count_of_keys = (key_value_block.shape[1], key_value_block.shape[2])
    block_keys = key_value_block[0].reshape(
        sequence_count, count_of_keys, KEY_VALUE_HEADS, HEAD_SIZE
    )
    block_values = key_value_block[1].reshape(
        sequence_count, count_of_keys, KEY_VALUE_HEADS, HEAD_SIZE
    )
    mask_wide = allowed[:, :, None, None, :]
    scores = (
        jnp.einsum("sqhgd,snhd->sqhgn", queries, block_keys, preferred_element_type=jnp.float32)
        * score_scale
    )
    new_top = jnp.maximum(top_now, jnp.max(jnp.where(mask_wide, scores, MASKED), axis=-1))
    weights = jnp.where(mask_wide, jnp.exp(scores - new_top[..., None]), 0.0)
    factor = jnp.exp(top_now - new_top)
    total_now = total_now * factor + jnp.sum(weights, axis=-1)
    running = running * factor[..., None] + jnp.einsum(
        "sqhgn,snhd->sqhgd",
        weights.astype(jnp.bfloat16),
        block_values,
        preferred_element_type=jnp.float32,
    )
    return (running, new_top, total_now)


def backward_block(
    queries, attention_gradient, log_total, delta, key_value_block, allowed, score_scale
):
    sequence_count, count_of_keys = (key_value_block.shape[1], key_value_block.shape[2])
    block_keys = key_value_block[0].reshape(
        sequence_count, count_of_keys, KEY_VALUE_HEADS, HEAD_SIZE
    )
    block_values = key_value_block[1].reshape(
        sequence_count, count_of_keys, KEY_VALUE_HEADS, HEAD_SIZE
    )
    mask_wide = allowed[:, :, None, None, :]
    scores = (
        jnp.einsum("sqhgd,snhd->sqhgn", queries, block_keys, preferred_element_type=jnp.float32)
        * score_scale
    )
    probabilities = jnp.where(mask_wide, jnp.exp(scores - log_total[..., None]), 0.0)
    value_gradient = jnp.einsum(
        "sqhgn,sqhgd->snhd",
        probabilities.astype(jnp.bfloat16),
        attention_gradient,
        preferred_element_type=jnp.float32,
    )
    grad_probs = jnp.einsum(
        "sqhgd,snhd->sqhgn", attention_gradient, block_values, preferred_element_type=jnp.float32
    )
    grad_scores = (probabilities * (grad_probs - delta[..., None])).astype(jnp.bfloat16)
    grad_queries = (
        jnp.einsum("sqhgn,snhd->sqhgd", grad_scores, block_keys, preferred_element_type=jnp.float32)
        * score_scale
    )
    key_gradient = (
        jnp.einsum("sqhgn,sqhgd->snhd", grad_scores, queries, preferred_element_type=jnp.float32)
        * score_scale
    )
    grad_pair = jnp.stack(
        [
            key_gradient.reshape(sequence_count, count_of_keys, KEY_VALUE_HEADS * HEAD_SIZE),
            value_gradient.reshape(sequence_count, count_of_keys, KEY_VALUE_HEADS * HEAD_SIZE),
        ]
    )
    return (grad_queries, grad_pair)


def summed(part, count_of_shards):
    return lax.psum_scatter(
        part.reshape(-1), ("ctx", "fsdp"), scatter_dimension=0, tiled=True
    )


def local(tokens, cotangent, stretch_order, doc_lengths, master, first_moment, second_moment):
    cycle_size = lax.axis_size("ctx")
    ctx_index = lax.axis_index("ctx")
    count_of_shards = cycle_size * lax.axis_size("fsdp")
    sequence_count, count_of_rows, _ = tokens.shape
    seq_length = count_of_rows * cycle_size
    query_groups = QUERY_HEADS // KEY_VALUE_HEADS
    score_scale = HEAD_SIZE ** (-0.5)
    gathered = lax.all_gather(master.astype(jnp.bfloat16), ("ctx", "fsdp"), axis=0, tiled=True)
    w_qkv, w_out, w_gate_up, w_down, gain_column = unpack(gathered, count_of_shards)
    gains = gain_column.reshape(-1).astype(jnp.float32)
    g_attn = gains[:MODEL_WIDTH]
    g_mlp = gains[MODEL_WIDTH : 2 * MODEL_WIDTH]
    g_query = gains[2 * MODEL_WIDTH : 2 * MODEL_WIDTH + HEAD_SIZE]
    g_key = gains[2 * MODEL_WIDTH + HEAD_SIZE :]
    query_pos = slot_positions(stretch_order, ctx_index * count_of_rows, count_of_rows)
    query_doc, relative = documents(query_pos, doc_lengths)
    cosine_table, sine_values = rope_tables(relative)
    x_in = tokens.astype(jnp.float32)
    normed_one = rms_norm(x_in, g_attn).astype(jnp.bfloat16)
    projected_output = jnp.einsum(
        "sqd,de->sqe", normed_one, w_qkv, preferred_element_type=jnp.float32
    )
    query_raw = projected_output[:, :, : QUERY_HEADS * HEAD_SIZE].reshape(
        sequence_count, count_of_rows, QUERY_HEADS, HEAD_SIZE
    )
    unrotated_keys = projected_output[
        :, :, QUERY_HEADS * HEAD_SIZE : (QUERY_HEADS + KEY_VALUE_HEADS) * HEAD_SIZE
    ].reshape(sequence_count, count_of_rows, KEY_VALUE_HEADS, HEAD_SIZE)
    unprojected_values = projected_output[:, :, (QUERY_HEADS + KEY_VALUE_HEADS) * HEAD_SIZE :]
    queries = (
        rotate(rms_norm(query_raw, g_query), cosine_table, sine_values)
        .astype(jnp.bfloat16)
        .reshape(sequence_count, count_of_rows, KEY_VALUE_HEADS, query_groups, HEAD_SIZE)
    )
    keys_rot = rotate(rms_norm(unrotated_keys, g_key), cosine_table, sine_values).reshape(
        sequence_count, count_of_rows, KEY_VALUE_HEADS * HEAD_SIZE
    )
    kv_local = jnp.stack([keys_rot, unprojected_values]).astype(jnp.bfloat16)
    statistic_shape = (sequence_count, count_of_rows, KEY_VALUE_HEADS, query_groups)
    initial = (
        jnp.zeros(statistic_shape + (HEAD_SIZE,), jnp.float32),
        jnp.full(statistic_shape, MASKED, jnp.float32),
        jnp.zeros(statistic_shape, jnp.float32),
    )
    state = initial
    piece = lax.all_gather(kv_local, "ctx", axis=2, tiled=True)
    key_total = piece.shape[2]

    def key_step(inner, block_index):
        first_row = block_index * count_of_rows
        key_value_block = lax.dynamic_slice_in_dim(piece, first_row, count_of_rows, 2)
        allowed = key_mask(
            stretch_order, doc_lengths, query_pos, query_doc, first_row, count_of_rows
        )
        return (attend_block(inner, queries, key_value_block, allowed, score_scale), None)

    state, _ = lax.scan(key_step, state, jnp.arange(key_total // count_of_rows, dtype=jnp.int32))
    running, top_now, total_now = state
    attn = running / total_now[..., None]
    log_total = top_now + jnp.log(total_now)
    attn_low = attn.reshape(sequence_count, count_of_rows, QUERY_HEADS * HEAD_SIZE).astype(
        jnp.bfloat16
    )
    resid = x_in + jnp.einsum("sqa,ad->sqd", attn_low, w_out, preferred_element_type=jnp.float32)
    normed_two = rms_norm(resid, g_mlp).astype(jnp.bfloat16)
    gate_up = jnp.einsum("sqd,de->sqe", normed_two, w_gate_up, preferred_element_type=jnp.float32)
    gate = gate_up[:, :, :FEED_WIDTH]
    up_part = gate_up[:, :, FEED_WIDTH:]
    sigmoid_gate = jax.nn.sigmoid(gate)
    hidden = (gate * sigmoid_gate * up_part).astype(jnp.bfloat16)
    mlp_out = jnp.einsum("sqf,fd->sqd", hidden, w_down, preferred_element_type=jnp.float32)
    layer_out = (resid + mlp_out).astype(jnp.bfloat16)
    grad_w_down = jnp.einsum("sqf,sqd->fd", hidden, cotangent, preferred_element_type=jnp.float32)
    grad_hidden = jnp.einsum("sqd,fd->sqf", cotangent, w_down, preferred_element_type=jnp.float32)
    grad_gate = grad_hidden * up_part * sigmoid_gate * (1.0 + gate * (1.0 - sigmoid_gate))
    grad_up = grad_hidden * gate * sigmoid_gate
    grad_gate_up = jnp.concatenate([grad_gate, grad_up], axis=-1).astype(jnp.bfloat16)
    grad_w_gate_up = jnp.einsum(
        "sqd,sqe->de", normed_two, grad_gate_up, preferred_element_type=jnp.float32
    )
    grad_normed_two = jnp.einsum(
        "sqe,de->sqd", grad_gate_up, w_gate_up, preferred_element_type=jnp.float32
    )
    back_two, mlp_gain_terms = norm_back(resid, grad_normed_two, g_mlp)
    grad_resid = cotangent.astype(jnp.float32) + back_two
    grad_branch = grad_resid.astype(jnp.bfloat16)
    grad_w_out = jnp.einsum(
        "sqa,sqd->ad", attn_low, grad_branch, preferred_element_type=jnp.float32
    )
    attention_gradient = jnp.einsum(
        "sqd,ad->sqa", grad_branch, w_out, preferred_element_type=jnp.float32
    ).astype(jnp.bfloat16)
    attention_head_gradient = attention_gradient.reshape(
        sequence_count, count_of_rows, KEY_VALUE_HEADS, query_groups, HEAD_SIZE
    )
    delta = jnp.sum(attention_head_gradient.astype(jnp.float32) * attn, axis=-1)

    def grads_from(turn_index, kv_now, key_value_gradients, grad_queries):
        source_dev = (ctx_index - turn_index) % cycle_size
        allowed = key_mask(
            stretch_order,
            doc_lengths,
            query_pos,
            query_doc,
            source_dev * count_of_rows,
            count_of_rows,
        )
        part_queries, part_pair = backward_block(
            queries, attention_head_gradient, log_total, delta, kv_now, allowed, score_scale
        )
        return (key_value_gradients + part_pair, grad_queries + part_queries)

    def pass_grads(key_value_gradients):
        return from_behind(key_value_gradients.astype(jnp.bfloat16), "ctx", 1).astype(
            key_value_gradients.dtype
        )

    def turn_step(turn_index, state):
        kv_now, key_value_gradients, grad_queries = state
        key_value_gradients, grad_queries = grads_from(
            turn_index, kv_now, key_value_gradients, grad_queries
        )
        kv_now = from_behind(kv_now, "ctx", 1)
        key_value_gradients = pass_grads(key_value_gradients)
        return (kv_now, key_value_gradients, grad_queries)

    start_state = (
        kv_local,
        jnp.zeros(kv_local.shape, jnp.float32),
        jnp.zeros(statistic_shape + (HEAD_SIZE,), jnp.float32),
    )
    kv_now, key_value_gradients, grad_queries = lax.fori_loop(
        0, cycle_size - 1, turn_step, start_state
    )
    key_value_gradients, grad_queries = grads_from(
        cycle_size - 1, kv_now, key_value_gradients, grad_queries
    )
    key_value_gradients = pass_grads(key_value_gradients)
    grad_query_rot = rotate_back(
        grad_queries.reshape(sequence_count, count_of_rows, QUERY_HEADS, HEAD_SIZE),
        cosine_table,
        sine_values,
    )
    grad_key_rot = rotate_back(
        key_value_gradients[0].reshape(sequence_count, count_of_rows, KEY_VALUE_HEADS, HEAD_SIZE),
        cosine_table,
        sine_values,
    )
    grad_query_raw, query_gain_terms = norm_back(query_raw, grad_query_rot, g_query)
    unrotated_key_gradient, key_gain_terms = norm_back(unrotated_keys, grad_key_rot, g_key)
    grad_projected = jnp.concatenate(
        [
            grad_query_raw.reshape(sequence_count, count_of_rows, QUERY_HEADS * HEAD_SIZE),
            unrotated_key_gradient.reshape(
                sequence_count, count_of_rows, KEY_VALUE_HEADS * HEAD_SIZE
            ),
            key_value_gradients[1],
        ],
        axis=-1,
    ).astype(jnp.bfloat16)
    grad_w_qkv = jnp.einsum(
        "sqd,sqe->de", normed_one, grad_projected, preferred_element_type=jnp.float32
    )
    grad_normed_one = jnp.einsum(
        "sqe,de->sqd", grad_projected, w_qkv, preferred_element_type=jnp.float32
    )
    back_one, attn_gain_terms = norm_back(x_in, grad_normed_one, g_attn)
    input_grad = (grad_resid + back_one).astype(jnp.bfloat16)
    grad_gains = jnp.concatenate(
        [
            jnp.sum(attn_gain_terms, axis=(0, 1)),
            jnp.sum(mlp_gain_terms, axis=(0, 1)),
            jnp.sum(query_gain_terms, axis=(0, 1, 2)),
            jnp.sum(key_gain_terms, axis=(0, 1, 2)),
        ]
    ).reshape(-1, 1)
    grad = jnp.concatenate(
        [
            summed(part, count_of_shards)
            for part in (grad_w_qkv, grad_w_out, grad_w_gate_up, grad_w_down, grad_gains)
        ]
    )
    new_master, new_first, new_second = adam(
        grad, master, first_moment, second_moment, count_of_shards, seq_length
    )
    return (layer_out, input_grad, new_master, new_first, new_second)


MESH = pl.DeviceIdType.MESH
F32 = jnp.float32
BF16 = jnp.bfloat16
CTX = 8
CHIPS = 4
GROUP = QUERY_HEADS // KEY_VALUE_HEADS
QCOLS = GROUP * HEAD_SIZE
PCOLS = QCOLS + 2 * HEAD_SIZE
HID = FEED_WIDTH // CTX
GAIN_WIDTH = 2 * MODEL_WIDTH + 2 * HEAD_SIZE
TILE = 256
WIDE = 512


def dot(a, b, dims=((1,), (0,))):
    return lax.dot_general(a, b, (dims, ((), ())), preferred_element_type=F32)


NT = ((1,), (1,))
TN = ((0,), (0,))


def layer_kernel(
    order_hbm,
    doc_hbm,
    x_hbm,
    cot_hbm,
    master_hbm,
    out_hbm,
    xgrad_hbm,
    lin_ref,
    order_ref,
    doc_ref,
    out_ref,
    xgrad_ref,
    flat,
    flat_down,
    flat_gains,
    lines,
    wq_in,
    wgu_in,
    gains_in,
    cos_ref,
    sin_ref,
    kpos_ref,
    qpos_ref,
    qstart_ref,
    xg,
    n1,
    cot,
    n2,
    x_own,
    wq,
    wo,
    wgu,
    wd,
    qraw,
    kraw,
    q_s,
    k_s,
    v_s,
    kt_s,
    vt_s,
    probs,
    attn,
    shares,
    attn_low,
    hidden,
    ggu,
    gattn,
    dk_s,
    dv_s,
    gp,
    psnd,
    prcv,
    csnd,
    crcv,
    own,
    acc,
    resid_s,
    gresid_s,
    gwq,
    gwo,
    gwgu,
    gwd,
    lwq,
    lwo,
    lwgu,
    lwd,
    asq,
    asg,
    arq,
    arg_,
    gz,
    gpl,
    gains,
    hz,
    hpl,
    hrow,
    ag_s,
    ag_r,
    rs_ps,
    rs_pr,
    rs_cs,
    rs_cr,
    a2a_s,
    a2a_r,
    zg_s,
    zg_r,
    zr_s,
    zr_r,
    g_s,
    g_r,
    loc,
):
    c = lax.axis_index("ctx")
    z = lax.axis_index("fsdp")
    core = c % 2
    chip = c // 2
    cx = chip % 2
    cy = chip // 2
    slot = core * CHIPS + chip
    sib = c + 1 - 2 * core
    tiles = n1.shape[0] * n1.shape[1] // TILE
    rows = n1.shape[1]
    half = CHIPS * rows

    def chip_at(i):
        return ((cy + i // 2) % 2) * 2 + (cx + i % 2) % 2

    def rcopy(src, dst, ssem, rsem, to_c, to_z):
        return pltpu.make_async_remote_copy(
            src_ref=src,
            dst_ref=dst,
            send_sem=ssem,
            recv_sem=rsem,
            device_id=(to_c, to_z),
            device_id_type=MESH,
        )

    def loop(lo, hi, body):
        def step(i, carry):
            body(i)
            return carry

        lax.fori_loop(lo, hi, step, 0)

    spans = [r // (4 * CTX) * w for r, w in segment_shapes()]
    ends = [sum(spans[: i + 1]) for i in range(5)]
    tail = ends[3]
    fetch = [
        pltpu.make_async_copy(master_hbm.at[pl.ds(0, ends[1])], flat, loc.at[0]),
        pltpu.make_async_copy(master_hbm.at[pl.ds(tail, spans[4])], flat_gains, loc.at[3]),
        pltpu.make_async_copy(master_hbm.at[pl.ds(ends[2], spans[3])], flat_down, loc.at[4]),
        pltpu.make_async_copy(x_hbm.at[0], xg.at[slot], loc.at[1]),
        pltpu.make_async_copy(cot_hbm.at[0], cot.at[slot], loc.at[2]),
        pltpu.make_async_copy(order_hbm, order_ref, loc.at[5]),
        pltpu.make_async_copy(doc_hbm, doc_ref, loc.at[6]),
    ]
    for copy in fetch:
        copy.start()
    fetch_feed = pltpu.make_async_copy(
        master_hbm.at[pl.ds(ends[1], spans[2])], flat, loc.at[0]
    )
    barrier = pltpu.get_barrier_semaphore()

    def greet_plane(i):
        pl.semaphore_signal(
            barrier, inc=1, device_id=((c + i) % CTX, z), device_id_type=MESH
        )

    def greet_z(i):
        pl.semaphore_signal(
            barrier, inc=1, device_id=(c, (z + i) % 4), device_id_type=MESH
        )

    loop(1, CTX, greet_plane)
    loop(1, 4, greet_z)

    def to_lines(src, first, last):
        block = 128 * 128

        def one(i):
            lines[pl.ds(pl.multiple_of(first // 128 + i * 128, 128), 128), :] = src[
                pl.ds(pl.multiple_of(i * block, block), block)
            ].reshape(128, 128)

        loop(0, (last - first) // block, one)

    def qkv_group(j, part):
        return (GROUP * j + part) if part < GROUP else KEY_VALUE_HEADS * part + j

    def feed_group(j, part):
        per = HID // 128
        return j * per + part if part < per else CTX * per + j * per + part - per

    def line_rows(first, group, groups, count):
        return pl.ds(first // 128 + group, count, stride=groups)

    per_run = wq_in.shape[2]
    fetch[0].wait()
    fetch[1].wait()
    to_lines(flat, 0, ends[1])
    fetch_feed.start()
    for g in range(MODEL_WIDTH // 128):
        wo[z, :, g * 128 : (g + 1) * 128] = lines[
            line_rows(ends[0], g, MODEL_WIDTH // 128, wo.shape[1]), :
        ].astype(BF16)
    qkv_groups = CTX * PCOLS // 128
    for j in range(CTX):
        for part in range(PCOLS // 128):
            wq_in[part // 2, j, :, part % 2 * 128 : (part % 2 + 1) * 128] = lines[
                line_rows(0, qkv_group(j, part), qkv_groups, per_run), :
            ].astype(BF16)
    own_gains = flat_gains[...].reshape(1, spans[4]).astype(BF16).astype(F32)
    gains_in[...] = pltpu.roll(
        jnp.concatenate([own_gains, jnp.zeros((1, GAIN_WIDTH - spans[4]), F32)], axis=1),
        spans[4] * (4 * c + z),
        1,
    )

    fetch[2].wait()
    to_lines(flat_down, ends[2], ends[3])
    for g in range(MODEL_WIDTH // 128):
        wd[z, :, g * 128 : (g + 1) * 128] = lines[
            line_rows(ends[2], g, MODEL_WIDTH // 128, wd.shape[1]), :
        ].astype(BF16)
    pl.semaphore_wait(barrier, CTX - 1 + 4 - 1)

    mid = rows // 2
    XN, YN, ACROSS = 1, 2, 3
    whole, top, bottom = pl.ds(0, rows), pl.ds(0, mid), pl.ds(mid, mid)

    def ag_piece(n, buf, k):
        origin, part, to = (
            (0, whole, sib),
            (0, top, XN),
            (0, bottom, XN),
            (0, bottom, YN),
            (0, top, YN),
            (XN, top, YN),
            (YN, bottom, XN),
            (XN, whole, sib),
            (YN, whole, sib),
            (ACROSS, top, sib),
            (ACROSS, bottom, sib),
        )[k]
        there = buf.at[core * CHIPS + chip_at(origin), part]
        target = sib if to is sib else chip_at(to) * 2 + core
        return rcopy(there, there, ag_s.at[n], ag_r.at[n % 3, k], target, z)

    def ag_landed(n, buf, k):
        origin, part, own_core = (
            (0, whole, False),
            (XN, top, True),
            (XN, bottom, True),
            (YN, bottom, True),
            (YN, top, True),
            (ACROSS, top, True),
            (ACROSS, bottom, True),
            (XN, whole, False),
            (YN, whole, False),
            (ACROSS, top, False),
            (ACROSS, bottom, False),
        )[k]
        which = core if own_core else 1 - core
        there = buf.at[which * CHIPS + chip_at(origin), part]
        return rcopy(there, there, ag_s.at[n], ag_r.at[n % 3, k], sib, z)

    def ag_start(n, buf):
        for k in (1, 3, 2, 4, 0):
            ag_piece(n, buf, k).start()

    def ag_pass_near(n, buf):
        for landed, onward in ((1, 5), (3, 6), (2, 7), (4, 8)):
            ag_landed(n, buf, landed).wait_recv()
            ag_piece(n, buf, onward).start()

    def ag_pass_across(n, buf):
        for landed, onward in ((5, 9), (6, 10)):
            ag_landed(n, buf, landed).wait_recv()
            ag_piece(n, buf, onward).start()

    def ag_finish_near(n, buf):
        for k in (0, 7):
            ag_landed(n, buf, k).wait_recv()

    def ag_finish(n, buf):
        for k in (8, 9, 10):
            ag_landed(n, buf, k).wait_recv()

    def ag_drain(n, buf):
        seven = buf.at[pl.ds(0, 7)]
        rcopy(seven, seven, ag_s.at[n], ag_r.at[0, 0], sib, z).wait_send()

    def gathered_tiles(n, buf, body, between=None):
        ag_pass_near(n, buf)
        ag_finish_near(n, buf)
        loop(0, 2, lambda k: body(2 * k + cy))
        if between is not None:
            between()
        ag_pass_across(n, buf)
        ag_finish(n, buf)
        loop(0, 2, lambda k: body(2 * k + 1 - cy))

    wide = MODEL_WIDTH // 2

    def rs_pair(r, h):
        return rcopy(psnd.at[h], prcv.at[r % 2, h], rs_ps.at[h], rs_pr.at[r % 2, h], sib, z)

    def rs_chip(r, k):
        to = chip_at((XN, XN, YN, YN, YN, XN)[k]) * 2 + core
        return rcopy(csnd.at[k], crcv.at[r % 2, k], rs_cs.at[k], rs_cr.at[r % 2, k], to, z)

    def rs_give(r, part, h):
        if r > 0:
            rs_pair(r - 1, h).wait_send()
        psnd[h] = part(1 - core, h).astype(BF16).reshape(CHIPS, rows, wide)
        rs_pair(r, h).start()

    def rs_keep(r, part, h):
        own[h] = part(core, h).reshape(CHIPS, rows, wide)

    def pair_sum(r, h, i):
        return own[h, chip_at(i)] + prcv[r % 2, h, chip_at(i)].astype(F32)

    def rs_send(r, h):
        rs_pair(r, h).wait_recv()
        if r > 0 and h == 0:
            for k in range(6):
                rs_chip(r - 1, k).wait_send()
        csnd[2 * h] = pair_sum(r, h, ACROSS).astype(BF16)
        rs_chip(r, 2 * h).start()
        csnd[2 * h + 1] = pair_sum(r, h, (XN, YN)[h]).astype(BF16)
        rs_chip(r, 2 * h + 1).start()
        acc[r % 2, :, h * wide : (h + 1) * wide] = pair_sum(r, h, 0)

    def rs_begin(r, part):
        for h in range(2):
            rs_give(r, part, h)
        for h in range(2):
            rs_keep(r, part, h)
            rs_send(r, h)

    def rs_compute(r, part):
        for h in range(2):
            rs_give(r, part, h)
        for h in range(2):
            rs_keep(r, part, h)

    def rs_drain(r):
        for h in range(2):
            rs_pair(r, h).wait_send()
        for k in range(6):
            rs_chip(r, k).wait_send()

    def rs_relay(r):
        for h, second in ((0, YN), (1, XN)):
            rs_chip(r, 2 * h).wait_recv()
            csnd[4 + h] = (pair_sum(r, h, second) + crcv[r % 2, 2 * h].astype(F32)).astype(BF16)
            rs_chip(r, 4 + h).start()

    def rs_finish(r):
        halves = []
        for h in range(2):
            rs_chip(r, 2 * h + 1).wait_recv()
            rs_chip(r, 4 + h).wait_recv()
            halves.append(
                acc[r % 2, :, h * wide : (h + 1) * wide]
                + crcv[r % 2, 2 * h + 1].astype(F32)
                + crcv[r % 2, 4 + h].astype(F32)
            )
        return jnp.concatenate(halves, axis=1)

    def a2a(n, src, dst_of, i, sem=0):
        to = (c + i) % CTX
        return rcopy(src.at[to], dst_of(c), a2a_s.at[n], a2a_r.at[n, sem], to, z)

    def a2a_landed(n, dst_of, i):
        frm = (c + CTX - i) % CTX
        return rcopy(dst_of(frm), dst_of(frm), a2a_s.at[n], a2a_r.at[n, i - 1], sib, z)

    def a2a_start(n, src, dst_of, apart=False):
        loop(1, CTX, lambda i: a2a(n, src, dst_of, i, i - 1 if apart else 0).start())

    def a2a_half(n, src, dst_of, h):
        def one(i):
            pl.when((c + i) % CTX // (CTX // 2) == h)(a2a(n, src, dst_of, i).start)

        loop(1, CTX, one)

    def a2a_wait(n, dst):
        seven = dst.at[pl.ds(0, CTX - 1)]
        rcopy(seven, seven, a2a_s.at[n], a2a_r.at[n, 0], sib, z).wait_recv()

    def a2a_drain(n, src):
        seven = src.at[pl.ds(0, CTX - 1)]
        rcopy(seven, seven, a2a_s.at[n], a2a_r.at[n, 0], sib, z).wait_send()

    inner = (z == 1) | (z == 2)
    outer = jnp.logical_not(inner)
    far = 3 * (2 - z)

    def zg(n, of, j, to, sem):
        return rcopy(of(j), of(j), zg_s.at[n, sem], zg_r.at[n, j], c, to)

    def zg_own(n, of):
        return (
            (z < 3, zg(n, of, z, z + 1, 0)),
            (z > 0, zg(n, of, z, z - 1, 0)),
        )

    def zg_onward(n, of):
        return (
            zg(n, of, z - 1, z + 1, 1),
            zg(n, of, z + 1, z - 1, 1),
            zg(n, of, far, 3 * (z - 1), 1),
        )

    def zg_start(n, of, who=None):
        for there, copy in zg_own(n, of):
            pl.when(there if who is None else there & who)(copy.start)

    def zg_pass(n, of, k, when, j):
        def run():
            zg(n, of, j, z, 0).wait_recv()
            zg_onward(n, of)[k].start()

        pl.when(when)(run)

    def zg_across(n, of):
        zg_pass(n, of, 0, z == 1, z - 1)
        zg_pass(n, of, 1, z == 2, z + 1)

    def zg_back(n, of):
        zg_pass(n, of, 1, z == 1, z + 1)
        zg_pass(n, of, 0, z == 2, z - 1)

    def zg_near(n, of):
        zg_across(n, of)
        zg_back(n, of)

    def zg_far(n, of):
        def run():
            zg(n, of, far, z, 0).wait_recv()
            zg_onward(n, of)[2].start()

        pl.when(inner)(run)

    def zg_wait(n, of):
        def run():
            for i in (1, 2, 3):
                zg(n, of, (z + i) % 4, z, 0).wait_recv()

        pl.when(outer)(run)

    def zg_drain(n, some):
        def sent(count, sem):
            part = some(count)
            rcopy(part, part, zg_s.at[n, sem], zg_r.at[n, 0], c, c).wait_send()

        def run():
            sent(2, 0)
            sent(3, 1)

        pl.when(inner)(run)
        pl.when(outer)(lambda: sent(1, 0))

    def zr(n, of, land, d, to, spot):
        return rcopy(of(d), land(spot), zr_s.at[n], zr_r.at[n, spot], c, to)

    def zr_add(n, of, land, d):
        rcopy(land(d), land(d), zr_s.at[n], zr_r.at[n, d], sib, z).wait_recv()
        mine = of(d)
        mine[...] = (mine[...].astype(F32) + land(d)[...].astype(F32)).astype(BF16)

    ENDS = (
        ((0, 3, 1, 3), (3, 0, 2, 0)),
        ((0, 2, 1, 2), (3, 1, 2, 1)),
        ((0, 1, 1, 1), (3, 2, 2, 4)),
    )
    FIRST = ((1, 3, 2, 3), (2, 0, 1, 0))
    SECOND = ((1, 2, 2, 2), (2, 1, 1, 4), (1, 0, 0, 4), (2, 3, 3, 3))

    def zr_send(n, of, land, k):
        for device, d, to, spot in ENDS[k]:
            pl.when(z == device)(zr(n, of, land, d, to, spot).start)

    def zr_start(*items, part=range(3)):
        for k in part:
            for item in items:
                zr_send(*item, k)

    def zr_pass(n, of, land, steps):
        for device, d, to, spot in steps:

            def run(d=d, to=to, spot=spot):
                zr_add(n, of, land, d)
                zr(n, of, land, d, to, spot).start()

            pl.when(z == device)(run)

    def zr_first(n, of, land):
        zr_pass(n, of, land, FIRST)

    def zr_second(n, of, land):
        zr_pass(n, of, land, SECOND)

    def zr_finish(n, of, land):
        def landed(spot):
            rcopy(land(spot), land(spot), zr_s.at[n], zr_r.at[n, spot], sib, z).wait_recv()

        pl.when(z > 0)(lambda: landed(z))
        pl.when(z < 3)(lambda: landed(4))
        return of(z)[...].astype(F32) + land(z)[...].astype(F32) + land(4)[...].astype(F32)

    def row_z(n, src, land, i):
        return rcopy(src, land.at[z], g_s.at[n, 0], g_r.at[n, 0], c, (z + i) % 4)

    def row_plane(n, src, land, i):
        return rcopy(src, land.at[c], g_s.at[n, 1], g_r.at[n, 1], (c + i) % CTX, z)

    def rows_of(n, land, k):
        others = land.at[pl.ds(0, (3, CTX - 1)[k])]
        return rcopy(others, others, g_s.at[n, k], g_r.at[n, k], sib, z)

    def row_z_wait(n, land):
        rows_of(n, land, 0).wait_recv()

    def row_plane_wait(n, land):
        rows_of(n, land, 1).wait_recv()

    def halves(ref):
        half_of = lambda h: lambda j: ref.at[pl.ds(h * (CTX // 2), CTX // 2), j]
        return half_of(0), half_of(1)

    def land_halves(ref):
        half_of = lambda h: lambda j: ref.at[j, pl.ds(h * (CTX // 2), CTX // 2)]
        return half_of(0), half_of(1)

    wq_at = lambda j: wq.at[0, j, z]
    wkv_at = lambda j: wq.at[1, j, z]
    wgu_at = lambda j: wgu.at[j, z]
    g_q = (0, lambda j: wq.at[0, :, j])
    g_kv = (5, lambda j: wq.at[1, :, j])
    g_o = (1, lambda j: wo.at[j])
    g_gu1, g_gu2 = ((2 + h, of) for h, of in enumerate(halves(wgu)))
    g_d = (4, lambda j: wd.at[j])
    r_d = (0, lambda j: gwd.at[j], lambda j: lwd.at[j])
    r_gu1, r_gu2 = (
        (1 + h, *both) for h, both in enumerate(zip(halves(gwgu), land_halves(lwgu)))
    )
    r_o = (3, lambda j: gwo.at[j], lambda j: lwo.at[j])
    r_q1, r_q2 = (
        (4 + h, *both) for h, both in enumerate(zip(halves(gwq), land_halves(lwq)))
    )

    lines[pl.ds(tail // 128, 8), :] = jnp.zeros((8, 128), F32)
    gz[z] = gains_in[...]
    loop(1, 4, lambda i: row_z(0, gains_in, gz, i).start())
    a2a_start(0, wq_in.at[0], wq_at, apart=True)
    a2a_start(4, wq_in.at[1], wkv_at, apart=True)
    zg_start(*g_o)

    def share(part, frm):
        there = wq.at[part, frm, z]
        n = 5 * part
        for to, here in ((z + 1, z < 3), (z - 1, z > 0)):
            pl.when(here)(rcopy(there, there, zg_s.at[n, 0], zg_r.at[n, z], c, to).start)

    def shares_landed(part, n, at):
        def one(i):
            a2a_landed(n, at, i).wait_recv()
            share(part, (c + CTX - i) % CTX)

        loop(1, CTX, one)

    for part in range(2):
        wq[part, c, z] = wq_in[part, c]
        share(part, c)
    fetch_feed.wait()
    to_lines(flat, ends[1], ends[2])
    feed_groups = 2 * FEED_WIDTH // 128
    for j in range(CTX):
        for part in range(2 * HID // 128):
            wgu_in[j, :, part * 128 : (part + 1) * 128] = lines[
                line_rows(ends[1], feed_group(j, part), feed_groups, per_run), :
            ].astype(BF16)
    fetch[3].wait()
    ag_start(0, xg)
    shares_landed(0, 0, wq_at)
    shares_landed(1, 4, wkv_at)
    row_z_wait(0, gz)
    gpl[c] = jnp.sum(gz[...], axis=0)
    loop(1, CTX, lambda i: row_plane(0, gpl.at[c], gpl, i).start())
    wgu[c, z] = wgu_in[c]
    for copy in fetch[4:]:
        copy.wait()
    doc_ends = [doc_ref[0, 0]]
    for j in range(1, doc_ref.shape[1] - 1):
        doc_ends.append(doc_ends[-1] + doc_ref[0, j])

    def doc_start(pos):
        start = jnp.zeros_like(pos)
        for end in doc_ends:
            start = jnp.where(pos >= end, end, start)
        return start

    def tables(s):
        first = 2 * (2 * (s % CHIPS) + s // CHIPS)
        lead = order_ref[first] * STRETCH
        trail = order_ref[first + 1] * STRETCH - STRETCH
        at = pl.ds(pl.multiple_of(s * rows, rows), rows)

        def positions(shape, axis):
            index = lax.broadcasted_iota(jnp.int32, shape, axis)
            return index + jnp.where(index < STRETCH, lead, trail)

        across = positions((1, rows), 1)
        qpos_ref[:, at] = across
        qstart_ref[:, at] = doc_start(across)
        down = positions((rows, HEAD_SIZE), 0)
        kpos_ref[at, :] = down
        lane = lax.broadcasted_iota(jnp.int32, (1, HEAD_SIZE), 1)
        upper = lane >= HEAD_SIZE // 2
        index = jnp.where(upper, lane - HEAD_SIZE // 2, lane).astype(F32)
        frequency = jnp.exp(index * (-2.0 / HEAD_SIZE * math.log(ROPE_BASE)))
        angles = (down - doc_start(down)).astype(F32) * frequency
        sine = jnp.sin(angles)
        cos_ref[at, :] = jnp.cos(angles)
        sin_ref[at, :] = jnp.where(upper, sine, -sine)

    loop(0, CTX // 2, tables)
    for land in (lwq, lwo, lwgu, lwd):
        for end, spot in ((0, 0), (3, 4)):

            def blank(land=land, spot=spot):
                land[spot] = jnp.zeros(land.shape[1:], BF16)

            pl.when(z == end)(blank)
    zg_near(*g_q)
    loop(CTX // 2, CTX, tables)
    ag_pass_near(0, xg)
    zg_near(*g_kv)
    ag_finish_near(0, xg)
    ag_pass_across(0, xg)
    zg_far(*g_q)
    ag_finish(0, xg)
    a2a_start(1, wgu_in, wgu_at)
    ag_start(1, cot)
    zg_far(*g_kv)
    zg_near(*g_o)
    row_plane_wait(0, gpl)
    gains[...] = jnp.sum(gpl[...], axis=0)
    g_attn = gains[:, :MODEL_WIDTH]
    def normed(t):
        at = pl.ds(t * (TILE // rows), TILE // rows)
        x_tile = xg[at].astype(F32)
        x_scale = lax.rsqrt(jnp.mean(x_tile * x_tile, axis=-1, keepdims=True) + NORM_EPS)
        n1[at] = (x_tile * x_scale * g_attn.reshape(1, 1, MODEL_WIDTH)).astype(BF16)

    loop(0, tiles, normed)
    x_own[...] = xg[slot]
    pl.when(outer)(lambda: a2a_wait(1, wgu_in))
    zg_start(*g_gu1, outer)
    zg_start(*g_gu2, outer)
    zg_start(*g_d, outer)
    zg_wait(*g_q)
    zg_wait(*g_kv)

    g_query = gains[:, 2 * MODEL_WIDTH : 2 * MODEL_WIDTH + HEAD_SIZE]
    g_key = gains[:, 2 * MODEL_WIDTH + HEAD_SIZE :]

    def tile_rows(t):
        return pl.ds(pl.multiple_of(t * TILE, TILE), TILE)

    def two(buf, t):
        return buf[pl.ds(t * (TILE // rows), TILE // rows)].reshape(TILE, buf.shape[-1])

    def turned(v):
        return pltpu.roll(v, HEAD_SIZE // 2, 1)

    def project(t):
        at = tile_rows(t)
        cosine, sine = cos_ref[at, :], sin_ref[at, :]

        def normed(raw, gain):
            scale = lax.rsqrt(jnp.mean(raw * raw, axis=-1, keepdims=True) + NORM_EPS)
            y = raw * scale * gain
            return y * cosine + turned(y) * sine

        out = dot(two(n1, t), wq[0].reshape(MODEL_WIDTH, QCOLS))
        both = dot(two(n1, t), wq[1].reshape(MODEL_WIDTH, 2 * HEAD_SIZE))
        for h in range(GROUP):
            raw = out[:, h * HEAD_SIZE : (h + 1) * HEAD_SIZE]
            qraw[at, h * HEAD_SIZE : (h + 1) * HEAD_SIZE] = raw
            q_s[h, at, :] = normed(raw, g_query).astype(BF16)
        raw = both[:, :HEAD_SIZE]
        kraw[at, :] = raw
        keys = normed(raw, g_key)
        values = both[:, HEAD_SIZE:]
        k_s[at, :] = keys.astype(BF16)
        v_s[at, :] = values.astype(BF16)
        kt_s[:, at] = keys.T.astype(BF16)
        vt_s[:, at] = values.T.astype(BF16)

    loop(0, tiles, project)
    ag_drain(0, xg)
    zg_far(*g_o)
    pl.when(inner)(lambda: a2a_wait(1, wgu_in))
    zg_start(*g_gu1, inner)
    zg_start(*g_gu2, inner)
    def n_cols(n):
        return pl.ds(pl.multiple_of(n * WIDE, WIDE), WIDE)

    def half_rows(which):
        return pl.ds(pl.multiple_of(which * half, half), half)

    def half_slots(buf, which):
        return buf[pl.ds(which * CHIPS, CHIPS)].reshape(half, buf.shape[-1])

    def out_part(which, n):
        return dot(
            attn_low[half_rows(which), :], wo[:, :, n_cols(n)].reshape(QCOLS, WIDE)
        )

    scale = HEAD_SIZE ** (-0.5)

    def attend(t):
        at = half_rows(t)
        kpos = jnp.concatenate([kpos_ref[...]] * (half // HEAD_SIZE), axis=1)
        kept = (kpos <= qpos_ref[:, at]) & (kpos >= qstart_ref[:, at])
        for h in range(GROUP):
            scores = jnp.where(kept, dot(k_s[...], q_s[h, at, :], NT) * scale, MASKED)
            weights = jnp.exp(scores - jnp.max(scores, axis=0, keepdims=True))
            low = weights.astype(BF16)
            probs[h, t] = low
            share = 1.0 / jnp.sum(weights, axis=0, keepdims=True)
            shares[h, :, at] = share
            mixed = dot(vt_s[...], low) * share
            attn[h, :, at] = mixed
            attn_low[at, h * HEAD_SIZE : (h + 1) * HEAD_SIZE] = mixed.T.astype(BF16)

    attend(1 - core)
    zg_across(*g_gu1)
    zg_wait(*g_o)
    rs_give(0, out_part, 0)
    rs_give(0, out_part, 1)
    ag_pass_near(1, cot)
    attend(core)
    ag_pass_across(1, cot)
    for h in range(2):
        rs_keep(0, out_part, h)
        rs_send(0, h)
    zg_across(*g_gu2)
    zg_back(*g_gu1)
    zg_back(*g_gu2)
    rs_relay(0)
    zg_far(*g_gu1)
    resid = x_own[...].astype(F32) + rs_finish(0)
    resid_s[...] = resid
    g_mlp = gains[:, MODEL_WIDTH : 2 * MODEL_WIDTH]
    s_two = lax.rsqrt(jnp.mean(resid * resid, axis=-1, keepdims=True) + NORM_EPS)
    n2[slot] = (resid * s_two * g_mlp).astype(BF16)
    ag_start(2, n2)
    ag_finish_near(1, cot)
    ag_finish(1, cot)
    zg_far(*g_gu2)
    zg_start(*g_d, inner)
    zg_across(*g_d)
    ag_pass_near(2, n2)
    ag_finish_near(2, n2)
    zg_back(*g_d)
    ag_pass_across(2, n2)
    ag_finish(2, n2)
    zg_far(*g_d)
    zg_wait(*g_gu1)
    zg_wait(*g_gu2)

    def feed(t):
        at = tile_rows(t)
        both = dot(two(n2, t), wgu[...].reshape(MODEL_WIDTH, 2 * HID))
        gate, up = both[:, :HID], both[:, HID:]
        sig = 1.0 / (1.0 + jnp.exp(-gate))
        silu = gate * sig
        hidden[at, :] = (silu * up).astype(BF16)
        ggu[at, :HID] = (up * sig * (1.0 + gate * (1.0 - sig))).astype(BF16)
        ggu[at, HID:] = silu.astype(BF16)

    loop(0, tiles, feed)

    def down_grad(n):
        there = cot[:, :, n_cols(n)].reshape(2 * half, WIDE)
        gwd[:, :, n_cols(n)] = (
            dot(hidden[...], there, TN).astype(BF16).reshape(4, HID // 4, WIDE)
        )

    loop(0, MODEL_WIDTH // WIDE, down_grad)
    zr_start(r_d)
    zg_wait(*g_d)

    def feed_back(t):
        at = tile_rows(t)
        ghid = dot(two(cot, t), wd[...].reshape(HID, MODEL_WIDTH), NT)
        ggu[at, :HID] = (ghid * ggu[at, :HID].astype(F32)).astype(BF16)
        ggu[at, HID:] = (ghid * ggu[at, HID:].astype(F32)).astype(BF16)

    loop(0, tiles, feed_back)

    def back_two_part(which, n):
        per = MODEL_WIDTH // CTX
        there = wgu[pl.ds(n * (WIDE // per), WIDE // per)].reshape(WIDE, 2 * HID)
        return dot(ggu[half_rows(which), :], there, NT)

    rs_begin(1, back_two_part)

    def gate_up_grad(n):
        per = MODEL_WIDTH // CTX
        there = n2[:, :, n_cols(n)].reshape(2 * half, WIDE)
        gwgu[pl.ds(n * (WIDE // per), WIDE // per)] = (
            dot(there, ggu[...], TN)
            .astype(BF16)
            .reshape(WIDE // per, 4, per // 4, 2 * HID)
        )

    gate_up_grad(0)
    zr_start(r_gu1)
    gate_up_grad(1)
    zr_start(r_gu2)
    zr_first(*r_d)
    rs_relay(1)


    def norm_back(values, grads, gain):
        factor = lax.rsqrt(jnp.mean(values * values, axis=-1, keepdims=True) + NORM_EPS)
        unit = values * factor
        scaled = grads * gain
        inner = jnp.mean(scaled * unit, axis=-1, keepdims=True)
        return factor * (scaled - unit * inner), jnp.sum(grads * unit, axis=0, keepdims=True)

    back, terms = norm_back(resid_s[...], rs_finish(1), g_mlp)
    hrow[:, MODEL_WIDTH : 2 * MODEL_WIDTH] = terms
    gresid = cot[slot].astype(F32) + back
    gresid_s[...] = gresid
    gb = xg
    gb[slot] = gresid.astype(BF16)
    def down_part(which, n):
        return dot(hidden[half_rows(which), :], wd[:, :, n_cols(n)].reshape(HID, WIDE))

    ag_start(3, gb)
    rs_compute(2, down_part)
    zr_second(*r_d)

    def attn_grad(t):
        gattn[tile_rows(t), :] = dot(
            two(gb, t), wo[...].reshape(QCOLS, MODEL_WIDTH), NT
        ).astype(BF16)

    gathered_tiles(3, gb, attn_grad, lambda: zr_first(*r_gu1))
    rs_send(2, 0)
    rs_send(2, 1)

    def out_grad(n):
        there = gb[:, :, n_cols(n)].reshape(2 * half, WIDE)
        gwo[:, :, n_cols(n)] = (
            dot(attn_low[...], there, TN).astype(BF16).reshape(4, QCOLS // 4, WIDE)
        )

    loop(0, MODEL_WIDTH // WIDE, out_grad)
    zr_start(r_o, part=(0, 1))

    dk_s[...] = jnp.zeros_like(dk_s)
    dv_s[...] = jnp.zeros_like(dv_s)

    hrow[:, 2 * MODEL_WIDTH :] = jnp.zeros((1, 2 * HEAD_SIZE), F32)

    def head_back(raw, grads, at, gain):
        grads = grads * scale
        grads = grads * cos_ref[at, :] - turned(grads) * sin_ref[at, :]
        return norm_back(raw, grads, gain)

    q_terms = pl.ds(2 * MODEL_WIDTH, HEAD_SIZE)
    k_terms = pl.ds(2 * MODEL_WIDTH + HEAD_SIZE, HEAD_SIZE)

    def attend_back(t):
        at = pl.ds(t * half, half)
        for h in range(GROUP):
            head = slice(h * HEAD_SIZE, (h + 1) * HEAD_SIZE)
            grads = gattn[at, head]
            turned_grads = grads.astype(F32).T
            share = shares[h, :, at]
            delta = jnp.sum(turned_grads * attn[h, :, at], axis=0, keepdims=True)
            low = probs[h, t]
            gprobs = dot(v_s[...], grads, NT)
            gscores = (low.astype(F32) * ((gprobs - delta) * share)).astype(BF16)
            dv_s[...] += dot(low, (turned_grads * share).T.astype(BF16))
            dk_s[...] += dot(gscores, q_s[h, at, :])
            back, terms = head_back(qraw[at, head], dot(kt_s[...], gscores).T, at, g_query)
            gp[at, head] = back.astype(BF16)
            hrow[:, q_terms] += terms

    attend_back(0)
    zr_second(*r_gu1)
    attend_back(1)
    rs_relay(2)
    zr_first(*r_gu2)

    def project_back(t):
        at = tile_rows(t)
        back, terms = head_back(kraw[at, :], dk_s[at, :], at, g_key)
        gp[at, QCOLS : QCOLS + HEAD_SIZE] = back.astype(BF16)
        hrow[:, k_terms] += terms
        gp[at, QCOLS + HEAD_SIZE :] = dv_s[at, :].astype(BF16)

    loop(0, tiles, project_back)

    def qkv_grad(n):
        per = MODEL_WIDTH // CTX
        there = n1[:, :, n_cols(n)].reshape(2 * half, WIDE)
        gwq[pl.ds(n * (WIDE // per), WIDE // per)] = (
            dot(there, gp[...], TN)
            .astype(BF16)
            .reshape(WIDE // per, 4, per // 4, PCOLS)
        )

    qkv_grad(0)
    qkv_grad(1)
    zr_start(r_q1, r_q2, part=(0, 1))
    def back_one_part(which, n):
        per = MODEL_WIDTH // CTX
        at = pl.ds(n * (WIDE // per), WIDE // per)
        rows_at = half_rows(which)
        return dot(gp[rows_at, :QCOLS], wq[0, at].reshape(WIDE, QCOLS), NT) + dot(
            gp[rows_at, QCOLS:], wq[1, at].reshape(WIDE, 2 * HEAD_SIZE), NT
        )

    rs_begin(3, back_one_part)
    zr_second(*r_gu2)
    rs_relay(3)
    zr_first(*r_o)
    zr_first(*r_q1)
    zr_first(*r_q2)
    zr_second(*r_o)
    sum_d = zr_finish(*r_d)
    for g in range(MODEL_WIDTH // 128):
        lines[line_rows(ends[2], g, MODEL_WIDTH // 128, sum_d.shape[0]), :] = sum_d[
            :, g * 128 : (g + 1) * 128
        ]
    first_half, second_half = pl.ds(0, CTX // 2), pl.ds(CTX // 2, CTX // 2)
    asg[first_half] = zr_finish(*r_gu1).astype(BF16)
    asg[second_half] = zr_finish(*r_gu2).astype(BF16)
    arg_[c] = asg[c]
    zr_second(*r_q1)
    back, terms = norm_back(x_own[...].astype(F32), rs_finish(3), gains[:, :MODEL_WIDTH])
    xgrad_ref[...] = (gresid_s[...] + back).astype(BF16)
    store_xgrad = pltpu.make_async_copy(xgrad_ref, xgrad_hbm.at[0], loc.at[5])
    store_xgrad.start()
    hrow[:, :MODEL_WIDTH] = terms
    hz[z] = hrow[...]
    loop(1, 4, lambda i: row_z(1, hrow, hz, i).start())
    zr_start(r_q1, r_q2, part=(2,))
    zr_start(r_o, part=(2,))
    arg_at = lambda j: arg_.at[j]
    a2a_start(2, asg, arg_at)
    zr_second(*r_q2)
    out_ref[...] = (resid_s[...] + rs_finish(2)).astype(BF16)
    store_out = pltpu.make_async_copy(out_ref, out_hbm.at[0], loc.at[6])
    store_out.start()
    row_z_wait(1, hz)
    hpl[c] = jnp.sum(hz[...], axis=0)
    loop(1, CTX, lambda i: row_plane(1, hpl.at[c], hpl, i).start())
    arq_at = lambda j: arq.at[j]
    asq[first_half] = zr_finish(*r_q1).astype(BF16)
    a2a_half(3, asq, arq_at, 0)
    asq[second_half] = zr_finish(*r_q2).astype(BF16)
    a2a_half(3, asq, arq_at, 1)
    arq[c] = asq[c]
    a2a_wait(2, arg_)
    for j in range(CTX):
        for part in range(2 * HID // 128):
            lines[line_rows(ends[1], feed_group(j, part), feed_groups, per_run), :] = arg_[
                j, :, part * 128 : (part + 1) * 128
            ].astype(F32)
    a2a_wait(3, arq)
    for j in range(CTX):
        for part in range(PCOLS // 128):
            lines[line_rows(0, qkv_group(j, part), qkv_groups, per_run), :] = arq[
                j, :, part * 128 : (part + 1) * 128
            ].astype(F32)
    split = ends[0] // 128, ends[1] // 128
    stores = [
        pltpu.make_async_copy(
            lines.at[pl.ds(first, last - first)], lin_ref.at[pl.ds(first, last - first)], loc.at[k]
        )
        for k, (first, last) in enumerate(
            ((0, split[0]), (split[1], tail // 128), split, (tail // 128, tail // 128 + 8))
        )
    ]
    stores[0].start()
    stores[1].start()
    sum_o = zr_finish(*r_o)
    for g in range(MODEL_WIDTH // 128):
        lines[line_rows(ends[0], g, MODEL_WIDTH // 128, sum_o.shape[0]), :] = sum_o[
            :, g * 128 : (g + 1) * 128
        ]
    stores[2].start()
    row_plane_wait(1, hpl)
    total = jnp.sum(hpl[...], axis=0)
    lines[pl.ds(tail // 128, 1), :] = pltpu.roll(
        total, GAIN_WIDTH - spans[4] * (4 * c + z), 1
    )[:, :128]
    stores[3].start()

    for n, buf in ((1, cot), (2, n2), (3, gb)):
        ag_drain(n, buf)
    rs_drain(3)
    a2a_drain(0, wq_in.at[0])
    a2a_drain(4, wq_in.at[1])
    a2a_drain(1, wgu_in)
    a2a_drain(2, asg)
    a2a_drain(3, asq)
    first_four = pl.ds(0, CTX // 2)
    for n, some in (
        (0, lambda count: wq.at[0, :, pl.ds(0, count)]),
        (5, lambda count: wq.at[1, :, pl.ds(0, count)]),
        (1, lambda count: wo.at[pl.ds(0, count)]),
        (2, lambda count: wgu.at[first_four, pl.ds(0, count)]),
        (3, lambda count: wgu.at[first_four, pl.ds(0, count)]),
        (4, lambda count: wd.at[pl.ds(0, count)]),
    ):
        zg_drain(n, some)
    three = pl.ds(0, 3)
    for n, part in (
        (0, lwd.at[three]),
        (1, lwgu.at[three, first_four]),
        (2, lwgu.at[three, first_four]),
        (3, lwo.at[three]),
        (4, lwq.at[three, first_four]),
        (5, lwq.at[three, first_four]),
    ):
        rcopy(part, part, zr_s.at[n], zr_r.at[n, 0], sib, z).wait_send()
    for n, lands in enumerate(((gz, gpl), (hz, hpl))):
        for k, land in enumerate(lands):
            rows_of(n, land, k).wait_send()
    for copy in (store_out, store_xgrad, *stores):
        copy.wait()


def layer_call(tokens, cotangent, stretch_order, doc_lengths, master):
    _, rows, width = tokens.shape
    length = CTX * rows
    tiles = length // TILE
    per = width // CTX // 4
    entries = master.shape[0] // 1024 * 1024
    vm = pltpu.VMEM
    dma = pltpu.SemaphoreType.DMA
    shape = jax.ShapeDtypeStruct
    full = vm((CTX, rows, width), BF16)
    scratch = [
        pltpu.SMEM(stretch_order.shape, jnp.int32),
        pltpu.SMEM(doc_lengths.shape, jnp.int32),
        vm((rows, width), BF16),
        vm((rows, width), BF16),
        vm((width * 4 * width // 32 + 2 * width * width // 32,), F32),
        vm((FEED_WIDTH * width // 32,), F32),
        vm((master.shape[0] - entries,), F32),
        vm((entries // 128 + 8, 128), F32),
        vm((2, CTX, per, QCOLS), BF16),
        vm((CTX, per, 2 * HID), BF16),
        vm((1, GAIN_WIDTH), F32),
        vm((length, HEAD_SIZE), F32),
        vm((length, HEAD_SIZE), F32),
        vm((length, HEAD_SIZE), jnp.int32),
        vm((1, length), jnp.int32),
        vm((1, length), jnp.int32),
        full,
        full,
        full,
        full,
        vm((rows, width), BF16),
        vm((2, CTX, 4, per, QCOLS), BF16),
        vm((4, QCOLS // 4, width), BF16),
        vm((CTX, 4, per, 2 * HID), BF16),
        vm((4, HID // 4, width), BF16),
        vm((length, QCOLS), F32),
        vm((length, HEAD_SIZE), F32),
        vm((GROUP, length, HEAD_SIZE), BF16),
        vm((length, HEAD_SIZE), BF16),
        vm((length, HEAD_SIZE), BF16),
        vm((HEAD_SIZE, length), BF16),
        vm((HEAD_SIZE, length), BF16),
        vm((GROUP, 2, length, length // 2), BF16),
        vm((GROUP, HEAD_SIZE, length), F32),
        vm((GROUP, 1, length), F32),
        vm((length, QCOLS), BF16),
        vm((length, HID), BF16),
        vm((length, 2 * HID), BF16),
        vm((length, QCOLS), BF16),
        vm((length, HEAD_SIZE), F32),
        vm((length, HEAD_SIZE), F32),
        vm((length, PCOLS), BF16),
        vm((2, CHIPS, rows, width // 2), BF16),
        vm((2, 2, CHIPS, rows, width // 2), BF16),
        vm((6, rows, width // 2), BF16),
        vm((2, 6, rows, width // 2), BF16),
        vm((2, CHIPS, rows, width // 2), F32),
        vm((2, rows, width), F32),
        vm((rows, width), F32),
        vm((rows, width), F32),
        vm((CTX, 4, per, PCOLS), BF16),
        vm((4, QCOLS // 4, width), BF16),
        vm((CTX, 4, per, 2 * HID), BF16),
        vm((4, HID // 4, width), BF16),
        vm((5, CTX, per, PCOLS), BF16),
        vm((5, QCOLS // 4, width), BF16),
        vm((5, CTX, per, 2 * HID), BF16),
        vm((5, HID // 4, width), BF16),
        vm((CTX, per, PCOLS), BF16),
        vm((CTX, per, 2 * HID), BF16),
        vm((CTX, per, PCOLS), BF16),
        vm((CTX, per, 2 * HID), BF16),
        vm((4, 1, GAIN_WIDTH), F32),
        vm((CTX, 1, GAIN_WIDTH), F32),
        vm((1, GAIN_WIDTH), F32),
        vm((4, 1, GAIN_WIDTH), F32),
        vm((CTX, 1, GAIN_WIDTH), F32),
        vm((1, GAIN_WIDTH), F32),
        dma((4,)),
        dma((3, 11)),
        dma((2,)),
        dma((2, 2)),
        dma((6,)),
        dma((2, 6)),
        dma((5,)),
        dma((5, CTX - 1)),
        dma((6, 2)),
        dma((6, 4)),
        dma((6,)),
        dma((6, 5)),
        dma((2, 2)),
        dma((2, 2)),
        dma((8,)),
    ]
    anywhere = pl.BlockSpec(memory_space=pl.ANY)
    return pl.pallas_call(
        layer_kernel,
        out_shape=(
            shape((1, rows, width), BF16),
            shape((1, rows, width), BF16),
            shape((entries // 128 + 8, 128), F32),
        ),
        in_specs=[anywhere] * 5,
        out_specs=[anywhere] * 3,
        scratch_shapes=scratch,
        compiler_params=pltpu.CompilerParams(
            collective_id=1, has_side_effects=True, vmem_limit_bytes=63 << 20
        ),
        name="layer",
    )(stretch_order, doc_lengths, tokens, cotangent, master)


def local_planes(tokens, cotangent, stretch_order, doc_lengths, master, first_moment, second_moment):
    shards = lax.axis_size("ctx") * lax.axis_size("fsdp")
    length = tokens.shape[1] * lax.axis_size("ctx")
    out, xgrad, lines = layer_call(
        tokens, cotangent, stretch_order, doc_lengths, master
    )
    grad = lines.reshape(-1)[: master.shape[0]]
    new = adam(grad, master, first_moment, second_moment, shards, length)
    return (out, xgrad, *new)


def step_settings(length):
    return [
        (MODEL_WIDTH ** (-0.5), DECAY_RATE),
        ((length / (3.0 * QUERY_HEADS * HEAD_SIZE)) ** 0.5, DECAY_RATE),
        (MODEL_WIDTH ** (-0.5), DECAY_RATE),
        (FEED_WIDTH ** (-0.5), DECAY_RATE),
        (0.2, 0.0),
    ]


def rates(shards, length):
    settings = step_settings(length)
    spans = [r // shards * w for r, w in segment_shapes()]
    index = lax.iota(jnp.int32, sum(spans))
    step_rate = jnp.full(index.shape, settings[0][0], F32)
    decay_value = jnp.full(index.shape, settings[0][1], F32)
    first = 0
    for span, (step, decay) in zip(spans, settings):
        step_rate = jnp.where(index >= first, step, step_rate)
        decay_value = jnp.where(index >= first, decay, decay_value)
        first += span
    return step_rate, decay_value


def adam(grad, master, first_moment, second_moment, shards, length):
    step_rate, decay_value = rates(shards, length)
    new_first = BETA_ONE * first_moment + (1.0 - BETA_ONE) * grad
    new_second = BETA_TWO * second_moment + (1.0 - BETA_TWO) * grad * grad
    normalized = (
        new_first
        / (1.0 - BETA_ONE**STEP)
        / (jnp.sqrt(new_second / (1.0 - BETA_TWO**STEP)) + ADAM_EPS)
    )
    new_master = master - step_rate * (normalized + decay_value * master)
    return new_master, new_first, new_second


def solution(mesh):
    placed = (
        P("fsdp", "ctx", None),
        P("fsdp", "ctx", None),
        P(),
        P("fsdp", None),
        P(("ctx", "fsdp")),
        P(("ctx", "fsdp")),
        P(("ctx", "fsdp")),
    )
    plane = mesh.shape["ctx"] == CTX == KEY_VALUE_HEADS and mesh.shape["fsdp"] == 4
    return jax.shard_map(
        local_planes if plane else local,
        mesh=mesh,
        in_specs=placed,
        out_specs=(
            P("fsdp", "ctx", None),
            P("fsdp", "ctx", None),
            P(("ctx", "fsdp")),
            P(("ctx", "fsdp")),
            P(("ctx", "fsdp")),
        ),
        check_vma=False,
    )
```

```python
import functools
import math

import jax
import jax.numpy as jnp
from jax import lax
from jax.experimental import pallas as pl
from jax.experimental.pallas import tpu as pltpu
from jax.sharding import PartitionSpec as P

MODEL_WIDTH = 1024
QUERY_HEADS = 16
KEY_VALUE_HEADS = 8
HEAD_SIZE = 128
FEED_WIDTH = 3072
STRETCH = 64
STEP = 7


NORM_EPS = 1e-06
ROPE_BASE = 1000000.0
BETA_ONE = 0.5
BETA_TWO = 0.5
DECAY_RATE = 0.1
ADAM_EPS = 1e-08
MASKED = -1e30


def from_behind(x, axis, by):
    peers = lax.axis_size(axis)
    return lax.ppermute(x, axis, [(i, (i + by) % peers) for i in range(peers)])


def segment_shapes():
    return [
        (MODEL_WIDTH, (QUERY_HEADS + 2 * KEY_VALUE_HEADS) * HEAD_SIZE),
        (QUERY_HEADS * HEAD_SIZE, MODEL_WIDTH),
        (MODEL_WIDTH, 2 * FEED_WIDTH),
        (FEED_WIDTH, MODEL_WIDTH),
        (2 * MODEL_WIDTH + 2 * HEAD_SIZE, 1),
    ]


def unpack(flat_params, count_of_shards):
    param_table = flat_params.reshape(count_of_shards, -1)
    pieces = []
    offset = 0
    for row_total, column_total in segment_shapes():
        shard_span = row_total // count_of_shards * column_total
        pieces.append(param_table[:, offset : offset + shard_span].reshape(row_total, column_total))
        offset += shard_span
    return pieces


def pack(matrices, count_of_shards):
    return jnp.concatenate(
        [matrix.reshape(count_of_shards, -1) for matrix in matrices], axis=1
    ).reshape(-1)


def slot_positions(stretch_order, first_row, count_of_rows):
    row_ids = first_row + jnp.arange(count_of_rows, dtype=jnp.int32)
    slot_ids = row_ids // STRETCH
    slot_table = jnp.arange(stretch_order.shape[0], dtype=jnp.int32)
    stretch_ids = jnp.sum(
        jnp.where(slot_ids[:, None] == slot_table[None, :], stretch_order[None, :], 0), axis=1
    )
    return stretch_ids * STRETCH + row_ids % STRETCH


def documents(positions, doc_lengths):
    doc_ends = jnp.cumsum(doc_lengths, axis=1)
    doc_starts = doc_ends - doc_lengths
    passed = positions[None, :, None] >= doc_ends[:, None, :-1]
    doc_ids = jnp.sum(passed.astype(jnp.int32), axis=2)
    doc_table = jnp.arange(doc_lengths.shape[1], dtype=jnp.int32)
    owner = doc_ids[:, :, None] == doc_table[None, None, :]
    start_of = jnp.sum(jnp.where(owner, doc_starts[:, None, :], 0), axis=2)
    return (doc_ids, positions[None, :] - start_of)


def key_mask(stretch_order, doc_lengths, query_pos, query_doc, first_row, count_of_rows):
    key_pos = slot_positions(stretch_order, first_row, count_of_rows)
    key_doc, _ = documents(key_pos, doc_lengths)
    same_doc = query_doc[:, :, None] == key_doc[:, None, :]
    return same_doc & (key_pos[None, None, :] <= query_pos[None, :, None])


def rope_tables(relative):
    half_dim = HEAD_SIZE // 2
    frequency = ROPE_BASE ** (-(jnp.arange(half_dim, dtype=jnp.float32) * 2.0 / HEAD_SIZE))
    angles = relative.astype(jnp.float32)[..., None] * frequency
    cosine_table = jnp.cos(angles)
    sine_values = jnp.sin(angles)
    return (
        jnp.concatenate([cosine_table, cosine_table], axis=-1),
        jnp.concatenate([sine_values, sine_values], axis=-1),
    )


def rotate(values, cosine_table, sine_values):
    half_dim = values.shape[-1] // 2
    turned = jnp.concatenate([-values[..., half_dim:], values[..., :half_dim]], axis=-1)
    return values * cosine_table[..., None, :] + turned * sine_values[..., None, :]


def rotate_back(grads, cosine_table, sine_values):
    half_dim = grads.shape[-1] // 2
    moved = grads * sine_values[..., None, :]
    unturned = jnp.concatenate([moved[..., half_dim:], -moved[..., :half_dim]], axis=-1)
    return grads * cosine_table[..., None, :] + unturned


def rms_norm(values, scaling):
    factor = lax.rsqrt(jnp.mean(values * values, axis=-1, keepdims=True) + NORM_EPS)
    return values * factor * scaling


def norm_back(values, grads, scaling):
    factor = lax.rsqrt(jnp.mean(values * values, axis=-1, keepdims=True) + NORM_EPS)
    unit_values = values * factor
    scaled_grads = grads * scaling
    inner = jnp.mean(scaled_grads * unit_values, axis=-1, keepdims=True)
    return (factor * (scaled_grads - unit_values * inner), grads * unit_values)


def attend_block(state, queries, key_value_block, allowed, score_scale):
    running, top_now, total_now = state
    sequence_count, count_of_keys = (key_value_block.shape[1], key_value_block.shape[2])
    block_keys = key_value_block[0].reshape(
        sequence_count, count_of_keys, KEY_VALUE_HEADS, HEAD_SIZE
    )
    block_values = key_value_block[1].reshape(
        sequence_count, count_of_keys, KEY_VALUE_HEADS, HEAD_SIZE
    )
    mask_wide = allowed[:, :, None, None, :]
    scores = (
        jnp.einsum("sqhgd,snhd->sqhgn", queries, block_keys, preferred_element_type=jnp.float32)
        * score_scale
    )
    new_top = jnp.maximum(top_now, jnp.max(jnp.where(mask_wide, scores, MASKED), axis=-1))
    weights = jnp.where(mask_wide, jnp.exp(scores - new_top[..., None]), 0.0)
    factor = jnp.exp(top_now - new_top)
    total_now = total_now * factor + jnp.sum(weights, axis=-1)
    running = running * factor[..., None] + jnp.einsum(
        "sqhgn,snhd->sqhgd",
        weights.astype(jnp.bfloat16),
        block_values,
        preferred_element_type=jnp.float32,
    )
    return (running, new_top, total_now)


def backward_block(
    queries, attention_gradient, log_total, delta, key_value_block, allowed, score_scale
):
    sequence_count, count_of_keys = (key_value_block.shape[1], key_value_block.shape[2])
    block_keys = key_value_block[0].reshape(
        sequence_count, count_of_keys, KEY_VALUE_HEADS, HEAD_SIZE
    )
    block_values = key_value_block[1].reshape(
        sequence_count, count_of_keys, KEY_VALUE_HEADS, HEAD_SIZE
    )
    mask_wide = allowed[:, :, None, None, :]
    scores = (
        jnp.einsum("sqhgd,snhd->sqhgn", queries, block_keys, preferred_element_type=jnp.float32)
        * score_scale
    )
    probabilities = jnp.where(mask_wide, jnp.exp(scores - log_total[..., None]), 0.0)
    value_gradient = jnp.einsum(
        "sqhgn,sqhgd->snhd",
        probabilities.astype(jnp.bfloat16),
        attention_gradient,
        preferred_element_type=jnp.float32,
    )
    grad_probs = jnp.einsum(
        "sqhgd,snhd->sqhgn", attention_gradient, block_values, preferred_element_type=jnp.float32
    )
    grad_scores = (probabilities * (grad_probs - delta[..., None])).astype(jnp.bfloat16)
    grad_queries = (
        jnp.einsum("sqhgn,snhd->sqhgd", grad_scores, block_keys, preferred_element_type=jnp.float32)
        * score_scale
    )
    key_gradient = (
        jnp.einsum("sqhgn,sqhgd->snhd", grad_scores, queries, preferred_element_type=jnp.float32)
        * score_scale
    )
    grad_pair = jnp.stack(
        [
            key_gradient.reshape(sequence_count, count_of_keys, KEY_VALUE_HEADS * HEAD_SIZE),
            value_gradient.reshape(sequence_count, count_of_keys, KEY_VALUE_HEADS * HEAD_SIZE),
        ]
    )
    return (grad_queries, grad_pair)


def summed(part, count_of_shards):
    return lax.psum_scatter(
        part.reshape(-1), ("ctx", "fsdp"), scatter_dimension=0, tiled=True
    )


def local(tokens, cotangent, stretch_order, doc_lengths, master, first_moment, second_moment):
    cycle_size = lax.axis_size("ctx")
    ctx_index = lax.axis_index("ctx")
    count_of_shards = cycle_size * lax.axis_size("fsdp")
    sequence_count, count_of_rows, _ = tokens.shape
    seq_length = count_of_rows * cycle_size
    query_groups = QUERY_HEADS // KEY_VALUE_HEADS
    score_scale = HEAD_SIZE ** (-0.5)
    gathered = lax.all_gather(master.astype(jnp.bfloat16), ("ctx", "fsdp"), axis=0, tiled=True)
    w_qkv, w_out, w_gate_up, w_down, gain_column = unpack(gathered, count_of_shards)
    gains = gain_column.reshape(-1).astype(jnp.float32)
    g_attn = gains[:MODEL_WIDTH]
    g_mlp = gains[MODEL_WIDTH : 2 * MODEL_WIDTH]
    g_query = gains[2 * MODEL_WIDTH : 2 * MODEL_WIDTH + HEAD_SIZE]
    g_key = gains[2 * MODEL_WIDTH + HEAD_SIZE :]
    query_pos = slot_positions(stretch_order, ctx_index * count_of_rows, count_of_rows)
    query_doc, relative = documents(query_pos, doc_lengths)
    cosine_table, sine_values = rope_tables(relative)
    x_in = tokens.astype(jnp.float32)
    normed_one = rms_norm(x_in, g_attn).astype(jnp.bfloat16)
    projected_output = jnp.einsum(
        "sqd,de->sqe", normed_one, w_qkv, preferred_element_type=jnp.float32
    )
    query_raw = projected_output[:, :, : QUERY_HEADS * HEAD_SIZE].reshape(
        sequence_count, count_of_rows, QUERY_HEADS, HEAD_SIZE
    )
    unrotated_keys = projected_output[
        :, :, QUERY_HEADS * HEAD_SIZE : (QUERY_HEADS + KEY_VALUE_HEADS) * HEAD_SIZE
    ].reshape(sequence_count, count_of_rows, KEY_VALUE_HEADS, HEAD_SIZE)
    unprojected_values = projected_output[:, :, (QUERY_HEADS + KEY_VALUE_HEADS) * HEAD_SIZE :]
    queries = (
        rotate(rms_norm(query_raw, g_query), cosine_table, sine_values)
        .astype(jnp.bfloat16)
        .reshape(sequence_count, count_of_rows, KEY_VALUE_HEADS, query_groups, HEAD_SIZE)
    )
    keys_rot = rotate(rms_norm(unrotated_keys, g_key), cosine_table, sine_values).reshape(
        sequence_count, count_of_rows, KEY_VALUE_HEADS * HEAD_SIZE
    )
    kv_local = jnp.stack([keys_rot, unprojected_values]).astype(jnp.bfloat16)
    statistic_shape = (sequence_count, count_of_rows, KEY_VALUE_HEADS, query_groups)
    initial = (
        jnp.zeros(statistic_shape + (HEAD_SIZE,), jnp.float32),
        jnp.full(statistic_shape, MASKED, jnp.float32),
        jnp.zeros(statistic_shape, jnp.float32),
    )
    state = initial
    piece = lax.all_gather(kv_local, "ctx", axis=2, tiled=True)
    key_total = piece.shape[2]

    def key_step(inner, block_index):
        first_row = block_index * count_of_rows
        key_value_block = lax.dynamic_slice_in_dim(piece, first_row, count_of_rows, 2)
        allowed = key_mask(
            stretch_order, doc_lengths, query_pos, query_doc, first_row, count_of_rows
        )
        return (attend_block(inner, queries, key_value_block, allowed, score_scale), None)

    state, _ = lax.scan(key_step, state, jnp.arange(key_total // count_of_rows, dtype=jnp.int32))
    running, top_now, total_now = state
    attn = running / total_now[..., None]
    log_total = top_now + jnp.log(total_now)
    attn_low = attn.reshape(sequence_count, count_of_rows, QUERY_HEADS * HEAD_SIZE).astype(
        jnp.bfloat16
    )
    resid = x_in + jnp.einsum("sqa,ad->sqd", attn_low, w_out, preferred_element_type=jnp.float32)
    normed_two = rms_norm(resid, g_mlp).astype(jnp.bfloat16)
    gate_up = jnp.einsum("sqd,de->sqe", normed_two, w_gate_up, preferred_element_type=jnp.float32)
    gate = gate_up[:, :, :FEED_WIDTH]
    up_part = gate_up[:, :, FEED_WIDTH:]
    sigmoid_gate = jax.nn.sigmoid(gate)
    hidden = (gate * sigmoid_gate * up_part).astype(jnp.bfloat16)
    mlp_out = jnp.einsum("sqf,fd->sqd", hidden, w_down, preferred_element_type=jnp.float32)
    layer_out = (resid + mlp_out).astype(jnp.bfloat16)
    grad_w_down = jnp.einsum("sqf,sqd->fd", hidden, cotangent, preferred_element_type=jnp.float32)
    grad_hidden = jnp.einsum("sqd,fd->sqf", cotangent, w_down, preferred_element_type=jnp.float32)
    grad_gate = grad_hidden * up_part * sigmoid_gate * (1.0 + gate * (1.0 - sigmoid_gate))
    grad_up = grad_hidden * gate * sigmoid_gate
    grad_gate_up = jnp.concatenate([grad_gate, grad_up], axis=-1).astype(jnp.bfloat16)
    grad_w_gate_up = jnp.einsum(
        "sqd,sqe->de", normed_two, grad_gate_up, preferred_element_type=jnp.float32
    )
    grad_normed_two = jnp.einsum(
        "sqe,de->sqd", grad_gate_up, w_gate_up, preferred_element_type=jnp.float32
    )
    back_two, mlp_gain_terms = norm_back(resid, grad_normed_two, g_mlp)
    grad_resid = cotangent.astype(jnp.float32) + back_two
    grad_branch = grad_resid.astype(jnp.bfloat16)
    grad_w_out = jnp.einsum(
        "sqa,sqd->ad", attn_low, grad_branch, preferred_element_type=jnp.float32
    )
    attention_gradient = jnp.einsum(
        "sqd,ad->sqa", grad_branch, w_out, preferred_element_type=jnp.float32
    ).astype(jnp.bfloat16)
    attention_head_gradient = attention_gradient.reshape(
        sequence_count, count_of_rows, KEY_VALUE_HEADS, query_groups, HEAD_SIZE
    )
    delta = jnp.sum(attention_head_gradient.astype(jnp.float32) * attn, axis=-1)

    def grads_from(turn_index, kv_now, key_value_gradients, grad_queries):
        source_dev = (ctx_index - turn_index) % cycle_size
        allowed = key_mask(
            stretch_order,
            doc_lengths,
            query_pos,
            query_doc,
            source_dev * count_of_rows,
            count_of_rows,
        )
        part_queries, part_pair = backward_block(
            queries, attention_head_gradient, log_total, delta, kv_now, allowed, score_scale
        )
        return (key_value_gradients + part_pair, grad_queries + part_queries)

    def pass_grads(key_value_gradients):
        return from_behind(key_value_gradients.astype(jnp.bfloat16), "ctx", 1).astype(
            key_value_gradients.dtype
        )

    def turn_step(turn_index, state):
        kv_now, key_value_gradients, grad_queries = state
        key_value_gradients, grad_queries = grads_from(
            turn_index, kv_now, key_value_gradients, grad_queries
        )
        kv_now = from_behind(kv_now, "ctx", 1)
        key_value_gradients = pass_grads(key_value_gradients)
        return (kv_now, key_value_gradients, grad_queries)

    start_state = (
        kv_local,
        jnp.zeros(kv_local.shape, jnp.float32),
        jnp.zeros(statistic_shape + (HEAD_SIZE,), jnp.float32),
    )
    kv_now, key_value_gradients, grad_queries = lax.fori_loop(
        0, cycle_size - 1, turn_step, start_state
    )
    key_value_gradients, grad_queries = grads_from(
        cycle_size - 1, kv_now, key_value_gradients, grad_queries
    )
    key_value_gradients = pass_grads(key_value_gradients)
    grad_query_rot = rotate_back(
        grad_queries.reshape(sequence_count, count_of_rows, QUERY_HEADS, HEAD_SIZE),
        cosine_table,
        sine_values,
    )
    grad_key_rot = rotate_back(
        key_value_gradients[0].reshape(sequence_count, count_of_rows, KEY_VALUE_HEADS, HEAD_SIZE),
        cosine_table,
        sine_values,
    )
    grad_query_raw, query_gain_terms = norm_back(query_raw, grad_query_rot, g_query)
    unrotated_key_gradient, key_gain_terms = norm_back(unrotated_keys, grad_key_rot, g_key)
    grad_projected = jnp.concatenate(
        [
            grad_query_raw.reshape(sequence_count, count_of_rows, QUERY_HEADS * HEAD_SIZE),
            unrotated_key_gradient.reshape(
                sequence_count, count_of_rows, KEY_VALUE_HEADS * HEAD_SIZE
            ),
            key_value_gradients[1],
        ],
        axis=-1,
    ).astype(jnp.bfloat16)
    grad_w_qkv = jnp.einsum(
        "sqd,sqe->de", normed_one, grad_projected, preferred_element_type=jnp.float32
    )
    grad_normed_one = jnp.einsum(
        "sqe,de->sqd", grad_projected, w_qkv, preferred_element_type=jnp.float32
    )
    back_one, attn_gain_terms = norm_back(x_in, grad_normed_one, g_attn)
    input_grad = (grad_resid + back_one).astype(jnp.bfloat16)
    grad_gains = jnp.concatenate(
        [
            jnp.sum(attn_gain_terms, axis=(0, 1)),
            jnp.sum(mlp_gain_terms, axis=(0, 1)),
            jnp.sum(query_gain_terms, axis=(0, 1, 2)),
            jnp.sum(key_gain_terms, axis=(0, 1, 2)),
        ]
    ).reshape(-1, 1)
    grad = jnp.concatenate(
        [
            summed(part, count_of_shards)
            for part in (grad_w_qkv, grad_w_out, grad_w_gate_up, grad_w_down, grad_gains)
        ]
    )
    new_master, new_first, new_second = adam(
        grad, master, first_moment, second_moment, count_of_shards, seq_length
    )
    return (layer_out, input_grad, new_master, new_first, new_second)


MESH = pl.DeviceIdType.MESH
F32 = jnp.float32
BF16 = jnp.bfloat16
CTX = 8
CHIPS = 4
GROUP = QUERY_HEADS // KEY_VALUE_HEADS
QCOLS = GROUP * HEAD_SIZE
PCOLS = QCOLS + 2 * HEAD_SIZE
HID = FEED_WIDTH // CTX
GAIN_WIDTH = 2 * MODEL_WIDTH + 2 * HEAD_SIZE
TILE = 256
WIDE = 512


def dot(a, b, dims=((1,), (0,))):
    return lax.dot_general(a, b, (dims, ((), ())), preferred_element_type=F32)


NT = ((1,), (1,))
TN = ((0,), (0,))


def layer_kernel(
    order_hbm,
    doc_hbm,
    x_hbm,
    cot_hbm,
    master_hbm,
    out_hbm,
    xgrad_hbm,
    lin_ref,
    order_ref,
    doc_ref,
    out_ref,
    xgrad_ref,
    flat,
    flat_down,
    flat_gains,
    lines,
    wq_in,
    wgu_in,
    gains_in,
    cos_ref,
    sin_ref,
    kpos_ref,
    qpos_ref,
    qstart_ref,
    xg,
    n1,
    cot,
    n2,
    x_own,
    wq,
    wo,
    wgu,
    wd,
    qraw,
    kraw,
    q_s,
    k_s,
    v_s,
    kt_s,
    vt_s,
    probs,
    attn,
    shares,
    attn_low,
    hidden,
    ggu,
    gattn,
    dk_s,
    dv_s,
    gp,
    psnd,
    prcv,
    csnd,
    crcv,
    own,
    acc,
    resid_s,
    gresid_s,
    gwq,
    gwo,
    gwgu,
    gwd,
    lwq,
    lwo,
    lwgu,
    lwd,
    asq,
    asg,
    arq,
    arg_,
    gz,
    gpl,
    gains,
    hz,
    hpl,
    hrow,
    ag_s,
    ag_r,
    rs_ps,
    rs_pr,
    rs_cs,
    rs_cr,
    a2a_s,
    a2a_r,
    zg_s,
    zg_r,
    zr_s,
    zr_r,
    g_s,
    g_r,
    loc,
):
    c = lax.axis_index("ctx")
    z = lax.axis_index("fsdp")
    core = c % 2
    chip = c // 2
    cx = chip % 2
    cy = chip // 2
    slot = core * CHIPS + chip
    sib = c + 1 - 2 * core
    tiles = n1.shape[0] * n1.shape[1] // TILE
    rows = n1.shape[1]
    half = CHIPS * rows

    def chip_at(i):
        return ((cy + i // 2) % 2) * 2 + (cx + i % 2) % 2

    def rcopy(src, dst, ssem, rsem, to_c, to_z):
        return pltpu.make_async_remote_copy(
            src_ref=src,
            dst_ref=dst,
            send_sem=ssem,
            recv_sem=rsem,
            device_id=(to_c, to_z),
            device_id_type=MESH,
        )

    def loop(lo, hi, body):
        def step(i, carry):
            body(i)
            return carry

        lax.fori_loop(lo, hi, step, 0)

    spans = [r // (4 * CTX) * w for r, w in segment_shapes()]
    ends = [sum(spans[: i + 1]) for i in range(5)]
    tail = ends[3]
    fetch = [
        pltpu.make_async_copy(master_hbm.at[pl.ds(0, ends[1])], flat, loc.at[0]),
        pltpu.make_async_copy(master_hbm.at[pl.ds(tail, spans[4])], flat_gains, loc.at[3]),
        pltpu.make_async_copy(master_hbm.at[pl.ds(ends[2], spans[3])], flat_down, loc.at[4]),
        pltpu.make_async_copy(x_hbm.at[0], xg.at[slot], loc.at[1]),
        pltpu.make_async_copy(cot_hbm.at[0], cot.at[slot], loc.at[2]),
        pltpu.make_async_copy(order_hbm, order_ref, loc.at[5]),
        pltpu.make_async_copy(doc_hbm, doc_ref, loc.at[6]),
    ]
    for copy in fetch:
        copy.start()
    fetch_feed = pltpu.make_async_copy(
        master_hbm.at[pl.ds(ends[1], spans[2])], flat, loc.at[0]
    )
    barrier = pltpu.get_barrier_semaphore()

    def greet_plane(i):
        pl.semaphore_signal(
            barrier, inc=1, device_id=((c + i) % CTX, z), device_id_type=MESH
        )

    def greet_z(i):
        pl.semaphore_signal(
            barrier, inc=1, device_id=(c, (z + i) % 4), device_id_type=MESH
        )

    loop(1, CTX, greet_plane)
    loop(1, 4, greet_z)

    def to_lines(src, first, last):
        block = 128 * 128

        def one(i):
            lines[pl.ds(pl.multiple_of(first // 128 + i * 128, 128), 128), :] = src[
                pl.ds(pl.multiple_of(i * block, block), block)
            ].reshape(128, 128)

        loop(0, (last - first) // block, one)

    def qkv_group(j, part):
        return (GROUP * j + part) if part < GROUP else KEY_VALUE_HEADS * part + j

    def feed_group(j, part):
        per = HID // 128
        return j * per + part if part < per else CTX * per + j * per + part - per

    def line_rows(first, group, groups, count):
        return pl.ds(first // 128 + group, count, stride=groups)

    per_run = wq_in.shape[2]
    fetch[0].wait()
    fetch[1].wait()
    to_lines(flat, 0, ends[1])
    fetch_feed.start()
    for g in range(MODEL_WIDTH // 128):
        wo[z, :, g * 128 : (g + 1) * 128] = lines[
            line_rows(ends[0], g, MODEL_WIDTH // 128, wo.shape[1]), :
        ].astype(BF16)
    qkv_groups = CTX * PCOLS // 128
    for j in range(CTX):
        for part in range(PCOLS // 128):
            wq_in[part // 2, j, :, part % 2 * 128 : (part % 2 + 1) * 128] = lines[
                line_rows(0, qkv_group(j, part), qkv_groups, per_run), :
            ].astype(BF16)
    own_gains = flat_gains[...].reshape(1, spans[4]).astype(BF16).astype(F32)
    gains_in[...] = pltpu.roll(
        jnp.concatenate([own_gains, jnp.zeros((1, GAIN_WIDTH - spans[4]), F32)], axis=1),
        spans[4] * (4 * c + z),
        1,
    )

    fetch[2].wait()
    to_lines(flat_down, ends[2], ends[3])
    for g in range(MODEL_WIDTH // 128):
        wd[z, :, g * 128 : (g + 1) * 128] = lines[
            line_rows(ends[2], g, MODEL_WIDTH // 128, wd.shape[1]), :
        ].astype(BF16)
    pl.semaphore_wait(barrier, CTX - 1 + 4 - 1)

    mid = rows // 2
    XN, YN, ACROSS = 1, 2, 3
    whole, top, bottom = pl.ds(0, rows), pl.ds(0, mid), pl.ds(mid, mid)

    AG_SEM = (0, 1, 2, 3, 4, 5, 6, 0, 7, 7, 7)

    def ag_piece(n, buf, k):
        origin, part, to = (
            (0, whole, sib),
            (0, top, XN),
            (0, bottom, XN),
            (0, bottom, YN),
            (0, top, YN),
            (XN, top, YN),
            (YN, bottom, XN),
            (XN, whole, sib),
            (YN, whole, sib),
            (ACROSS, top, sib),
            (ACROSS, bottom, sib),
        )[k]
        there = buf.at[core * CHIPS + chip_at(origin), part]
        target = sib if to is sib else chip_at(to) * 2 + core
        return rcopy(there, there, ag_s.at[n], ag_r.at[n % 3, AG_SEM[k]], target, z)

    def ag_landed(n, buf, k):
        origin, part, own_core = (
            (0, whole, False),
            (XN, top, True),
            (XN, bottom, True),
            (YN, bottom, True),
            (YN, top, True),
            (ACROSS, top, True),
            (ACROSS, bottom, True),
            (XN, whole, False),
            (YN, whole, False),
            (ACROSS, top, False),
            (ACROSS, bottom, False),
        )[k]
        which = core if own_core else 1 - core
        there = buf.at[which * CHIPS + chip_at(origin), part]
        return rcopy(there, there, ag_s.at[n], ag_r.at[n % 3, AG_SEM[k]], sib, z)

    def ag_start(n, buf):
        for k in (1, 3, 2, 4, 0):
            ag_piece(n, buf, k).start()

    def ag_pass_near(n, buf):
        for landed, onward in ((1, 5), (3, 6), (2, 7), (4, 8)):
            ag_landed(n, buf, landed).wait_recv()
            ag_piece(n, buf, onward).start()

    def ag_pass_across(n, buf):
        for landed, onward in ((5, 9), (6, 10)):
            ag_landed(n, buf, landed).wait_recv()
            ag_piece(n, buf, onward).start()

    def ag_handed(n, buf, sem):
        two_rows = buf.at[pl.ds(0, 2)]
        rcopy(two_rows, two_rows, ag_s.at[n], ag_r.at[n % 3, sem], sib, z).wait_recv()

    def ag_finish_near(n, buf):
        ag_handed(n, buf, 0)

    def ag_finish(n, buf):
        ag_handed(n, buf, 7)

    def ag_drain(n, buf):
        seven = buf.at[pl.ds(0, 7)]
        rcopy(seven, seven, ag_s.at[n], ag_r.at[0, 0], sib, z).wait_send()

    def gathered_tiles(n, buf, body, between, before=None):
        ag_pass_near(n, buf)
        ag_finish_near(n, buf)
        if before is not None:
            before()
        loop(0, 2, lambda k: body(2 * k + cy))
        between()
        ag_pass_across(n, buf)
        ag_finish(n, buf)
        loop(0, 2, lambda k: body(2 * k + 1 - cy))

    wide = MODEL_WIDTH // 2

    def rs_pair(r, h):
        return rcopy(psnd.at[h], prcv.at[r % 2, h], rs_ps.at[h], rs_pr.at[r % 2, h], sib, z)

    def rs_chip(r, k):
        to = chip_at((XN, XN, YN, YN, YN, XN)[k]) * 2 + core
        return rcopy(csnd.at[k], crcv.at[r % 2, k], rs_cs.at[k], rs_cr.at[r % 2, k], to, z)

    def rs_give(r, part, h):
        if r > 0:
            rs_pair(r - 1, h).wait_send()
        psnd[h] = part(1 - core, h).astype(BF16).reshape(CHIPS, rows, wide)
        rs_pair(r, h).start()

    def rs_keep(r, part, h):
        own[h] = part(core, h).reshape(CHIPS, rows, wide)

    def pair_sum(r, h, i):
        return own[h, chip_at(i)] + prcv[r % 2, h, chip_at(i)].astype(F32)

    def rs_send(r, h):
        rs_pair(r, h).wait_recv()
        if r > 0 and h == 0:
            for k in range(6):
                rs_chip(r - 1, k).wait_send()
        csnd[2 * h] = pair_sum(r, h, ACROSS).astype(BF16)
        rs_chip(r, 2 * h).start()
        csnd[2 * h + 1] = pair_sum(r, h, (XN, YN)[h]).astype(BF16)
        rs_chip(r, 2 * h + 1).start()
        acc[r % 2, :, h * wide : (h + 1) * wide] = pair_sum(r, h, 0)

    def rs_begin(r, part):
        for h in range(2):
            rs_give(r, part, h)
        for h in range(2):
            rs_keep(r, part, h)
            rs_send(r, h)

    def rs_compute(r, part):
        for h in range(2):
            rs_give(r, part, h)
        for h in range(2):
            rs_keep(r, part, h)

    def rs_drain(r):
        for h in range(2):
            rs_pair(r, h).wait_send()
        for k in range(6):
            rs_chip(r, k).wait_send()

    def rs_relay(r):
        for h, second in ((0, YN), (1, XN)):
            rs_chip(r, 2 * h).wait_recv()
            csnd[4 + h] = (pair_sum(r, h, second) + crcv[r % 2, 2 * h].astype(F32)).astype(BF16)
            rs_chip(r, 4 + h).start()

    def rs_finish(r):
        halves = []
        for h in range(2):
            rs_chip(r, 2 * h + 1).wait_recv()
            rs_chip(r, 4 + h).wait_recv()
            halves.append(
                acc[r % 2, :, h * wide : (h + 1) * wide]
                + crcv[r % 2, 2 * h + 1].astype(F32)
                + crcv[r % 2, 4 + h].astype(F32)
            )
        return jnp.concatenate(halves, axis=1)

    A2A_SEM = (0, 2 * CTX - 2, 2 * CTX - 1, 2 * CTX, CTX - 1)

    def a2a(n, src, dst_of, i, sem=0):
        to = (c + i) % CTX
        return rcopy(src.at[to], dst_of(c), a2a_s.at[n], a2a_r.at[A2A_SEM[n] + sem], to, z)

    def a2a_landed(n, dst_of, i):
        frm = (c + CTX - i) % CTX
        return rcopy(dst_of(frm), dst_of(frm), a2a_s.at[n], a2a_r.at[A2A_SEM[n] + i - 1], sib, z)

    def a2a_start(n, src, dst_of, apart=False):
        loop(1, CTX, lambda i: a2a(n, src, dst_of, i, i - 1 if apart else 0).start())

    def a2a_half(n, src, dst_of, h):
        def one(i):
            pl.when((c + i) % CTX // (CTX // 2) == h)(a2a(n, src, dst_of, i).start)

        loop(1, CTX, one)

    def a2a_wait(n, dst):
        seven = dst.at[pl.ds(0, CTX - 1)]
        rcopy(seven, seven, a2a_s.at[n], a2a_r.at[A2A_SEM[n]], sib, z).wait_recv()

    def a2a_drain(n, src):
        seven = src.at[pl.ds(0, CTX - 1)]
        rcopy(seven, seven, a2a_s.at[n], a2a_r.at[A2A_SEM[n]], sib, z).wait_send()

    inner = (z == 1) | (z == 2)
    outer = jnp.logical_not(inner)
    far = 3 * (2 - z)

    def zg(n, of, j, to, sem):
        return rcopy(of(j), of(j), zg_s.at[n, sem], zg_r.at[n, j], c, to)

    def zg_own(n, of):
        return (
            (z < 3, zg(n, of, z, z + 1, 0)),
            (z > 0, zg(n, of, z, z - 1, 0)),
        )

    def zg_onward(n, of):
        return (
            zg(n, of, z - 1, z + 1, 1),
            zg(n, of, z + 1, z - 1, 1),
            zg(n, of, far, 3 * (z - 1), 1),
        )

    def zg_start(n, of, who=None):
        for there, copy in zg_own(n, of):
            pl.when(there if who is None else there & who)(copy.start)

    def zg_pass(n, of, k, when, j):
        def run():
            zg(n, of, j, z, 0).wait_recv()
            zg_onward(n, of)[k].start()

        pl.when(when)(run)

    def zg_across(n, of):
        zg_pass(n, of, 0, z == 1, z - 1)
        zg_pass(n, of, 1, z == 2, z + 1)

    def zg_back(n, of):
        zg_pass(n, of, 1, z == 1, z + 1)
        zg_pass(n, of, 0, z == 2, z - 1)

    def zg_near(n, of):
        zg_across(n, of)
        zg_back(n, of)

    def zg_far(n, of):
        def run():
            zg(n, of, far, z, 0).wait_recv()
            zg_onward(n, of)[2].start()

        pl.when(inner)(run)

    def zg_wait(n, of):
        def run():
            for i in (1, 2, 3):
                zg(n, of, (z + i) % 4, z, 0).wait_recv()

        pl.when(outer)(run)

    def zg_drain(n, some):
        def sent(count, sem):
            part = some(count)
            rcopy(part, part, zg_s.at[n, sem], zg_r.at[n, 0], c, c).wait_send()

        def run():
            sent(2, 0)
            sent(3, 1)

        pl.when(inner)(run)
        pl.when(outer)(lambda: sent(1, 0))

    def zr(n, of, land, d, to, spot):
        return rcopy(of(d), land(spot), zr_s.at[n], zr_r.at[n, spot], c, to)

    def zr_add(n, of, land, d):
        rcopy(land(d), land(d), zr_s.at[n], zr_r.at[n, d], sib, z).wait_recv()
        mine = of(d)
        mine[...] = (mine[...].astype(F32) + land(d)[...].astype(F32)).astype(BF16)

    ENDS = (
        ((0, 3, 1, 3), (3, 0, 2, 0)),
        ((0, 2, 1, 2), (3, 1, 2, 1)),
        ((0, 1, 1, 1), (3, 2, 2, 4)),
    )
    FIRST = ((1, 3, 2, 3), (2, 0, 1, 0))
    SECOND = ((1, 2, 2, 2), (2, 1, 1, 4), (1, 0, 0, 4), (2, 3, 3, 3))

    def zr_send(n, of, land, k):
        for device, d, to, spot in ENDS[k]:
            pl.when(z == device)(zr(n, of, land, d, to, spot).start)

    def zr_start(*items, part=range(3)):
        for k in part:
            for item in items:
                zr_send(*item, k)

    def zr_pass(n, of, land, steps):
        for device, d, to, spot in steps:

            def run(d=d, to=to, spot=spot):
                zr_add(n, of, land, d)
                zr(n, of, land, d, to, spot).start()

            pl.when(z == device)(run)

    def zr_first(n, of, land):
        zr_pass(n, of, land, FIRST)

    def zr_second(n, of, land):
        zr_pass(n, of, land, SECOND)

    def zr_finish(n, of, land):
        def landed(spot):
            rcopy(land(spot), land(spot), zr_s.at[n], zr_r.at[n, spot], sib, z).wait_recv()

        pl.when(z > 0)(lambda: landed(z))
        pl.when(z < 3)(lambda: landed(4))
        return of(z)[...].astype(F32) + land(z)[...].astype(F32) + land(4)[...].astype(F32)

    def row_z(n, src, land, i):
        return rcopy(src, land.at[z], g_s.at[n, 0], g_r.at[n, 0], c, (z + i) % 4)

    def row_plane(n, src, land, i):
        return rcopy(src, land.at[c], g_s.at[n, 1], g_r.at[n, 1], (c + i) % CTX, z)

    def rows_of(n, land, k):
        others = land.at[pl.ds(0, (3, CTX - 1)[k])]
        return rcopy(others, others, g_s.at[n, k], g_r.at[n, k], sib, z)

    def row_z_wait(n, land):
        rows_of(n, land, 0).wait_recv()

    def row_plane_wait(n, land):
        rows_of(n, land, 1).wait_recv()

    def halves(ref):
        half_of = lambda h: lambda j: ref.at[pl.ds(h * (CTX // 2), CTX // 2), j]
        return half_of(0), half_of(1)

    def land_halves(ref):
        half_of = lambda h: lambda j: ref.at[j, pl.ds(h * (CTX // 2), CTX // 2)]
        return half_of(0), half_of(1)

    wq_at = lambda j: wq.at[0, j, z]
    wkv_at = lambda j: wq.at[1, j, z]
    wgu_at = lambda j: wgu.at[j, z]
    g_q = (0, lambda j: wq.at[0, :, j])
    g_kv = (5, lambda j: wq.at[1, :, j])
    g_o = (1, lambda j: wo.at[j])
    g_gu1, g_gu2 = ((2 + h, of) for h, of in enumerate(halves(wgu)))
    g_d = (4, lambda j: wd.at[j])
    r_d = (0, lambda j: gwd.at[j], lambda j: lwd.at[j])
    r_gu1, r_gu2 = (
        (1 + h, *both) for h, both in enumerate(zip(halves(gwgu), land_halves(lwgu)))
    )
    r_o = (3, lambda j: gwo.at[j], lambda j: lwo.at[j])
    r_q1, r_q2 = (
        (4 + h, *both) for h, both in enumerate(zip(halves(gwq), land_halves(lwq)))
    )

    lines[pl.ds(tail // 128, 8), :] = jnp.zeros((8, 128), F32)
    gz[z] = gains_in[...]
    loop(1, 4, lambda i: row_z(0, gains_in, gz, i).start())
    a2a_start(0, wq_in.at[0], wq_at, apart=True)
    a2a_start(4, wq_in.at[1], wkv_at, apart=True)
    zg_start(*g_o)

    def share(part, frm):
        there = wq.at[part, frm, z]
        n = 5 * part
        for to, here in ((z + 1, z < 3), (z - 1, z > 0)):
            pl.when(here)(rcopy(there, there, zg_s.at[n, 0], zg_r.at[n, z], c, to).start)

    def shares_landed(part, n, at):
        def one(i):
            a2a_landed(n, at, i).wait_recv()
            share(part, (c + CTX - i) % CTX)

        loop(1, CTX, one)

    for part in range(2):
        wq[part, c, z] = wq_in[part, c]
        share(part, c)
    fetch_feed.wait()
    to_lines(flat, ends[1], ends[2])
    feed_groups = 2 * FEED_WIDTH // 128
    for j in range(CTX):
        for part in range(2 * HID // 128):
            wgu_in[j, :, part * 128 : (part + 1) * 128] = lines[
                line_rows(ends[1], feed_group(j, part), feed_groups, per_run), :
            ].astype(BF16)
    fetch[3].wait()
    ag_start(0, xg)
    shares_landed(0, 0, wq_at)
    shares_landed(1, 4, wkv_at)
    row_z_wait(0, gz)
    gpl[c] = jnp.sum(gz[...], axis=0)
    loop(1, CTX, lambda i: row_plane(0, gpl.at[c], gpl, i).start())
    wgu[c, z] = wgu_in[c]
    for copy in fetch[4:]:
        copy.wait()
    doc_ends = [doc_ref[0, 0]]
    for j in range(1, doc_ref.shape[1] - 1):
        doc_ends.append(doc_ends[-1] + doc_ref[0, j])

    def doc_start(pos):
        start = jnp.zeros_like(pos)
        for end in doc_ends:
            start = jnp.where(pos >= end, end, start)
        return start

    def tables(s):
        first = 2 * (2 * (s % CHIPS) + s // CHIPS)
        lead = order_ref[first] * STRETCH
        trail = order_ref[first + 1] * STRETCH - STRETCH
        at = pl.ds(pl.multiple_of(s * rows, rows), rows)

        def positions(shape, axis):
            index = lax.broadcasted_iota(jnp.int32, shape, axis)
            return index + jnp.where(index < STRETCH, lead, trail)

        across = positions((1, rows), 1)
        qpos_ref[:, at] = across
        qstart_ref[:, at] = doc_start(across)
        down = positions((rows, HEAD_SIZE), 0)
        kpos_ref[at, :] = down
        lane = lax.broadcasted_iota(jnp.int32, (1, HEAD_SIZE), 1)
        upper = lane >= HEAD_SIZE // 2
        index = jnp.where(upper, lane - HEAD_SIZE // 2, lane).astype(F32)
        frequency = jnp.exp(index * (-2.0 / HEAD_SIZE * math.log(ROPE_BASE)))
        angles = (down - doc_start(down)).astype(F32) * frequency
        sine = jnp.sin(angles)
        cos_ref[at, :] = jnp.cos(angles)
        sin_ref[at, :] = jnp.where(upper, sine, -sine)

    loop(0, CTX // 2, tables)
    for land in (lwq, lwo, lwgu, lwd):
        for end, spot in ((0, 0), (3, 4)):

            def blank(land=land, spot=spot):
                land[spot] = jnp.zeros(land.shape[1:], BF16)

            pl.when(z == end)(blank)
    zg_near(*g_q)
    loop(CTX // 2, CTX, tables)
    ag_pass_near(0, xg)
    zg_near(*g_kv)
    ag_finish_near(0, xg)
    ag_pass_across(0, xg)
    zg_far(*g_q)
    ag_finish(0, xg)
    a2a_start(1, wgu_in, wgu_at)
    ag_start(1, cot)
    zg_far(*g_kv)
    zg_near(*g_o)
    row_plane_wait(0, gpl)
    gains[...] = jnp.sum(gpl[...], axis=0)
    g_attn = gains[:, :MODEL_WIDTH]
    def normed(t):
        at = pl.ds(t * (TILE // rows), TILE // rows)
        x_tile = xg[at].astype(F32)
        x_scale = lax.rsqrt(jnp.mean(x_tile * x_tile, axis=-1, keepdims=True) + NORM_EPS)
        n1[at] = (x_tile * x_scale * g_attn.reshape(1, 1, MODEL_WIDTH)).astype(BF16)

    loop(0, tiles, normed)
    x_own[...] = xg[slot]
    g_query = gains[:, 2 * MODEL_WIDTH : 2 * MODEL_WIDTH + HEAD_SIZE]
    g_key = gains[:, 2 * MODEL_WIDTH + HEAD_SIZE :]

    def tile_rows(t):
        return pl.ds(pl.multiple_of(t * TILE, TILE), TILE)

    def two(buf, t):
        return buf[pl.ds(t * (TILE // rows), TILE // rows)].reshape(TILE, buf.shape[-1])

    def turned(v):
        return pltpu.roll(v, HEAD_SIZE // 2, 1)

    def normed_rope(raw, gain, at):
        scale = lax.rsqrt(jnp.mean(raw * raw, axis=-1, keepdims=True) + NORM_EPS)
        y = raw * scale * gain
        return y * cos_ref[at, :] + turned(y) * sin_ref[at, :]

    def project_queries(t):
        at = tile_rows(t)
        out = dot(two(n1, t), wq[0].reshape(MODEL_WIDTH, QCOLS))
        for h in range(GROUP):
            raw = out[:, h * HEAD_SIZE : (h + 1) * HEAD_SIZE]
            qraw[at, h * HEAD_SIZE : (h + 1) * HEAD_SIZE] = raw
            q_s[h, at, :] = normed_rope(raw, g_query, at).astype(BF16)

    def project_pairs(t):
        at = tile_rows(t)
        both = dot(two(n1, t), wq[1].reshape(MODEL_WIDTH, 2 * HEAD_SIZE))
        raw = both[:, :HEAD_SIZE]
        kraw[at, :] = raw
        keys = normed_rope(raw, g_key, at)
        values = both[:, HEAD_SIZE:]
        k_s[at, :] = keys.astype(BF16)
        v_s[at, :] = values.astype(BF16)
        kt_s[:, at] = keys.T.astype(BF16)
        vt_s[:, at] = values.T.astype(BF16)

    zg_wait(*g_q)
    loop(0, tiles, project_queries)
    pl.when(outer)(lambda: a2a_wait(1, wgu_in))
    zg_start(*g_gu1, outer)
    zg_start(*g_gu2, outer)
    zg_start(*g_d, outer)
    zg_wait(*g_kv)
    loop(0, tiles, project_pairs)
    ag_drain(0, xg)
    zg_far(*g_o)
    pl.when(inner)(lambda: a2a_wait(1, wgu_in))
    zg_start(*g_gu1, inner)
    zg_start(*g_gu2, inner)
    def n_cols(n):
        return pl.ds(pl.multiple_of(n * WIDE, WIDE), WIDE)

    def half_rows(which):
        return pl.ds(pl.multiple_of(which * half, half), half)

    def half_slots(buf, which):
        return buf[pl.ds(which * CHIPS, CHIPS)].reshape(half, buf.shape[-1])

    def out_part(which, n):
        return dot(
            attn_low[half_rows(which), :], wo[:, :, n_cols(n)].reshape(QCOLS, WIDE)
        )

    scale = HEAD_SIZE ** (-0.5)

    def attend(t):
        at = half_rows(t)
        kpos = jnp.concatenate([kpos_ref[...]] * (half // HEAD_SIZE), axis=1)
        kept = (kpos <= qpos_ref[:, at]) & (kpos >= qstart_ref[:, at])
        for h in range(GROUP):
            scores = jnp.where(kept, dot(k_s[...], q_s[h, at, :], NT) * scale, MASKED)
            weights = jnp.exp(scores - jnp.max(scores, axis=0, keepdims=True))
            low = weights.astype(BF16)
            probs[h, t] = low
            share = 1.0 / jnp.sum(weights, axis=0, keepdims=True)
            shares[h, :, at] = share
            mixed = dot(vt_s[...], low) * share
            attn[h, :, at] = mixed
            attn_low[at, h * HEAD_SIZE : (h + 1) * HEAD_SIZE] = mixed.T.astype(BF16)

    attend(1 - core)
    zg_across(*g_gu1)
    zg_wait(*g_o)
    rs_give(0, out_part, 0)
    rs_give(0, out_part, 1)
    ag_pass_near(1, cot)
    attend(core)
    zg_back(*g_gu1)
    for h in range(2):
        rs_keep(0, out_part, h)
        rs_send(0, h)
    zg_across(*g_gu2)
    zg_back(*g_gu2)
    rs_relay(0)
    ag_pass_across(1, cot)
    zg_far(*g_gu1)
    resid = x_own[...].astype(F32) + rs_finish(0)
    resid_s[...] = resid
    g_mlp = gains[:, MODEL_WIDTH : 2 * MODEL_WIDTH]
    s_two = lax.rsqrt(jnp.mean(resid * resid, axis=-1, keepdims=True) + NORM_EPS)
    n2[slot] = (resid * s_two * g_mlp).astype(BF16)
    ag_start(2, n2)
    ag_finish_near(1, cot)
    ag_finish(1, cot)
    zg_far(*g_gu2)
    zg_start(*g_d, inner)
    zg_across(*g_d)
    def feed(t):
        at = tile_rows(t)
        both = dot(two(n2, t), wgu[...].reshape(MODEL_WIDTH, 2 * HID))
        gate, up = both[:, :HID], both[:, HID:]
        sig = 1.0 / (1.0 + jnp.exp(-gate))
        silu = gate * sig
        hidden[at, :] = (silu * up).astype(BF16)
        ggu[at, :HID] = (up * sig * (1.0 + gate * (1.0 - sig))).astype(BF16)
        ggu[at, HID:] = silu.astype(BF16)

    def wgu_there():
        zg_wait(*g_gu1)
        zg_wait(*g_gu2)

    def pass_down():
        zg_back(*g_d)

    gathered_tiles(2, n2, feed, pass_down, wgu_there)
    zg_far(*g_d)

    def down_grad(n):
        there = cot[:, :, n_cols(n)].reshape(2 * half, WIDE)
        gwd[:, :, n_cols(n)] = (
            dot(hidden[...], there, TN).astype(BF16).reshape(4, HID // 4, WIDE)
        )

    loop(0, MODEL_WIDTH // WIDE, down_grad)
    zr_start(r_d)
    zg_wait(*g_d)

    def feed_back(t):
        at = tile_rows(t)
        ghid = dot(two(cot, t), wd[...].reshape(HID, MODEL_WIDTH), NT)
        ggu[at, :HID] = (ghid * ggu[at, :HID].astype(F32)).astype(BF16)
        ggu[at, HID:] = (ghid * ggu[at, HID:].astype(F32)).astype(BF16)

    loop(0, tiles, feed_back)

    def back_two_part(which, n):
        per = MODEL_WIDTH // CTX
        there = wgu[pl.ds(n * (WIDE // per), WIDE // per)].reshape(WIDE, 2 * HID)
        return dot(ggu[half_rows(which), :], there, NT)

    rs_begin(1, back_two_part)

    def gate_up_grad(n):
        per = MODEL_WIDTH // CTX
        there = n2[:, :, n_cols(n)].reshape(2 * half, WIDE)
        gwgu[pl.ds(n * (WIDE // per), WIDE // per)] = (
            dot(there, ggu[...], TN)
            .astype(BF16)
            .reshape(WIDE // per, 4, per // 4, 2 * HID)
        )

    gate_up_grad(0)
    zr_start(r_gu1)
    gate_up_grad(1)
    zr_start(r_gu2)
    zr_first(*r_d)
    rs_relay(1)


    def norm_back(values, grads, gain):
        factor = lax.rsqrt(jnp.mean(values * values, axis=-1, keepdims=True) + NORM_EPS)
        unit = values * factor
        scaled = grads * gain
        inner = jnp.mean(scaled * unit, axis=-1, keepdims=True)
        return factor * (scaled - unit * inner), jnp.sum(grads * unit, axis=0, keepdims=True)

    back, terms = norm_back(resid_s[...], rs_finish(1), g_mlp)
    hrow[:, MODEL_WIDTH : 2 * MODEL_WIDTH] = terms
    gresid = cot[slot].astype(F32) + back
    gresid_s[...] = gresid
    gb = xg
    gb[slot] = gresid.astype(BF16)
    def down_part(which, n):
        return dot(hidden[half_rows(which), :], wd[:, :, n_cols(n)].reshape(HID, WIDE))

    ag_start(3, gb)
    rs_compute(2, down_part)
    zr_second(*r_d)

    def attn_grad(t):
        gattn[tile_rows(t), :] = dot(
            two(gb, t), wo[...].reshape(QCOLS, MODEL_WIDTH), NT
        ).astype(BF16)

    gathered_tiles(3, gb, attn_grad, lambda: zr_first(*r_gu1))
    rs_send(2, 0)
    rs_send(2, 1)

    def out_grad(n):
        there = gb[:, :, n_cols(n)].reshape(2 * half, WIDE)
        gwo[:, :, n_cols(n)] = (
            dot(attn_low[...], there, TN).astype(BF16).reshape(4, QCOLS // 4, WIDE)
        )

    loop(0, MODEL_WIDTH // WIDE, out_grad)
    zr_start(r_o, part=(0, 1))

    dk_s[...] = jnp.zeros_like(dk_s)
    dv_s[...] = jnp.zeros_like(dv_s)

    hrow[:, 2 * MODEL_WIDTH :] = jnp.zeros((1, 2 * HEAD_SIZE), F32)

    def head_back(raw, grads, at, gain):
        grads = grads * scale
        grads = grads * cos_ref[at, :] - turned(grads) * sin_ref[at, :]
        return norm_back(raw, grads, gain)

    q_terms = pl.ds(2 * MODEL_WIDTH, HEAD_SIZE)
    k_terms = pl.ds(2 * MODEL_WIDTH + HEAD_SIZE, HEAD_SIZE)

    def attend_back(t):
        at = pl.ds(t * half, half)
        for h in range(GROUP):
            head = slice(h * HEAD_SIZE, (h + 1) * HEAD_SIZE)
            grads = gattn[at, head]
            turned_grads = grads.astype(F32).T
            share = shares[h, :, at]
            delta = jnp.sum(turned_grads * attn[h, :, at], axis=0, keepdims=True)
            low = probs[h, t]
            gprobs = dot(v_s[...], grads, NT)
            gscores = (low.astype(F32) * ((gprobs - delta) * share)).astype(BF16)
            dv_s[...] += dot(low, (turned_grads * share).T.astype(BF16))
            dk_s[...] += dot(gscores, q_s[h, at, :])
            back, terms = head_back(qraw[at, head], dot(kt_s[...], gscores).T, at, g_query)
            gp[at, head] = back.astype(BF16)
            hrow[:, q_terms] += terms

    attend_back(0)
    zr_second(*r_gu1)
    attend_back(1)
    rs_relay(2)
    zr_first(*r_gu2)

    def project_back(t):
        at = tile_rows(t)
        back, terms = head_back(kraw[at, :], dk_s[at, :], at, g_key)
        gp[at, QCOLS : QCOLS + HEAD_SIZE] = back.astype(BF16)
        hrow[:, k_terms] += terms
        gp[at, QCOLS + HEAD_SIZE :] = dv_s[at, :].astype(BF16)

    loop(0, tiles, project_back)

    def qkv_grad(n):
        per = MODEL_WIDTH // CTX
        there = n1[:, :, n_cols(n)].reshape(2 * half, WIDE)
        gwq[pl.ds(n * (WIDE // per), WIDE // per)] = (
            dot(there, gp[...], TN)
            .astype(BF16)
            .reshape(WIDE // per, 4, per // 4, PCOLS)
        )

    qkv_grad(0)
    qkv_grad(1)
    zr_start(r_q1, r_q2)
    def back_one_part(which, n):
        per = MODEL_WIDTH // CTX
        at = pl.ds(n * (WIDE // per), WIDE // per)
        rows_at = half_rows(which)
        return dot(gp[rows_at, :QCOLS], wq[0, at].reshape(WIDE, QCOLS), NT) + dot(
            gp[rows_at, QCOLS:], wq[1, at].reshape(WIDE, 2 * HEAD_SIZE), NT
        )

    rs_begin(3, back_one_part)
    zr_second(*r_gu2)
    zr_first(*r_o)
    rs_relay(3)
    zr_second(*r_o)
    zr_first(*r_q1)
    zr_first(*r_q2)
    sum_d = zr_finish(*r_d)
    for g in range(MODEL_WIDTH // 128):
        lines[line_rows(ends[2], g, MODEL_WIDTH // 128, sum_d.shape[0]), :] = sum_d[
            :, g * 128 : (g + 1) * 128
        ]
    first_half, second_half = pl.ds(0, CTX // 2), pl.ds(CTX // 2, CTX // 2)
    asg[first_half] = zr_finish(*r_gu1).astype(BF16)
    asg[second_half] = zr_finish(*r_gu2).astype(BF16)
    arg_[c] = asg[c]
    zr_second(*r_q1)
    back, terms = norm_back(x_own[...].astype(F32), rs_finish(3), gains[:, :MODEL_WIDTH])
    xgrad_ref[...] = (gresid_s[...] + back).astype(BF16)
    store_xgrad = pltpu.make_async_copy(xgrad_ref, xgrad_hbm.at[0], loc.at[5])
    store_xgrad.start()
    hrow[:, :MODEL_WIDTH] = terms
    hz[z] = hrow[...]
    loop(1, 4, lambda i: row_z(1, hrow, hz, i).start())
    zr_start(r_o, part=(2,))
    arg_at = lambda j: arg_.at[j]
    a2a_start(2, asg, arg_at)
    zr_second(*r_q2)
    out_ref[...] = (resid_s[...] + rs_finish(2)).astype(BF16)
    store_out = pltpu.make_async_copy(out_ref, out_hbm.at[0], loc.at[6])
    store_out.start()
    arq_at = lambda j: arq.at[j]
    asq[first_half] = zr_finish(*r_q1).astype(BF16)
    a2a_half(3, asq, arq_at, 0)
    asq[second_half] = zr_finish(*r_q2).astype(BF16)
    a2a_half(3, asq, arq_at, 1)
    arq[c] = asq[c]
    row_z_wait(1, hz)
    hpl[c] = jnp.sum(hz[...], axis=0)
    loop(1, CTX, lambda i: row_plane(1, hpl.at[c], hpl, i).start())
    a2a_wait(2, arg_)
    for j in range(CTX):
        for part in range(2 * HID // 128):
            lines[line_rows(ends[1], feed_group(j, part), feed_groups, per_run), :] = arg_[
                j, :, part * 128 : (part + 1) * 128
            ].astype(F32)
    a2a_wait(3, arq)
    for j in range(CTX):
        for part in range(PCOLS // 128):
            lines[line_rows(0, qkv_group(j, part), qkv_groups, per_run), :] = arq[
                j, :, part * 128 : (part + 1) * 128
            ].astype(F32)
    split = ends[0] // 128, ends[1] // 128
    stores = [
        pltpu.make_async_copy(
            lines.at[pl.ds(first, last - first)], lin_ref.at[pl.ds(first, last - first)], loc.at[k]
        )
        for k, (first, last) in enumerate(
            ((0, split[0]), (split[1], tail // 128), split, (tail // 128, tail // 128 + 8))
        )
    ]
    stores[0].start()
    stores[1].start()
    sum_o = zr_finish(*r_o)
    for g in range(MODEL_WIDTH // 128):
        lines[line_rows(ends[0], g, MODEL_WIDTH // 128, sum_o.shape[0]), :] = sum_o[
            :, g * 128 : (g + 1) * 128
        ]
    stores[2].start()
    row_plane_wait(1, hpl)
    total = jnp.sum(hpl[...], axis=0)
    lines[pl.ds(tail // 128, 1), :] = pltpu.roll(
        total, GAIN_WIDTH - spans[4] * (4 * c + z), 1
    )[:, :128]
    stores[3].start()

    for n, buf in ((1, cot), (2, n2), (3, gb)):
        ag_drain(n, buf)
    rs_drain(3)
    a2a_drain(0, wq_in.at[0])
    a2a_drain(4, wq_in.at[1])
    a2a_drain(1, wgu_in)
    a2a_drain(2, asg)
    a2a_drain(3, asq)
    first_four = pl.ds(0, CTX // 2)
    for n, some in (
        (0, lambda count: wq.at[0, :, pl.ds(0, count)]),
        (5, lambda count: wq.at[1, :, pl.ds(0, count)]),
        (1, lambda count: wo.at[pl.ds(0, count)]),
        (2, lambda count: wgu.at[first_four, pl.ds(0, count)]),
        (3, lambda count: wgu.at[first_four, pl.ds(0, count)]),
        (4, lambda count: wd.at[pl.ds(0, count)]),
    ):
        zg_drain(n, some)
    three = pl.ds(0, 3)
    for n, part in (
        (0, lwd.at[three]),
        (1, lwgu.at[three, first_four]),
        (2, lwgu.at[three, first_four]),
        (3, lwo.at[three]),
        (4, lwq.at[three, first_four]),
        (5, lwq.at[three, first_four]),
    ):
        rcopy(part, part, zr_s.at[n], zr_r.at[n, 0], sib, z).wait_send()
    for n, lands in enumerate(((gz, gpl), (hz, hpl))):
        for k, land in enumerate(lands):
            rows_of(n, land, k).wait_send()
    for copy in (store_out, store_xgrad, *stores):
        copy.wait()


def layer_call(tokens, cotangent, stretch_order, doc_lengths, master):
    _, rows, width = tokens.shape
    length = CTX * rows
    tiles = length // TILE
    per = width // CTX // 4
    entries = master.shape[0] // 1024 * 1024
    vm = pltpu.VMEM
    dma = pltpu.SemaphoreType.DMA
    shape = jax.ShapeDtypeStruct
    full = vm((CTX, rows, width), BF16)
    scratch = [
        pltpu.SMEM(stretch_order.shape, jnp.int32),
        pltpu.SMEM(doc_lengths.shape, jnp.int32),
        vm((rows, width), BF16),
        vm((rows, width), BF16),
        vm((width * 4 * width // 32 + 2 * width * width // 32,), F32),
        vm((FEED_WIDTH * width // 32,), F32),
        vm((master.shape[0] - entries,), F32),
        vm((entries // 128 + 8, 128), F32),
        vm((2, CTX, per, QCOLS), BF16),
        vm((CTX, per, 2 * HID), BF16),
        vm((1, GAIN_WIDTH), F32),
        vm((length, HEAD_SIZE), F32),
        vm((length, HEAD_SIZE), F32),
        vm((length, HEAD_SIZE), jnp.int32),
        vm((1, length), jnp.int32),
        vm((1, length), jnp.int32),
        full,
        full,
        full,
        full,
        vm((rows, width), BF16),
        vm((2, CTX, 4, per, QCOLS), BF16),
        vm((4, QCOLS // 4, width), BF16),
        vm((CTX, 4, per, 2 * HID), BF16),
        vm((4, HID // 4, width), BF16),
        vm((length, QCOLS), F32),
        vm((length, HEAD_SIZE), F32),
        vm((GROUP, length, HEAD_SIZE), BF16),
        vm((length, HEAD_SIZE), BF16),
        vm((length, HEAD_SIZE), BF16),
        vm((HEAD_SIZE, length), BF16),
        vm((HEAD_SIZE, length), BF16),
        vm((GROUP, 2, length, length // 2), BF16),
        vm((GROUP, HEAD_SIZE, length), F32),
        vm((GROUP, 1, length), F32),
        vm((length, QCOLS), BF16),
        vm((length, HID), BF16),
        vm((length, 2 * HID), BF16),
        vm((length, QCOLS), BF16),
        vm((length, HEAD_SIZE), F32),
        vm((length, HEAD_SIZE), F32),
        vm((length, PCOLS), BF16),
        vm((2, CHIPS, rows, width // 2), BF16),
        vm((2, 2, CHIPS, rows, width // 2), BF16),
        vm((6, rows, width // 2), BF16),
        vm((2, 6, rows, width // 2), BF16),
        vm((2, CHIPS, rows, width // 2), F32),
        vm((2, rows, width), F32),
        vm((rows, width), F32),
        vm((rows, width), F32),
        vm((CTX, 4, per, PCOLS), BF16),
        vm((4, QCOLS // 4, width), BF16),
        vm((CTX, 4, per, 2 * HID), BF16),
        vm((4, HID // 4, width), BF16),
        vm((5, CTX, per, PCOLS), BF16),
        vm((5, QCOLS // 4, width), BF16),
        vm((5, CTX, per, 2 * HID), BF16),
        vm((5, HID // 4, width), BF16),
        vm((CTX, per, PCOLS), BF16),
        vm((CTX, per, 2 * HID), BF16),
        vm((CTX, per, PCOLS), BF16),
        vm((CTX, per, 2 * HID), BF16),
        vm((4, 1, GAIN_WIDTH), F32),
        vm((CTX, 1, GAIN_WIDTH), F32),
        vm((1, GAIN_WIDTH), F32),
        vm((4, 1, GAIN_WIDTH), F32),
        vm((CTX, 1, GAIN_WIDTH), F32),
        vm((1, GAIN_WIDTH), F32),
        dma((4,)),
        dma((3, 8)),
        dma((2,)),
        dma((2, 2)),
        dma((6,)),
        dma((2, 6)),
        dma((5,)),
        dma((2 * CTX + 1,)),
        dma((6, 2)),
        dma((6, 4)),
        dma((6,)),
        dma((6, 5)),
        dma((2, 2)),
        dma((2, 2)),
        dma((8,)),
    ]
    anywhere = pl.BlockSpec(memory_space=pl.ANY)
    return pl.pallas_call(
        layer_kernel,
        out_shape=(
            shape((1, rows, width), BF16),
            shape((1, rows, width), BF16),
            shape((entries // 128 + 8, 128), F32),
        ),
        in_specs=[anywhere] * 5,
        out_specs=[anywhere] * 3,
        scratch_shapes=scratch,
        compiler_params=pltpu.CompilerParams(
            collective_id=1, has_side_effects=True, vmem_limit_bytes=63 << 20
        ),
        name="layer",
    )(stretch_order, doc_lengths, tokens, cotangent, master)


def local_planes(tokens, cotangent, stretch_order, doc_lengths, master, first_moment, second_moment):
    shards = lax.axis_size("ctx") * lax.axis_size("fsdp")
    length = tokens.shape[1] * lax.axis_size("ctx")
    out, xgrad, lines = layer_call(
        tokens, cotangent, stretch_order, doc_lengths, master
    )
    return adam_call(out, xgrad, lines, master, first_moment, second_moment, shards, length)


def adam_kernel(
    spans,
    settings,
    out_hbm,
    xgrad_hbm,
    grad_hbm,
    master_hbm,
    first_hbm,
    second_hbm,
    out_to,
    xgrad_to,
    master_to,
    first_to,
    second_to,
    out,
    xgrad,
    grad,
    master,
    first,
    second,
    sems,
):
    held = (grad, first, second, master, out, xgrad)
    fetch = [
        pltpu.make_async_copy(src, dst, sems.at[0, k])
        for k, (src, dst) in enumerate(
            zip((grad_hbm, first_hbm, second_hbm, master_hbm, out_hbm, xgrad_hbm), held)
        )
    ]
    store = [
        pltpu.make_async_copy(src, dst, sems.at[1, k])
        for k, (src, dst) in enumerate(
            zip(held[1:], (first_to, second_to, master_to, out_to, xgrad_to))
        )
    ]
    for copy in fetch:
        copy.start()

    def each(body):
        begin = 0
        for k, span in enumerate(spans[:-1]):
            block = span // -(-span // 65536)

            def step(i, carry, begin=begin, k=k, block=block):
                at = pl.ds(pl.multiple_of(begin + i * block, block), block)
                line = pl.ds(pl.multiple_of(begin // 128 + i * (block // 128), 8), block // 128)
                body(at, (block // 128, 128), grad[line, :], k)
                return carry

            lax.fori_loop(0, span // block, step, 0)
            begin += span
        last = spans[-1]
        body(pl.ds(begin, last), (1, last), grad[pl.ds(begin // 128, 1), :last], len(spans) - 1)

    def step_first(at, shape, g, k):
        new = BETA_ONE * first[at].reshape(shape) + (1.0 - BETA_ONE) * g
        first[at] = new.reshape(-1)

    def step_second(at, shape, g, k):
        new = BETA_TWO * second[at].reshape(shape) + (1.0 - BETA_TWO) * g * g
        second[at] = new.reshape(-1)

    def step_master(at, shape, g, k):
        rate, decay = settings[k]
        old = master[at].reshape(shape)
        mean = first[at].reshape(shape) * (1.0 / (1.0 - BETA_ONE**STEP))
        root = jnp.sqrt(second[at].reshape(shape) * (1.0 / (1.0 - BETA_TWO**STEP)))
        new = old - rate * (mean / (root + ADAM_EPS) + decay * old)
        master[at] = new.reshape(-1)

    fetch[0].wait()
    for k, body in enumerate((step_first, step_second, step_master)):
        fetch[k + 1].wait()
        each(body)
        store[k].start()
        if k == 1:
            for j in (4, 5):
                fetch[j].wait()
                store[j - 1].start()
    for copy in store:
        copy.wait()


def adam_call(out, xgrad, lines, master, first_moment, second_moment, shards, length):
    spans = [r // shards * w for r, w in segment_shapes()]
    shape = lambda v: jax.ShapeDtypeStruct(v.shape, v.dtype)
    operands = (out, xgrad, lines, master, first_moment, second_moment)
    results = (out, xgrad, master, first_moment, second_moment)
    anywhere = pl.BlockSpec(memory_space=pl.ANY)
    return pl.pallas_call(
        functools.partial(adam_kernel, spans, step_settings(length)),
        out_shape=[shape(v) for v in results],
        in_specs=[anywhere] * 6,
        out_specs=[anywhere] * 5,
        scratch_shapes=[pltpu.VMEM(v.shape, v.dtype) for v in operands]
        + [pltpu.SemaphoreType.DMA((2, 6))],
        compiler_params=pltpu.CompilerParams(vmem_limit_bytes=63 << 20),
        name="adam",
    )(*operands)


def step_settings(length):
    return [
        (MODEL_WIDTH ** (-0.5), DECAY_RATE),
        ((length / (3.0 * QUERY_HEADS * HEAD_SIZE)) ** 0.5, DECAY_RATE),
        (MODEL_WIDTH ** (-0.5), DECAY_RATE),
        (FEED_WIDTH ** (-0.5), DECAY_RATE),
        (0.2, 0.0),
    ]


def rates(shards, length):
    settings = step_settings(length)
    spans = [r // shards * w for r, w in segment_shapes()]
    index = lax.iota(jnp.int32, sum(spans))
    step_rate = jnp.full(index.shape, settings[0][0], F32)
    decay_value = jnp.full(index.shape, settings[0][1], F32)
    first = 0
    for span, (step, decay) in zip(spans, settings):
        step_rate = jnp.where(index >= first, step, step_rate)
        decay_value = jnp.where(index >= first, decay, decay_value)
        first += span
    return step_rate, decay_value


def adam(grad, master, first_moment, second_moment, shards, length):
    step_rate, decay_value = rates(shards, length)
    new_first = BETA_ONE * first_moment + (1.0 - BETA_ONE) * grad
    new_second = BETA_TWO * second_moment + (1.0 - BETA_TWO) * grad * grad
    normalized = (
        new_first
        / (1.0 - BETA_ONE**STEP)
        / (jnp.sqrt(new_second / (1.0 - BETA_TWO**STEP)) + ADAM_EPS)
    )
    new_master = master - step_rate * (normalized + decay_value * master)
    return new_master, new_first, new_second


def solution(mesh):
    placed = (
        P("fsdp", "ctx", None),
        P("fsdp", "ctx", None),
        P(),
        P("fsdp", None),
        P(("ctx", "fsdp")),
        P(("ctx", "fsdp")),
        P(("ctx", "fsdp")),
    )
    plane = mesh.shape["ctx"] == CTX == KEY_VALUE_HEADS and mesh.shape["fsdp"] == 4
    return jax.shard_map(
        local_planes if plane else local,
        mesh=mesh,
        in_specs=placed,
        out_specs=(
            P("fsdp", "ctx", None),
            P("fsdp", "ctx", None),
            P(("ctx", "fsdp")),
            P(("ctx", "fsdp")),
            P(("ctx", "fsdp")),
        ),
        check_vma=False,
    )
```

```python
import functools
import math

import jax
import jax.numpy as jnp
from jax import lax
from jax.experimental import pallas as pl
from jax.experimental.pallas import tpu as pltpu
from jax.sharding import PartitionSpec as P

MODEL_WIDTH = 1024
QUERY_HEADS = 16
KEY_VALUE_HEADS = 8
HEAD_SIZE = 128
FEED_WIDTH = 3072
STRETCH = 64
STEP = 7


NORM_EPS = 1e-06
ROPE_BASE = 1000000.0
BETA_ONE = 0.5
BETA_TWO = 0.5
DECAY_RATE = 0.1
ADAM_EPS = 1e-08
MASKED = -1e30


def from_behind(x, axis, by):
    peers = lax.axis_size(axis)
    return lax.ppermute(x, axis, [(i, (i + by) % peers) for i in range(peers)])


def segment_shapes():
    return [
        (MODEL_WIDTH, (QUERY_HEADS + 2 * KEY_VALUE_HEADS) * HEAD_SIZE),
        (QUERY_HEADS * HEAD_SIZE, MODEL_WIDTH),
        (MODEL_WIDTH, 2 * FEED_WIDTH),
        (FEED_WIDTH, MODEL_WIDTH),
        (2 * MODEL_WIDTH + 2 * HEAD_SIZE, 1),
    ]


def unpack(flat_params, count_of_shards):
    param_table = flat_params.reshape(count_of_shards, -1)
    pieces = []
    offset = 0
    for row_total, column_total in segment_shapes():
        shard_span = row_total // count_of_shards * column_total
        pieces.append(param_table[:, offset : offset + shard_span].reshape(row_total, column_total))
        offset += shard_span
    return pieces


def pack(matrices, count_of_shards):
    return jnp.concatenate(
        [matrix.reshape(count_of_shards, -1) for matrix in matrices], axis=1
    ).reshape(-1)


def slot_positions(stretch_order, first_row, count_of_rows):
    row_ids = first_row + jnp.arange(count_of_rows, dtype=jnp.int32)
    slot_ids = row_ids // STRETCH
    slot_table = jnp.arange(stretch_order.shape[0], dtype=jnp.int32)
    stretch_ids = jnp.sum(
        jnp.where(slot_ids[:, None] == slot_table[None, :], stretch_order[None, :], 0), axis=1
    )
    return stretch_ids * STRETCH + row_ids % STRETCH


def documents(positions, doc_lengths):
    doc_ends = jnp.cumsum(doc_lengths, axis=1)
    doc_starts = doc_ends - doc_lengths
    passed = positions[None, :, None] >= doc_ends[:, None, :-1]
    doc_ids = jnp.sum(passed.astype(jnp.int32), axis=2)
    doc_table = jnp.arange(doc_lengths.shape[1], dtype=jnp.int32)
    owner = doc_ids[:, :, None] == doc_table[None, None, :]
    start_of = jnp.sum(jnp.where(owner, doc_starts[:, None, :], 0), axis=2)
    return (doc_ids, positions[None, :] - start_of)


def key_mask(stretch_order, doc_lengths, query_pos, query_doc, first_row, count_of_rows):
    key_pos = slot_positions(stretch_order, first_row, count_of_rows)
    key_doc, _ = documents(key_pos, doc_lengths)
    same_doc = query_doc[:, :, None] == key_doc[:, None, :]
    return same_doc & (key_pos[None, None, :] <= query_pos[None, :, None])


def rope_tables(relative):
    half_dim = HEAD_SIZE // 2
    frequency = ROPE_BASE ** (-(jnp.arange(half_dim, dtype=jnp.float32) * 2.0 / HEAD_SIZE))
    angles = relative.astype(jnp.float32)[..., None] * frequency
    cosine_table = jnp.cos(angles)
    sine_values = jnp.sin(angles)
    return (
        jnp.concatenate([cosine_table, cosine_table], axis=-1),
        jnp.concatenate([sine_values, sine_values], axis=-1),
    )


def rotate(values, cosine_table, sine_values):
    half_dim = values.shape[-1] // 2
    turned = jnp.concatenate([-values[..., half_dim:], values[..., :half_dim]], axis=-1)
    return values * cosine_table[..., None, :] + turned * sine_values[..., None, :]


def rotate_back(grads, cosine_table, sine_values):
    half_dim = grads.shape[-1] // 2
    moved = grads * sine_values[..., None, :]
    unturned = jnp.concatenate([moved[..., half_dim:], -moved[..., :half_dim]], axis=-1)
    return grads * cosine_table[..., None, :] + unturned


def rms_norm(values, scaling):
    factor = lax.rsqrt(jnp.mean(values * values, axis=-1, keepdims=True) + NORM_EPS)
    return values * factor * scaling


def norm_back(values, grads, scaling):
    factor = lax.rsqrt(jnp.mean(values * values, axis=-1, keepdims=True) + NORM_EPS)
    unit_values = values * factor
    scaled_grads = grads * scaling
    inner = jnp.mean(scaled_grads * unit_values, axis=-1, keepdims=True)
    return (factor * (scaled_grads - unit_values * inner), grads * unit_values)


def attend_block(state, queries, key_value_block, allowed, score_scale):
    running, top_now, total_now = state
    sequence_count, count_of_keys = (key_value_block.shape[1], key_value_block.shape[2])
    block_keys = key_value_block[0].reshape(
        sequence_count, count_of_keys, KEY_VALUE_HEADS, HEAD_SIZE
    )
    block_values = key_value_block[1].reshape(
        sequence_count, count_of_keys, KEY_VALUE_HEADS, HEAD_SIZE
    )
    mask_wide = allowed[:, :, None, None, :]
    scores = (
        jnp.einsum("sqhgd,snhd->sqhgn", queries, block_keys, preferred_element_type=jnp.float32)
        * score_scale
    )
    new_top = jnp.maximum(top_now, jnp.max(jnp.where(mask_wide, scores, MASKED), axis=-1))
    weights = jnp.where(mask_wide, jnp.exp(scores - new_top[..., None]), 0.0)
    factor = jnp.exp(top_now - new_top)
    total_now = total_now * factor + jnp.sum(weights, axis=-1)
    running = running * factor[..., None] + jnp.einsum(
        "sqhgn,snhd->sqhgd",
        weights.astype(jnp.bfloat16),
        block_values,
        preferred_element_type=jnp.float32,
    )
    return (running, new_top, total_now)


def backward_block(
    queries, attention_gradient, log_total, delta, key_value_block, allowed, score_scale
):
    sequence_count, count_of_keys = (key_value_block.shape[1], key_value_block.shape[2])
    block_keys = key_value_block[0].reshape(
        sequence_count, count_of_keys, KEY_VALUE_HEADS, HEAD_SIZE
    )
    block_values = key_value_block[1].reshape(
        sequence_count, count_of_keys, KEY_VALUE_HEADS, HEAD_SIZE
    )
    mask_wide = allowed[:, :, None, None, :]
    scores = (
        jnp.einsum("sqhgd,snhd->sqhgn", queries, block_keys, preferred_element_type=jnp.float32)
        * score_scale
    )
    probabilities = jnp.where(mask_wide, jnp.exp(scores - log_total[..., None]), 0.0)
    value_gradient = jnp.einsum(
        "sqhgn,sqhgd->snhd",
        probabilities.astype(jnp.bfloat16),
        attention_gradient,
        preferred_element_type=jnp.float32,
    )
    grad_probs = jnp.einsum(
        "sqhgd,snhd->sqhgn", attention_gradient, block_values, preferred_element_type=jnp.float32
    )
    grad_scores = (probabilities * (grad_probs - delta[..., None])).astype(jnp.bfloat16)
    grad_queries = (
        jnp.einsum("sqhgn,snhd->sqhgd", grad_scores, block_keys, preferred_element_type=jnp.float32)
        * score_scale
    )
    key_gradient = (
        jnp.einsum("sqhgn,sqhgd->snhd", grad_scores, queries, preferred_element_type=jnp.float32)
        * score_scale
    )
    grad_pair = jnp.stack(
        [
            key_gradient.reshape(sequence_count, count_of_keys, KEY_VALUE_HEADS * HEAD_SIZE),
            value_gradient.reshape(sequence_count, count_of_keys, KEY_VALUE_HEADS * HEAD_SIZE),
        ]
    )
    return (grad_queries, grad_pair)


def summed(part, count_of_shards):
    return lax.psum_scatter(
        part.reshape(-1), ("ctx", "fsdp"), scatter_dimension=0, tiled=True
    )


def local(tokens, cotangent, stretch_order, doc_lengths, master, first_moment, second_moment):
    cycle_size = lax.axis_size("ctx")
    ctx_index = lax.axis_index("ctx")
    count_of_shards = cycle_size * lax.axis_size("fsdp")
    sequence_count, count_of_rows, _ = tokens.shape
    seq_length = count_of_rows * cycle_size
    query_groups = QUERY_HEADS // KEY_VALUE_HEADS
    score_scale = HEAD_SIZE ** (-0.5)
    gathered = lax.all_gather(master.astype(jnp.bfloat16), ("ctx", "fsdp"), axis=0, tiled=True)
    w_qkv, w_out, w_gate_up, w_down, gain_column = unpack(gathered, count_of_shards)
    gains = gain_column.reshape(-1).astype(jnp.float32)
    g_attn = gains[:MODEL_WIDTH]
    g_mlp = gains[MODEL_WIDTH : 2 * MODEL_WIDTH]
    g_query = gains[2 * MODEL_WIDTH : 2 * MODEL_WIDTH + HEAD_SIZE]
    g_key = gains[2 * MODEL_WIDTH + HEAD_SIZE :]
    query_pos = slot_positions(stretch_order, ctx_index * count_of_rows, count_of_rows)
    query_doc, relative = documents(query_pos, doc_lengths)
    cosine_table, sine_values = rope_tables(relative)
    x_in = tokens.astype(jnp.float32)
    normed_one = rms_norm(x_in, g_attn).astype(jnp.bfloat16)
    projected_output = jnp.einsum(
        "sqd,de->sqe", normed_one, w_qkv, preferred_element_type=jnp.float32
    )
    query_raw = projected_output[:, :, : QUERY_HEADS * HEAD_SIZE].reshape(
        sequence_count, count_of_rows, QUERY_HEADS, HEAD_SIZE
    )
    unrotated_keys = projected_output[
        :, :, QUERY_HEADS * HEAD_SIZE : (QUERY_HEADS + KEY_VALUE_HEADS) * HEAD_SIZE
    ].reshape(sequence_count, count_of_rows, KEY_VALUE_HEADS, HEAD_SIZE)
    unprojected_values = projected_output[:, :, (QUERY_HEADS + KEY_VALUE_HEADS) * HEAD_SIZE :]
    queries = (
        rotate(rms_norm(query_raw, g_query), cosine_table, sine_values)
        .astype(jnp.bfloat16)
        .reshape(sequence_count, count_of_rows, KEY_VALUE_HEADS, query_groups, HEAD_SIZE)
    )
    keys_rot = rotate(rms_norm(unrotated_keys, g_key), cosine_table, sine_values).reshape(
        sequence_count, count_of_rows, KEY_VALUE_HEADS * HEAD_SIZE
    )
    kv_local = jnp.stack([keys_rot, unprojected_values]).astype(jnp.bfloat16)
    statistic_shape = (sequence_count, count_of_rows, KEY_VALUE_HEADS, query_groups)
    initial = (
        jnp.zeros(statistic_shape + (HEAD_SIZE,), jnp.float32),
        jnp.full(statistic_shape, MASKED, jnp.float32),
        jnp.zeros(statistic_shape, jnp.float32),
    )
    state = initial
    piece = lax.all_gather(kv_local, "ctx", axis=2, tiled=True)
    key_total = piece.shape[2]

    def key_step(inner, block_index):
        first_row = block_index * count_of_rows
        key_value_block = lax.dynamic_slice_in_dim(piece, first_row, count_of_rows, 2)
        allowed = key_mask(
            stretch_order, doc_lengths, query_pos, query_doc, first_row, count_of_rows
        )
        return (attend_block(inner, queries, key_value_block, allowed, score_scale), None)

    state, _ = lax.scan(key_step, state, jnp.arange(key_total // count_of_rows, dtype=jnp.int32))
    running, top_now, total_now = state
    attn = running / total_now[..., None]
    log_total = top_now + jnp.log(total_now)
    attn_low = attn.reshape(sequence_count, count_of_rows, QUERY_HEADS * HEAD_SIZE).astype(
        jnp.bfloat16
    )
    resid = x_in + jnp.einsum("sqa,ad->sqd", attn_low, w_out, preferred_element_type=jnp.float32)
    normed_two = rms_norm(resid, g_mlp).astype(jnp.bfloat16)
    gate_up = jnp.einsum("sqd,de->sqe", normed_two, w_gate_up, preferred_element_type=jnp.float32)
    gate = gate_up[:, :, :FEED_WIDTH]
    up_part = gate_up[:, :, FEED_WIDTH:]
    sigmoid_gate = jax.nn.sigmoid(gate)
    hidden = (gate * sigmoid_gate * up_part).astype(jnp.bfloat16)
    mlp_out = jnp.einsum("sqf,fd->sqd", hidden, w_down, preferred_element_type=jnp.float32)
    layer_out = (resid + mlp_out).astype(jnp.bfloat16)
    grad_w_down = jnp.einsum("sqf,sqd->fd", hidden, cotangent, preferred_element_type=jnp.float32)
    grad_hidden = jnp.einsum("sqd,fd->sqf", cotangent, w_down, preferred_element_type=jnp.float32)
    grad_gate = grad_hidden * up_part * sigmoid_gate * (1.0 + gate * (1.0 - sigmoid_gate))
    grad_up = grad_hidden * gate * sigmoid_gate
    grad_gate_up = jnp.concatenate([grad_gate, grad_up], axis=-1).astype(jnp.bfloat16)
    grad_w_gate_up = jnp.einsum(
        "sqd,sqe->de", normed_two, grad_gate_up, preferred_element_type=jnp.float32
    )
    grad_normed_two = jnp.einsum(
        "sqe,de->sqd", grad_gate_up, w_gate_up, preferred_element_type=jnp.float32
    )
    back_two, mlp_gain_terms = norm_back(resid, grad_normed_two, g_mlp)
    grad_resid = cotangent.astype(jnp.float32) + back_two
    grad_branch = grad_resid.astype(jnp.bfloat16)
    grad_w_out = jnp.einsum(
        "sqa,sqd->ad", attn_low, grad_branch, preferred_element_type=jnp.float32
    )
    attention_gradient = jnp.einsum(
        "sqd,ad->sqa", grad_branch, w_out, preferred_element_type=jnp.float32
    ).astype(jnp.bfloat16)
    attention_head_gradient = attention_gradient.reshape(
        sequence_count, count_of_rows, KEY_VALUE_HEADS, query_groups, HEAD_SIZE
    )
    delta = jnp.sum(attention_head_gradient.astype(jnp.float32) * attn, axis=-1)

    def grads_from(turn_index, kv_now, key_value_gradients, grad_queries):
        source_dev = (ctx_index - turn_index) % cycle_size
        allowed = key_mask(
            stretch_order,
            doc_lengths,
            query_pos,
            query_doc,
            source_dev * count_of_rows,
            count_of_rows,
        )
        part_queries, part_pair = backward_block(
            queries, attention_head_gradient, log_total, delta, kv_now, allowed, score_scale
        )
        return (key_value_gradients + part_pair, grad_queries + part_queries)

    def pass_grads(key_value_gradients):
        return from_behind(key_value_gradients.astype(jnp.bfloat16), "ctx", 1).astype(
            key_value_gradients.dtype
        )

    def turn_step(turn_index, state):
        kv_now, key_value_gradients, grad_queries = state
        key_value_gradients, grad_queries = grads_from(
            turn_index, kv_now, key_value_gradients, grad_queries
        )
        kv_now = from_behind(kv_now, "ctx", 1)
        key_value_gradients = pass_grads(key_value_gradients)
        return (kv_now, key_value_gradients, grad_queries)

    start_state = (
        kv_local,
        jnp.zeros(kv_local.shape, jnp.float32),
        jnp.zeros(statistic_shape + (HEAD_SIZE,), jnp.float32),
    )
    kv_now, key_value_gradients, grad_queries = lax.fori_loop(
        0, cycle_size - 1, turn_step, start_state
    )
    key_value_gradients, grad_queries = grads_from(
        cycle_size - 1, kv_now, key_value_gradients, grad_queries
    )
    key_value_gradients = pass_grads(key_value_gradients)
    grad_query_rot = rotate_back(
        grad_queries.reshape(sequence_count, count_of_rows, QUERY_HEADS, HEAD_SIZE),
        cosine_table,
        sine_values,
    )
    grad_key_rot = rotate_back(
        key_value_gradients[0].reshape(sequence_count, count_of_rows, KEY_VALUE_HEADS, HEAD_SIZE),
        cosine_table,
        sine_values,
    )
    grad_query_raw, query_gain_terms = norm_back(query_raw, grad_query_rot, g_query)
    unrotated_key_gradient, key_gain_terms = norm_back(unrotated_keys, grad_key_rot, g_key)
    grad_projected = jnp.concatenate(
        [
            grad_query_raw.reshape(sequence_count, count_of_rows, QUERY_HEADS * HEAD_SIZE),
            unrotated_key_gradient.reshape(
                sequence_count, count_of_rows, KEY_VALUE_HEADS * HEAD_SIZE
            ),
            key_value_gradients[1],
        ],
        axis=-1,
    ).astype(jnp.bfloat16)
    grad_w_qkv = jnp.einsum(
        "sqd,sqe->de", normed_one, grad_projected, preferred_element_type=jnp.float32
    )
    grad_normed_one = jnp.einsum(
        "sqe,de->sqd", grad_projected, w_qkv, preferred_element_type=jnp.float32
    )
    back_one, attn_gain_terms = norm_back(x_in, grad_normed_one, g_attn)
    input_grad = (grad_resid + back_one).astype(jnp.bfloat16)
    grad_gains = jnp.concatenate(
        [
            jnp.sum(attn_gain_terms, axis=(0, 1)),
            jnp.sum(mlp_gain_terms, axis=(0, 1)),
            jnp.sum(query_gain_terms, axis=(0, 1, 2)),
            jnp.sum(key_gain_terms, axis=(0, 1, 2)),
        ]
    ).reshape(-1, 1)
    grad = jnp.concatenate(
        [
            summed(part, count_of_shards)
            for part in (grad_w_qkv, grad_w_out, grad_w_gate_up, grad_w_down, grad_gains)
        ]
    )
    new_master, new_first, new_second = adam(
        grad, master, first_moment, second_moment, count_of_shards, seq_length
    )
    return (layer_out, input_grad, new_master, new_first, new_second)


MESH = pl.DeviceIdType.MESH
F32 = jnp.float32
BF16 = jnp.bfloat16
CTX = 8
CHIPS = 4
GROUP = QUERY_HEADS // KEY_VALUE_HEADS
QCOLS = GROUP * HEAD_SIZE
PCOLS = QCOLS + 2 * HEAD_SIZE
HID = FEED_WIDTH // CTX
GAIN_WIDTH = 2 * MODEL_WIDTH + 2 * HEAD_SIZE
TILE = 256
WIDE = 512


def dot(a, b, dims=((1,), (0,))):
    return lax.dot_general(a, b, (dims, ((), ())), preferred_element_type=F32)


NT = ((1,), (1,))
TN = ((0,), (0,))


def layer_kernel(
    order_hbm,
    doc_hbm,
    x_hbm,
    cot_hbm,
    master_hbm,
    out_hbm,
    xgrad_hbm,
    lin_ref,
    order_ref,
    doc_ref,
    out_ref,
    xgrad_ref,
    flat,
    flat_down,
    flat_gains,
    lines,
    wq_in,
    wgu_in,
    gains_in,
    cos_ref,
    sin_ref,
    kpos_ref,
    qpos_ref,
    qstart_ref,
    xg,
    n1,
    cot,
    n2,
    x_own,
    wq,
    wo,
    wgu,
    wd,
    qraw,
    kraw,
    q_s,
    k_s,
    v_s,
    kt_s,
    vt_s,
    probs,
    attn,
    shares,
    attn_low,
    hidden,
    ggu,
    gattn,
    dk_s,
    dv_s,
    gp,
    psnd,
    prcv,
    csnd,
    crcv,
    own,
    acc,
    resid_s,
    gresid_s,
    gwq,
    gwo,
    gwgu,
    gwd,
    lwq,
    lwo,
    lwgu,
    lwd,
    asq,
    asg,
    arq,
    arg_,
    gz,
    gpl,
    gains,
    hz,
    hpl,
    hrow,
    ag_s,
    ag_r,
    rs_ps,
    rs_pr,
    rs_cs,
    rs_cr,
    a2a_s,
    a2a_r,
    zg_s,
    zg_r,
    zr_s,
    zr_r,
    g_s,
    g_r,
    loc,
):
    c = lax.axis_index("ctx")
    z = lax.axis_index("fsdp")
    core = c % 2
    chip = c // 2
    cx = chip % 2
    cy = chip // 2
    slot = core * CHIPS + chip
    sib = c + 1 - 2 * core
    tiles = n1.shape[0] * n1.shape[1] // TILE
    rows = n1.shape[1]
    half = CHIPS * rows

    def chip_at(i):
        return ((cy + i // 2) % 2) * 2 + (cx + i % 2) % 2

    def rcopy(src, dst, ssem, rsem, to_c, to_z):
        return pltpu.make_async_remote_copy(
            src_ref=src,
            dst_ref=dst,
            send_sem=ssem,
            recv_sem=rsem,
            device_id=(to_c, to_z),
            device_id_type=MESH,
        )

    def loop(lo, hi, body):
        def step(i, carry):
            body(i)
            return carry

        lax.fori_loop(lo, hi, step, 0)

    spans = [r // (4 * CTX) * w for r, w in segment_shapes()]
    ends = [sum(spans[: i + 1]) for i in range(5)]
    tail = ends[3]
    fetch = [
        pltpu.make_async_copy(master_hbm.at[pl.ds(0, ends[1])], flat, loc.at[0]),
        pltpu.make_async_copy(master_hbm.at[pl.ds(tail, spans[4])], flat_gains, loc.at[3]),
        pltpu.make_async_copy(master_hbm.at[pl.ds(ends[2], spans[3])], flat_down, loc.at[4]),
        pltpu.make_async_copy(x_hbm.at[0], xg.at[slot], loc.at[1]),
        pltpu.make_async_copy(cot_hbm.at[0], cot.at[slot], loc.at[2]),
        pltpu.make_async_copy(order_hbm, order_ref, loc.at[5]),
        pltpu.make_async_copy(doc_hbm, doc_ref, loc.at[6]),
    ]
    for copy in fetch:
        copy.start()
    fetch_feed = pltpu.make_async_copy(
        master_hbm.at[pl.ds(ends[1], spans[2])], flat, loc.at[0]
    )
    barrier = pltpu.get_barrier_semaphore()

    def greet_plane(i):
        pl.semaphore_signal(
            barrier, inc=1, device_id=((c + i) % CTX, z), device_id_type=MESH
        )

    def greet_z(i):
        pl.semaphore_signal(
            barrier, inc=1, device_id=(c, (z + i) % 4), device_id_type=MESH
        )

    loop(1, CTX, greet_plane)
    loop(1, 4, greet_z)

    def to_lines(src, first, last):
        block = 128 * 128

        def one(i):
            lines[pl.ds(pl.multiple_of(first // 128 + i * 128, 128), 128), :] = src[
                pl.ds(pl.multiple_of(i * block, block), block)
            ].reshape(128, 128)

        loop(0, (last - first) // block, one)

    def qkv_group(j, part):
        return (GROUP * j + part) if part < GROUP else KEY_VALUE_HEADS * part + j

    def feed_group(j, part):
        per = HID // 128
        return j * per + part if part < per else CTX * per + j * per + part - per

    def line_rows(first, group, groups, count):
        return pl.ds(first // 128 + group, count, stride=groups)

    per_run = wq_in.shape[2]
    fetch[0].wait()
    fetch[1].wait()
    to_lines(flat, 0, ends[1])
    fetch_feed.start()
    for g in range(MODEL_WIDTH // 128):
        wo[z, :, g * 128 : (g + 1) * 128] = lines[
            line_rows(ends[0], g, MODEL_WIDTH // 128, wo.shape[1]), :
        ].astype(BF16)
    qkv_groups = CTX * PCOLS // 128
    for j in range(CTX):
        for part in range(PCOLS // 128):
            wq_in[part // 2, j, :, part % 2 * 128 : (part % 2 + 1) * 128] = lines[
                line_rows(0, qkv_group(j, part), qkv_groups, per_run), :
            ].astype(BF16)
    own_gains = flat_gains[...].reshape(1, spans[4]).astype(BF16).astype(F32)
    gains_in[...] = pltpu.roll(
        jnp.concatenate([own_gains, jnp.zeros((1, GAIN_WIDTH - spans[4]), F32)], axis=1),
        spans[4] * (4 * c + z),
        1,
    )

    fetch[2].wait()
    to_lines(flat_down, ends[2], ends[3])
    for g in range(MODEL_WIDTH // 128):
        wd[z, :, g * 128 : (g + 1) * 128] = lines[
            line_rows(ends[2], g, MODEL_WIDTH // 128, wd.shape[1]), :
        ].astype(BF16)
    pl.semaphore_wait(barrier, CTX - 1 + 4 - 1)

    mid = rows // 2
    XN, YN, ACROSS = 1, 2, 3
    whole, top, bottom = pl.ds(0, rows), pl.ds(0, mid), pl.ds(mid, mid)

    AG_SEM = (0, 1, 2, 3, 4, 5, 6, 0, 7, 7, 7)

    def ag_piece(n, buf, k):
        origin, part, to = (
            (0, whole, sib),
            (0, top, XN),
            (0, bottom, XN),
            (0, bottom, YN),
            (0, top, YN),
            (XN, top, YN),
            (YN, bottom, XN),
            (XN, whole, sib),
            (YN, whole, sib),
            (ACROSS, top, sib),
            (ACROSS, bottom, sib),
        )[k]
        there = buf.at[core * CHIPS + chip_at(origin), part]
        target = sib if to is sib else chip_at(to) * 2 + core
        return rcopy(there, there, ag_s.at[n], ag_r.at[n % 3, AG_SEM[k]], target, z)

    def ag_landed(n, buf, k):
        origin, part, own_core = (
            (0, whole, False),
            (XN, top, True),
            (XN, bottom, True),
            (YN, bottom, True),
            (YN, top, True),
            (ACROSS, top, True),
            (ACROSS, bottom, True),
            (XN, whole, False),
            (YN, whole, False),
            (ACROSS, top, False),
            (ACROSS, bottom, False),
        )[k]
        which = core if own_core else 1 - core
        there = buf.at[which * CHIPS + chip_at(origin), part]
        return rcopy(there, there, ag_s.at[n], ag_r.at[n % 3, AG_SEM[k]], sib, z)

    def ag_start(n, buf):
        for k in (1, 3, 2, 4, 0):
            ag_piece(n, buf, k).start()

    def ag_pass_near(n, buf):
        for landed, onward in ((1, 5), (3, 6), (2, 7), (4, 8)):
            ag_landed(n, buf, landed).wait_recv()
            ag_piece(n, buf, onward).start()

    def ag_pass_across(n, buf):
        for landed, onward in ((5, 9), (6, 10)):
            ag_landed(n, buf, landed).wait_recv()
            ag_piece(n, buf, onward).start()

    def ag_handed(n, buf, sem):
        two_rows = buf.at[pl.ds(0, 2)]
        rcopy(two_rows, two_rows, ag_s.at[n], ag_r.at[n % 3, sem], sib, z).wait_recv()

    def ag_finish_near(n, buf):
        ag_handed(n, buf, 0)

    def ag_finish(n, buf):
        ag_handed(n, buf, 7)

    def ag_drain(n, buf):
        seven = buf.at[pl.ds(0, 7)]
        rcopy(seven, seven, ag_s.at[n], ag_r.at[0, 0], sib, z).wait_send()

    def gathered_tiles(n, buf, body, between, before=None):
        ag_pass_near(n, buf)
        ag_finish_near(n, buf)
        if before is not None:
            before()
        loop(0, 2, lambda k: body(2 * k + cy))
        between()
        ag_pass_across(n, buf)
        ag_finish(n, buf)
        loop(0, 2, lambda k: body(2 * k + 1 - cy))

    wide = MODEL_WIDTH // 2

    def rs_pair(r, h):
        return rcopy(psnd.at[h], prcv.at[r % 2, h], rs_ps.at[h], rs_pr.at[r % 2, h], sib, z)

    def rs_chip(r, k):
        to = chip_at((XN, XN, YN, YN, YN, XN)[k]) * 2 + core
        return rcopy(csnd.at[k], crcv.at[r % 2, k], rs_cs.at[k], rs_cr.at[r % 2, k], to, z)

    def rs_give(r, part, h):
        if r > 0:
            rs_pair(r - 1, h).wait_send()
        psnd[h] = part(1 - core, h).astype(BF16).reshape(CHIPS, rows, wide)
        rs_pair(r, h).start()

    def rs_keep(r, part, h):
        own[h] = part(core, h).reshape(CHIPS, rows, wide)

    def pair_sum(r, h, i):
        return own[h, chip_at(i)] + prcv[r % 2, h, chip_at(i)].astype(F32)

    def rs_send(r, h):
        rs_pair(r, h).wait_recv()
        if r > 0 and h == 0:
            for k in range(6):
                rs_chip(r - 1, k).wait_send()
        csnd[2 * h] = pair_sum(r, h, ACROSS).astype(BF16)
        rs_chip(r, 2 * h).start()
        csnd[2 * h + 1] = pair_sum(r, h, (XN, YN)[h]).astype(BF16)
        rs_chip(r, 2 * h + 1).start()
        acc[r % 2, :, h * wide : (h + 1) * wide] = pair_sum(r, h, 0)

    def rs_begin(r, part):
        for h in range(2):
            rs_give(r, part, h)
        for h in range(2):
            rs_keep(r, part, h)
            rs_send(r, h)

    def rs_compute(r, part):
        for h in range(2):
            rs_give(r, part, h)
        for h in range(2):
            rs_keep(r, part, h)

    def rs_drain(r):
        for h in range(2):
            rs_pair(r, h).wait_send()
        for k in range(6):
            rs_chip(r, k).wait_send()

    def rs_relay(r):
        for h, second in ((0, YN), (1, XN)):
            rs_chip(r, 2 * h).wait_recv()
            csnd[4 + h] = (pair_sum(r, h, second) + crcv[r % 2, 2 * h].astype(F32)).astype(BF16)
            rs_chip(r, 4 + h).start()

    def rs_finish(r):
        halves = []
        for h in range(2):
            rs_chip(r, 2 * h + 1).wait_recv()
            rs_chip(r, 4 + h).wait_recv()
            halves.append(
                acc[r % 2, :, h * wide : (h + 1) * wide]
                + crcv[r % 2, 2 * h + 1].astype(F32)
                + crcv[r % 2, 4 + h].astype(F32)
            )
        return jnp.concatenate(halves, axis=1)

    A2A_SEM = (0, 2 * CTX - 2, 2 * CTX - 1, 2 * CTX, CTX - 1)

    def a2a(n, src, dst_of, i, sem=0):
        to = (c + i) % CTX
        return rcopy(src.at[to], dst_of(c), a2a_s.at[n], a2a_r.at[A2A_SEM[n] + sem], to, z)

    def a2a_landed(n, dst_of, i):
        frm = (c + CTX - i) % CTX
        return rcopy(dst_of(frm), dst_of(frm), a2a_s.at[n], a2a_r.at[A2A_SEM[n] + i - 1], sib, z)

    def a2a_start(n, src, dst_of, apart=False):
        loop(1, CTX, lambda i: a2a(n, src, dst_of, i, i - 1 if apart else 0).start())

    def a2a_half(n, src, dst_of, h):
        def one(i):
            pl.when((c + i) % CTX // (CTX // 2) == h)(a2a(n, src, dst_of, i).start)

        loop(1, CTX, one)

    def a2a_wait(n, dst):
        seven = dst.at[pl.ds(0, CTX - 1)]
        rcopy(seven, seven, a2a_s.at[n], a2a_r.at[A2A_SEM[n]], sib, z).wait_recv()

    def a2a_drain(n, src):
        seven = src.at[pl.ds(0, CTX - 1)]
        rcopy(seven, seven, a2a_s.at[n], a2a_r.at[A2A_SEM[n]], sib, z).wait_send()

    inner = (z == 1) | (z == 2)
    outer = jnp.logical_not(inner)
    far = 3 * (2 - z)

    def zg(n, of, j, to, sem):
        return rcopy(of(j), of(j), zg_s.at[n, sem], zg_r.at[n, j], c, to)

    def zg_own(n, of):
        return (
            (z < 3, zg(n, of, z, z + 1, 0)),
            (z > 0, zg(n, of, z, z - 1, 0)),
        )

    def zg_onward(n, of):
        return (
            zg(n, of, z - 1, z + 1, 1),
            zg(n, of, z + 1, z - 1, 1),
            zg(n, of, far, 3 * (z - 1), 1),
        )

    def zg_start(n, of, who=None):
        for there, copy in zg_own(n, of):
            pl.when(there if who is None else there & who)(copy.start)

    def zg_pass(n, of, k, when, j):
        def run():
            zg(n, of, j, z, 0).wait_recv()
            zg_onward(n, of)[k].start()

        pl.when(when)(run)

    def zg_across(n, of):
        zg_pass(n, of, 0, z == 1, z - 1)
        zg_pass(n, of, 1, z == 2, z + 1)

    def zg_back(n, of):
        zg_pass(n, of, 1, z == 1, z + 1)
        zg_pass(n, of, 0, z == 2, z - 1)

    def zg_near(n, of):
        zg_across(n, of)
        zg_back(n, of)

    def zg_far(n, of):
        def run():
            zg(n, of, far, z, 0).wait_recv()
            zg_onward(n, of)[2].start()

        pl.when(inner)(run)

    def zg_wait(n, of):
        def run():
            for i in (1, 2, 3):
                zg(n, of, (z + i) % 4, z, 0).wait_recv()

        pl.when(outer)(run)

    def zg_drain(n, some):
        def sent(count, sem):
            part = some(count)
            rcopy(part, part, zg_s.at[n, sem], zg_r.at[n, 0], c, c).wait_send()

        def run():
            sent(2, 0)
            sent(3, 1)

        pl.when(inner)(run)
        pl.when(outer)(lambda: sent(1, 0))

    def zr(n, of, land, d, to, spot):
        return rcopy(of(d), land(spot), zr_s.at[n], zr_r.at[n, spot], c, to)

    def zr_add(n, of, land, d):
        rcopy(land(d), land(d), zr_s.at[n], zr_r.at[n, d], sib, z).wait_recv()
        mine = of(d)
        mine[...] = (mine[...].astype(F32) + land(d)[...].astype(F32)).astype(BF16)

    ENDS = (
        ((0, 3, 1, 3), (3, 0, 2, 0)),
        ((0, 2, 1, 2), (3, 1, 2, 1)),
        ((0, 1, 1, 1), (3, 2, 2, 4)),
    )
    FIRST = ((1, 3, 2, 3), (2, 0, 1, 0))
    SECOND = ((1, 2, 2, 2), (2, 1, 1, 4), (1, 0, 0, 4), (2, 3, 3, 3))

    def zr_send(n, of, land, k):
        for device, d, to, spot in ENDS[k]:
            pl.when(z == device)(zr(n, of, land, d, to, spot).start)

    def zr_start(*items, part=range(3)):
        for k in part:
            for item in items:
                zr_send(*item, k)

    def zr_pass(n, of, land, steps):
        for device, d, to, spot in steps:

            def run(d=d, to=to, spot=spot):
                zr_add(n, of, land, d)
                zr(n, of, land, d, to, spot).start()

            pl.when(z == device)(run)

    def zr_first(n, of, land):
        zr_pass(n, of, land, FIRST)

    def zr_second(n, of, land):
        zr_pass(n, of, land, SECOND)

    def zr_finish(n, of, land):
        def landed(spot):
            rcopy(land(spot), land(spot), zr_s.at[n], zr_r.at[n, spot], sib, z).wait_recv()

        pl.when(z > 0)(lambda: landed(z))
        pl.when(z < 3)(lambda: landed(4))
        return of(z)[...].astype(F32) + land(z)[...].astype(F32) + land(4)[...].astype(F32)

    def row_z(n, src, land, i):
        return rcopy(src, land.at[z], g_s.at[n, 0], g_r.at[n, 0], c, (z + i) % 4)

    def row_plane(n, src, land, i):
        return rcopy(src, land.at[c], g_s.at[n, 1], g_r.at[n, 1], (c + i) % CTX, z)

    def rows_of(n, land, k):
        others = land.at[pl.ds(0, (3, CTX - 1)[k])]
        return rcopy(others, others, g_s.at[n, k], g_r.at[n, k], sib, z)

    def row_z_wait(n, land):
        rows_of(n, land, 0).wait_recv()

    def row_plane_wait(n, land):
        rows_of(n, land, 1).wait_recv()

    def halves(ref):
        half_of = lambda h: lambda j: ref.at[pl.ds(h * (CTX // 2), CTX // 2), j]
        return half_of(0), half_of(1)

    def land_halves(ref):
        half_of = lambda h: lambda j: ref.at[j, pl.ds(h * (CTX // 2), CTX // 2)]
        return half_of(0), half_of(1)

    wq_at = lambda j: wq.at[0, j, z]
    wkv_at = lambda j: wq.at[1, j, z]
    wgu_at = lambda j: wgu.at[j, z]
    g_q = (0, lambda j: wq.at[0, :, j])
    g_kv = (5, lambda j: wq.at[1, :, j])
    g_o = (1, lambda j: wo.at[j])
    g_gu1, g_gu2 = ((2 + h, of) for h, of in enumerate(halves(wgu)))
    g_d = (4, lambda j: wd.at[j])
    def column_half(ref, h):
        return lambda j: ref.at[j, :, pl.ds(h * WIDE, WIDE)]

    r_d1, r_d2 = (
        (6 * h, column_half(gwd, h), column_half(lwd, h)) for h in range(2)
    )
    r_gu1, r_gu2 = (
        (1 + h, *both) for h, both in enumerate(zip(halves(gwgu), land_halves(lwgu)))
    )
    r_o = (3, lambda j: gwo.at[j], lambda j: lwo.at[j])
    r_q1, r_q2 = (
        (4 + h, *both) for h, both in enumerate(zip(halves(gwq), land_halves(lwq)))
    )

    lines[pl.ds(tail // 128, 8), :] = jnp.zeros((8, 128), F32)
    gz[z] = gains_in[...]
    loop(1, 4, lambda i: row_z(0, gains_in, gz, i).start())
    a2a_start(0, wq_in.at[0], wq_at, apart=True)
    a2a_start(4, wq_in.at[1], wkv_at, apart=True)
    zg_start(*g_o)

    def share(part, frm):
        there = wq.at[part, frm, z]
        n = 5 * part
        for to, here in ((z + 1, z < 3), (z - 1, z > 0)):
            pl.when(here)(rcopy(there, there, zg_s.at[n, 0], zg_r.at[n, z], c, to).start)

    def shares_landed(part, n, at):
        def one(i):
            a2a_landed(n, at, i).wait_recv()
            share(part, (c + CTX - i) % CTX)

        loop(1, CTX, one)

    for part in range(2):
        wq[part, c, z] = wq_in[part, c]
        share(part, c)
    fetch_feed.wait()
    to_lines(flat, ends[1], ends[2])
    feed_groups = 2 * FEED_WIDTH // 128
    for j in range(CTX):
        for part in range(2 * HID // 128):
            wgu_in[j, :, part * 128 : (part + 1) * 128] = lines[
                line_rows(ends[1], feed_group(j, part), feed_groups, per_run), :
            ].astype(BF16)
    fetch[3].wait()
    ag_start(0, xg)
    shares_landed(0, 0, wq_at)
    shares_landed(1, 4, wkv_at)
    row_z_wait(0, gz)
    gpl[c] = jnp.sum(gz[...], axis=0)
    loop(1, CTX, lambda i: row_plane(0, gpl.at[c], gpl, i).start())
    wgu[c, z] = wgu_in[c]
    for copy in fetch[4:]:
        copy.wait()
    doc_ends = [doc_ref[0, 0]]
    for j in range(1, doc_ref.shape[1] - 1):
        doc_ends.append(doc_ends[-1] + doc_ref[0, j])

    def doc_start(pos):
        start = jnp.zeros_like(pos)
        for end in doc_ends:
            start = jnp.where(pos >= end, end, start)
        return start

    def tables(s):
        first = 2 * (2 * (s % CHIPS) + s // CHIPS)
        lead = order_ref[first] * STRETCH
        trail = order_ref[first + 1] * STRETCH - STRETCH
        at = pl.ds(pl.multiple_of(s * rows, rows), rows)

        def positions(shape, axis):
            index = lax.broadcasted_iota(jnp.int32, shape, axis)
            return index + jnp.where(index < STRETCH, lead, trail)

        across = positions((1, rows), 1)
        qpos_ref[:, at] = across
        qstart_ref[:, at] = doc_start(across)
        down = positions((rows, HEAD_SIZE), 0)
        kpos_ref[at, :] = down
        lane = lax.broadcasted_iota(jnp.int32, (1, HEAD_SIZE), 1)
        upper = lane >= HEAD_SIZE // 2
        index = jnp.where(upper, lane - HEAD_SIZE // 2, lane).astype(F32)
        frequency = jnp.exp(index * (-2.0 / HEAD_SIZE * math.log(ROPE_BASE)))
        angles = (down - doc_start(down)).astype(F32) * frequency
        sine = jnp.sin(angles)
        cos_ref[at, :] = jnp.cos(angles)
        sin_ref[at, :] = jnp.where(upper, sine, -sine)

    loop(0, CTX // 2, tables)
    for land in (lwq, lwo, lwgu, lwd):
        for end, spot in ((0, 0), (3, 4)):

            def blank(land=land, spot=spot):
                land[spot] = jnp.zeros(land.shape[1:], BF16)

            pl.when(z == end)(blank)
    zg_near(*g_q)
    loop(CTX // 2, CTX, tables)
    ag_pass_near(0, xg)
    zg_near(*g_kv)
    ag_finish_near(0, xg)
    ag_pass_across(0, xg)
    zg_far(*g_q)
    ag_finish(0, xg)
    a2a_start(1, wgu_in, wgu_at)
    ag_start(1, cot)
    zg_far(*g_kv)
    zg_near(*g_o)
    row_plane_wait(0, gpl)
    gains[...] = jnp.sum(gpl[...], axis=0)
    g_attn = gains[:, :MODEL_WIDTH]
    def normed(t):
        at = pl.ds(t * (TILE // rows), TILE // rows)
        x_tile = xg[at].astype(F32)
        x_scale = lax.rsqrt(jnp.mean(x_tile * x_tile, axis=-1, keepdims=True) + NORM_EPS)
        n1[at] = (x_tile * x_scale * g_attn.reshape(1, 1, MODEL_WIDTH)).astype(BF16)

    loop(0, tiles, normed)
    x_own[...] = xg[slot]
    g_query = gains[:, 2 * MODEL_WIDTH : 2 * MODEL_WIDTH + HEAD_SIZE]
    g_key = gains[:, 2 * MODEL_WIDTH + HEAD_SIZE :]

    def tile_rows(t):
        return pl.ds(pl.multiple_of(t * TILE, TILE), TILE)

    def two(buf, t):
        return buf[pl.ds(t * (TILE // rows), TILE // rows)].reshape(TILE, buf.shape[-1])

    def turned(v):
        return pltpu.roll(v, HEAD_SIZE // 2, 1)

    def normed_rope(raw, gain, at):
        scale = lax.rsqrt(jnp.mean(raw * raw, axis=-1, keepdims=True) + NORM_EPS)
        y = raw * scale * gain
        return y * cos_ref[at, :] + turned(y) * sin_ref[at, :]

    def project_queries(t):
        at = tile_rows(t)
        out = dot(two(n1, t), wq[0].reshape(MODEL_WIDTH, QCOLS))
        for h in range(GROUP):
            raw = out[:, h * HEAD_SIZE : (h + 1) * HEAD_SIZE]
            qraw[at, h * HEAD_SIZE : (h + 1) * HEAD_SIZE] = raw
            q_s[h, at, :] = normed_rope(raw, g_query, at).astype(BF16)

    def project_pairs(t):
        at = tile_rows(t)
        both = dot(two(n1, t), wq[1].reshape(MODEL_WIDTH, 2 * HEAD_SIZE))
        raw = both[:, :HEAD_SIZE]
        kraw[at, :] = raw
        keys = normed_rope(raw, g_key, at)
        values = both[:, HEAD_SIZE:]
        k_s[at, :] = keys.astype(BF16)
        v_s[at, :] = values.astype(BF16)
        kt_s[:, at] = keys.T.astype(BF16)
        vt_s[:, at] = values.T.astype(BF16)

    zg_wait(*g_q)
    loop(0, tiles, project_queries)
    pl.when(outer)(lambda: a2a_wait(1, wgu_in))
    zg_start(*g_gu1, outer)
    zg_start(*g_gu2, outer)
    zg_start(*g_d, outer)
    zg_wait(*g_kv)
    loop(0, tiles, project_pairs)
    ag_drain(0, xg)
    zg_far(*g_o)
    pl.when(inner)(lambda: a2a_wait(1, wgu_in))
    zg_start(*g_gu1, inner)
    zg_start(*g_gu2, inner)
    def n_cols(n):
        return pl.ds(pl.multiple_of(n * WIDE, WIDE), WIDE)

    def half_rows(which):
        return pl.ds(pl.multiple_of(which * half, half), half)

    def half_slots(buf, which):
        return buf[pl.ds(which * CHIPS, CHIPS)].reshape(half, buf.shape[-1])

    def out_part(which, n):
        return dot(
            attn_low[half_rows(which), :], wo[:, :, n_cols(n)].reshape(QCOLS, WIDE)
        )

    scale = HEAD_SIZE ** (-0.5)

    def attend(t):
        at = half_rows(t)
        kpos = jnp.concatenate([kpos_ref[...]] * (half // HEAD_SIZE), axis=1)
        kept = (kpos <= qpos_ref[:, at]) & (kpos >= qstart_ref[:, at])
        for h in range(GROUP):
            scores = jnp.where(kept, dot(k_s[...], q_s[h, at, :], NT) * scale, MASKED)
            weights = jnp.exp(scores - jnp.max(scores, axis=0, keepdims=True))
            low = weights.astype(BF16)
            probs[h, t] = low
            share = 1.0 / jnp.sum(weights, axis=0, keepdims=True)
            shares[h, :, at] = share
            mixed = dot(vt_s[...], low) * share
            attn[h, :, at] = mixed
            attn_low[at, h * HEAD_SIZE : (h + 1) * HEAD_SIZE] = mixed.T.astype(BF16)

    attend(1 - core)
    zg_across(*g_gu1)
    zg_wait(*g_o)
    rs_give(0, out_part, 0)
    rs_give(0, out_part, 1)
    ag_pass_near(1, cot)
    attend(core)
    zg_back(*g_gu1)
    for h in range(2):
        rs_keep(0, out_part, h)
        rs_send(0, h)
    zg_across(*g_gu2)
    zg_back(*g_gu2)
    rs_relay(0)
    ag_pass_across(1, cot)
    zg_far(*g_gu1)
    resid = x_own[...].astype(F32) + rs_finish(0)
    resid_s[...] = resid
    g_mlp = gains[:, MODEL_WIDTH : 2 * MODEL_WIDTH]
    s_two = lax.rsqrt(jnp.mean(resid * resid, axis=-1, keepdims=True) + NORM_EPS)
    n2[slot] = (resid * s_two * g_mlp).astype(BF16)
    ag_start(2, n2)
    ag_finish_near(1, cot)
    ag_finish(1, cot)
    zg_far(*g_gu2)
    zg_start(*g_d, inner)
    zg_across(*g_d)
    def feed(t):
        at = tile_rows(t)
        both = dot(two(n2, t), wgu[...].reshape(MODEL_WIDTH, 2 * HID))
        gate, up = both[:, :HID], both[:, HID:]
        sig = 1.0 / (1.0 + jnp.exp(-gate))
        silu = gate * sig
        hidden[at, :] = (silu * up).astype(BF16)
        ggu[at, :HID] = (up * sig * (1.0 + gate * (1.0 - sig))).astype(BF16)
        ggu[at, HID:] = silu.astype(BF16)

    def wgu_there():
        zg_wait(*g_gu1)
        zg_wait(*g_gu2)

    def pass_down():
        zg_back(*g_d)

    gathered_tiles(2, n2, feed, pass_down, wgu_there)
    zg_far(*g_d)

    def down_grad(n):
        there = cot[:, :, n_cols(n)].reshape(2 * half, WIDE)
        gwd[:, :, n_cols(n)] = (
            dot(hidden[...], there, TN).astype(BF16).reshape(4, HID // 4, WIDE)
        )

    down_grad(0)
    zr_start(r_d1)
    down_grad(1)
    zr_start(r_d2)
    zg_wait(*g_d)

    def feed_back(t):
        at = half_rows(t)
        ghid = dot(half_slots(cot, t), wd[...].reshape(HID, MODEL_WIDTH), NT)
        ggu[at, :HID] = (ghid * ggu[at, :HID].astype(F32)).astype(BF16)
        ggu[at, HID:] = (ghid * ggu[at, HID:].astype(F32)).astype(BF16)

    for t in range(2):
        feed_back(t)

    def back_two_part(which, n):
        per = MODEL_WIDTH // CTX
        there = wgu[pl.ds(n * (WIDE // per), WIDE // per)].reshape(WIDE, 2 * HID)
        return dot(ggu[half_rows(which), :], there, NT)

    rs_begin(1, back_two_part)

    def gate_up_grad(n):
        per = MODEL_WIDTH // CTX
        there = n2[:, :, n_cols(n)].reshape(2 * half, WIDE)
        gwgu[pl.ds(n * (WIDE // per), WIDE // per)] = (
            dot(there, ggu[...], TN)
            .astype(BF16)
            .reshape(WIDE // per, 4, per // 4, 2 * HID)
        )

    gate_up_grad(0)
    zr_start(r_gu1)
    gate_up_grad(1)
    zr_start(r_gu2)
    zr_first(*r_d1)
    zr_first(*r_d2)
    rs_relay(1)


    def norm_back(values, grads, gain):
        factor = lax.rsqrt(jnp.mean(values * values, axis=-1, keepdims=True) + NORM_EPS)
        unit = values * factor
        scaled = grads * gain
        inner = jnp.mean(scaled * unit, axis=-1, keepdims=True)
        return factor * (scaled - unit * inner), jnp.sum(grads * unit, axis=0, keepdims=True)

    back, terms = norm_back(resid_s[...], rs_finish(1), g_mlp)
    hrow[:, MODEL_WIDTH : 2 * MODEL_WIDTH] = terms
    gresid = cot[slot].astype(F32) + back
    gresid_s[...] = gresid
    gb = xg
    gb[slot] = gresid.astype(BF16)
    def down_part(which, n):
        return dot(hidden[half_rows(which), :], wd[:, :, n_cols(n)].reshape(HID, WIDE))

    ag_start(3, gb)
    rs_compute(2, down_part)
    zr_second(*r_d1)
    zr_second(*r_d2)

    def attn_grad(t):
        gattn[tile_rows(t), :] = dot(
            two(gb, t), wo[...].reshape(QCOLS, MODEL_WIDTH), NT
        ).astype(BF16)

    gathered_tiles(3, gb, attn_grad, lambda: zr_first(*r_gu1))
    rs_send(2, 0)
    rs_send(2, 1)

    def out_grad(n):
        there = gb[:, :, n_cols(n)].reshape(2 * half, WIDE)
        gwo[:, :, n_cols(n)] = (
            dot(attn_low[...], there, TN).astype(BF16).reshape(4, QCOLS // 4, WIDE)
        )

    loop(0, MODEL_WIDTH // WIDE, out_grad)
    zr_start(r_o, part=(0, 1))

    dk_s[...] = jnp.zeros_like(dk_s)
    dv_s[...] = jnp.zeros_like(dv_s)

    hrow[:, 2 * MODEL_WIDTH :] = jnp.zeros((1, 2 * HEAD_SIZE), F32)

    def head_back(raw, grads, at, gain):
        grads = grads * scale
        grads = grads * cos_ref[at, :] - turned(grads) * sin_ref[at, :]
        return norm_back(raw, grads, gain)

    q_terms = pl.ds(2 * MODEL_WIDTH, HEAD_SIZE)
    k_terms = pl.ds(2 * MODEL_WIDTH + HEAD_SIZE, HEAD_SIZE)

    def attend_back(t):
        at = pl.ds(t * half, half)
        for h in range(GROUP):
            head = slice(h * HEAD_SIZE, (h + 1) * HEAD_SIZE)
            grads = gattn[at, head]
            turned_grads = grads.astype(F32).T
            share = shares[h, :, at]
            delta = jnp.sum(turned_grads * attn[h, :, at], axis=0, keepdims=True)
            low = probs[h, t]
            gprobs = dot(v_s[...], grads, NT)
            gscores = (low.astype(F32) * ((gprobs - delta) * share)).astype(BF16)
            dv_s[...] += dot(low, (turned_grads * share).T.astype(BF16))
            dk_s[...] += dot(gscores, q_s[h, at, :])
            back, terms = head_back(qraw[at, head], dot(kt_s[...], gscores).T, at, g_query)
            gp[at, head] = back.astype(BF16)
            hrow[:, q_terms] += terms

    attend_back(0)
    zr_second(*r_gu1)
    attend_back(1)
    rs_relay(2)
    zr_first(*r_gu2)

    def project_back(t):
        at = tile_rows(t)
        back, terms = head_back(kraw[at, :], dk_s[at, :], at, g_key)
        gp[at, QCOLS : QCOLS + HEAD_SIZE] = back.astype(BF16)
        hrow[:, k_terms] += terms
        gp[at, QCOLS + HEAD_SIZE :] = dv_s[at, :].astype(BF16)

    loop(0, tiles, project_back)

    def qkv_grad(n):
        per = MODEL_WIDTH // CTX
        there = n1[:, :, n_cols(n)].reshape(2 * half, WIDE)
        gwq[pl.ds(n * (WIDE // per), WIDE // per)] = (
            dot(there, gp[...], TN)
            .astype(BF16)
            .reshape(WIDE // per, 4, per // 4, PCOLS)
        )

    qkv_grad(0)
    qkv_grad(1)
    zr_start(r_q1, r_q2)
    def back_one_part(which, n):
        per = MODEL_WIDTH // CTX
        at = pl.ds(n * (WIDE // per), WIDE // per)
        rows_at = half_rows(which)
        return dot(gp[rows_at, :QCOLS], wq[0, at].reshape(WIDE, QCOLS), NT) + dot(
            gp[rows_at, QCOLS:], wq[1, at].reshape(WIDE, 2 * HEAD_SIZE), NT
        )

    rs_begin(3, back_one_part)
    zr_second(*r_gu2)
    zr_first(*r_o)
    rs_relay(3)
    zr_second(*r_o)
    zr_first(*r_q1)
    zr_first(*r_q2)
    for h, item in enumerate((r_d1, r_d2)):
        sum_d = zr_finish(*item)
        for g in range(WIDE // 128):
            at = line_rows(ends[2], h * (WIDE // 128) + g, MODEL_WIDTH // 128, HID // 4)
            lines[at, :] = sum_d[:, g * 128 : (g + 1) * 128]
    first_half, second_half = pl.ds(0, CTX // 2), pl.ds(CTX // 2, CTX // 2)
    asg[first_half] = zr_finish(*r_gu1).astype(BF16)
    asg[second_half] = zr_finish(*r_gu2).astype(BF16)
    arg_[c] = asg[c]
    zr_second(*r_q1)
    back, terms = norm_back(x_own[...].astype(F32), rs_finish(3), gains[:, :MODEL_WIDTH])
    xgrad_ref[...] = (gresid_s[...] + back).astype(BF16)
    store_xgrad = pltpu.make_async_copy(xgrad_ref, xgrad_hbm.at[0], loc.at[5])
    store_xgrad.start()
    hrow[:, :MODEL_WIDTH] = terms
    hz[z] = hrow[...]
    loop(1, 4, lambda i: row_z(1, hrow, hz, i).start())
    zr_start(r_o, part=(2,))
    arg_at = lambda j: arg_.at[j]
    a2a_start(2, asg, arg_at)
    zr_second(*r_q2)
    out_ref[...] = (resid_s[...] + rs_finish(2)).astype(BF16)
    store_out = pltpu.make_async_copy(out_ref, out_hbm.at[0], loc.at[6])
    store_out.start()
    arq_at = lambda j: arq.at[j]
    asq[first_half] = zr_finish(*r_q1).astype(BF16)
    a2a_half(3, asq, arq_at, 0)
    asq[second_half] = zr_finish(*r_q2).astype(BF16)
    a2a_half(3, asq, arq_at, 1)
    arq[c] = asq[c]
    row_z_wait(1, hz)
    hpl[c] = jnp.sum(hz[...], axis=0)
    loop(1, CTX, lambda i: row_plane(1, hpl.at[c], hpl, i).start())
    a2a_wait(2, arg_)
    for j in range(CTX):
        for part in range(2 * HID // 128):
            lines[line_rows(ends[1], feed_group(j, part), feed_groups, per_run), :] = arg_[
                j, :, part * 128 : (part + 1) * 128
            ].astype(F32)
    a2a_wait(3, arq)
    for j in range(CTX):
        for part in range(PCOLS // 128):
            lines[line_rows(0, qkv_group(j, part), qkv_groups, per_run), :] = arq[
                j, :, part * 128 : (part + 1) * 128
            ].astype(F32)
    split = ends[0] // 128, ends[1] // 128
    stores = [
        pltpu.make_async_copy(
            lines.at[pl.ds(first, last - first)], lin_ref.at[pl.ds(first, last - first)], loc.at[k]
        )
        for k, (first, last) in enumerate(
            ((0, split[0]), (split[1], tail // 128), split, (tail // 128, tail // 128 + 8))
        )
    ]
    stores[0].start()
    stores[1].start()
    sum_o = zr_finish(*r_o)
    for g in range(MODEL_WIDTH // 128):
        lines[line_rows(ends[0], g, MODEL_WIDTH // 128, sum_o.shape[0]), :] = sum_o[
            :, g * 128 : (g + 1) * 128
        ]
    stores[2].start()
    row_plane_wait(1, hpl)
    total = jnp.sum(hpl[...], axis=0)
    lines[pl.ds(tail // 128, 1), :] = pltpu.roll(
        total, GAIN_WIDTH - spans[4] * (4 * c + z), 1
    )[:, :128]
    stores[3].start()

    for n, buf in ((1, cot), (2, n2), (3, gb)):
        ag_drain(n, buf)
    rs_drain(3)
    a2a_drain(0, wq_in.at[0])
    a2a_drain(4, wq_in.at[1])
    a2a_drain(1, wgu_in)
    a2a_drain(2, asg)
    a2a_drain(3, asq)
    first_four = pl.ds(0, CTX // 2)
    for n, some in (
        (0, lambda count: wq.at[0, :, pl.ds(0, count)]),
        (5, lambda count: wq.at[1, :, pl.ds(0, count)]),
        (1, lambda count: wo.at[pl.ds(0, count)]),
        (2, lambda count: wgu.at[first_four, pl.ds(0, count)]),
        (3, lambda count: wgu.at[first_four, pl.ds(0, count)]),
        (4, lambda count: wd.at[pl.ds(0, count)]),
    ):
        zg_drain(n, some)
    three = pl.ds(0, 3)
    for n, part in (
        (0, lwd.at[three, :, pl.ds(0, WIDE)]),
        (6, lwd.at[three, :, pl.ds(WIDE, WIDE)]),
        (1, lwgu.at[three, first_four]),
        (2, lwgu.at[three, first_four]),
        (3, lwo.at[three]),
        (4, lwq.at[three, first_four]),
        (5, lwq.at[three, first_four]),
    ):
        rcopy(part, part, zr_s.at[n], zr_r.at[n, 0], sib, z).wait_send()
    for n, lands in enumerate(((gz, gpl), (hz, hpl))):
        for k, land in enumerate(lands):
            rows_of(n, land, k).wait_send()
    for copy in (store_out, store_xgrad, *stores):
        copy.wait()


def layer_call(tokens, cotangent, stretch_order, doc_lengths, master):
    _, rows, width = tokens.shape
    length = CTX * rows
    tiles = length // TILE
    per = width // CTX // 4
    entries = master.shape[0] // 1024 * 1024
    vm = pltpu.VMEM
    dma = pltpu.SemaphoreType.DMA
    shape = jax.ShapeDtypeStruct
    full = vm((CTX, rows, width), BF16)
    scratch = [
        pltpu.SMEM(stretch_order.shape, jnp.int32),
        pltpu.SMEM(doc_lengths.shape, jnp.int32),
        vm((rows, width), BF16),
        vm((rows, width), BF16),
        vm((width * 4 * width // 32 + 2 * width * width // 32,), F32),
        vm((FEED_WIDTH * width // 32,), F32),
        vm((master.shape[0] - entries,), F32),
        vm((entries // 128 + 8, 128), F32),
        vm((2, CTX, per, QCOLS), BF16),
        vm((CTX, per, 2 * HID), BF16),
        vm((1, GAIN_WIDTH), F32),
        vm((length, HEAD_SIZE), F32),
        vm((length, HEAD_SIZE), F32),
        vm((length, HEAD_SIZE), jnp.int32),
        vm((1, length), jnp.int32),
        vm((1, length), jnp.int32),
        full,
        full,
        full,
        full,
        vm((rows, width), BF16),
        vm((2, CTX, 4, per, QCOLS), BF16),
        vm((4, QCOLS // 4, width), BF16),
        vm((CTX, 4, per, 2 * HID), BF16),
        vm((4, HID // 4, width), BF16),
        vm((length, QCOLS), F32),
        vm((length, HEAD_SIZE), F32),
        vm((GROUP, length, HEAD_SIZE), BF16),
        vm((length, HEAD_SIZE), BF16),
        vm((length, HEAD_SIZE), BF16),
        vm((HEAD_SIZE, length), BF16),
        vm((HEAD_SIZE, length), BF16),
        vm((GROUP, 2, length, length // 2), BF16),
        vm((GROUP, HEAD_SIZE, length), F32),
        vm((GROUP, 1, length), F32),
        vm((length, QCOLS), BF16),
        vm((length, HID), BF16),
        vm((length, 2 * HID), BF16),
        vm((length, QCOLS), BF16),
        vm((length, HEAD_SIZE), F32),
        vm((length, HEAD_SIZE), F32),
        vm((length, PCOLS), BF16),
        vm((2, CHIPS, rows, width // 2), BF16),
        vm((2, 2, CHIPS, rows, width // 2), BF16),
        vm((6, rows, width // 2), BF16),
        vm((2, 6, rows, width // 2), BF16),
        vm((2, CHIPS, rows, width // 2), F32),
        vm((2, rows, width), F32),
        vm((rows, width), F32),
        vm((rows, width), F32),
        vm((CTX, 4, per, PCOLS), BF16),
        vm((4, QCOLS // 4, width), BF16),
        vm((CTX, 4, per, 2 * HID), BF16),
        vm((4, HID // 4, width), BF16),
        vm((5, CTX, per, PCOLS), BF16),
        vm((5, QCOLS // 4, width), BF16),
        vm((5, CTX, per, 2 * HID), BF16),
        vm((5, HID // 4, width), BF16),
        vm((CTX, per, PCOLS), BF16),
        vm((CTX, per, 2 * HID), BF16),
        vm((CTX, per, PCOLS), BF16),
        vm((CTX, per, 2 * HID), BF16),
        vm((4, 1, GAIN_WIDTH), F32),
        vm((CTX, 1, GAIN_WIDTH), F32),
        vm((1, GAIN_WIDTH), F32),
        vm((4, 1, GAIN_WIDTH), F32),
        vm((CTX, 1, GAIN_WIDTH), F32),
        vm((1, GAIN_WIDTH), F32),
        dma((4,)),
        dma((3, 8)),
        dma((2,)),
        dma((2, 2)),
        dma((6,)),
        dma((2, 6)),
        dma((5,)),
        dma((2 * CTX + 1,)),
        dma((6, 2)),
        dma((6, 4)),
        dma((7,)),
        dma((7, 5)),
        dma((2, 2)),
        dma((2, 2)),
        dma((8,)),
    ]
    anywhere = pl.BlockSpec(memory_space=pl.ANY)
    return pl.pallas_call(
        layer_kernel,
        out_shape=(
            shape((1, rows, width), BF16),
            shape((1, rows, width), BF16),
            shape((entries // 128 + 8, 128), F32),
        ),
        in_specs=[anywhere] * 5,
        out_specs=[anywhere] * 3,
        scratch_shapes=scratch,
        compiler_params=pltpu.CompilerParams(
            collective_id=1, has_side_effects=True, vmem_limit_bytes=63 << 20
        ),
        name="layer",
    )(stretch_order, doc_lengths, tokens, cotangent, master)


def local_planes(tokens, cotangent, stretch_order, doc_lengths, master, first_moment, second_moment):
    shards = lax.axis_size("ctx") * lax.axis_size("fsdp")
    length = tokens.shape[1] * lax.axis_size("ctx")
    out, xgrad, lines = layer_call(
        tokens, cotangent, stretch_order, doc_lengths, master
    )
    return adam_call(out, xgrad, lines, master, first_moment, second_moment, shards, length)


def adam_kernel(
    spans,
    settings,
    out_hbm,
    xgrad_hbm,
    grad_hbm,
    master_hbm,
    first_hbm,
    second_hbm,
    out_to,
    xgrad_to,
    master_to,
    first_to,
    second_to,
    out,
    xgrad,
    grad,
    master,
    first,
    second,
    sems,
):
    held = (grad, first, second, master, out, xgrad)
    fetch = [
        pltpu.make_async_copy(src, dst, sems.at[0, k])
        for k, (src, dst) in enumerate(
            zip((grad_hbm, first_hbm, second_hbm, master_hbm, out_hbm, xgrad_hbm), held)
        )
    ]
    store = [
        pltpu.make_async_copy(src, dst, sems.at[1, k])
        for k, (src, dst) in enumerate(
            zip(held[1:], (first_to, second_to, master_to, out_to, xgrad_to))
        )
    ]
    for copy in fetch:
        copy.start()

    def each(body):
        begin = 0
        for k, span in enumerate(spans[:-1]):
            block = span // -(-span // 65536)

            def step(i, carry, begin=begin, k=k, block=block):
                at = pl.ds(pl.multiple_of(begin + i * block, block), block)
                line = pl.ds(pl.multiple_of(begin // 128 + i * (block // 128), 8), block // 128)
                body(at, (block // 128, 128), grad[line, :], k)
                return carry

            lax.fori_loop(0, span // block, step, 0)
            begin += span
        last = spans[-1]
        body(pl.ds(begin, last), (1, last), grad[pl.ds(begin // 128, 1), :last], len(spans) - 1)

    def step_first(at, shape, g, k):
        new = BETA_ONE * first[at].reshape(shape) + (1.0 - BETA_ONE) * g
        first[at] = new.reshape(-1)

    def step_second(at, shape, g, k):
        new = BETA_TWO * second[at].reshape(shape) + (1.0 - BETA_TWO) * g * g
        second[at] = new.reshape(-1)

    def step_master(at, shape, g, k):
        rate, decay = settings[k]
        old = master[at].reshape(shape)
        mean = first[at].reshape(shape) * (1.0 / (1.0 - BETA_ONE**STEP))
        root = jnp.sqrt(second[at].reshape(shape) * (1.0 / (1.0 - BETA_TWO**STEP)))
        new = old - rate * (mean / (root + ADAM_EPS) + decay * old)
        master[at] = new.reshape(-1)

    fetch[0].wait()
    for k, body in enumerate((step_first, step_second, step_master)):
        fetch[k + 1].wait()
        each(body)
        store[k].start()
        if k == 1:
            for j in (4, 5):
                fetch[j].wait()
                store[j - 1].start()
    for copy in store:
        copy.wait()


def adam_call(out, xgrad, lines, master, first_moment, second_moment, shards, length):
    spans = [r // shards * w for r, w in segment_shapes()]
    shape = lambda v: jax.ShapeDtypeStruct(v.shape, v.dtype)
    operands = (out, xgrad, lines, master, first_moment, second_moment)
    results = (out, xgrad, master, first_moment, second_moment)
    anywhere = pl.BlockSpec(memory_space=pl.ANY)
    return pl.pallas_call(
        functools.partial(adam_kernel, spans, step_settings(length)),
        out_shape=[shape(v) for v in results],
        in_specs=[anywhere] * 6,
        out_specs=[anywhere] * 5,
        scratch_shapes=[pltpu.VMEM(v.shape, v.dtype) for v in operands]
        + [pltpu.SemaphoreType.DMA((2, 6))],
        compiler_params=pltpu.CompilerParams(vmem_limit_bytes=63 << 20),
        name="adam",
    )(*operands)


def step_settings(length):
    return [
        (MODEL_WIDTH ** (-0.5), DECAY_RATE),
        ((length / (3.0 * QUERY_HEADS * HEAD_SIZE)) ** 0.5, DECAY_RATE),
        (MODEL_WIDTH ** (-0.5), DECAY_RATE),
        (FEED_WIDTH ** (-0.5), DECAY_RATE),
        (0.2, 0.0),
    ]


def rates(shards, length):
    settings = step_settings(length)
    spans = [r // shards * w for r, w in segment_shapes()]
    index = lax.iota(jnp.int32, sum(spans))
    step_rate = jnp.full(index.shape, settings[0][0], F32)
    decay_value = jnp.full(index.shape, settings[0][1], F32)
    first = 0
    for span, (step, decay) in zip(spans, settings):
        step_rate = jnp.where(index >= first, step, step_rate)
        decay_value = jnp.where(index >= first, decay, decay_value)
        first += span
    return step_rate, decay_value


def adam(grad, master, first_moment, second_moment, shards, length):
    step_rate, decay_value = rates(shards, length)
    new_first = BETA_ONE * first_moment + (1.0 - BETA_ONE) * grad
    new_second = BETA_TWO * second_moment + (1.0 - BETA_TWO) * grad * grad
    normalized = (
        new_first
        / (1.0 - BETA_ONE**STEP)
        / (jnp.sqrt(new_second / (1.0 - BETA_TWO**STEP)) + ADAM_EPS)
    )
    new_master = master - step_rate * (normalized + decay_value * master)
    return new_master, new_first, new_second


def solution(mesh):
    placed = (
        P("fsdp", "ctx", None),
        P("fsdp", "ctx", None),
        P(),
        P("fsdp", None),
        P(("ctx", "fsdp")),
        P(("ctx", "fsdp")),
        P(("ctx", "fsdp")),
    )
    plane = mesh.shape["ctx"] == CTX == KEY_VALUE_HEADS and mesh.shape["fsdp"] == 4
    return jax.shard_map(
        local_planes if plane else local,
        mesh=mesh,
        in_specs=placed,
        out_specs=(
            P("fsdp", "ctx", None),
            P("fsdp", "ctx", None),
            P(("ctx", "fsdp")),
            P(("ctx", "fsdp")),
            P(("ctx", "fsdp")),
        ),
        check_vma=False,
    )
```

```python
import functools
import math

import jax
import jax.numpy as jnp
from jax import lax
from jax.experimental import pallas as pl
from jax.experimental.pallas import tpu as pltpu
from jax.sharding import PartitionSpec as P

MODEL_WIDTH = 1024
QUERY_HEADS = 16
KEY_VALUE_HEADS = 8
HEAD_SIZE = 128
FEED_WIDTH = 3072
STRETCH = 64
STEP = 7


NORM_EPS = 1e-06
ROPE_BASE = 1000000.0
BETA_ONE = 0.5
BETA_TWO = 0.5
DECAY_RATE = 0.1
ADAM_EPS = 1e-08
MASKED = -1e30


def from_behind(x, axis, by):
    peers = lax.axis_size(axis)
    return lax.ppermute(x, axis, [(i, (i + by) % peers) for i in range(peers)])


def segment_shapes():
    return [
        (MODEL_WIDTH, (QUERY_HEADS + 2 * KEY_VALUE_HEADS) * HEAD_SIZE),
        (QUERY_HEADS * HEAD_SIZE, MODEL_WIDTH),
        (MODEL_WIDTH, 2 * FEED_WIDTH),
        (FEED_WIDTH, MODEL_WIDTH),
        (2 * MODEL_WIDTH + 2 * HEAD_SIZE, 1),
    ]


def unpack(flat_params, count_of_shards):
    param_table = flat_params.reshape(count_of_shards, -1)
    pieces = []
    offset = 0
    for row_total, column_total in segment_shapes():
        shard_span = row_total // count_of_shards * column_total
        pieces.append(param_table[:, offset : offset + shard_span].reshape(row_total, column_total))
        offset += shard_span
    return pieces


def pack(matrices, count_of_shards):
    return jnp.concatenate(
        [matrix.reshape(count_of_shards, -1) for matrix in matrices], axis=1
    ).reshape(-1)


def slot_positions(stretch_order, first_row, count_of_rows):
    row_ids = first_row + jnp.arange(count_of_rows, dtype=jnp.int32)
    slot_ids = row_ids // STRETCH
    slot_table = jnp.arange(stretch_order.shape[0], dtype=jnp.int32)
    stretch_ids = jnp.sum(
        jnp.where(slot_ids[:, None] == slot_table[None, :], stretch_order[None, :], 0), axis=1
    )
    return stretch_ids * STRETCH + row_ids % STRETCH


def documents(positions, doc_lengths):
    doc_ends = jnp.cumsum(doc_lengths, axis=1)
    doc_starts = doc_ends - doc_lengths
    passed = positions[None, :, None] >= doc_ends[:, None, :-1]
    doc_ids = jnp.sum(passed.astype(jnp.int32), axis=2)
    doc_table = jnp.arange(doc_lengths.shape[1], dtype=jnp.int32)
    owner = doc_ids[:, :, None] == doc_table[None, None, :]
    start_of = jnp.sum(jnp.where(owner, doc_starts[:, None, :], 0), axis=2)
    return (doc_ids, positions[None, :] - start_of)


def key_mask(stretch_order, doc_lengths, query_pos, query_doc, first_row, count_of_rows):
    key_pos = slot_positions(stretch_order, first_row, count_of_rows)
    key_doc, _ = documents(key_pos, doc_lengths)
    same_doc = query_doc[:, :, None] == key_doc[:, None, :]
    return same_doc & (key_pos[None, None, :] <= query_pos[None, :, None])


def rope_tables(relative):
    half_dim = HEAD_SIZE // 2
    frequency = ROPE_BASE ** (-(jnp.arange(half_dim, dtype=jnp.float32) * 2.0 / HEAD_SIZE))
    angles = relative.astype(jnp.float32)[..., None] * frequency
    cosine_table = jnp.cos(angles)
    sine_values = jnp.sin(angles)
    return (
        jnp.concatenate([cosine_table, cosine_table], axis=-1),
        jnp.concatenate([sine_values, sine_values], axis=-1),
    )


def rotate(values, cosine_table, sine_values):
    half_dim = values.shape[-1] // 2
    turned = jnp.concatenate([-values[..., half_dim:], values[..., :half_dim]], axis=-1)
    return values * cosine_table[..., None, :] + turned * sine_values[..., None, :]


def rotate_back(grads, cosine_table, sine_values):
    half_dim = grads.shape[-1] // 2
    moved = grads * sine_values[..., None, :]
    unturned = jnp.concatenate([moved[..., half_dim:], -moved[..., :half_dim]], axis=-1)
    return grads * cosine_table[..., None, :] + unturned


def rms_norm(values, scaling):
    factor = lax.rsqrt(jnp.mean(values * values, axis=-1, keepdims=True) + NORM_EPS)
    return values * factor * scaling


def norm_back(values, grads, scaling):
    factor = lax.rsqrt(jnp.mean(values * values, axis=-1, keepdims=True) + NORM_EPS)
    unit_values = values * factor
    scaled_grads = grads * scaling
    inner = jnp.mean(scaled_grads * unit_values, axis=-1, keepdims=True)
    return (factor * (scaled_grads - unit_values * inner), grads * unit_values)


def attend_block(state, queries, key_value_block, allowed, score_scale):
    running, top_now, total_now = state
    sequence_count, count_of_keys = (key_value_block.shape[1], key_value_block.shape[2])
    block_keys = key_value_block[0].reshape(
        sequence_count, count_of_keys, KEY_VALUE_HEADS, HEAD_SIZE
    )
    block_values = key_value_block[1].reshape(
        sequence_count, count_of_keys, KEY_VALUE_HEADS, HEAD_SIZE
    )
    mask_wide = allowed[:, :, None, None, :]
    scores = (
        jnp.einsum("sqhgd,snhd->sqhgn", queries, block_keys, preferred_element_type=jnp.float32)
        * score_scale
    )
    new_top = jnp.maximum(top_now, jnp.max(jnp.where(mask_wide, scores, MASKED), axis=-1))
    weights = jnp.where(mask_wide, jnp.exp(scores - new_top[..., None]), 0.0)
    factor = jnp.exp(top_now - new_top)
    total_now = total_now * factor + jnp.sum(weights, axis=-1)
    running = running * factor[..., None] + jnp.einsum(
        "sqhgn,snhd->sqhgd",
        weights.astype(jnp.bfloat16),
        block_values,
        preferred_element_type=jnp.float32,
    )
    return (running, new_top, total_now)


def backward_block(
    queries, attention_gradient, log_total, delta, key_value_block, allowed, score_scale
):
    sequence_count, count_of_keys = (key_value_block.shape[1], key_value_block.shape[2])
    block_keys = key_value_block[0].reshape(
        sequence_count, count_of_keys, KEY_VALUE_HEADS, HEAD_SIZE
    )
    block_values = key_value_block[1].reshape(
        sequence_count, count_of_keys, KEY_VALUE_HEADS, HEAD_SIZE
    )
    mask_wide = allowed[:, :, None, None, :]
    scores = (
        jnp.einsum("sqhgd,snhd->sqhgn", queries, block_keys, preferred_element_type=jnp.float32)
        * score_scale
    )
    probabilities = jnp.where(mask_wide, jnp.exp(scores - log_total[..., None]), 0.0)
    value_gradient = jnp.einsum(
        "sqhgn,sqhgd->snhd",
        probabilities.astype(jnp.bfloat16),
        attention_gradient,
        preferred_element_type=jnp.float32,
    )
    grad_probs = jnp.einsum(
        "sqhgd,snhd->sqhgn", attention_gradient, block_values, preferred_element_type=jnp.float32
    )
    grad_scores = (probabilities * (grad_probs - delta[..., None])).astype(jnp.bfloat16)
    grad_queries = (
        jnp.einsum("sqhgn,snhd->sqhgd", grad_scores, block_keys, preferred_element_type=jnp.float32)
        * score_scale
    )
    key_gradient = (
        jnp.einsum("sqhgn,sqhgd->snhd", grad_scores, queries, preferred_element_type=jnp.float32)
        * score_scale
    )
    grad_pair = jnp.stack(
        [
            key_gradient.reshape(sequence_count, count_of_keys, KEY_VALUE_HEADS * HEAD_SIZE),
            value_gradient.reshape(sequence_count, count_of_keys, KEY_VALUE_HEADS * HEAD_SIZE),
        ]
    )
    return (grad_queries, grad_pair)


def summed(part, count_of_shards):
    return lax.psum_scatter(
        part.reshape(-1), ("ctx", "fsdp"), scatter_dimension=0, tiled=True
    )


def local(tokens, cotangent, stretch_order, doc_lengths, master, first_moment, second_moment):
    cycle_size = lax.axis_size("ctx")
    ctx_index = lax.axis_index("ctx")
    count_of_shards = cycle_size * lax.axis_size("fsdp")
    sequence_count, count_of_rows, _ = tokens.shape
    seq_length = count_of_rows * cycle_size
    query_groups = QUERY_HEADS // KEY_VALUE_HEADS
    score_scale = HEAD_SIZE ** (-0.5)
    gathered = lax.all_gather(master.astype(jnp.bfloat16), ("ctx", "fsdp"), axis=0, tiled=True)
    w_qkv, w_out, w_gate_up, w_down, gain_column = unpack(gathered, count_of_shards)
    gains = gain_column.reshape(-1).astype(jnp.float32)
    g_attn = gains[:MODEL_WIDTH]
    g_mlp = gains[MODEL_WIDTH : 2 * MODEL_WIDTH]
    g_query = gains[2 * MODEL_WIDTH : 2 * MODEL_WIDTH + HEAD_SIZE]
    g_key = gains[2 * MODEL_WIDTH + HEAD_SIZE :]
    query_pos = slot_positions(stretch_order, ctx_index * count_of_rows, count_of_rows)
    query_doc, relative = documents(query_pos, doc_lengths)
    cosine_table, sine_values = rope_tables(relative)
    x_in = tokens.astype(jnp.float32)
    normed_one = rms_norm(x_in, g_attn).astype(jnp.bfloat16)
    projected_output = jnp.einsum(
        "sqd,de->sqe", normed_one, w_qkv, preferred_element_type=jnp.float32
    )
    query_raw = projected_output[:, :, : QUERY_HEADS * HEAD_SIZE].reshape(
        sequence_count, count_of_rows, QUERY_HEADS, HEAD_SIZE
    )
    unrotated_keys = projected_output[
        :, :, QUERY_HEADS * HEAD_SIZE : (QUERY_HEADS + KEY_VALUE_HEADS) * HEAD_SIZE
    ].reshape(sequence_count, count_of_rows, KEY_VALUE_HEADS, HEAD_SIZE)
    unprojected_values = projected_output[:, :, (QUERY_HEADS + KEY_VALUE_HEADS) * HEAD_SIZE :]
    queries = (
        rotate(rms_norm(query_raw, g_query), cosine_table, sine_values)
        .astype(jnp.bfloat16)
        .reshape(sequence_count, count_of_rows, KEY_VALUE_HEADS, query_groups, HEAD_SIZE)
    )
    keys_rot = rotate(rms_norm(unrotated_keys, g_key), cosine_table, sine_values).reshape(
        sequence_count, count_of_rows, KEY_VALUE_HEADS * HEAD_SIZE
    )
    kv_local = jnp.stack([keys_rot, unprojected_values]).astype(jnp.bfloat16)
    statistic_shape = (sequence_count, count_of_rows, KEY_VALUE_HEADS, query_groups)
    initial = (
        jnp.zeros(statistic_shape + (HEAD_SIZE,), jnp.float32),
        jnp.full(statistic_shape, MASKED, jnp.float32),
        jnp.zeros(statistic_shape, jnp.float32),
    )
    state = initial
    piece = lax.all_gather(kv_local, "ctx", axis=2, tiled=True)
    key_total = piece.shape[2]

    def key_step(inner, block_index):
        first_row = block_index * count_of_rows
        key_value_block = lax.dynamic_slice_in_dim(piece, first_row, count_of_rows, 2)
        allowed = key_mask(
            stretch_order, doc_lengths, query_pos, query_doc, first_row, count_of_rows
        )
        return (attend_block(inner, queries, key_value_block, allowed, score_scale), None)

    state, _ = lax.scan(key_step, state, jnp.arange(key_total // count_of_rows, dtype=jnp.int32))
    running, top_now, total_now = state
    attn = running / total_now[..., None]
    log_total = top_now + jnp.log(total_now)
    attn_low = attn.reshape(sequence_count, count_of_rows, QUERY_HEADS * HEAD_SIZE).astype(
        jnp.bfloat16
    )
    resid = x_in + jnp.einsum("sqa,ad->sqd", attn_low, w_out, preferred_element_type=jnp.float32)
    normed_two = rms_norm(resid, g_mlp).astype(jnp.bfloat16)
    gate_up = jnp.einsum("sqd,de->sqe", normed_two, w_gate_up, preferred_element_type=jnp.float32)
    gate = gate_up[:, :, :FEED_WIDTH]
    up_part = gate_up[:, :, FEED_WIDTH:]
    sigmoid_gate = jax.nn.sigmoid(gate)
    hidden = (gate * sigmoid_gate * up_part).astype(jnp.bfloat16)
    mlp_out = jnp.einsum("sqf,fd->sqd", hidden, w_down, preferred_element_type=jnp.float32)
    layer_out = (resid + mlp_out).astype(jnp.bfloat16)
    grad_w_down = jnp.einsum("sqf,sqd->fd", hidden, cotangent, preferred_element_type=jnp.float32)
    grad_hidden = jnp.einsum("sqd,fd->sqf", cotangent, w_down, preferred_element_type=jnp.float32)
    grad_gate = grad_hidden * up_part * sigmoid_gate * (1.0 + gate * (1.0 - sigmoid_gate))
    grad_up = grad_hidden * gate * sigmoid_gate
    grad_gate_up = jnp.concatenate([grad_gate, grad_up], axis=-1).astype(jnp.bfloat16)
    grad_w_gate_up = jnp.einsum(
        "sqd,sqe->de", normed_two, grad_gate_up, preferred_element_type=jnp.float32
    )
    grad_normed_two = jnp.einsum(
        "sqe,de->sqd", grad_gate_up, w_gate_up, preferred_element_type=jnp.float32
    )
    back_two, mlp_gain_terms = norm_back(resid, grad_normed_two, g_mlp)
    grad_resid = cotangent.astype(jnp.float32) + back_two
    grad_branch = grad_resid.astype(jnp.bfloat16)
    grad_w_out = jnp.einsum(
        "sqa,sqd->ad", attn_low, grad_branch, preferred_element_type=jnp.float32
    )
    attention_gradient = jnp.einsum(
        "sqd,ad->sqa", grad_branch, w_out, preferred_element_type=jnp.float32
    ).astype(jnp.bfloat16)
    attention_head_gradient = attention_gradient.reshape(
        sequence_count, count_of_rows, KEY_VALUE_HEADS, query_groups, HEAD_SIZE
    )
    delta = jnp.sum(attention_head_gradient.astype(jnp.float32) * attn, axis=-1)

    def grads_from(turn_index, kv_now, key_value_gradients, grad_queries):
        source_dev = (ctx_index - turn_index) % cycle_size
        allowed = key_mask(
            stretch_order,
            doc_lengths,
            query_pos,
            query_doc,
            source_dev * count_of_rows,
            count_of_rows,
        )
        part_queries, part_pair = backward_block(
            queries, attention_head_gradient, log_total, delta, kv_now, allowed, score_scale
        )
        return (key_value_gradients + part_pair, grad_queries + part_queries)

    def pass_grads(key_value_gradients):
        return from_behind(key_value_gradients.astype(jnp.bfloat16), "ctx", 1).astype(
            key_value_gradients.dtype
        )

    def turn_step(turn_index, state):
        kv_now, key_value_gradients, grad_queries = state
        key_value_gradients, grad_queries = grads_from(
            turn_index, kv_now, key_value_gradients, grad_queries
        )
        kv_now = from_behind(kv_now, "ctx", 1)
        key_value_gradients = pass_grads(key_value_gradients)
        return (kv_now, key_value_gradients, grad_queries)

    start_state = (
        kv_local,
        jnp.zeros(kv_local.shape, jnp.float32),
        jnp.zeros(statistic_shape + (HEAD_SIZE,), jnp.float32),
    )
    kv_now, key_value_gradients, grad_queries = lax.fori_loop(
        0, cycle_size - 1, turn_step, start_state
    )
    key_value_gradients, grad_queries = grads_from(
        cycle_size - 1, kv_now, key_value_gradients, grad_queries
    )
    key_value_gradients = pass_grads(key_value_gradients)
    grad_query_rot = rotate_back(
        grad_queries.reshape(sequence_count, count_of_rows, QUERY_HEADS, HEAD_SIZE),
        cosine_table,
        sine_values,
    )
    grad_key_rot = rotate_back(
        key_value_gradients[0].reshape(sequence_count, count_of_rows, KEY_VALUE_HEADS, HEAD_SIZE),
        cosine_table,
        sine_values,
    )
    grad_query_raw, query_gain_terms = norm_back(query_raw, grad_query_rot, g_query)
    unrotated_key_gradient, key_gain_terms = norm_back(unrotated_keys, grad_key_rot, g_key)
    grad_projected = jnp.concatenate(
        [
            grad_query_raw.reshape(sequence_count, count_of_rows, QUERY_HEADS * HEAD_SIZE),
            unrotated_key_gradient.reshape(
                sequence_count, count_of_rows, KEY_VALUE_HEADS * HEAD_SIZE
            ),
            key_value_gradients[1],
        ],
        axis=-1,
    ).astype(jnp.bfloat16)
    grad_w_qkv = jnp.einsum(
        "sqd,sqe->de", normed_one, grad_projected, preferred_element_type=jnp.float32
    )
    grad_normed_one = jnp.einsum(
        "sqe,de->sqd", grad_projected, w_qkv, preferred_element_type=jnp.float32
    )
    back_one, attn_gain_terms = norm_back(x_in, grad_normed_one, g_attn)
    input_grad = (grad_resid + back_one).astype(jnp.bfloat16)
    grad_gains = jnp.concatenate(
        [
            jnp.sum(attn_gain_terms, axis=(0, 1)),
            jnp.sum(mlp_gain_terms, axis=(0, 1)),
            jnp.sum(query_gain_terms, axis=(0, 1, 2)),
            jnp.sum(key_gain_terms, axis=(0, 1, 2)),
        ]
    ).reshape(-1, 1)
    grad = jnp.concatenate(
        [
            summed(part, count_of_shards)
            for part in (grad_w_qkv, grad_w_out, grad_w_gate_up, grad_w_down, grad_gains)
        ]
    )
    new_master, new_first, new_second = adam(
        grad, master, first_moment, second_moment, count_of_shards, seq_length
    )
    return (layer_out, input_grad, new_master, new_first, new_second)


MESH = pl.DeviceIdType.MESH
F32 = jnp.float32
BF16 = jnp.bfloat16
CTX = 8
CHIPS = 4
GROUP = QUERY_HEADS // KEY_VALUE_HEADS
QCOLS = GROUP * HEAD_SIZE
PCOLS = QCOLS + 2 * HEAD_SIZE
HID = FEED_WIDTH // CTX
GAIN_WIDTH = 2 * MODEL_WIDTH + 2 * HEAD_SIZE
TILE = 256
WIDE = 512


def dot(a, b, dims=((1,), (0,))):
    return lax.dot_general(a, b, (dims, ((), ())), preferred_element_type=F32)


NT = ((1,), (1,))
TN = ((0,), (0,))


def layer_kernel(
    order_hbm,
    doc_hbm,
    x_hbm,
    cot_hbm,
    master_hbm,
    out_hbm,
    xgrad_hbm,
    lin_ref,
    order_ref,
    doc_ref,
    out_ref,
    xgrad_ref,
    flat,
    flat_down,
    flat_gains,
    lines,
    wq_in,
    wgu_in,
    gains_in,
    cos_ref,
    sin_ref,
    kpos_ref,
    qpos_ref,
    qstart_ref,
    xg,
    n1,
    cot,
    n2,
    x_own,
    wq,
    wo,
    wgu,
    wd,
    qraw,
    kraw,
    q_s,
    k_s,
    v_s,
    kt_s,
    vt_s,
    probs,
    attn,
    shares,
    attn_low,
    hidden,
    ggu,
    gattn,
    dk_s,
    dv_s,
    gp,
    psnd,
    prcv,
    csnd,
    crcv,
    own,
    acc,
    resid_s,
    gresid_s,
    gwq,
    gwo,
    gwgu,
    gwd,
    lwq,
    lwo,
    lwgu,
    lwd,
    asq,
    asg,
    arq,
    arg_,
    gz,
    gpl,
    gains,
    hz,
    hpl,
    hrow,
    ag_s,
    ag_r,
    rs_ps,
    rs_pr,
    rs_cs,
    rs_cr,
    a2a_s,
    a2a_r,
    zg_s,
    zg_r,
    zr_s,
    zr_r,
    g_s,
    g_r,
    loc,
):
    c = lax.axis_index("ctx")
    z = lax.axis_index("fsdp")
    core = c % 2
    chip = c // 2
    cx = chip % 2
    cy = chip // 2
    slot = core * CHIPS + chip
    sib = c + 1 - 2 * core
    tiles = n1.shape[0] * n1.shape[1] // TILE
    rows = n1.shape[1]
    half = CHIPS * rows

    def chip_at(i):
        return ((cy + i // 2) % 2) * 2 + (cx + i % 2) % 2

    def rcopy(src, dst, ssem, rsem, to_c, to_z):
        return pltpu.make_async_remote_copy(
            src_ref=src,
            dst_ref=dst,
            send_sem=ssem,
            recv_sem=rsem,
            device_id=(to_c, to_z),
            device_id_type=MESH,
        )

    def loop(lo, hi, body):
        def step(i, carry):
            body(i)
            return carry

        lax.fori_loop(lo, hi, step, 0)

    spans = [r // (4 * CTX) * w for r, w in segment_shapes()]
    ends = [sum(spans[: i + 1]) for i in range(5)]
    tail = ends[3]
    fetch = [
        pltpu.make_async_copy(master_hbm.at[pl.ds(0, ends[1])], flat, loc.at[0]),
        pltpu.make_async_copy(master_hbm.at[pl.ds(tail, spans[4])], flat_gains, loc.at[3]),
        pltpu.make_async_copy(master_hbm.at[pl.ds(ends[2], spans[3])], flat_down, loc.at[4]),
        pltpu.make_async_copy(x_hbm.at[0], xg.at[slot], loc.at[1]),
        pltpu.make_async_copy(cot_hbm.at[0], cot.at[slot], loc.at[2]),
        pltpu.make_async_copy(order_hbm, order_ref, loc.at[5]),
        pltpu.make_async_copy(doc_hbm, doc_ref, loc.at[6]),
    ]
    for copy in fetch:
        copy.start()
    fetch_feed = pltpu.make_async_copy(
        master_hbm.at[pl.ds(ends[1], spans[2])], flat, loc.at[0]
    )
    barrier = pltpu.get_barrier_semaphore()

    def greet_plane(i):
        pl.semaphore_signal(
            barrier, inc=1, device_id=((c + i) % CTX, z), device_id_type=MESH
        )

    def greet_z(i):
        pl.semaphore_signal(
            barrier, inc=1, device_id=(c, (z + i) % 4), device_id_type=MESH
        )

    loop(1, CTX, greet_plane)
    loop(1, 4, greet_z)

    def to_lines(src, first, last):
        block = 128 * 128

        def one(i):
            lines[pl.ds(pl.multiple_of(first // 128 + i * 128, 128), 128), :] = src[
                pl.ds(pl.multiple_of(i * block, block), block)
            ].reshape(128, 128)

        loop(0, (last - first) // block, one)

    def qkv_group(j, part):
        return (GROUP * j + part) if part < GROUP else KEY_VALUE_HEADS * part + j

    def feed_group(j, part):
        per = HID // 128
        return j * per + part if part < per else CTX * per + j * per + part - per

    def line_rows(first, group, groups, count):
        return pl.ds(first // 128 + group, count, stride=groups)

    per_run = wq_in.shape[2]
    fetch[0].wait()
    fetch[1].wait()
    to_lines(flat, 0, ends[1])
    fetch_feed.start()
    for g in range(MODEL_WIDTH // 128):
        wo[z, :, g * 128 : (g + 1) * 128] = lines[
            line_rows(ends[0], g, MODEL_WIDTH // 128, wo.shape[1]), :
        ].astype(BF16)
    qkv_groups = CTX * PCOLS // 128
    for j in range(CTX):
        for part in range(PCOLS // 128):
            wq_in[part // 2, j, :, part % 2 * 128 : (part % 2 + 1) * 128] = lines[
                line_rows(0, qkv_group(j, part), qkv_groups, per_run), :
            ].astype(BF16)
    own_gains = flat_gains[...].reshape(1, spans[4]).astype(BF16).astype(F32)
    gains_in[...] = pltpu.roll(
        jnp.concatenate([own_gains, jnp.zeros((1, GAIN_WIDTH - spans[4]), F32)], axis=1),
        spans[4] * (4 * c + z),
        1,
    )

    fetch[2].wait()
    to_lines(flat_down, ends[2], ends[3])
    for g in range(MODEL_WIDTH // 128):
        wd[z, :, g * 128 : (g + 1) * 128] = lines[
            line_rows(ends[2], g, MODEL_WIDTH // 128, wd.shape[1]), :
        ].astype(BF16)
    pl.semaphore_wait(barrier, CTX - 1 + 4 - 1)

    mid = rows // 2
    XN, YN, ACROSS = 1, 2, 3
    whole, top, bottom = pl.ds(0, rows), pl.ds(0, mid), pl.ds(mid, mid)

    AG_SEM = (0, 1, 2, 3, 4, 5, 6, 0, 7, 7, 7)

    def ag_piece(n, buf, k):
        origin, part, to = (
            (0, whole, sib),
            (0, top, XN),
            (0, bottom, XN),
            (0, bottom, YN),
            (0, top, YN),
            (XN, top, YN),
            (YN, bottom, XN),
            (XN, whole, sib),
            (YN, whole, sib),
            (ACROSS, top, sib),
            (ACROSS, bottom, sib),
        )[k]
        there = buf.at[core * CHIPS + chip_at(origin), part]
        target = sib if to is sib else chip_at(to) * 2 + core
        return rcopy(there, there, ag_s.at[n], ag_r.at[n % 3, AG_SEM[k]], target, z)

    def ag_landed(n, buf, k):
        origin, part, own_core = (
            (0, whole, False),
            (XN, top, True),
            (XN, bottom, True),
            (YN, bottom, True),
            (YN, top, True),
            (ACROSS, top, True),
            (ACROSS, bottom, True),
            (XN, whole, False),
            (YN, whole, False),
            (ACROSS, top, False),
            (ACROSS, bottom, False),
        )[k]
        which = core if own_core else 1 - core
        there = buf.at[which * CHIPS + chip_at(origin), part]
        return rcopy(there, there, ag_s.at[n], ag_r.at[n % 3, AG_SEM[k]], sib, z)

    def ag_start(n, buf):
        for k in (1, 3, 2, 4, 0):
            ag_piece(n, buf, k).start()

    def ag_pass_near(n, buf):
        for landed, onward in ((1, 5), (3, 6), (2, 7), (4, 8)):
            ag_landed(n, buf, landed).wait_recv()
            ag_piece(n, buf, onward).start()

    def ag_pass_across(n, buf):
        for landed, onward in ((5, 9), (6, 10)):
            ag_landed(n, buf, landed).wait_recv()
            ag_piece(n, buf, onward).start()

    def ag_handed(n, buf, sem):
        two_rows = buf.at[pl.ds(0, 2)]
        rcopy(two_rows, two_rows, ag_s.at[n], ag_r.at[n % 3, sem], sib, z).wait_recv()

    def ag_finish_near(n, buf):
        ag_handed(n, buf, 0)

    def ag_finish(n, buf):
        ag_handed(n, buf, 7)

    def ag_drain(n, buf):
        seven = buf.at[pl.ds(0, 7)]
        rcopy(seven, seven, ag_s.at[n], ag_r.at[0, 0], sib, z).wait_send()

    def gathered_tiles(n, buf, body, between, before=None):
        ag_pass_near(n, buf)
        ag_finish_near(n, buf)
        if before is not None:
            before()
        loop(0, 2, lambda k: body(2 * k + cy))
        between()
        ag_pass_across(n, buf)
        ag_finish(n, buf)
        loop(0, 2, lambda k: body(2 * k + 1 - cy))

    wide = MODEL_WIDTH // 2

    def rs_pair(r, h):
        return rcopy(psnd.at[h], prcv.at[r % 2, h], rs_ps.at[h], rs_pr.at[r % 2, h], sib, z)

    def rs_chip(r, k):
        to = chip_at((XN, XN, YN, YN, YN, XN)[k]) * 2 + core
        return rcopy(csnd.at[k], crcv.at[r % 2, k], rs_cs.at[0], rs_cr.at[r % 2, k], to, z)

    def rs_give(r, part, h):
        if r > 0:
            rs_pair(r - 1, h).wait_send()
        psnd[h] = part(1 - core, h).astype(BF16).reshape(CHIPS, rows, wide)
        rs_pair(r, h).start()

    def rs_keep(r, part, h):
        own[h] = part(core, h).reshape(CHIPS, rows, wide)

    def pair_sum(r, h, i):
        return own[h, chip_at(i)] + prcv[r % 2, h, chip_at(i)].astype(F32)

    def rs_sent():
        rcopy(csnd, csnd, rs_cs.at[0], rs_cr.at[0, 0], sib, z).wait_send()

    def rs_send(r, h):
        rs_pair(r, h).wait_recv()
        if r > 0 and h == 0:
            rs_sent()
        csnd[2 * h] = pair_sum(r, h, ACROSS).astype(BF16)
        rs_chip(r, 2 * h).start()
        csnd[2 * h + 1] = pair_sum(r, h, (XN, YN)[h]).astype(BF16)
        rs_chip(r, 2 * h + 1).start()
        acc[r % 2, :, h * wide : (h + 1) * wide] = pair_sum(r, h, 0)

    def rs_begin(r, part):
        for h in range(2):
            rs_give(r, part, h)
        for h in range(2):
            rs_keep(r, part, h)
            rs_send(r, h)

    def rs_compute(r, part):
        for h in range(2):
            rs_give(r, part, h)
        for h in range(2):
            rs_keep(r, part, h)

    def rs_drain(r):
        for h in range(2):
            rs_pair(r, h).wait_send()
        rs_sent()

    def rs_relay(r):
        for h, second in ((0, YN), (1, XN)):
            rs_chip(r, 2 * h).wait_recv()
            csnd[4 + h] = (pair_sum(r, h, second) + crcv[r % 2, 2 * h].astype(F32)).astype(BF16)
            rs_chip(r, 4 + h).start()

    def rs_finish(r):
        halves = []
        for h in range(2):
            rs_chip(r, 2 * h + 1).wait_recv()
            rs_chip(r, 4 + h).wait_recv()
            halves.append(
                acc[r % 2, :, h * wide : (h + 1) * wide]
                + crcv[r % 2, 2 * h + 1].astype(F32)
                + crcv[r % 2, 4 + h].astype(F32)
            )
        return jnp.concatenate(halves, axis=1)

    A2A_SEM = (0, 2 * CTX - 2, 2 * CTX - 1, 2 * CTX, CTX - 1)

    PARTNERS = ((3, 0), (3, 1), (1, 0), (2, 0), (1, 1), (2, 1), (0, 1))

    def partner(i):
        chip_of, other = PARTNERS[i - 1]
        return chip_at(chip_of) * 2 + (1 - core if other else core)

    def a2a(n, src, dst_of, i, sem=0):
        to = partner(i)
        return rcopy(src.at[to], dst_of(c), a2a_s.at[n], a2a_r.at[A2A_SEM[n] + sem], to, z)

    def a2a_landed(n, dst_of, i):
        frm = partner(i)
        return rcopy(dst_of(frm), dst_of(frm), a2a_s.at[n], a2a_r.at[A2A_SEM[n] + i - 1], sib, z)

    def a2a_start(n, src, dst_of, apart=False):
        for i in range(1, CTX):
            a2a(n, src, dst_of, i, i - 1 if apart else 0).start()

    def a2a_half(n, src, dst_of, h):
        for i in range(1, CTX):
            pl.when(partner(i) // (CTX // 2) == h)(a2a(n, src, dst_of, i).start)

    def a2a_wait(n, dst):
        seven = dst.at[pl.ds(0, CTX - 1)]
        rcopy(seven, seven, a2a_s.at[n], a2a_r.at[A2A_SEM[n]], sib, z).wait_recv()

    def a2a_drain(n, src):
        seven = src.at[pl.ds(0, CTX - 1)]
        rcopy(seven, seven, a2a_s.at[n], a2a_r.at[A2A_SEM[n]], sib, z).wait_send()

    inner = (z == 1) | (z == 2)
    outer = jnp.logical_not(inner)
    far = 3 * (2 - z)

    def zg(n, of, j, to):
        return rcopy(of(j), of(j), zg_s.at[n], zg_r.at[n, j], c, to)

    def zg_own(n, of):
        return (
            (z < 3, zg(n, of, z, z + 1)),
            (z > 0, zg(n, of, z, z - 1)),
        )

    def zg_onward(n, of):
        return (
            zg(n, of, z - 1, z + 1),
            zg(n, of, z + 1, z - 1),
            zg(n, of, far, 3 * (z - 1)),
        )

    def zg_start(n, of, who=None):
        for there, copy in zg_own(n, of):
            pl.when(there if who is None else there & who)(copy.start)

    def zg_pass(n, of, k, when, j):
        def run():
            zg(n, of, j, z).wait_recv()
            zg_onward(n, of)[k].start()

        pl.when(when)(run)

    def zg_across(n, of):
        zg_pass(n, of, 0, z == 1, z - 1)
        zg_pass(n, of, 1, z == 2, z + 1)

    def zg_back(n, of):
        zg_pass(n, of, 1, z == 1, z + 1)
        zg_pass(n, of, 0, z == 2, z - 1)

    def zg_near(n, of):
        zg_across(n, of)
        zg_back(n, of)

    def zg_far(n, of):
        def run():
            zg(n, of, far, z).wait_recv()
            zg_onward(n, of)[2].start()

        pl.when(inner)(run)

    def zg_wait(n, of):
        def run():
            for i in (1, 2, 3):
                zg(n, of, (z + i) % 4, z).wait_recv()

        pl.when(outer)(run)

    def zg_drain(n, some):
        def sent(count):
            part = some(count)
            rcopy(part, part, zg_s.at[n], zg_r.at[n, 0], sib, z).wait_send()

        pl.when(inner)(lambda: sent(5))
        pl.when(outer)(lambda: sent(1))

    def zr(n, of, land, d, to, spot):
        return rcopy(of(d), land(spot), zr_s.at[n], zr_r.at[n, spot], c, to)

    def zr_add(n, of, land, d):
        rcopy(land(d), land(d), zr_s.at[n], zr_r.at[n, d], sib, z).wait_recv()
        mine = of(d)
        mine[...] = (mine[...].astype(F32) + land(d)[...].astype(F32)).astype(BF16)

    ENDS = (
        ((0, 3, 1, 3), (3, 0, 2, 0)),
        ((0, 2, 1, 2), (3, 1, 2, 1)),
        ((0, 1, 1, 1), (3, 2, 2, 4)),
    )
    FIRST = ((1, 3, 2, 3), (2, 0, 1, 0))
    SECOND = ((1, 2, 2, 2), (2, 1, 1, 4), (1, 0, 0, 4), (2, 3, 3, 3))

    def zr_send(n, of, land, k):
        for device, d, to, spot in ENDS[k]:
            pl.when(z == device)(zr(n, of, land, d, to, spot).start)

    def zr_start(*items, part=range(3)):
        for k in part:
            for item in items:
                zr_send(*item, k)

    def zr_pass(n, of, land, steps):
        for device, d, to, spot in steps:

            def run(d=d, to=to, spot=spot):
                zr_add(n, of, land, d)
                zr(n, of, land, d, to, spot).start()

            pl.when(z == device)(run)

    def zr_first(n, of, land):
        zr_pass(n, of, land, FIRST)

    def zr_second(n, of, land):
        zr_pass(n, of, land, SECOND)

    def zr_finish(n, of, land):
        def landed(spot):
            rcopy(land(spot), land(spot), zr_s.at[n], zr_r.at[n, spot], sib, z).wait_recv()

        pl.when(z > 0)(lambda: landed(z))
        pl.when(z < 3)(lambda: landed(4))
        return of(z)[...].astype(F32) + land(z)[...].astype(F32) + land(4)[...].astype(F32)

    def row_z(n, src, land, i):
        return rcopy(src, land.at[z], g_s.at[n, 0], g_r.at[n, 0], c, (z + i) % 4)

    def row_plane(n, src, land, i):
        return rcopy(src, land.at[c], g_s.at[n, 1], g_r.at[n, 1], (c + i) % CTX, z)

    def rows_of(n, land, k):
        others = land.at[pl.ds(0, (3, CTX - 1)[k])]
        return rcopy(others, others, g_s.at[n, k], g_r.at[n, k], sib, z)

    def row_z_wait(n, land):
        rows_of(n, land, 0).wait_recv()

    def row_plane_wait(n, land):
        rows_of(n, land, 1).wait_recv()

    def halves(ref):
        half_of = lambda h: lambda j: ref.at[pl.ds(h * (CTX // 2), CTX // 2), j]
        return half_of(0), half_of(1)

    def land_halves(ref):
        half_of = lambda h: lambda j: ref.at[j, pl.ds(h * (CTX // 2), CTX // 2)]
        return half_of(0), half_of(1)

    wq_at = lambda j: wq.at[0, j, z]
    wkv_at = lambda j: wq.at[1, j, z]
    wgu_at = lambda j: wgu.at[j, z]
    g_q = (0, lambda j: wq.at[0, :, j])
    g_kv = (5, lambda j: wq.at[1, :, j])
    g_o = (1, lambda j: wo.at[j])
    g_gu1, g_gu2 = ((2 + h, of) for h, of in enumerate(halves(wgu)))
    g_d = (4, lambda j: wd.at[j])
    def column_half(ref, h):
        return lambda j: ref.at[j, :, pl.ds(h * WIDE, WIDE)]

    r_d1, r_d2 = (
        (6 * h, column_half(gwd, h), column_half(lwd, h)) for h in range(2)
    )
    r_gu1, r_gu2 = (
        (1 + h, *both) for h, both in enumerate(zip(halves(gwgu), land_halves(lwgu)))
    )
    r_o = (3, lambda j: gwo.at[j], lambda j: lwo.at[j])
    r_q1, r_q2 = (
        (4 + h, *both) for h, both in enumerate(zip(halves(gwq), land_halves(lwq)))
    )

    lines[pl.ds(tail // 128, 8), :] = jnp.zeros((8, 128), F32)
    gz[z] = gains_in[...]
    loop(1, 4, lambda i: row_z(0, gains_in, gz, i).start())
    a2a_start(0, wq_in.at[0], wq_at, apart=True)
    a2a_start(4, wq_in.at[1], wkv_at, apart=True)
    zg_start(*g_o)

    def share(part, frm):
        there = wq.at[part, frm, z]
        n = 5 * part
        for to, here in ((z + 1, z < 3), (z - 1, z > 0)):
            pl.when(here)(rcopy(there, there, zg_s.at[n], zg_r.at[n, z], c, to).start)

    def shares_landed(part, n, at):
        for i in (7, 3, 4, 5, 6, 1, 2):
            a2a_landed(n, at, i).wait_recv()
            share(part, partner(i))

    for part in range(2):
        wq[part, c, z] = wq_in[part, c]
        share(part, c)
    fetch_feed.wait()
    to_lines(flat, ends[1], ends[2])
    feed_groups = 2 * FEED_WIDTH // 128
    for j in range(CTX):
        for part in range(2 * HID // 128):
            wgu_in[j, :, part * 128 : (part + 1) * 128] = lines[
                line_rows(ends[1], feed_group(j, part), feed_groups, per_run), :
            ].astype(BF16)
    fetch[3].wait()
    ag_start(0, xg)
    shares_landed(0, 0, wq_at)
    shares_landed(1, 4, wkv_at)
    row_z_wait(0, gz)
    gpl[c] = jnp.sum(gz[...], axis=0)
    loop(1, CTX, lambda i: row_plane(0, gpl.at[c], gpl, i).start())
    wgu[c, z] = wgu_in[c]
    for copy in fetch[4:]:
        copy.wait()
    doc_ends = [doc_ref[0, 0]]
    for j in range(1, doc_ref.shape[1] - 1):
        doc_ends.append(doc_ends[-1] + doc_ref[0, j])

    def doc_start(pos):
        start = jnp.zeros_like(pos)
        for end in doc_ends:
            start = jnp.where(pos >= end, end, start)
        return start

    def tables(s):
        first = 2 * (2 * (s % CHIPS) + s // CHIPS)
        lead = order_ref[first] * STRETCH
        trail = order_ref[first + 1] * STRETCH - STRETCH
        at = pl.ds(pl.multiple_of(s * rows, rows), rows)

        def positions(shape, axis):
            index = lax.broadcasted_iota(jnp.int32, shape, axis)
            return index + jnp.where(index < STRETCH, lead, trail)

        across = positions((1, rows), 1)
        qpos_ref[:, at] = across
        qstart_ref[:, at] = doc_start(across)
        down = positions((rows, HEAD_SIZE), 0)
        kpos_ref[at, :] = down
        lane = lax.broadcasted_iota(jnp.int32, (1, HEAD_SIZE), 1)
        upper = lane >= HEAD_SIZE // 2
        index = jnp.where(upper, lane - HEAD_SIZE // 2, lane).astype(F32)
        frequency = jnp.exp(index * (-2.0 / HEAD_SIZE * math.log(ROPE_BASE)))
        angles = (down - doc_start(down)).astype(F32) * frequency
        sine = jnp.sin(angles)
        cos_ref[at, :] = jnp.cos(angles)
        sin_ref[at, :] = jnp.where(upper, sine, -sine)

    loop(0, CTX // 2, tables)
    for land in (lwq, lwo, lwgu, lwd):
        for end, spot in ((0, 0), (3, 4)):

            def blank(land=land, spot=spot):
                land[spot] = jnp.zeros(land.shape[1:], BF16)

            pl.when(z == end)(blank)
    zg_near(*g_q)
    loop(CTX // 2, CTX, tables)
    ag_pass_near(0, xg)
    zg_near(*g_kv)
    ag_finish_near(0, xg)
    ag_pass_across(0, xg)
    zg_far(*g_q)
    ag_finish(0, xg)
    a2a_start(1, wgu_in, wgu_at)
    ag_start(1, cot)
    zg_far(*g_kv)
    zg_near(*g_o)
    row_plane_wait(0, gpl)
    gains[...] = jnp.sum(gpl[...], axis=0)
    g_attn = gains[:, :MODEL_WIDTH]
    def normed(t):
        at = pl.ds(t * (TILE // rows), TILE // rows)
        x_tile = xg[at].astype(F32)
        x_scale = lax.rsqrt(jnp.mean(x_tile * x_tile, axis=-1, keepdims=True) + NORM_EPS)
        n1[at] = (x_tile * x_scale * g_attn.reshape(1, 1, MODEL_WIDTH)).astype(BF16)

    loop(0, tiles, normed)
    x_own[...] = xg[slot]
    g_query = gains[:, 2 * MODEL_WIDTH : 2 * MODEL_WIDTH + HEAD_SIZE]
    g_key = gains[:, 2 * MODEL_WIDTH + HEAD_SIZE :]

    def tile_rows(t):
        return pl.ds(pl.multiple_of(t * TILE, TILE), TILE)

    def two(buf, t):
        return buf[pl.ds(t * (TILE // rows), TILE // rows)].reshape(TILE, buf.shape[-1])

    def turned(v):
        return pltpu.roll(v, HEAD_SIZE // 2, 1)

    def normed_rope(raw, gain, at):
        scale = lax.rsqrt(jnp.mean(raw * raw, axis=-1, keepdims=True) + NORM_EPS)
        y = raw * scale * gain
        return y * cos_ref[at, :] + turned(y) * sin_ref[at, :]

    def project_queries(t):
        at = tile_rows(t)
        out = dot(two(n1, t), wq[0].reshape(MODEL_WIDTH, QCOLS))
        for h in range(GROUP):
            raw = out[:, h * HEAD_SIZE : (h + 1) * HEAD_SIZE]
            qraw[at, h * HEAD_SIZE : (h + 1) * HEAD_SIZE] = raw
            q_s[h, at, :] = normed_rope(raw, g_query, at).astype(BF16)

    def project_pairs(t):
        at = tile_rows(t)
        both = dot(two(n1, t), wq[1].reshape(MODEL_WIDTH, 2 * HEAD_SIZE))
        raw = both[:, :HEAD_SIZE]
        kraw[at, :] = raw
        keys = normed_rope(raw, g_key, at)
        values = both[:, HEAD_SIZE:]
        k_s[at, :] = keys.astype(BF16)
        v_s[at, :] = values.astype(BF16)
        kt_s[:, at] = keys.T.astype(BF16)
        vt_s[:, at] = values.T.astype(BF16)

    zg_wait(*g_q)
    loop(0, tiles, project_queries)
    pl.when(outer)(lambda: a2a_wait(1, wgu_in))
    zg_start(*g_gu1, outer)
    zg_start(*g_gu2, outer)
    zg_start(*g_d, outer)
    zg_wait(*g_kv)
    loop(0, tiles, project_pairs)
    ag_drain(0, xg)
    zg_far(*g_o)
    pl.when(inner)(lambda: a2a_wait(1, wgu_in))
    zg_start(*g_gu1, inner)
    zg_start(*g_gu2, inner)
    def n_cols(n):
        return pl.ds(pl.multiple_of(n * WIDE, WIDE), WIDE)

    def half_rows(which):
        return pl.ds(pl.multiple_of(which * half, half), half)

    def half_slots(buf, which):
        return buf[pl.ds(which * CHIPS, CHIPS)].reshape(half, buf.shape[-1])

    def out_part(which, n):
        return dot(
            attn_low[half_rows(which), :], wo[:, :, n_cols(n)].reshape(QCOLS, WIDE)
        )

    scale = HEAD_SIZE ** (-0.5)

    def attend(t):
        at = half_rows(t)
        kpos = jnp.concatenate([kpos_ref[...]] * (half // HEAD_SIZE), axis=1)
        kept = (kpos <= qpos_ref[:, at]) & (kpos >= qstart_ref[:, at])
        for h in range(GROUP):
            scores = jnp.where(kept, dot(k_s[...], q_s[h, at, :], NT) * scale, MASKED)
            weights = jnp.exp(scores - jnp.max(scores, axis=0, keepdims=True))
            low = weights.astype(BF16)
            probs[h, t] = low
            share = 1.0 / jnp.sum(weights, axis=0, keepdims=True)
            shares[h, :, at] = share
            mixed = dot(vt_s[...], low) * share
            attn[h, :, at] = mixed
            attn_low[at, h * HEAD_SIZE : (h + 1) * HEAD_SIZE] = mixed.T.astype(BF16)

    attend(1 - core)
    zg_across(*g_gu1)
    zg_wait(*g_o)
    rs_give(0, out_part, 0)
    rs_give(0, out_part, 1)
    ag_pass_near(1, cot)
    attend(core)
    zg_back(*g_gu1)
    for h in range(2):
        rs_keep(0, out_part, h)
        rs_send(0, h)
    zg_across(*g_gu2)
    zg_back(*g_gu2)
    rs_relay(0)
    ag_pass_across(1, cot)
    zg_far(*g_gu1)
    resid = x_own[...].astype(F32) + rs_finish(0)
    resid_s[...] = resid
    g_mlp = gains[:, MODEL_WIDTH : 2 * MODEL_WIDTH]
    s_two = lax.rsqrt(jnp.mean(resid * resid, axis=-1, keepdims=True) + NORM_EPS)
    n2[slot] = (resid * s_two * g_mlp).astype(BF16)
    ag_start(2, n2)
    ag_finish_near(1, cot)
    ag_finish(1, cot)
    zg_far(*g_gu2)
    zg_start(*g_d, inner)
    zg_across(*g_d)
    def feed(t):
        at = tile_rows(t)
        both = dot(two(n2, t), wgu[...].reshape(MODEL_WIDTH, 2 * HID))
        gate, up = both[:, :HID], both[:, HID:]
        sig = 1.0 / (1.0 + jnp.exp(-gate))
        silu = gate * sig
        hidden[at, :] = (silu * up).astype(BF16)
        ggu[at, :HID] = (up * sig * (1.0 + gate * (1.0 - sig))).astype(BF16)
        ggu[at, HID:] = silu.astype(BF16)

    def wgu_there():
        zg_wait(*g_gu1)
        zg_wait(*g_gu2)

    def pass_down():
        zg_back(*g_d)

    gathered_tiles(2, n2, feed, pass_down, wgu_there)
    zg_far(*g_d)

    def down_grad(n):
        there = cot[:, :, n_cols(n)].reshape(2 * half, WIDE)
        gwd[:, :, n_cols(n)] = (
            dot(hidden[...], there, TN).astype(BF16).reshape(4, HID // 4, WIDE)
        )

    down_grad(0)
    zr_start(r_d1)
    down_grad(1)
    zr_start(r_d2)
    zg_wait(*g_d)

    def feed_back(t):
        at = half_rows(t)
        ghid = dot(half_slots(cot, t), wd[...].reshape(HID, MODEL_WIDTH), NT)
        ggu[at, :HID] = (ghid * ggu[at, :HID].astype(F32)).astype(BF16)
        ggu[at, HID:] = (ghid * ggu[at, HID:].astype(F32)).astype(BF16)

    for t in range(2):
        feed_back(t)

    def back_two_part(which, n):
        per = MODEL_WIDTH // CTX
        there = wgu[pl.ds(n * (WIDE // per), WIDE // per)].reshape(WIDE, 2 * HID)
        return dot(ggu[half_rows(which), :], there, NT)

    rs_begin(1, back_two_part)

    def gate_up_grad(n):
        per = MODEL_WIDTH // CTX
        there = n2[:, :, n_cols(n)].reshape(2 * half, WIDE)
        gwgu[pl.ds(n * (WIDE // per), WIDE // per)] = (
            dot(there, ggu[...], TN)
            .astype(BF16)
            .reshape(WIDE // per, 4, per // 4, 2 * HID)
        )

    gate_up_grad(0)
    zr_start(r_gu1)
    gate_up_grad(1)
    zr_start(r_gu2)
    zr_first(*r_d1)
    zr_first(*r_d2)
    rs_relay(1)


    def norm_back(values, grads, gain):
        factor = lax.rsqrt(jnp.mean(values * values, axis=-1, keepdims=True) + NORM_EPS)
        unit = values * factor
        scaled = grads * gain
        inner = jnp.mean(scaled * unit, axis=-1, keepdims=True)
        return factor * (scaled - unit * inner), jnp.sum(grads * unit, axis=0, keepdims=True)

    back, terms = norm_back(resid_s[...], rs_finish(1), g_mlp)
    hrow[:, MODEL_WIDTH : 2 * MODEL_WIDTH] = terms
    gresid = cot[slot].astype(F32) + back
    gresid_s[...] = gresid
    gb = xg
    gb[slot] = gresid.astype(BF16)
    def down_part(which, n):
        return dot(hidden[half_rows(which), :], wd[:, :, n_cols(n)].reshape(HID, WIDE))

    ag_start(3, gb)
    rs_compute(2, down_part)
    zr_second(*r_d1)
    zr_second(*r_d2)

    def attn_grad(t):
        gattn[tile_rows(t), :] = dot(
            two(gb, t), wo[...].reshape(QCOLS, MODEL_WIDTH), NT
        ).astype(BF16)

    gathered_tiles(3, gb, attn_grad, lambda: zr_first(*r_gu1))
    rs_send(2, 0)
    rs_send(2, 1)

    def out_grad(n):
        there = gb[:, :, n_cols(n)].reshape(2 * half, WIDE)
        gwo[:, :, n_cols(n)] = (
            dot(attn_low[...], there, TN).astype(BF16).reshape(4, QCOLS // 4, WIDE)
        )

    loop(0, MODEL_WIDTH // WIDE, out_grad)
    zr_start(r_o, part=(0, 1))

    dk_s[...] = jnp.zeros_like(dk_s)
    dv_s[...] = jnp.zeros_like(dv_s)

    hrow[:, 2 * MODEL_WIDTH :] = jnp.zeros((1, 2 * HEAD_SIZE), F32)

    def head_back(raw, grads, at, gain):
        grads = grads * scale
        grads = grads * cos_ref[at, :] - turned(grads) * sin_ref[at, :]
        return norm_back(raw, grads, gain)

    q_terms = pl.ds(2 * MODEL_WIDTH, HEAD_SIZE)
    k_terms = pl.ds(2 * MODEL_WIDTH + HEAD_SIZE, HEAD_SIZE)

    def attend_back(t):
        at = pl.ds(t * half, half)
        for h in range(GROUP):
            head = slice(h * HEAD_SIZE, (h + 1) * HEAD_SIZE)
            grads = gattn[at, head]
            turned_grads = grads.astype(F32).T
            share = shares[h, :, at]
            delta = jnp.sum(turned_grads * attn[h, :, at], axis=0, keepdims=True)
            low = probs[h, t]
            gprobs = dot(v_s[...], grads, NT)
            gscores = (low.astype(F32) * ((gprobs - delta) * share)).astype(BF16)
            dv_s[...] += dot(low, (turned_grads * share).T.astype(BF16))
            dk_s[...] += dot(gscores, q_s[h, at, :])
            back, terms = head_back(qraw[at, head], dot(kt_s[...], gscores).T, at, g_query)
            gp[at, head] = back.astype(BF16)
            hrow[:, q_terms] += terms

    attend_back(0)
    zr_second(*r_gu1)
    attend_back(1)
    rs_relay(2)
    zr_first(*r_gu2)

    def project_back(t):
        at = tile_rows(t)
        back, terms = head_back(kraw[at, :], dk_s[at, :], at, g_key)
        gp[at, QCOLS : QCOLS + HEAD_SIZE] = back.astype(BF16)
        hrow[:, k_terms] += terms
        gp[at, QCOLS + HEAD_SIZE :] = dv_s[at, :].astype(BF16)

    loop(0, tiles, project_back)

    def qkv_grad(n):
        per = MODEL_WIDTH // CTX
        there = n1[:, :, n_cols(n)].reshape(2 * half, WIDE)
        gwq[pl.ds(n * (WIDE // per), WIDE // per)] = (
            dot(there, gp[...], TN)
            .astype(BF16)
            .reshape(WIDE // per, 4, per // 4, PCOLS)
        )

    qkv_grad(0)
    qkv_grad(1)
    zr_start(r_q1, r_q2)
    def back_one_part(which, n):
        per = MODEL_WIDTH // CTX
        at = pl.ds(n * (WIDE // per), WIDE // per)
        rows_at = half_rows(which)
        return dot(gp[rows_at, :QCOLS], wq[0, at].reshape(WIDE, QCOLS), NT) + dot(
            gp[rows_at, QCOLS:], wq[1, at].reshape(WIDE, 2 * HEAD_SIZE), NT
        )

    rs_begin(3, back_one_part)
    zr_second(*r_gu2)
    zr_first(*r_o)
    rs_relay(3)
    zr_second(*r_o)
    zr_first(*r_q1)
    zr_first(*r_q2)
    for h, item in enumerate((r_d1, r_d2)):
        sum_d = zr_finish(*item)
        for g in range(WIDE // 128):
            at = line_rows(ends[2], h * (WIDE // 128) + g, MODEL_WIDTH // 128, HID // 4)
            lines[at, :] = sum_d[:, g * 128 : (g + 1) * 128]
    first_half, second_half = pl.ds(0, CTX // 2), pl.ds(CTX // 2, CTX // 2)
    asg[first_half] = zr_finish(*r_gu1).astype(BF16)
    asg[second_half] = zr_finish(*r_gu2).astype(BF16)
    arg_[c] = asg[c]
    zr_second(*r_q1)
    back, terms = norm_back(x_own[...].astype(F32), rs_finish(3), gains[:, :MODEL_WIDTH])
    xgrad_ref[...] = (gresid_s[...] + back).astype(BF16)
    store_xgrad = pltpu.make_async_copy(xgrad_ref, xgrad_hbm.at[0], loc.at[5])
    store_xgrad.start()
    hrow[:, :MODEL_WIDTH] = terms
    hpl[c] = hrow[...]
    loop(1, CTX, lambda i: row_plane(1, hpl.at[c], hpl, i).start())
    zr_start(r_o, part=(2,))
    arg_at = lambda j: arg_.at[j]
    a2a_start(2, asg, arg_at)
    zr_second(*r_q2)
    out_ref[...] = (resid_s[...] + rs_finish(2)).astype(BF16)
    store_out = pltpu.make_async_copy(out_ref, out_hbm.at[0], loc.at[6])
    store_out.start()
    row_plane_wait(1, hpl)
    hz[z] = jnp.sum(hpl[...], axis=0)
    loop(1, 4, lambda i: row_z(1, hz.at[z], hz, i).start())
    arq_at = lambda j: arq.at[j]
    asq[first_half] = zr_finish(*r_q1).astype(BF16)
    a2a_half(3, asq, arq_at, 0)
    asq[second_half] = zr_finish(*r_q2).astype(BF16)
    a2a_half(3, asq, arq_at, 1)
    arq[c] = asq[c]
    a2a_wait(2, arg_)
    for j in range(CTX):
        for part in range(2 * HID // 128):
            lines[line_rows(ends[1], feed_group(j, part), feed_groups, per_run), :] = arg_[
                j, :, part * 128 : (part + 1) * 128
            ].astype(F32)
    a2a_wait(3, arq)
    for j in range(CTX):
        for part in range(PCOLS // 128):
            lines[line_rows(0, qkv_group(j, part), qkv_groups, per_run), :] = arq[
                j, :, part * 128 : (part + 1) * 128
            ].astype(F32)
    split = ends[0] // 128, ends[1] // 128
    stores = [
        pltpu.make_async_copy(
            lines.at[pl.ds(first, last - first)], lin_ref.at[pl.ds(first, last - first)], loc.at[k]
        )
        for k, (first, last) in enumerate(
            ((0, split[0]), (split[1], tail // 128), split, (tail // 128, tail // 128 + 8))
        )
    ]
    stores[0].start()
    stores[1].start()
    sum_o = zr_finish(*r_o)
    for g in range(MODEL_WIDTH // 128):
        lines[line_rows(ends[0], g, MODEL_WIDTH // 128, sum_o.shape[0]), :] = sum_o[
            :, g * 128 : (g + 1) * 128
        ]
    stores[2].start()
    row_z_wait(1, hz)
    total = jnp.sum(hz[...], axis=0)
    lines[pl.ds(tail // 128, 1), :] = pltpu.roll(
        total, GAIN_WIDTH - spans[4] * (4 * c + z), 1
    )[:, :128]
    stores[3].start()

    for n, buf in ((1, cot), (2, n2), (3, gb)):
        ag_drain(n, buf)
    rs_drain(3)
    a2a_drain(0, wq_in.at[0])
    a2a_drain(4, wq_in.at[1])
    a2a_drain(1, wgu_in)
    a2a_drain(2, asg)
    a2a_drain(3, asq)
    first_four = pl.ds(0, CTX // 2)
    for n, some in (
        (0, lambda count: lwq.at[pl.ds(0, count), first_four]),
        (5, lambda count: lwq.at[pl.ds(0, count), first_four]),
        (1, lambda count: lwo.at[pl.ds(0, count)]),
        (2, lambda count: lwgu.at[pl.ds(0, count), first_four]),
        (3, lambda count: lwgu.at[pl.ds(0, count), first_four]),
        (4, lambda count: lwd.at[pl.ds(0, count)]),
    ):
        zg_drain(n, some)
    three = pl.ds(0, 3)
    for n, part in (
        (0, lwd.at[three, :, pl.ds(0, WIDE)]),
        (6, lwd.at[three, :, pl.ds(WIDE, WIDE)]),
        (1, lwgu.at[three, first_four]),
        (2, lwgu.at[three, first_four]),
        (3, lwo.at[three]),
        (4, lwq.at[three, first_four]),
        (5, lwq.at[three, first_four]),
    ):
        rcopy(part, part, zr_s.at[n], zr_r.at[n, 0], sib, z).wait_send()
    for n, lands in enumerate(((gz, gpl), (hz, hpl))):
        for k, land in enumerate(lands):
            rows_of(n, land, k).wait_send()
    for copy in (store_out, store_xgrad, *stores):
        copy.wait()


def layer_call(tokens, cotangent, stretch_order, doc_lengths, master):
    _, rows, width = tokens.shape
    length = CTX * rows
    tiles = length // TILE
    per = width // CTX // 4
    entries = master.shape[0] // 1024 * 1024
    vm = pltpu.VMEM
    dma = pltpu.SemaphoreType.DMA
    shape = jax.ShapeDtypeStruct
    full = vm((CTX, rows, width), BF16)
    scratch = [
        pltpu.SMEM(stretch_order.shape, jnp.int32),
        pltpu.SMEM(doc_lengths.shape, jnp.int32),
        vm((rows, width), BF16),
        vm((rows, width), BF16),
        vm((width * 4 * width // 32 + 2 * width * width // 32,), F32),
        vm((FEED_WIDTH * width // 32,), F32),
        vm((master.shape[0] - entries,), F32),
        vm((entries // 128 + 8, 128), F32),
        vm((2, CTX, per, QCOLS), BF16),
        vm((CTX, per, 2 * HID), BF16),
        vm((1, GAIN_WIDTH), F32),
        vm((length, HEAD_SIZE), F32),
        vm((length, HEAD_SIZE), F32),
        vm((length, HEAD_SIZE), jnp.int32),
        vm((1, length), jnp.int32),
        vm((1, length), jnp.int32),
        full,
        full,
        full,
        full,
        vm((rows, width), BF16),
        vm((2, CTX, 4, per, QCOLS), BF16),
        vm((4, QCOLS // 4, width), BF16),
        vm((CTX, 4, per, 2 * HID), BF16),
        vm((4, HID // 4, width), BF16),
        vm((length, QCOLS), F32),
        vm((length, HEAD_SIZE), F32),
        vm((GROUP, length, HEAD_SIZE), BF16),
        vm((length, HEAD_SIZE), BF16),
        vm((length, HEAD_SIZE), BF16),
        vm((HEAD_SIZE, length), BF16),
        vm((HEAD_SIZE, length), BF16),
        vm((GROUP, 2, length, length // 2), BF16),
        vm((GROUP, HEAD_SIZE, length), F32),
        vm((GROUP, 1, length), F32),
        vm((length, QCOLS), BF16),
        vm((length, HID), BF16),
        vm((length, 2 * HID), BF16),
        vm((length, QCOLS), BF16),
        vm((length, HEAD_SIZE), F32),
        vm((length, HEAD_SIZE), F32),
        vm((length, PCOLS), BF16),
        vm((2, CHIPS, rows, width // 2), BF16),
        vm((2, 2, CHIPS, rows, width // 2), BF16),
        vm((6, rows, width // 2), BF16),
        vm((2, 6, rows, width // 2), BF16),
        vm((2, CHIPS, rows, width // 2), F32),
        vm((2, rows, width), F32),
        vm((rows, width), F32),
        vm((rows, width), F32),
        vm((CTX, 4, per, PCOLS), BF16),
        vm((4, QCOLS // 4, width), BF16),
        vm((CTX, 4, per, 2 * HID), BF16),
        vm((4, HID // 4, width), BF16),
        vm((5, CTX, per, PCOLS), BF16),
        vm((5, QCOLS // 4, width), BF16),
        vm((5, CTX, per, 2 * HID), BF16),
        vm((5, HID // 4, width), BF16),
        vm((CTX, per, PCOLS), BF16),
        vm((CTX, per, 2 * HID), BF16),
        vm((CTX, per, PCOLS), BF16),
        vm((CTX, per, 2 * HID), BF16),
        vm((4, 1, GAIN_WIDTH), F32),
        vm((CTX, 1, GAIN_WIDTH), F32),
        vm((1, GAIN_WIDTH), F32),
        vm((4, 1, GAIN_WIDTH), F32),
        vm((CTX, 1, GAIN_WIDTH), F32),
        vm((1, GAIN_WIDTH), F32),
        dma((4,)),
        dma((3, 8)),
        dma((2,)),
        dma((2, 2)),
        dma((1,)),
        dma((2, 6)),
        dma((5,)),
        dma((2 * CTX + 1,)),
        dma((6,)),
        dma((6, 4)),
        dma((7,)),
        dma((7, 5)),
        dma((2, 2)),
        dma((2, 2)),
        dma((8,)),
    ]
    anywhere = pl.BlockSpec(memory_space=pl.ANY)
    return pl.pallas_call(
        layer_kernel,
        out_shape=(
            shape((1, rows, width), BF16),
            shape((1, rows, width), BF16),
            shape((entries // 128 + 8, 128), F32),
        ),
        in_specs=[anywhere] * 5,
        out_specs=[anywhere] * 3,
        scratch_shapes=scratch,
        compiler_params=pltpu.CompilerParams(
            collective_id=1, has_side_effects=True, vmem_limit_bytes=63 << 20
        ),
        name="layer",
    )(stretch_order, doc_lengths, tokens, cotangent, master)


def local_planes(tokens, cotangent, stretch_order, doc_lengths, master, first_moment, second_moment):
    shards = lax.axis_size("ctx") * lax.axis_size("fsdp")
    length = tokens.shape[1] * lax.axis_size("ctx")
    out, xgrad, lines = layer_call(
        tokens, cotangent, stretch_order, doc_lengths, master
    )
    return adam_call(out, xgrad, lines, master, first_moment, second_moment, shards, length)


def adam_kernel(
    spans,
    settings,
    out_hbm,
    xgrad_hbm,
    grad_hbm,
    master_hbm,
    first_hbm,
    second_hbm,
    out_to,
    xgrad_to,
    master_to,
    first_to,
    second_to,
    out,
    xgrad,
    grad,
    master,
    first,
    second,
    sems,
):
    held = (grad, first, second, master, out, xgrad)
    fetch = [
        pltpu.make_async_copy(src, dst, sems.at[0, k])
        for k, (src, dst) in enumerate(
            zip((grad_hbm, first_hbm, second_hbm, master_hbm, out_hbm, xgrad_hbm), held)
        )
    ]
    store = [
        pltpu.make_async_copy(src, dst, sems.at[1, k])
        for k, (src, dst) in enumerate(
            zip(held[1:], (first_to, second_to, master_to, out_to, xgrad_to))
        )
    ]
    for copy in fetch:
        copy.start()

    def each(body):
        begin = 0
        for k, span in enumerate(spans[:-1]):
            block = span // -(-span // 65536)

            def step(i, carry, begin=begin, k=k, block=block):
                at = pl.ds(pl.multiple_of(begin + i * block, block), block)
                line = pl.ds(pl.multiple_of(begin // 128 + i * (block // 128), 8), block // 128)
                body(at, (block // 128, 128), grad[line, :], k)
                return carry

            lax.fori_loop(0, span // block, step, 0)
            begin += span
        last = spans[-1]
        body(pl.ds(begin, last), (1, last), grad[pl.ds(begin // 128, 1), :last], len(spans) - 1)

    def step_first(at, shape, g, k):
        new = BETA_ONE * first[at].reshape(shape) + (1.0 - BETA_ONE) * g
        first[at] = new.reshape(-1)

    def step_second(at, shape, g, k):
        new = BETA_TWO * second[at].reshape(shape) + (1.0 - BETA_TWO) * g * g
        second[at] = new.reshape(-1)

    def step_master(at, shape, g, k):
        rate, decay = settings[k]
        old = master[at].reshape(shape)
        mean = first[at].reshape(shape) * (1.0 / (1.0 - BETA_ONE**STEP))
        root = jnp.sqrt(second[at].reshape(shape) * (1.0 / (1.0 - BETA_TWO**STEP)))
        new = old - rate * (mean / (root + ADAM_EPS) + decay * old)
        master[at] = new.reshape(-1)

    fetch[0].wait()
    for k, body in enumerate((step_first, step_second, step_master)):
        fetch[k + 1].wait()
        each(body)
        store[k].start()
        if k == 1:
            for j in (4, 5):
                fetch[j].wait()
                store[j - 1].start()
    for copy in store:
        copy.wait()


def adam_call(out, xgrad, lines, master, first_moment, second_moment, shards, length):
    spans = [r // shards * w for r, w in segment_shapes()]
    shape = lambda v: jax.ShapeDtypeStruct(v.shape, v.dtype)
    operands = (out, xgrad, lines, master, first_moment, second_moment)
    results = (out, xgrad, master, first_moment, second_moment)
    anywhere = pl.BlockSpec(memory_space=pl.ANY)
    return pl.pallas_call(
        functools.partial(adam_kernel, spans, step_settings(length)),
        out_shape=[shape(v) for v in results],
        in_specs=[anywhere] * 6,
        out_specs=[anywhere] * 5,
        scratch_shapes=[pltpu.VMEM(v.shape, v.dtype) for v in operands]
        + [pltpu.SemaphoreType.DMA((2, 6))],
        compiler_params=pltpu.CompilerParams(vmem_limit_bytes=63 << 20),
        name="adam",
    )(*operands)


def step_settings(length):
    return [
        (MODEL_WIDTH ** (-0.5), DECAY_RATE),
        ((length / (3.0 * QUERY_HEADS * HEAD_SIZE)) ** 0.5, DECAY_RATE),
        (MODEL_WIDTH ** (-0.5), DECAY_RATE),
        (FEED_WIDTH ** (-0.5), DECAY_RATE),
        (0.2, 0.0),
    ]


def rates(shards, length):
    settings = step_settings(length)
    spans = [r // shards * w for r, w in segment_shapes()]
    index = lax.iota(jnp.int32, sum(spans))
    step_rate = jnp.full(index.shape, settings[0][0], F32)
    decay_value = jnp.full(index.shape, settings[0][1], F32)
    first = 0
    for span, (step, decay) in zip(spans, settings):
        step_rate = jnp.where(index >= first, step, step_rate)
        decay_value = jnp.where(index >= first, decay, decay_value)
        first += span
    return step_rate, decay_value


def adam(grad, master, first_moment, second_moment, shards, length):
    step_rate, decay_value = rates(shards, length)
    new_first = BETA_ONE * first_moment + (1.0 - BETA_ONE) * grad
    new_second = BETA_TWO * second_moment + (1.0 - BETA_TWO) * grad * grad
    normalized = (
        new_first
        / (1.0 - BETA_ONE**STEP)
        / (jnp.sqrt(new_second / (1.0 - BETA_TWO**STEP)) + ADAM_EPS)
    )
    new_master = master - step_rate * (normalized + decay_value * master)
    return new_master, new_first, new_second


def solution(mesh):
    placed = (
        P("fsdp", "ctx", None),
        P("fsdp", "ctx", None),
        P(),
        P("fsdp", None),
        P(("ctx", "fsdp")),
        P(("ctx", "fsdp")),
        P(("ctx", "fsdp")),
    )
    plane = mesh.shape["ctx"] == CTX == KEY_VALUE_HEADS and mesh.shape["fsdp"] == 4
    return jax.shard_map(
        local_planes if plane else local,
        mesh=mesh,
        in_specs=placed,
        out_specs=(
            P("fsdp", "ctx", None),
            P("fsdp", "ctx", None),
            P(("ctx", "fsdp")),
            P(("ctx", "fsdp")),
            P(("ctx", "fsdp")),
        ),
        check_vma=False,
    )
```
